32 devices in a mesh: wide: 8 (over y, x, core), narrow: 4 (over z).
Axes of the slice: x: 2, y: 2, z: 4, core: 2. Of those that a mesh axis runs over, the one named last changes fastest.
Arguments:
- tokens: bfloat16 [4096, 1280], P(('wide', 'narrow')), may hold values from -6 to 6
- seq_ids: int32 [4096], P(('wide', 'narrow')), may hold values from 0 to 4, as said below
- routes: int32 [4096, 7], P(('wide', 'narrow')), may hold values from 0 to 14, all different within a row; in each aligned block of 128 rows (0 to 127, 128 to 255, ...) at most 72 rows name the same one
- cotangent: bfloat16 [4096, 1280], P(('wide', 'narrow')), may hold values from -6 to 6
- gain_attn: bfloat16 [1280], P(('wide', 'narrow')), may hold values from 0.5 to 1.5
- w_qkv: bfloat16 [1280, 3840], P(('wide', 'narrow')), may hold values from -0.15625 to 0.15625
- w_out: bfloat16 [1280, 1280], P(('wide', 'narrow')), may hold values from -2.5 to 2.5
- gain_ffn: bfloat16 [1280], P(('wide', 'narrow')), may hold values from 0.5 to 1.5
- w_router: bfloat16 [1280, 15], P(('wide', 'narrow')), may hold values from -0.078125 to 0.078125
- w_up: bfloat16 [1280, 16, 1792], P(('wide', 'narrow')), may hold values from -0.15625 to 0.15625
- w_down: bfloat16 [1280, 16, 896], P(('wide', 'narrow')), may hold values from -0.75 to 0.75
Outputs:
- output: bfloat16 [4096, 1280], P(('wide', 'narrow'))
- grad_tokens: bfloat16 [4096, 1280], P(('wide', 'narrow'))
- grad_gain_attn: float32 [1280], P('narrow')
- grad_qkv: float32 [1280, 3840], P('narrow')
- grad_out: float32 [1280, 1280], P('narrow')
- grad_gain_ffn: float32 [1280], P('narrow')
- grad_router: float32 [1280, 15], P('narrow')
- grad_up: float32 [1280, 16, 1792], P('narrow')
- grad_down: float32 [1280, 16, 896], P('narrow')
The draws below stay inside these ranges and needn't reach their ends.
Inputs may be any that keep to these rules, and one draw needn't show every extreme that they name: `seq_ids`: within each sequence of 512 rows the document numbers start at 0, never fall and rise by at most one from row to row. `routes`: each row names 7 different routed experts; among the rows of one device no expert is named more than 72 times.
All inputs are finite; a program needn't handle non-finite values.
Results may differ from the reference program's by a relative error of at most 0.02.
Values may be sent and summed in bfloat16 or wider, within the bound.
A program may use at most 448 MiB of HBM per device.

```python
import math
import jax
import jax.numpy as jnp
import numpy as np
from jax import lax

D = 1280
HEADS = 10
HEAD_DIM = 128
FF = 896
EXPERTS = 15
TOP = 7
TOK_DEV = 128
EXPERTS_ALL = 16
CAP = 72
TOKENS = 4096
N_NARROW = 4


def draw_seq_ids(key, part):
    key = jax.random.fold_in(key, 11)
    seqlen = TOK_DEV * N_NARROW
    groups = TOKENS // seqlen
    key_first, key_last = jax.random.split(key)
    first_cuts = jax.random.randint(key_first, (groups, 2), 1, TOK_DEV)
    last_cuts = jax.random.randint(key_last, (groups, 2), seqlen - TOK_DEV + 1, seqlen)
    bounds = jnp.concatenate([first_cuts, last_cuts], axis=1)
    places = jnp.arange(seqlen, dtype=jnp.int32)
    doc_ids = jnp.sum((places[None, :, None] >= bounds[:, None, :]).astype(jnp.int32), axis=2)
    return doc_ids.reshape(groups * seqlen).astype(jnp.int32)


def steps_of(key, dims, cuts, smallest, largest):
    factor_of, own = 1.0, jax.random.fold_in(key, 6)
    for position, shards_of in cuts:
        draws = jnp.exp(jax.random.uniform(jax.random.fold_in(own, position), (shards_of,), jnp.float32, smallest / len(cuts), largest / len(cuts)))
        factor_of = factor_of * jnp.repeat(draws, dims[position] // shards_of).reshape([-1 if axis == position else 1 for axis in range(len(dims))])
    return factor_of


def assign_block(key, own, number, rows, amount, top, limit, skew):
    sequence = jax.random.permutation(key, amount)
    crowded, usual = shares(amount, rows * top, limit, skew, True), shares(amount, rows * top, limit, skew, False)
    places = jnp.arange(amount)

    def named(tallies, rotation):
        used = int((tallies > 0).sum())
        fixed = max(1, used // 4)
        passed = fixed + (places - fixed + rotation * (used - fixed)) % max(1, amount - fixed)
        return jnp.zeros((amount,), jnp.int32).at[sequence[jnp.where(places < fixed, places, passed)]].set(jnp.asarray(tallies, jnp.int32))

    tallies = jnp.where(number % 4 == 0, named(crowded, number // 4), named(usual, number - number // 4 - 1))
    mixed = jax.random.permutation(jax.random.fold_in(own, 3), amount)
    source_of, receiver = mixed[0:amount // 2 * 2:2], mixed[1:amount // 2 * 2:2]
    slack = jnp.minimum(tallies[source_of] - 1, limit - tallies[receiver]) // 2
    slack = jnp.where((source_of == sequence[0]) | (receiver == sequence[0]) | (tallies[receiver] == 0), 0, jnp.maximum(slack, 0))
    passed = jax.random.randint(jax.random.fold_in(own, 4), (amount // 2,), 0, 1 << 20) % (slack + 1)
    tallies = tallies.at[source_of].add(-passed).at[receiver].add(passed)
    labels = jnp.searchsorted(jnp.cumsum(tallies), jnp.arange(rows * top), side="right").astype(jnp.int32)
    listing = labels.reshape(top, rows).T
    listing = listing[jax.random.permutation(jax.random.fold_in(own, 1), rows)]
    rotation = jax.random.randint(jax.random.fold_in(own, 2), (rows, 1), 0, top)
    return jnp.take_along_axis(listing, (jnp.arange(top)[None, :] + rotation) % top, axis=1)


def shares(number_of, total, bound, slope, full):
    weights = [(1 << 20) // math.isqrt(rank ** slope) + 1 for rank in range(1, number_of + 1)]
    largest = bound if full else min(bound, max(-(-total // number_of), total * weights[0] // sum(weights)))
    least = 1 if total - largest >= number_of - 1 else 0
    counts, rest = [largest] + [least] * (number_of - 1), total - largest - least * (number_of - 1)
    while rest > 0:
        movable = [i for i in range(1, number_of) if counts[i] < largest] or [i for i in range(1, number_of) if counts[i] < bound]
        whole, budget = sum([weights[i] for i in movable]), rest
        for i in movable:
            addition = min(bound - counts[i], max(1, budget * weights[i] // whole), rest)
            counts[i] = counts[i] + addition
            rest = rest - addition
    return np.array(counts)


def gaussian(stream_key, dims, width, most, cuts=(), kind=jnp.bfloat16):
    entries = width * jax.random.normal(stream_key, dims, jnp.float32)
    if cuts:
        entries = entries * steps_of(stream_key, dims, cuts, -0.22, 0.18)
    return jnp.clip(entries, -most, most).astype(kind)


def setup_inputs(seed: int = 0) -> dict:
    seeds = jax.random.split(jax.random.key(seed), 12)
    tokens = gaussian(seeds[0], (TOKENS, D), 1.0, 6.0, ((0, 32),))
    seq_ids = draw_seq_ids(jax.random.fold_in(seeds[11], 71), 0)
    routes_keys = jax.random.split(jax.random.fold_in(seeds[2], 1), TOKENS // TOK_DEV)
    routes_turns = jax.random.permutation(jax.random.fold_in(seeds[2], 3), TOKENS // TOK_DEV)
    routes = jax.vmap(lambda own, number: assign_block(jax.random.fold_in(seeds[2], 2), own, number, TOK_DEV, EXPERTS, TOP, CAP, 0))(routes_keys, routes_turns).reshape((TOKENS, TOP))
    cotangent = gaussian(seeds[3], (TOKENS, D), 1.0, 6.0, ((0, 32),))
    gain_attn = jnp.clip(1.0 + 0.1 * jax.random.normal(seeds[4], (D,), jnp.float32), 0.5, 1.5).astype(jnp.bfloat16)
    w_qkv = gaussian(seeds[5], (D, 3 * D), D ** -0.5, 0.15625, ((0, 32),))
    w_out = gaussian(seeds[6], (D, D), (max(D // 256, 1)) ** -0.5, 2.5, ((0, 32),))
    gain_ffn = jnp.clip(1.0 + 0.1 * jax.random.normal(seeds[7], (D,), jnp.float32), 0.5, 1.5).astype(jnp.bfloat16)
    w_router = gaussian(seeds[8], (D, EXPERTS), (4 * D) ** -0.5, 0.078125, ((0, 32),))
    w_up = gaussian(seeds[9], (D, EXPERTS_ALL, 2 * FF), D ** -0.5, 0.15625, ((0, 32),))
    w_down = gaussian(seeds[10], (D, EXPERTS_ALL, FF), (max(FF // 16, 1)) ** -0.5, 0.75, ((0, 32),))
    return {"tokens": tokens, "seq_ids": seq_ids, "routes": routes, "cotangent": cotangent, "gain_attn": gain_attn, "w_qkv": w_qkv, "w_out": w_out, "gain_ffn": gain_ffn, "w_router": w_router, "w_up": w_up, "w_down": w_down}


@jax.custom_vjp
def low(v):
    return lax.optimization_barrier(v.astype(jnp.bfloat16)).astype(jnp.float32)

@jax.custom_vjp
def low_back(v):
    return v

def low_keep(v):
    return (low(v), None)

def low_pass(kept, grad):
    return (grad,)

def back_keep(v):
    return (v, None)

def back_low(kept, grad):
    return (low(grad),)
low.defvjp(low_keep, low_pass)
low_back.defvjp(back_keep, back_low)
highest = lax.Precision.HIGHEST

def rms_inverse(values):
    return lax.rsqrt(lax.optimization_barrier(jnp.mean(values * values, axis=-1, keepdims=True)) + 1e-06)

def rotary(positions):
    half_dim = HEAD_DIM // 2
    frequency = 10000.0 ** (-jnp.arange(half_dim, dtype=jnp.float32) / half_dim)
    angles = positions[:, None] * frequency[None, :]
    cosine = jnp.concatenate([jnp.cos(angles), jnp.cos(angles)], axis=1)[:, None, :]
    sine_table = jnp.concatenate([jnp.sin(angles), jnp.sin(angles)], axis=1)[:, None, :]
    return (cosine, sine_table)

def rotate(values, cosine, sine_table):
    half_dim = values.shape[-1] // 2
    turned = jnp.concatenate([-values[..., half_dim:], values[..., :half_dim]], axis=-1)
    return values * cosine + turned * sine_table

def group_attention(first_in, group_ids, w_qkv, w_out):
    seqlen = first_in.shape[0]
    projected = low_back(jnp.dot(first_in, w_qkv, precision=highest))
    places = jnp.arange(seqlen, dtype=jnp.int32)
    cosine, sine_table = rotary(places.astype(jnp.float32))
    query_rows = low(rotate(projected[:, :D].reshape(seqlen, HEADS, HEAD_DIM), cosine, sine_table) * HEAD_DIM ** (-0.5))
    key_rows = low(rotate(projected[:, D:2 * D].reshape(seqlen, HEADS, HEAD_DIM), cosine, sine_table))
    value_rows = low(projected[:, 2 * D:].reshape(seqlen, HEADS, HEAD_DIM))
    scores = low_back(jnp.einsum('qhd,khd->hqk', query_rows, key_rows, precision=highest))
    allowed = (places[:, None] >= places[None, :]) & (group_ids[:, None] == group_ids[None, :])
    scores = jnp.where(allowed[None], scores, -1e+30)
    attn_weights = low(jax.nn.softmax(scores, axis=-1))
    mixed = low_back(low(jnp.einsum('hqk,khd->qhd', attn_weights, value_rows, precision=highest)))
    return low_back(jnp.dot(mixed.reshape(seqlen, D), w_out, precision=highest))

def block_experts(second_in, route_block, w_router, w_up, w_down):
    row_count = second_in.shape[0]
    logits = low_back(jnp.dot(second_in, w_router, precision=highest))
    router_probs = jax.nn.softmax(logits, axis=-1)
    gate_weights = jnp.take_along_axis(router_probs, route_block, axis=1)
    member = lax.optimization_barrier(jnp.sum((route_block[:, :, None] == jnp.arange(EXPERTS, dtype=jnp.int32)[None, None, :]).astype(jnp.int32), axis=1))
    before = jnp.cumsum(member, axis=0) - member
    slot_of = jnp.take_along_axis(before, route_block, axis=1).astype(jnp.int32)
    hits = (member.T[:, None, :] == 1) & (before.T[:, None, :] == jnp.arange(CAP, dtype=jnp.int32)[None, :, None])
    token_index = lax.optimization_barrier(jnp.sum(jnp.where(hits, jnp.arange(row_count, dtype=jnp.int32)[None, None, :], 0), axis=2)).astype(jnp.int32)
    filled = jnp.any(hits, axis=2)
    gathered_in = jnp.where(filled[..., None], second_in[token_index], 0.0)
    gate_up = low_back(jnp.einsum('ecd,def->ecf', gathered_in, w_up[:, 1:], precision=highest))
    activated = low(jax.nn.silu(gate_up[..., :FF]) * gate_up[..., FF:])
    expert_rows = low_back(low(jnp.einsum('ecf,def->ecd', activated, w_down[:, 1:], precision=highest)))
    picked = expert_rows[route_block, slot_of]
    routed = lax.optimization_barrier(jnp.sum(gate_weights[..., None] * picked, axis=1))
    shared_up = low_back(jnp.dot(second_in, w_up[:, 0], precision=highest))
    shared_act = low(jax.nn.silu(shared_up[:, :FF]) * shared_up[:, FF:])
    shared_out = low_back(jnp.einsum('tf,df->td', shared_act, w_down[:, 0], precision=highest))
    return shared_out + routed

def forward(tokens, seq_ids, routes, gain_attn, w_qkv, w_out, gain_ffn, w_router, w_up, w_down):
    first_in = low(tokens * rms_inverse(tokens) * gain_attn)
    seqlen = TOK_DEV * N_NARROW
    groups = tokens.shape[0] // seqlen
    attend = jax.checkpoint(lambda pieces: group_attention(pieces[0], pieces[1], w_qkv, w_out))
    attention = lax.map(attend, (first_in.reshape(groups, seqlen, D), seq_ids.reshape(groups, seqlen)))
    middle = tokens + attention.reshape(-1, D)
    second_in = low(middle * rms_inverse(middle) * gain_ffn)
    blocks = tokens.shape[0] // TOK_DEV
    mix_experts = jax.checkpoint(lambda pieces: block_experts(pieces[0], pieces[1], w_router, w_up, w_down))
    expert_out = lax.map(mix_experts, (second_in.reshape(blocks, TOK_DEV, D), routes.reshape(blocks, TOK_DEV, TOP)))
    return middle + expert_out.reshape(-1, D)

def reference(tokens, seq_ids, routes, cotangent, gain_attn, w_qkv, w_out, gain_ffn, w_router, w_up, w_down):

    def layer(tok_f, gain_a, qkv_f, out_f, gain_f, router_f, up_f, down_f):
        return forward(tok_f, seq_ids, routes, gain_a, qkv_f, out_f, gain_f, router_f, up_f, down_f)
    result, pullback = jax.vjp(layer, tokens.astype(jnp.float32), gain_attn.astype(jnp.float32), w_qkv.astype(jnp.float32), w_out.astype(jnp.float32), gain_ffn.astype(jnp.float32), w_router.astype(jnp.float32), w_up.astype(jnp.float32), w_down.astype(jnp.float32))
    grads = pullback(cotangent.astype(jnp.float32))
    return (result.astype(jnp.bfloat16), grads[0].astype(jnp.bfloat16), grads[1], grads[2], grads[3], grads[4], grads[5], grads[6], grads[7])
```

```python
import jax
import jax.numpy as jnp
from jax import lax
from jax.experimental import pallas as pl
from jax.experimental.pallas import tpu as pltpu
from jax.sharding import PartitionSpec as P

HEADS = 10
HEAD_DIM = 128
FF = 896
CAP = 72


epsilon = 1e-06


def shortened(x):
    return jax.tree.map(lambda a: a.astype(jnp.bfloat16) if a.dtype == jnp.float32 else a, x)


def rms_inverse(values):
    return lax.rsqrt(jnp.mean(values * values, axis=-1, keepdims=True) + epsilon)


def rotary(positions, head_size):
    half_dim = head_size // 2
    frequency = 10000.0 ** (-jnp.arange(half_dim, dtype=jnp.float32) / half_dim)
    angles = positions[:, None] * frequency[None, :]
    cosine = jnp.concatenate([jnp.cos(angles), jnp.cos(angles)], axis=1)[:, None, :]
    sine_table = jnp.concatenate([jnp.sin(angles), jnp.sin(angles)], axis=1)[:, None, :]
    return (cosine, sine_table)


def rotate(values, cosine, sine_table):
    half_dim = values.shape[-1] // 2
    turned = jnp.concatenate([-values[..., half_dim:], values[..., :half_dim]], axis=-1)
    return values * cosine + turned * sine_table


def rotate_back(grads, cosine, sine_table):
    half_dim = grads.shape[-1] // 2
    scaled = grads * sine_table
    turned = jnp.concatenate([scaled[..., half_dim:], -scaled[..., :half_dim]], axis=-1)
    return grads * cosine + turned


def expert_weight_terms(
    routed_in, routed_grad, shared_in, shared_grad, slot_grads, slot_acts, shared_grads, shared_acts
):
    up_routed = jnp.einsum(
        "ecd,ecf->def", routed_in, slot_grads, preferred_element_type=jnp.float32
    )
    up_shared = jnp.einsum("td,tf->df", shared_in, shared_grads, preferred_element_type=jnp.float32)
    down_routed = jnp.einsum(
        "ecd,ecf->def", routed_grad, slot_acts, preferred_element_type=jnp.float32
    )
    down_shared = jnp.einsum(
        "td,tf->df", shared_grad, shared_acts, preferred_element_type=jnp.float32
    )
    up_all = jnp.concatenate([up_shared[:, None], up_routed], axis=1)
    down_all = jnp.concatenate([down_shared[:, None], down_routed], axis=1)
    combined = jnp.concatenate([up_all, down_all], axis=2)
    return combined.reshape(combined.shape[0], -1)


def local(
    tokens, seq_ids, routes, cotangent, gain_attn, w_qkv, w_out, gain_ffn, w_router, w_up, w_down
):
    row_count = tokens.shape[0]
    model_width = tokens.shape[1]
    query_scale = HEAD_DIM ** (-0.5)
    hidden = FF
    capacity = CAP
    inputs = tokens.astype(jnp.float32)
    gain_one, qkv_weight, out_weight = (
        lax.all_gather(gain_attn, ("wide", "narrow"), axis=0, tiled=True),
        lax.all_gather(w_qkv, ("wide", "narrow"), axis=0, tiled=True),
        lax.all_gather(w_out, ("wide", "narrow"), axis=0, tiled=True),
    )
    inverse_one = rms_inverse(inputs)
    normed_one = inputs * inverse_one
    first_in = (normed_one * gain_one.astype(jnp.float32)).astype(jnp.bfloat16)
    projected = jnp.dot(first_in, qkv_weight, preferred_element_type=jnp.float32)
    offset = lax.axis_index("narrow") * row_count
    query_pos = offset + jnp.arange(row_count, dtype=jnp.int32)
    cosine, sine_table = rotary(query_pos.astype(jnp.float32), HEAD_DIM)
    query_rows = (
        rotate(projected[:, :model_width].reshape(row_count, HEADS, HEAD_DIM), cosine, sine_table)
        * query_scale
    ).astype(jnp.bfloat16)
    key_rows = (
        rotate(
            projected[:, model_width : 2 * model_width].reshape(row_count, HEADS, HEAD_DIM),
            cosine,
            sine_table,
        )
        .astype(jnp.bfloat16)
        .reshape(row_count, model_width)
    )
    value_rows = projected[:, 2 * model_width :].astype(jnp.bfloat16)
    all_keys, all_values, all_ids = (
        lax.all_gather(key_rows, "narrow", axis=0, tiled=True),
        lax.all_gather(value_rows, "narrow", axis=0, tiled=True),
        lax.all_gather(seq_ids.astype(jnp.bfloat16), "narrow", axis=0, tiled=True),
    )
    seqlen = all_keys.shape[0]
    block_len = min(512, seqlen)
    num_blocks = seqlen // block_len
    own_ids = seq_ids.astype(jnp.float32)

    def block_parts(block_index):
        first_row = block_index * block_len
        key_pos = first_row + jnp.arange(block_len, dtype=jnp.int32)
        key_ids = lax.dynamic_slice_in_dim(all_ids, first_row, block_len, 0).astype(jnp.float32)
        allowed = (key_pos[None, :] <= query_pos[:, None]) & (key_ids[None, :] == own_ids[:, None])
        key_block = lax.dynamic_slice_in_dim(all_keys, first_row, block_len, 0).reshape(
            block_len, HEADS, HEAD_DIM
        )
        value_block = lax.dynamic_slice_in_dim(all_values, first_row, block_len, 0).reshape(
            block_len, HEADS, HEAD_DIM
        )
        scores = jnp.einsum(
            "qhd,khd->hqk", query_rows, key_block, preferred_element_type=jnp.float32
        )
        return (allowed[None], key_block, value_block, scores)

    def max_step(state_pair, block_index):
        running_max, running_sum = state_pair
        allowed, key_block, value_block, scores = block_parts(block_index)
        masked = jnp.where(allowed, scores, -1e30)
        new_max = jnp.maximum(running_max, jnp.max(masked, axis=2))
        added = jnp.sum(jnp.where(allowed, jnp.exp(masked - new_max[..., None]), 0.0), axis=2)
        return ((new_max, running_sum * jnp.exp(running_max - new_max) + added), None)

    start_max = jnp.full((HEADS, row_count), -1e30, jnp.float32)
    start_sum = jnp.zeros((HEADS, row_count), jnp.float32)
    (top_score, exp_total), unused = lax.scan(
        max_step, (start_max, start_sum), jnp.arange(num_blocks)
    )
    log_total = top_score + jnp.log(exp_total)

    def out_step(accum, block_index):
        allowed, key_block, value_block, scores = block_parts(block_index)
        weights_low = jnp.where(allowed, jnp.exp(scores - log_total[..., None]), 0.0).astype(
            jnp.bfloat16
        )
        return (
            accum
            + jnp.einsum(
                "hqk,khd->hqd", weights_low, value_block, preferred_element_type=jnp.float32
            ),
            None,
        )

    accum_start = jnp.zeros((HEADS, row_count, HEAD_DIM), jnp.float32)
    mixed_heads, unused = lax.scan(out_step, accum_start, jnp.arange(num_blocks))
    mixed_exact = jnp.transpose(mixed_heads, (1, 0, 2))
    mixed = mixed_exact.reshape(row_count, model_width).astype(jnp.bfloat16)
    middle = inputs + jnp.dot(mixed, out_weight, preferred_element_type=jnp.float32)
    gain_two, router_weight, up_weight, down_weight = (
        lax.all_gather(gain_ffn, ("wide", "narrow"), axis=0, tiled=True),
        lax.all_gather(w_router, ("wide", "narrow"), axis=0, tiled=True),
        lax.all_gather(w_up, ("wide", "narrow"), axis=0, tiled=True),
        lax.all_gather(w_down, ("wide", "narrow"), axis=0, tiled=True),
    )
    inverse_two = rms_inverse(middle)
    normed_two = middle * inverse_two
    second_in = (normed_two * gain_two.astype(jnp.float32)).astype(jnp.bfloat16)
    logits = jnp.dot(second_in, router_weight, preferred_element_type=jnp.float32)
    router_probs = jax.nn.softmax(logits, axis=-1)
    experts = logits.shape[1]
    choose = routes[:, :, None] == jnp.arange(experts, dtype=jnp.int32)[None, None, :]
    member = jnp.sum(choose.astype(jnp.float32), axis=1)
    earlier = (jnp.arange(row_count)[:, None] > jnp.arange(row_count)[None, :]).astype(jnp.bfloat16)
    before = jnp.dot(earlier, member.astype(jnp.bfloat16), preferred_element_type=jnp.float32)
    slot_hit = (member.T[:, None, :] > 0.5) & (
        before.T[:, None, :] == jnp.arange(capacity, dtype=jnp.float32)[None, :, None]
    )
    dispatch = slot_hit.astype(jnp.bfloat16)
    gathered_in = jnp.einsum(
        "ect,td->ecd", dispatch, second_in, preferred_element_type=jnp.float32
    ).astype(jnp.bfloat16)
    gate_weights = router_probs * member
    gate_up = jnp.einsum(
        "ecd,def->ecf", gathered_in, up_weight[:, 1:], preferred_element_type=jnp.float32
    )
    gate_part = gate_up[..., :hidden]
    up_part = gate_up[..., hidden:]
    activated = (jax.nn.silu(gate_part) * up_part).astype(jnp.bfloat16)
    expert_rows = jnp.einsum(
        "ecf,def->ecd", activated, down_weight[:, 1:], preferred_element_type=jnp.float32
    ).astype(jnp.bfloat16)
    selected = jnp.einsum("ect,ecd->etd", dispatch, expert_rows, preferred_element_type=jnp.float32)
    routed = jnp.sum(gate_weights.T[:, :, None] * selected, axis=0)
    shared_up = jnp.dot(second_in, up_weight[:, 0], preferred_element_type=jnp.float32)
    shared_gate = shared_up[:, :hidden]
    shared_lin = shared_up[:, hidden:]
    shared_act = (jax.nn.silu(shared_gate) * shared_lin).astype(jnp.bfloat16)
    shared_out = jnp.einsum(
        "tf,df->td", shared_act, down_weight[:, 0], preferred_element_type=jnp.float32
    )
    output = (middle + shared_out + routed).astype(jnp.bfloat16)
    gain_two, router_weight, up_weight, down_weight = (
        lax.all_gather(gain_ffn, ("wide", "narrow"), axis=0, tiled=True),
        lax.all_gather(w_router, ("wide", "narrow"), axis=0, tiled=True),
        lax.all_gather(w_up, ("wide", "narrow"), axis=0, tiled=True),
        lax.all_gather(w_down, ("wide", "narrow"), axis=0, tiled=True),
    )
    grad_output = cotangent.astype(jnp.float32)
    slot_token = jnp.sum(
        jnp.where(slot_hit, jnp.arange(row_count, dtype=jnp.int32)[None, None, :], 0), axis=2
    )
    slot_gate = jnp.sum(jnp.where(slot_hit, gate_weights.T[:, None, :], 0.0), axis=2)
    grad_rows = (slot_gate[..., None] * grad_output[slot_token]).astype(jnp.bfloat16)
    grad_probs = jnp.sum(selected * grad_output[None], axis=2).T * member
    grad_logits = (
        router_probs * (grad_probs - jnp.sum(router_probs * grad_probs, axis=1, keepdims=True))
    ).astype(jnp.bfloat16)
    grad_act = jnp.einsum(
        "ecd,def->ecf", grad_rows, down_weight[:, 1:], preferred_element_type=jnp.float32
    )
    sigmoid_gate = jax.nn.sigmoid(gate_part)
    grad_gate_up = jnp.concatenate(
        [
            grad_act * up_part * sigmoid_gate * (1.0 + gate_part * (1.0 - sigmoid_gate)),
            grad_act * jax.nn.silu(gate_part),
        ],
        axis=-1,
    ).astype(jnp.bfloat16)
    grad_gathered = jnp.einsum(
        "ecf,def->ecd", grad_gate_up, up_weight[:, 1:], preferred_element_type=jnp.float32
    )
    slot_index = jnp.sum(jnp.where(choose, before[:, None, :], 0.0), axis=2).astype(jnp.int32)
    flat_index = routes * capacity + slot_index
    grad_second = jnp.sum(grad_gathered.reshape(-1, model_width)[flat_index], axis=1)
    grad_shared_act = jnp.einsum(
        "td,df->tf", cotangent, down_weight[:, 0], preferred_element_type=jnp.float32
    )
    sigmoid_shared = jax.nn.sigmoid(shared_gate)
    grad_shared_up = jnp.concatenate(
        [
            grad_shared_act
            * shared_lin
            * sigmoid_shared
            * (1.0 + shared_gate * (1.0 - sigmoid_shared)),
            grad_shared_act * jax.nn.silu(shared_gate),
        ],
        axis=-1,
    ).astype(jnp.bfloat16)
    grad_second = grad_second + jnp.einsum(
        "tf,df->td", grad_shared_up, up_weight[:, 0], preferred_element_type=jnp.float32
    )
    grad_second = grad_second + jnp.einsum(
        "te,de->td", grad_logits, router_weight, preferred_element_type=jnp.float32
    )
    grad_normed_two = grad_second * gain_two.astype(jnp.float32)
    grad_gain_two = jnp.sum(grad_second * normed_two, axis=0)
    grad_middle = grad_output + inverse_two * (
        grad_normed_two
        - normed_two * jnp.mean(grad_normed_two * normed_two, axis=-1, keepdims=True)
    )
    grad_router = jnp.einsum(
        "td,te->de", second_in, grad_logits, preferred_element_type=jnp.float32
    )
    narrow_rows = model_width // lax.axis_size("narrow")
    routed_cols, grad_cols, shared_cols, cotangent_cols = (
        lax.all_to_all(gathered_in, "narrow", split_axis=2, concat_axis=1, tiled=True),
        lax.all_to_all(grad_rows, "narrow", split_axis=2, concat_axis=1, tiled=True),
        lax.all_to_all(second_in[None], "narrow", split_axis=2, concat_axis=1, tiled=True),
        lax.all_to_all(cotangent[None], "narrow", split_axis=2, concat_axis=1, tiled=True),
    )
    slot_grads, slot_acts, shared_grads, shared_acts = (
        lax.all_gather(grad_gate_up, "narrow", axis=1, tiled=True),
        lax.all_gather(activated, "narrow", axis=1, tiled=True),
        lax.all_gather(grad_shared_up[None], "narrow", axis=1, tiled=True),
        lax.all_gather(shared_act[None], "narrow", axis=1, tiled=True),
    )
    expert_grads = expert_weight_terms(
        routed_cols,
        grad_cols,
        shared_cols[0],
        cotangent_cols[0],
        slot_grads,
        slot_acts,
        shared_grads[0],
        shared_acts[0],
    )
    gain_one, qkv_weight, out_weight = (
        lax.all_gather(gain_attn, ("wide", "narrow"), axis=0, tiled=True),
        lax.all_gather(w_qkv, ("wide", "narrow"), axis=0, tiled=True),
        lax.all_gather(w_out, ("wide", "narrow"), axis=0, tiled=True),
    )
    grad_attention = grad_middle.astype(jnp.bfloat16)
    grad_out_weight = jnp.einsum(
        "td,te->de", mixed, grad_attention, preferred_element_type=jnp.float32
    )
    grad_mixed = jnp.einsum(
        "te,de->td", grad_attention, out_weight, preferred_element_type=jnp.float32
    ).astype(jnp.bfloat16)
    grad_heads = grad_mixed.reshape(row_count, HEADS, HEAD_DIM)
    row_delta = jnp.sum(grad_heads.astype(jnp.float32) * mixed_exact, axis=2).T

    def back_step(grad_query, block_index):
        allowed, key_block, value_block, scores = block_parts(block_index)
        weights_exact = jnp.where(allowed, jnp.exp(scores - log_total[..., None]), 0.0)
        weights_low = weights_exact.astype(jnp.bfloat16)
        grad_value = jnp.einsum(
            "hqk,qhd->khd", weights_low, grad_heads, preferred_element_type=jnp.float32
        )
        grad_weights = jnp.einsum(
            "qhd,khd->hqk", grad_heads, value_block, preferred_element_type=jnp.float32
        )
        grad_scores = (weights_exact * (grad_weights - row_delta[..., None])).astype(jnp.bfloat16)
        grad_query = grad_query + jnp.einsum(
            "hqk,khd->qhd", grad_scores, key_block, preferred_element_type=jnp.float32
        )
        grad_key = jnp.einsum(
            "hqk,qhd->khd", grad_scores, query_rows, preferred_element_type=jnp.float32
        )
        return (
            grad_query,
            (grad_key.reshape(block_len, model_width), grad_value.reshape(block_len, model_width)),
        )

    query_start = jnp.zeros((row_count, HEADS, HEAD_DIM), jnp.float32)
    grad_query, (key_blocks, value_blocks) = lax.scan(
        back_step, query_start, jnp.arange(num_blocks)
    )
    key_partial = key_blocks.reshape(seqlen, model_width)
    value_partial = value_blocks.reshape(seqlen, model_width)
    grad_keys, grad_values = (
        lax.psum_scatter(
            key_partial.astype(jnp.bfloat16), "narrow", scatter_dimension=0, tiled=True
        ).astype(jnp.float32),
        lax.psum_scatter(
            value_partial.astype(jnp.bfloat16), "narrow", scatter_dimension=0, tiled=True
        ).astype(jnp.float32),
    )
    grad_query_raw = rotate_back(grad_query, cosine, sine_table) * query_scale
    grad_key_raw = rotate_back(grad_keys.reshape(row_count, HEADS, HEAD_DIM), cosine, sine_table)
    grad_projected = jnp.concatenate(
        [
            grad_query_raw.reshape(row_count, model_width),
            grad_key_raw.reshape(row_count, model_width),
            grad_values,
        ],
        axis=1,
    ).astype(jnp.bfloat16)
    grad_qkv_weight = jnp.einsum(
        "td,tf->df", first_in, grad_projected, preferred_element_type=jnp.float32
    )
    grad_first = jnp.einsum(
        "tf,df->td", grad_projected, qkv_weight, preferred_element_type=jnp.float32
    )
    grad_normed_one = grad_first * gain_one.astype(jnp.float32)
    grad_gain_one = jnp.sum(grad_first * normed_one, axis=0)
    grad_inputs = grad_middle + inverse_one * (
        grad_normed_one
        - normed_one * jnp.mean(grad_normed_one * normed_one, axis=-1, keepdims=True)
    )
    dense_parts = (
        lax.psum_scatter(
            grad_gain_one.astype(jnp.bfloat16), "narrow", scatter_dimension=0, tiled=True
        ).astype(jnp.float32),
        lax.psum_scatter(
            grad_qkv_weight.astype(jnp.bfloat16), "narrow", scatter_dimension=0, tiled=True
        ).astype(jnp.float32),
        lax.psum_scatter(
            grad_out_weight.astype(jnp.bfloat16), "narrow", scatter_dimension=0, tiled=True
        ).astype(jnp.float32),
        lax.psum_scatter(
            grad_gain_two.astype(jnp.bfloat16), "narrow", scatter_dimension=0, tiled=True
        ).astype(jnp.float32),
        lax.psum_scatter(
            grad_router.astype(jnp.bfloat16), "narrow", scatter_dimension=0, tiled=True
        ).astype(jnp.float32),
    )
    summed = jax.tree.map(
        lambda part: part.astype(jnp.float32),
        lax.psum(shortened((expert_grads,) + tuple(dense_parts)), "wide"),
    )
    expert_grads = summed[0]
    dense_parts = summed[1:]
    gain_one_sum, qkv_sum, out_sum, gain_two_sum, router_sum = dense_parts
    expert_table = expert_grads.reshape(narrow_rows, up_weight.shape[1], 3 * hidden)
    up_sum = expert_table[:, :, : 2 * hidden]
    down_sum = expert_table[:, :, 2 * hidden :]
    return (
        output,
        grad_inputs.astype(jnp.bfloat16),
        gain_one_sum,
        qkv_sum,
        out_sum,
        gain_two_sum,
        router_sum,
        up_sum,
        down_sum,
    )


PLANES = 4
WINDOW = 3
STARTS = (0, 3, 6, 7)
KEEP = ((0, 3), (0, 3), (0, 2), (1, 3))
MESH_IDS = pl.DeviceIdType.MESH
BF16 = jnp.bfloat16
F32 = jnp.float32


def place():
    w = lax.axis_index("wide")
    z = lax.axis_index("narrow")
    return w, z


def other_plane(z, step):
    return lax.rem(z + step, PLANES), lax.rem(z + PLANES - step, PLANES)


class Net:
    def __init__(self, send_sems, recv_sems):
        self.send_sems, self.recv_sems, self.used, self.started = send_sems, recv_sems, 0, []

    def send(self, src, dst, device):
        copy = pltpu.make_async_remote_copy(
            src_ref=src,
            dst_ref=dst,
            send_sem=self.send_sems.at[self.used],
            recv_sem=self.recv_sems.at[self.used],
            device_id=device,
            device_id_type=MESH_IDS,
        )
        self.used += 1
        copy.start()
        self.started.append(copy)
        return copy

    def keep(self, src, dst):
        copy = pltpu.make_async_copy(src, dst, self.send_sems.at[self.used])
        self.used += 1
        copy.start()
        return copy

    def finish(self):
        for copy in self.started:
            copy.wait_send()


def greet(w, z):
    barrier = pltpu.get_barrier_semaphore()
    peers = [(w, lax.rem(z + step, PLANES)) for step in (1, 2, 3)]
    peers += [(w ^ flip, z) for flip in (1, 2, 4, 6)]
    for peer in peers:
        pl.semaphore_signal(barrier, inc=1, device_id=peer, device_id_type=MESH_IDS)
    pl.semaphore_wait(barrier, len(peers))


class PlaneGather:
    def __init__(self, net, w, z, slot, number, cores):
        self.net, self.w, self.z, self.slot, self.cores = net, w, z, slot, cores
        self.first, self.second = (2, 4) if number % 2 == 0 else (4, 2)

    def push(self, slot_of, flip):
        ref = self.slot(slot_of)
        return self.net.send(ref, ref, (self.w ^ flip, self.z))

    def begin(self):
        self.direct = {flip: self.push(self.w, flip) for flip in (2, 4)}
        self.core = [self.push(self.w, 1)] if self.cores else []

    def relay(self):
        self.direct[self.first].wait_recv()
        self.across = self.push(self.w ^ self.first, self.second)
        if self.cores:
            self.core.append(self.push(self.w ^ self.first, 1))
        self.direct[self.second].wait_recv()
        if self.cores:
            self.core.append(self.push(self.w ^ self.second, 1))

    def end(self):
        self.across.wait_recv()
        if self.cores:
            self.core.append(self.push(self.w ^ 6, 1))

    def settle(self):
        for copy in self.core:
            copy.wait_recv()


def comm_call(kernel, name, collective, out_shape, in_spaces, out_spaces, sems, scratch=(), moved=0):
    return pl.pallas_call(
        kernel,
        out_shape=out_shape,
        in_specs=[pl.BlockSpec(memory_space=space) for space in in_spaces],
        out_specs=[pl.BlockSpec(memory_space=space) for space in out_spaces],
        scratch_shapes=[
            *scratch,
            pltpu.SemaphoreType.DMA((sems,)),
            pltpu.SemaphoreType.DMA((sems,)),
        ],
        compiler_params=pltpu.CompilerParams(
            collective_id=collective, has_side_effects=True, vmem_limit_bytes=56 * 2**20
        ),
        name=name,
    )


def spread_inputs_kernel(
    tok, ids, wq, wo, we, cot, tok_o, ids_o, wq_o, wo_o, we_o, cot_o, hop, send_sems, recv_sems
):
    w, z = place()
    chip = w // 2
    greet(w, z)
    net = Net(send_sems, recv_sems)
    own = [
        net.keep(tok, tok_o.at[z]),
        net.keep(ids, ids_o.at[z]),
        net.keep(wq.at[z], wq_o.at[w, z]),
        net.keep(wo, wo_o.at[w, z]),
        net.keep(we.at[z, chip], we_o.at[w, z]),
        net.keep(cot, cot_o.at[chip, z]),
    ]
    ring, gathers = {}, {}
    for step in (1, 2, 3):
        to, _ = other_plane(z, step)
        ring["tok", step] = net.send(tok, tok_o.at[z], (w, to))
        ring["ids", step] = net.send(ids, ids_o.at[z], (w, to))
        ring["wq", step] = net.send(wq.at[to], wq_o.at[w, z], (w, to))
    for step in (1, 2, 3):
        to, _ = other_plane(z, step)
        for flip in (1, 2, 3):
            ring["we", step, flip] = net.send(
                we.at[to, chip ^ flip], hop.at[step - 1, flip - 1], (w, to)
            )
        ring["we", step, 0] = net.send(we.at[to, chip], we_o.at[w, z], (w, to))
        ring["cot", step] = net.send(cot, cot_o.at[chip, z], (w, to))
        ring["wo", step] = net.send(wo, wo_o.at[w, z], (w, to))
    for copy in own:
        copy.wait()
    weights = {}
    for flip in (1, 2, 3):
        weights[0, flip] = net.send(
            we.at[z, chip ^ flip], we_o.at[w, z], (w ^ (2 * flip), z)
        )
    core = [net.send(we_o.at[w, z], we_o.at[w, z], (w ^ 1, z))]

    def start_gather(kind, step):
        _, source = other_plane(z, step)
        slot = {
            "wq": lambda i: wq_o.at[i, source],
            "wo": lambda i: wo_o.at[i, source],
            "cot": lambda i: cot_o.at[i // 2, source],
        }[kind]
        gathers[kind, step] = PlaneGather(net, w, z, slot, step, kind != "cot")
        gathers[kind, step].begin()

    start_gather("wq", 0)
    start_gather("wo", 0)
    start_gather("cot", 0)
    for step in (1, 2, 3):
        ring["wq", step].wait_recv()
        start_gather("wq", step)
    for step in (0, 1, 2, 3):
        gathers["wq", step].relay()
    gathers["wo", 0].relay()
    gathers["cot", 0].relay()
    for step in (0, 1, 2, 3):
        gathers["wq", step].end()
    gathers["wo", 0].end()
    gathers["cot", 0].end()
    for step in (1, 2, 3):
        _, source = other_plane(z, step)
        for flip in (1, 2, 3):
            ring["we", step, flip].wait_recv()
            weights[step, flip] = net.send(
                hop.at[step - 1, flip - 1], we_o.at[w, source], (w ^ (2 * flip), z)
            )
        ring["we", step, 0].wait_recv()
        core.append(net.send(we_o.at[w, source], we_o.at[w, source], (w ^ 1, z)))
        for kind in ("cot", "wo"):
            ring[kind, step].wait_recv()
            start_gather(kind, step)
        ring["tok", step].wait_recv()
        ring["ids", step].wait_recv()
    for step in (0, 1, 2, 3):
        _, source = other_plane(z, step)
        for flip in (1, 2, 3):
            weights[step, flip].wait_recv()
            peer = w ^ (2 * flip)
            core.append(net.send(we_o.at[peer, source], we_o.at[peer, source], (w ^ 1, z)))
        if step:
            for kind in ("cot", "wo"):
                gathers[kind, step].relay()
    for step in (1, 2, 3):
        for kind in ("cot", "wo"):
            gathers[kind, step].end()
    for gather in gathers.values():
        gather.settle()
    for copy in core:
        copy.wait_recv()
    net.finish()


def spread_inputs(tok, ids, wq, wo, we, cot):
    rows, width = tok.shape
    own = wo.shape[0]
    hidden3 = we.shape[-1]
    shapes = [
        (PLANES, rows, width),
        (PLANES,) + ids.shape,
        (8, PLANES) + wq.shape[1:],
        (8, PLANES) + wo.shape,
        (8, PLANES, own, hidden3),
        (4, PLANES) + cot.shape,
        (3, 3, own, hidden3),
    ]
    out = comm_call(
        spread_inputs_kernel,
        "spread_inputs",
        1,
        [jax.ShapeDtypeStruct(shape, BF16) for shape in shapes],
        [pl.ANY] * 6,
        [pl.ANY] * 7,
        160,
    )(tok, ids, wq, wo, we, cot)
    return out[:6]


def swap_planes_kernel(x, out, send_sems, recv_sems):
    w, z = place()
    greet(w, z)
    net = Net(send_sems, recv_sems)
    own = net.keep(x.at[z], out.at[z])
    copies = []
    for step in (1, 2, 3):
        to, _ = other_plane(z, step)
        copies.append(net.send(x.at[to], out.at[z], (w, to)))
    own.wait()
    for copy in copies:
        copy.wait_recv()
    net.finish()


def swap_planes(x, collective):
    return comm_call(
        swap_planes_kernel,
        "swap_planes",
        collective,
        [jax.ShapeDtypeStruct(x.shape, x.dtype)],
        [pl.ANY],
        [pl.ANY],
        8,
    )(x)[0]


def gather_rows_kernel(x, out, send_sems, recv_sems):
    w, z = place()
    chip = w // 2
    greet(w, z)
    net = Net(send_sems, recv_sems)
    own = net.keep(x, out.at[chip, z])
    ring = {}
    for step in (1, 2, 3):
        to, _ = other_plane(z, step)
        ring[step] = net.send(x, out.at[chip, z], (w, to))
    own.wait()
    gathers = []
    for step in (0, 1, 2, 3):
        _, source = other_plane(z, step)
        if step:
            ring[step].wait_recv()
        gather = PlaneGather(
            net, w, z, lambda i, source=source: out.at[i // 2, source], step, False
        )
        gather.begin()
        gathers.append(gather)
    for gather in gathers:
        gather.relay()
    for gather in gathers:
        gather.end()
    net.finish()


def gather_rows(x, collective):
    return comm_call(
        gather_rows_kernel,
        "gather_rows",
        collective,
        [jax.ShapeDtypeStruct((4, PLANES) + x.shape, x.dtype)],
        [pl.ANY],
        [pl.ANY],
        40,
    )(x)[0]


def add_blocks(out, *terms):
    rows = out.shape[0]

    def body(i, carry):
        part = pl.ds(pl.multiple_of(i * 16, 16), 16)
        total = terms[0][part, :].astype(F32)
        for term in terms[1:]:
            total = total + term[part, :].astype(F32)
        out[part, :] = total.astype(out.dtype)
        return carry

    lax.fori_loop(0, rows // 16, body, 0)


def sum_rows_kernel(x, out, got_one, got_two, got_far, part, ready, send_sems, recv_sems):
    w, z = place()
    chip = w // 2
    greet(w, z)
    net = Net(send_sems, recv_sems)
    steps = (1, 2, 3, 0)
    near, cross, far = {}, {}, []
    for step in steps:
        to, _ = other_plane(z, step)
        first = 1 if step % 2 == 0 else 2
        peer = (w ^ (2 * first), z)
        near[step] = (
            net.send(x.at[chip ^ 3, to], got_one.at[step, 1], peer),
            net.send(x.at[chip ^ first, to], got_one.at[step, 0], peer),
        )
    for step in steps:
        to, _ = other_plane(z, step)
        first = 1 if step % 2 == 0 else 2
        second = 3 - first
        near[step][0].wait_recv()
        add_blocks(part.at[step], x.at[chip ^ second, to], got_one.at[step, 1])
        cross[step] = net.send(part.at[step], got_two.at[step], (w ^ (2 * second), z))
    for step in steps:
        to, _ = other_plane(z, step)
        near[step][1].wait_recv()
        cross[step].wait_recv()
        if step:
            add_blocks(ready.at[step - 1], x.at[chip, to], got_one.at[step, 0], got_two.at[step])
            far.append(net.send(ready.at[step - 1], got_far.at[step - 1], (w, to)))
    for copy in far:
        copy.wait_recv()
    add_blocks(
        out,
        x.at[chip, z],
        got_one.at[0, 0],
        got_two.at[0],
        got_far.at[0],
        got_far.at[1],
        got_far.at[2],
    )
    net.finish()


def sum_rows(x, collective):
    rows, width = x.shape[2:]
    return comm_call(
        sum_rows_kernel,
        "sum_rows",
        collective,
        [jax.ShapeDtypeStruct((rows, width), F32)],
        [pltpu.VMEM],
        [pltpu.VMEM],
        24,
        [
            pltpu.VMEM((4, 2, rows, width), BF16),
            pltpu.VMEM((4, rows, width), BF16),
            pltpu.VMEM((3, rows, width), BF16),
            pltpu.VMEM((4, rows, width), BF16),
            pltpu.VMEM((3, rows, width), BF16),
        ],
    )(x)[0]


def spread_grads_kernel(x, out, got, mine, total, send_sems, recv_sems):
    w, z = place()
    chip, core = w // 2, w % 2
    greet(w, z)
    net = Net(send_sems, recv_sems)
    steps = (1, 2, 3, 0)
    swap, load, ring, gathers = {}, {}, {}, []
    for step in steps:
        to, _ = other_plane(z, step)
        swap[step] = net.send(x.at[to, 1 - core], got.at[step], (w ^ 1, z))
        load[step] = net.keep(x.at[to, core], mine.at[step])
    for step in steps:
        to, _ = other_plane(z, step)
        load[step].wait()
        swap[step].wait_recv()
        add_blocks(total.at[step], mine.at[step], got.at[step])
        if step:
            ring[step] = net.send(total.at[step], out.at[chip, z, core], (w, to))
        else:
            own = net.keep(total.at[step], out.at[chip, z, core])
    own.wait()
    for step in (0, 1, 2, 3):
        _, source = other_plane(z, step)
        if step:
            ring[step].wait_recv()
        gather = PlaneGather(
            net, w, z, lambda i, source=source: out.at[i // 2, source, i % 2], step, True
        )
        gather.begin()
        gathers.append(gather)
    for gather in gathers:
        gather.relay()
    for gather in gathers:
        gather.end()
    for gather in gathers:
        gather.settle()
    net.finish()


def spread_grads(x, collective):
    rows, width = x.shape[2:]
    block = (4, rows, width)
    return comm_call(
        spread_grads_kernel,
        "spread_grads",
        collective,
        [jax.ShapeDtypeStruct((4, PLANES, 2, rows, width), BF16)],
        [pl.ANY],
        [pl.ANY],
        64,
        [pltpu.VMEM(block, BF16), pltpu.VMEM(block, BF16), pltpu.VMEM(block, BF16)],
    )(x)[0]


def sum_dense_kernel(
    first, x, first_o, q_o, o_o, got, mine, part, got_one, got_two, sent, ready, got_far, send_sems, recv_sems
):
    w, z = place()
    chip, core = w // 2, w % 2
    greet(w, z)
    net = Net(send_sems, recv_sems)
    steps = (1, 2, 3, 0)
    own = net.keep(first.at[z], first_o.at[z])
    swap, load, flow, near, cross, far, gathers = {}, {}, [], {}, {}, {}, []
    for step in steps:
        to, _ = other_plane(z, step)
        for kind in (0, 1):
            swap[step, kind] = net.send(x.at[kind, 1 - core, to], got.at[kind, step], (w ^ 1, z))
            load[step, kind] = net.keep(x.at[kind, core, to], mine.at[kind, step])
    for step in (1, 2, 3):
        to, _ = other_plane(z, step)
        flow.append(net.send(first.at[to], first_o.at[z], (w, to)))
    for step in steps:
        for kind in (0, 1):
            load[step, kind].wait()
            swap[step, kind].wait_recv()
            for block in range(4):
                add_blocks(
                    part.at[kind, step, block], mine.at[kind, step, block], got.at[kind, step, block]
                )
            first_flip = 1 + kind
            peer = (w ^ (2 * first_flip), z)
            near[step, kind] = (
                net.send(part.at[kind, step, chip ^ 3], got_one.at[kind, step, 1], peer),
                net.send(part.at[kind, step, chip ^ first_flip], got_one.at[kind, step, 0], peer),
            )
    for step in steps:
        for kind in (0, 1):
            second = 2 - kind
            near[step, kind][0].wait_recv()
            add_blocks(
                sent.at[kind, step], part.at[kind, step, chip ^ second], got_one.at[kind, step, 1]
            )
            cross[step, kind] = net.send(
                sent.at[kind, step], got_two.at[kind, step], (w ^ (2 * second), z)
            )
    for step in steps:
        to, _ = other_plane(z, step)
        for kind in (0, 1):
            near[step, kind][1].wait_recv()
            cross[step, kind].wait_recv()
            add_blocks(
                ready.at[kind, step],
                part.at[kind, step, chip],
                got_one.at[kind, step, 0],
                got_two.at[kind, step],
            )
        if step:
            far[step, 0] = net.send(ready.at[0, step], q_o.at[w, z], (w, to))
            far[step, 1] = net.send(ready.at[1, step], got_far.at[step - 1], (w, to))
        else:
            kept = net.keep(ready.at[0, 0], q_o.at[w, z])
    kept.wait()
    for step in (0, 1, 2, 3):
        _, source = other_plane(z, step)
        if step:
            far[step, 0].wait_recv()
        gather = PlaneGather(net, w, z, lambda i, source=source: q_o.at[i, source], step, True)
        gather.begin()
        gathers.append(gather)
    for step in (1, 2, 3):
        far[step, 1].wait_recv()
    add_blocks(mine.at[1, 0, 0], ready.at[1, 0], got_far.at[0], got_far.at[1], got_far.at[2])
    last = net.keep(mine.at[1, 0, 0], o_o.at[w])
    last.wait()
    gather = PlaneGather(net, w, z, lambda i: o_o.at[i], 0, True)
    gather.begin()
    gathers.append(gather)
    for gather in gathers:
        gather.relay()
    for gather in gathers:
        gather.end()
    for gather in gathers:
        gather.settle()
    own.wait()
    for copy in flow:
        copy.wait_recv()
    net.finish()


def sum_dense(first, x, collective):
    rows, width = x.shape[4:]
    block = (rows, width)
    return comm_call(
        sum_dense_kernel,
        "sum_dense",
        collective,
        [
            jax.ShapeDtypeStruct(first.shape, BF16),
            jax.ShapeDtypeStruct((8, PLANES) + block, BF16),
            jax.ShapeDtypeStruct((8,) + block, BF16),
        ],
        [pl.ANY, pl.ANY],
        [pl.ANY, pl.ANY, pl.ANY],
        140,
        [
            pltpu.VMEM((2, 4, 4) + block, BF16),
            pltpu.VMEM((2, 4, 4) + block, BF16),
            pltpu.VMEM((2, 4, 4) + block, BF16),
            pltpu.VMEM((2, 4, 2) + block, BF16),
            pltpu.VMEM((2, 4) + block, BF16),
            pltpu.VMEM((2, 4) + block, BF16),
            pltpu.VMEM((2, 4) + block, BF16),
            pltpu.VMEM((3,) + block, BF16),
        ],
    )(first, x)


def windows(x):
    size = WINDOW * HEAD_DIM
    return jnp.stack([x[:, s * HEAD_DIM : s * HEAD_DIM + size] for s in STARTS])


def from_windows(x):
    return jnp.concatenate(
        [x[p, :, a * HEAD_DIM : b * HEAD_DIM] for p, (a, b) in enumerate(KEEP)], axis=1
    )


def dot(a, b, dims, out=F32):
    return lax.dot_general(a, b, ((dims[0], dims[1]), ((), ())), preferred_element_type=F32).astype(out)


def expert_local(
    tokens, seq_ids, routes, cotangent, gain_attn, w_qkv, w_out, gain_ffn, w_router, w_up, w_down
):
    rows, width = tokens.shape
    own = w_out.shape[0]
    experts = w_router.shape[1]
    seqlen = PLANES * rows
    size = WINDOW * HEAD_DIM
    scale = HEAD_DIM ** (-0.5)
    w, z = place()
    expert = (w // 2) * PLANES + z

    misc = jnp.concatenate(
        [w_router, gain_attn[:, None], gain_ffn[:, None], jnp.zeros((own, 128 - experts - 2), BF16)],
        axis=1,
    )
    wq_send = jnp.concatenate(
        [windows(w_qkv[:, i * width : (i + 1) * width]) for i in range(3)]
        + [jnp.broadcast_to(misc[None], (PLANES, own, 128))],
        axis=2,
    )
    we_send = jnp.concatenate([w_up, w_down], axis=2).reshape(own, 4, PLANES, 3 * FF)
    we_send = jnp.transpose(we_send, (2, 1, 0, 3))
    choose = routes[:, :, None] == jnp.arange(experts, dtype=jnp.int32)[None, None, :]
    member = jnp.any(choose, axis=1)
    member_cols = jnp.concatenate(
        [jnp.ones((rows, 1), BF16), member.astype(BF16), jnp.zeros((rows, 127 - experts), BF16)],
        axis=1,
    )
    cot_send = jnp.concatenate([cotangent, member_cols], axis=1)
    ids_send = jnp.broadcast_to(seq_ids.astype(BF16)[None, :], (16, rows))
    tok_all, ids_all, wq_all, wo_all, we_all, cot_all = spread_inputs(
        tokens, ids_send, wq_send, w_out, we_send, cot_send
    )
    wq_all = wq_all.reshape(width, 3 * size + 128)
    misc_all = wq_all[:, 3 * size :]
    wq = wq_all[:, : 3 * size]
    router = misc_all[:, :experts]
    gain_one = misc_all[:, experts].astype(F32)
    gain_two = misc_all[:, experts + 1].astype(F32)
    out_weight = wo_all.reshape(width, width)

    seq_in = tok_all.reshape(seqlen, width).astype(F32)
    seq_normed = seq_in * rms_inverse(seq_in)
    first_in = (seq_normed * gain_one).astype(BF16)
    projected = dot(first_in, wq, ((1,), (0,)))
    cosine, sine_table = rotary(jnp.arange(seqlen, dtype=F32), HEAD_DIM)
    pq, pk, pv = (
        projected[:, i * size : (i + 1) * size].reshape(seqlen, WINDOW, HEAD_DIM) for i in range(3)
    )
    query_rows = (rotate(pq, cosine, sine_table) * scale).astype(BF16)
    key_rows = rotate(pk, cosine, sine_table).astype(BF16)
    value_rows = pv.astype(BF16)
    ids = ids_all[:, 0, :].reshape(seqlen)
    at = jnp.arange(seqlen, dtype=jnp.int32)
    allowed = ((at[None, :] <= at[:, None]) & (ids[None, :] == ids[:, None]))[None]
    scores = jnp.einsum("qhd,khd->hqk", query_rows, key_rows, preferred_element_type=F32)
    masked = jnp.where(allowed, scores, -1e30)
    top = jnp.max(masked, axis=2, keepdims=True)
    powers = jnp.where(allowed, jnp.exp(masked - top), 0.0)
    weights_exact = powers * (1.0 / jnp.sum(powers, axis=2, keepdims=True))
    weights_low = weights_exact.astype(BF16)
    mixed_exact = jnp.einsum("hqk,khd->qhd", weights_low, value_rows, preferred_element_type=F32)
    mixed_send = mixed_exact.astype(BF16).reshape(PLANES, rows, size)
    mixed = from_windows(swap_planes(mixed_send, 2))
    middle = tokens.astype(F32) + dot(mixed, out_weight, ((1,), (0,)))
    inverse_two = rms_inverse(middle)
    normed_two = middle * inverse_two
    second_in = (normed_two * gain_two).astype(BF16)

    x_all = gather_rows(second_in, 3).reshape(-1, width)
    cot_all = cot_all.reshape(-1, width + 128)
    cot_rows = cot_all[:, :width]
    members = cot_all[:, width : width + experts + 1].astype(F32)
    weights = we_all.reshape(width, 3 * FF)
    up, down = weights[:, : 2 * FF], weights[:, 2 * FF :]
    probs_all = jax.nn.softmax(dot(x_all, router, ((1,), (0,))), axis=-1)
    mine = (jnp.arange(experts + 1) == expert).astype(F32)[None, :]
    shared_one = jnp.ones((x_all.shape[0], 1), F32)
    member_own = jnp.sum(members * mine, axis=1, keepdims=True)
    gate = jnp.sum(
        jnp.concatenate([shared_one, probs_all], axis=1) * members * mine, axis=1, keepdims=True
    )
    gate_up = dot(x_all, up, ((1,), (0,)))
    gate_part, up_part = gate_up[:, :FF], gate_up[:, FF:]
    sigmoid = jax.nn.sigmoid(gate_part)
    activated = (gate_part * sigmoid * up_part).astype(BF16)
    expert_rows = dot(activated, down, ((1,), (1,)), BF16).astype(F32)
    cot_f = cot_rows.astype(F32)
    out_part = (gate * expert_rows).astype(BF16)
    grad_prob = jnp.sum(expert_rows * cot_f, axis=1, keepdims=True) * member_own
    prob_hi = grad_prob.astype(BF16)
    prob_lo = (grad_prob - prob_hi.astype(F32)).astype(BF16)
    lane = jnp.arange(128)[None, :]
    prob_cols = jnp.where(lane == expert, prob_hi, 0) + jnp.where(lane == expert + 32, prob_lo, 0)
    grad_rows = (gate * cot_f).astype(BF16)
    grad_act = dot(grad_rows, down, ((1,), (0,)))
    grad_gate_up = jnp.concatenate(
        [
            grad_act * up_part * sigmoid * (1.0 + gate_part * (1.0 - sigmoid)),
            grad_act * gate_part * sigmoid,
        ],
        axis=1,
    ).astype(BF16)
    grad_in = dot(grad_gate_up, up, ((1,), (1,)), BF16)
    grad_up = dot(x_all, grad_gate_up, ((0,), (0,)), BF16)
    grad_down = dot(grad_rows, activated, ((0,), (0,)), BF16)
    parts = jnp.concatenate([out_part, grad_in, prob_cols.astype(BF16)], axis=1)
    sums = sum_rows(parts.reshape(4, PLANES, rows, 2 * width + 128), 4)

    output = (middle + sums[:, :width]).astype(BF16)
    hi = sums[:, 2 * width + 1 : 2 * width + 1 + experts]
    lo = sums[:, 2 * width + 33 : 2 * width + 33 + experts]
    grad_probs = hi + lo
    probs = jax.nn.softmax(dot(second_in, router, ((1,), (0,))), axis=-1)
    grad_logits = (
        probs * (grad_probs - jnp.sum(probs * grad_probs, axis=1, keepdims=True))
    ).astype(BF16)
    grad_second = sums[:, width : 2 * width] + dot(grad_logits, router, ((1,), (1,)))
    grad_output = cotangent.astype(F32)
    grad_normed_two = grad_second * gain_two
    gain_two_part = jnp.sum(grad_second * normed_two, axis=0)
    grad_middle = grad_output + inverse_two * (
        grad_normed_two
        - normed_two * jnp.mean(grad_normed_two * normed_two, axis=-1, keepdims=True)
    )
    router_part = dot(second_in, grad_logits, ((0,), (0,)))
    grad_attention = grad_middle.astype(BF16)
    grad_out_part = dot(mixed, grad_attention, ((0,), (0,)), BF16)
    grad_mixed = dot(grad_attention, out_weight, ((1,), (1,)), BF16)

    valid = jnp.array(
        [[a <= i < b for i in range(WINDOW)] for a, b in KEEP], dtype=BF16
    )[z]
    grad_heads = swap_planes(windows(grad_mixed), 5).reshape(seqlen, WINDOW, HEAD_DIM)
    grad_heads = grad_heads * valid[None, :, None]
    row_delta = jnp.sum(grad_heads.astype(F32) * mixed_exact, axis=2).T
    grad_values = jnp.einsum("hqk,qhd->khd", weights_low, grad_heads, preferred_element_type=F32)
    grad_weights = jnp.einsum("qhd,khd->hqk", grad_heads, value_rows, preferred_element_type=F32)
    grad_scores = (weights_exact * (grad_weights - row_delta[..., None])).astype(BF16)
    grad_query = jnp.einsum("hqk,khd->qhd", grad_scores, key_rows, preferred_element_type=F32)
    grad_keys = jnp.einsum("hqk,qhd->khd", grad_scores, query_rows, preferred_element_type=F32)
    grad_projected = jnp.concatenate(
        [
            (rotate_back(grad_query, cosine, sine_table) * scale).reshape(seqlen, size),
            rotate_back(grad_keys, cosine, sine_table).reshape(seqlen, size),
            grad_values.reshape(seqlen, size),
        ],
        axis=1,
    ).astype(BF16)
    grad_qkv_part = dot(first_in, grad_projected, ((0,), (0,)), BF16)
    first_part = dot(grad_projected, wq, ((1,), (1,)))
    gain_one_part = jnp.sum(first_part * seq_normed, axis=0)
    misc_part = jnp.concatenate(
        [
            router_part,
            gain_one_part[:, None],
            gain_two_part[:, None],
            jnp.zeros((width, 128 - experts - 2), F32),
        ],
        axis=1,
    ).astype(BF16)
    half = width // 2
    dense = jnp.stack([jnp.concatenate([grad_qkv_part, misc_part], axis=1), grad_out_part])
    dense = dense.reshape(2, PLANES, 4, width // 16, 2, half)
    dense = jnp.transpose(dense, (0, 4, 1, 2, 3, 5))
    first_all, q_all, o_all = sum_dense(
        first_part.astype(BF16).reshape(PLANES, rows, width), dense, 6
    )
    grad_first = jnp.sum(first_all.astype(F32), axis=0)
    inputs = tokens.astype(F32)
    inverse_one = rms_inverse(inputs)
    normed_one = inputs * inverse_one
    grad_normed_one = grad_first * gain_one
    grad_tokens = grad_middle + inverse_one * (
        grad_normed_one
        - normed_one * jnp.mean(grad_normed_one * normed_one, axis=-1, keepdims=True)
    )
    q_all = q_all.reshape(4, 2, PLANES, width // 16, half)
    q_all = jnp.transpose(q_all, (2, 0, 3, 1, 4)).reshape(PLANES, 4 * (width // 16), width)
    o_all = o_all.reshape(4, 2, width // 16, half)
    out_sum = jnp.transpose(o_all, (0, 2, 1, 3)).reshape(4 * (width // 16), width).astype(F32)
    qkv_sum = jnp.concatenate(
        [from_windows(q_all[:, :, i * size : (i + 1) * size]) for i in range(3)], axis=1
    ).astype(F32)
    misc_sum = jnp.sum(q_all[:, :, 3 * size :].astype(F32), axis=0)

    grads = jnp.concatenate([grad_up, grad_down], axis=1).reshape(
        PLANES, 2, width // PLANES // 2, 3 * FF
    )
    table = spread_grads(grads, 7).reshape(experts + 1, width // PLANES, 3 * FF)
    up_sum = jnp.transpose(table[:, :, : 2 * FF], (1, 0, 2)).astype(F32)
    down_sum = jnp.transpose(table[:, :, 2 * FF :], (1, 0, 2)).astype(F32)
    return (
        output,
        grad_tokens.astype(BF16),
        misc_sum[:, experts],
        qkv_sum,
        out_sum,
        misc_sum[:, experts + 1],
        misc_sum[:, :experts],
        up_sum,
        down_sum,
    )


def solution(mesh):
    fits = mesh.shape["wide"] == 8 and mesh.shape["narrow"] == PLANES
    return jax.shard_map(
        expert_local if fits else local,
        mesh=mesh,
        in_specs=(
            P(("wide", "narrow"), None),
            P(("wide", "narrow")),
            P(("wide", "narrow"), None),
            P(("wide", "narrow"), None),
            P(("wide", "narrow")),
            P(("wide", "narrow"), None),
            P(("wide", "narrow"), None),
            P(("wide", "narrow")),
            P(("wide", "narrow"), None),
            P(("wide", "narrow"), None, None),
            P(("wide", "narrow"), None, None),
        ),
        out_specs=(
            P(("wide", "narrow"), None),
            P(("wide", "narrow"), None),
            P("narrow"),
            P("narrow", None),
            P("narrow", None),
            P("narrow"),
            P("narrow", None),
            P("narrow", None, None),
            P("narrow", None, None),
        ),
        check_vma=False,
    )
```

```python
import jax
import jax.numpy as jnp
from jax import lax
from jax.experimental import pallas as pl
from jax.experimental.pallas import tpu as pltpu
from jax.sharding import PartitionSpec as P

HEADS = 10
HEAD_DIM = 128
FF = 896
CAP = 72


epsilon = 1e-06


def shortened(x):
    return jax.tree.map(lambda a: a.astype(jnp.bfloat16) if a.dtype == jnp.float32 else a, x)


def rms_inverse(values):
    return lax.rsqrt(jnp.mean(values * values, axis=-1, keepdims=True) + epsilon)


def rotary(positions, head_size):
    half_dim = head_size // 2
    frequency = 10000.0 ** (-jnp.arange(half_dim, dtype=jnp.float32) / half_dim)
    angles = positions[:, None] * frequency[None, :]
    cosine = jnp.concatenate([jnp.cos(angles), jnp.cos(angles)], axis=1)[:, None, :]
    sine_table = jnp.concatenate([jnp.sin(angles), jnp.sin(angles)], axis=1)[:, None, :]
    return (cosine, sine_table)


def rotate(values, cosine, sine_table):
    half_dim = values.shape[-1] // 2
    turned = jnp.concatenate([-values[..., half_dim:], values[..., :half_dim]], axis=-1)
    return values * cosine + turned * sine_table


def rotate_back(grads, cosine, sine_table):
    half_dim = grads.shape[-1] // 2
    scaled = grads * sine_table
    turned = jnp.concatenate([scaled[..., half_dim:], -scaled[..., :half_dim]], axis=-1)
    return grads * cosine + turned


def expert_weight_terms(
    routed_in, routed_grad, shared_in, shared_grad, slot_grads, slot_acts, shared_grads, shared_acts
):
    up_routed = jnp.einsum(
        "ecd,ecf->def", routed_in, slot_grads, preferred_element_type=jnp.float32
    )
    up_shared = jnp.einsum("td,tf->df", shared_in, shared_grads, preferred_element_type=jnp.float32)
    down_routed = jnp.einsum(
        "ecd,ecf->def", routed_grad, slot_acts, preferred_element_type=jnp.float32
    )
    down_shared = jnp.einsum(
        "td,tf->df", shared_grad, shared_acts, preferred_element_type=jnp.float32
    )
    up_all = jnp.concatenate([up_shared[:, None], up_routed], axis=1)
    down_all = jnp.concatenate([down_shared[:, None], down_routed], axis=1)
    combined = jnp.concatenate([up_all, down_all], axis=2)
    return combined.reshape(combined.shape[0], -1)


def local(
    tokens, seq_ids, routes, cotangent, gain_attn, w_qkv, w_out, gain_ffn, w_router, w_up, w_down
):
    row_count = tokens.shape[0]
    model_width = tokens.shape[1]
    query_scale = HEAD_DIM ** (-0.5)
    hidden = FF
    capacity = CAP
    inputs = tokens.astype(jnp.float32)
    gain_one, qkv_weight, out_weight = (
        lax.all_gather(gain_attn, ("wide", "narrow"), axis=0, tiled=True),
        lax.all_gather(w_qkv, ("wide", "narrow"), axis=0, tiled=True),
        lax.all_gather(w_out, ("wide", "narrow"), axis=0, tiled=True),
    )
    inverse_one = rms_inverse(inputs)
    normed_one = inputs * inverse_one
    first_in = (normed_one * gain_one.astype(jnp.float32)).astype(jnp.bfloat16)
    projected = jnp.dot(first_in, qkv_weight, preferred_element_type=jnp.float32)
    offset = lax.axis_index("narrow") * row_count
    query_pos = offset + jnp.arange(row_count, dtype=jnp.int32)
    cosine, sine_table = rotary(query_pos.astype(jnp.float32), HEAD_DIM)
    query_rows = (
        rotate(projected[:, :model_width].reshape(row_count, HEADS, HEAD_DIM), cosine, sine_table)
        * query_scale
    ).astype(jnp.bfloat16)
    key_rows = (
        rotate(
            projected[:, model_width : 2 * model_width].reshape(row_count, HEADS, HEAD_DIM),
            cosine,
            sine_table,
        )
        .astype(jnp.bfloat16)
        .reshape(row_count, model_width)
    )
    value_rows = projected[:, 2 * model_width :].astype(jnp.bfloat16)
    all_keys, all_values, all_ids = (
        lax.all_gather(key_rows, "narrow", axis=0, tiled=True),
        lax.all_gather(value_rows, "narrow", axis=0, tiled=True),
        lax.all_gather(seq_ids.astype(jnp.bfloat16), "narrow", axis=0, tiled=True),
    )
    seqlen = all_keys.shape[0]
    block_len = min(512, seqlen)
    num_blocks = seqlen // block_len
    own_ids = seq_ids.astype(jnp.float32)

    def block_parts(block_index):
        first_row = block_index * block_len
        key_pos = first_row + jnp.arange(block_len, dtype=jnp.int32)
        key_ids = lax.dynamic_slice_in_dim(all_ids, first_row, block_len, 0).astype(jnp.float32)
        allowed = (key_pos[None, :] <= query_pos[:, None]) & (key_ids[None, :] == own_ids[:, None])
        key_block = lax.dynamic_slice_in_dim(all_keys, first_row, block_len, 0).reshape(
            block_len, HEADS, HEAD_DIM
        )
        value_block = lax.dynamic_slice_in_dim(all_values, first_row, block_len, 0).reshape(
            block_len, HEADS, HEAD_DIM
        )
        scores = jnp.einsum(
            "qhd,khd->hqk", query_rows, key_block, preferred_element_type=jnp.float32
        )
        return (allowed[None], key_block, value_block, scores)

    def max_step(state_pair, block_index):
        running_max, running_sum = state_pair
        allowed, key_block, value_block, scores = block_parts(block_index)
        masked = jnp.where(allowed, scores, -1e30)
        new_max = jnp.maximum(running_max, jnp.max(masked, axis=2))
        added = jnp.sum(jnp.where(allowed, jnp.exp(masked - new_max[..., None]), 0.0), axis=2)
        return ((new_max, running_sum * jnp.exp(running_max - new_max) + added), None)

    start_max = jnp.full((HEADS, row_count), -1e30, jnp.float32)
    start_sum = jnp.zeros((HEADS, row_count), jnp.float32)
    (top_score, exp_total), unused = lax.scan(
        max_step, (start_max, start_sum), jnp.arange(num_blocks)
    )
    log_total = top_score + jnp.log(exp_total)

    def out_step(accum, block_index):
        allowed, key_block, value_block, scores = block_parts(block_index)
        weights_low = jnp.where(allowed, jnp.exp(scores - log_total[..., None]), 0.0).astype(
            jnp.bfloat16
        )
        return (
            accum
            + jnp.einsum(
                "hqk,khd->hqd", weights_low, value_block, preferred_element_type=jnp.float32
            ),
            None,
        )

    accum_start = jnp.zeros((HEADS, row_count, HEAD_DIM), jnp.float32)
    mixed_heads, unused = lax.scan(out_step, accum_start, jnp.arange(num_blocks))
    mixed_exact = jnp.transpose(mixed_heads, (1, 0, 2))
    mixed = mixed_exact.reshape(row_count, model_width).astype(jnp.bfloat16)
    middle = inputs + jnp.dot(mixed, out_weight, preferred_element_type=jnp.float32)
    gain_two, router_weight, up_weight, down_weight = (
        lax.all_gather(gain_ffn, ("wide", "narrow"), axis=0, tiled=True),
        lax.all_gather(w_router, ("wide", "narrow"), axis=0, tiled=True),
        lax.all_gather(w_up, ("wide", "narrow"), axis=0, tiled=True),
        lax.all_gather(w_down, ("wide", "narrow"), axis=0, tiled=True),
    )
    inverse_two = rms_inverse(middle)
    normed_two = middle * inverse_two
    second_in = (normed_two * gain_two.astype(jnp.float32)).astype(jnp.bfloat16)
    logits = jnp.dot(second_in, router_weight, preferred_element_type=jnp.float32)
    router_probs = jax.nn.softmax(logits, axis=-1)
    experts = logits.shape[1]
    choose = routes[:, :, None] == jnp.arange(experts, dtype=jnp.int32)[None, None, :]
    member = jnp.sum(choose.astype(jnp.float32), axis=1)
    earlier = (jnp.arange(row_count)[:, None] > jnp.arange(row_count)[None, :]).astype(jnp.bfloat16)
    before = jnp.dot(earlier, member.astype(jnp.bfloat16), preferred_element_type=jnp.float32)
    slot_hit = (member.T[:, None, :] > 0.5) & (
        before.T[:, None, :] == jnp.arange(capacity, dtype=jnp.float32)[None, :, None]
    )
    dispatch = slot_hit.astype(jnp.bfloat16)
    gathered_in = jnp.einsum(
        "ect,td->ecd", dispatch, second_in, preferred_element_type=jnp.float32
    ).astype(jnp.bfloat16)
    gate_weights = router_probs * member
    gate_up = jnp.einsum(
        "ecd,def->ecf", gathered_in, up_weight[:, 1:], preferred_element_type=jnp.float32
    )
    gate_part = gate_up[..., :hidden]
    up_part = gate_up[..., hidden:]
    activated = (jax.nn.silu(gate_part) * up_part).astype(jnp.bfloat16)
    expert_rows = jnp.einsum(
        "ecf,def->ecd", activated, down_weight[:, 1:], preferred_element_type=jnp.float32
    ).astype(jnp.bfloat16)
    selected = jnp.einsum("ect,ecd->etd", dispatch, expert_rows, preferred_element_type=jnp.float32)
    routed = jnp.sum(gate_weights.T[:, :, None] * selected, axis=0)
    shared_up = jnp.dot(second_in, up_weight[:, 0], preferred_element_type=jnp.float32)
    shared_gate = shared_up[:, :hidden]
    shared_lin = shared_up[:, hidden:]
    shared_act = (jax.nn.silu(shared_gate) * shared_lin).astype(jnp.bfloat16)
    shared_out = jnp.einsum(
        "tf,df->td", shared_act, down_weight[:, 0], preferred_element_type=jnp.float32
    )
    output = (middle + shared_out + routed).astype(jnp.bfloat16)
    gain_two, router_weight, up_weight, down_weight = (
        lax.all_gather(gain_ffn, ("wide", "narrow"), axis=0, tiled=True),
        lax.all_gather(w_router, ("wide", "narrow"), axis=0, tiled=True),
        lax.all_gather(w_up, ("wide", "narrow"), axis=0, tiled=True),
        lax.all_gather(w_down, ("wide", "narrow"), axis=0, tiled=True),
    )
    grad_output = cotangent.astype(jnp.float32)
    slot_token = jnp.sum(
        jnp.where(slot_hit, jnp.arange(row_count, dtype=jnp.int32)[None, None, :], 0), axis=2
    )
    slot_gate = jnp.sum(jnp.where(slot_hit, gate_weights.T[:, None, :], 0.0), axis=2)
    grad_rows = (slot_gate[..., None] * grad_output[slot_token]).astype(jnp.bfloat16)
    grad_probs = jnp.sum(selected * grad_output[None], axis=2).T * member
    grad_logits = (
        router_probs * (grad_probs - jnp.sum(router_probs * grad_probs, axis=1, keepdims=True))
    ).astype(jnp.bfloat16)
    grad_act = jnp.einsum(
        "ecd,def->ecf", grad_rows, down_weight[:, 1:], preferred_element_type=jnp.float32
    )
    sigmoid_gate = jax.nn.sigmoid(gate_part)
    grad_gate_up = jnp.concatenate(
        [
            grad_act * up_part * sigmoid_gate * (1.0 + gate_part * (1.0 - sigmoid_gate)),
            grad_act * jax.nn.silu(gate_part),
        ],
        axis=-1,
    ).astype(jnp.bfloat16)
    grad_gathered = jnp.einsum(
        "ecf,def->ecd", grad_gate_up, up_weight[:, 1:], preferred_element_type=jnp.float32
    )
    slot_index = jnp.sum(jnp.where(choose, before[:, None, :], 0.0), axis=2).astype(jnp.int32)
    flat_index = routes * capacity + slot_index
    grad_second = jnp.sum(grad_gathered.reshape(-1, model_width)[flat_index], axis=1)
    grad_shared_act = jnp.einsum(
        "td,df->tf", cotangent, down_weight[:, 0], preferred_element_type=jnp.float32
    )
    sigmoid_shared = jax.nn.sigmoid(shared_gate)
    grad_shared_up = jnp.concatenate(
        [
            grad_shared_act
            * shared_lin
            * sigmoid_shared
            * (1.0 + shared_gate * (1.0 - sigmoid_shared)),
            grad_shared_act * jax.nn.silu(shared_gate),
        ],
        axis=-1,
    ).astype(jnp.bfloat16)
    grad_second = grad_second + jnp.einsum(
        "tf,df->td", grad_shared_up, up_weight[:, 0], preferred_element_type=jnp.float32
    )
    grad_second = grad_second + jnp.einsum(
        "te,de->td", grad_logits, router_weight, preferred_element_type=jnp.float32
    )
    grad_normed_two = grad_second * gain_two.astype(jnp.float32)
    grad_gain_two = jnp.sum(grad_second * normed_two, axis=0)
    grad_middle = grad_output + inverse_two * (
        grad_normed_two
        - normed_two * jnp.mean(grad_normed_two * normed_two, axis=-1, keepdims=True)
    )
    grad_router = jnp.einsum(
        "td,te->de", second_in, grad_logits, preferred_element_type=jnp.float32
    )
    narrow_rows = model_width // lax.axis_size("narrow")
    routed_cols, grad_cols, shared_cols, cotangent_cols = (
        lax.all_to_all(gathered_in, "narrow", split_axis=2, concat_axis=1, tiled=True),
        lax.all_to_all(grad_rows, "narrow", split_axis=2, concat_axis=1, tiled=True),
        lax.all_to_all(second_in[None], "narrow", split_axis=2, concat_axis=1, tiled=True),
        lax.all_to_all(cotangent[None], "narrow", split_axis=2, concat_axis=1, tiled=True),
    )
    slot_grads, slot_acts, shared_grads, shared_acts = (
        lax.all_gather(grad_gate_up, "narrow", axis=1, tiled=True),
        lax.all_gather(activated, "narrow", axis=1, tiled=True),
        lax.all_gather(grad_shared_up[None], "narrow", axis=1, tiled=True),
        lax.all_gather(shared_act[None], "narrow", axis=1, tiled=True),
    )
    expert_grads = expert_weight_terms(
        routed_cols,
        grad_cols,
        shared_cols[0],
        cotangent_cols[0],
        slot_grads,
        slot_acts,
        shared_grads[0],
        shared_acts[0],
    )
    gain_one, qkv_weight, out_weight = (
        lax.all_gather(gain_attn, ("wide", "narrow"), axis=0, tiled=True),
        lax.all_gather(w_qkv, ("wide", "narrow"), axis=0, tiled=True),
        lax.all_gather(w_out, ("wide", "narrow"), axis=0, tiled=True),
    )
    grad_attention = grad_middle.astype(jnp.bfloat16)
    grad_out_weight = jnp.einsum(
        "td,te->de", mixed, grad_attention, preferred_element_type=jnp.float32
    )
    grad_mixed = jnp.einsum(
        "te,de->td", grad_attention, out_weight, preferred_element_type=jnp.float32
    ).astype(jnp.bfloat16)
    grad_heads = grad_mixed.reshape(row_count, HEADS, HEAD_DIM)
    row_delta = jnp.sum(grad_heads.astype(jnp.float32) * mixed_exact, axis=2).T

    def back_step(grad_query, block_index):
        allowed, key_block, value_block, scores = block_parts(block_index)
        weights_exact = jnp.where(allowed, jnp.exp(scores - log_total[..., None]), 0.0)
        weights_low = weights_exact.astype(jnp.bfloat16)
        grad_value = jnp.einsum(
            "hqk,qhd->khd", weights_low, grad_heads, preferred_element_type=jnp.float32
        )
        grad_weights = jnp.einsum(
            "qhd,khd->hqk", grad_heads, value_block, preferred_element_type=jnp.float32
        )
        grad_scores = (weights_exact * (grad_weights - row_delta[..., None])).astype(jnp.bfloat16)
        grad_query = grad_query + jnp.einsum(
            "hqk,khd->qhd", grad_scores, key_block, preferred_element_type=jnp.float32
        )
        grad_key = jnp.einsum(
            "hqk,qhd->khd", grad_scores, query_rows, preferred_element_type=jnp.float32
        )
        return (
            grad_query,
            (grad_key.reshape(block_len, model_width), grad_value.reshape(block_len, model_width)),
        )

    query_start = jnp.zeros((row_count, HEADS, HEAD_DIM), jnp.float32)
    grad_query, (key_blocks, value_blocks) = lax.scan(
        back_step, query_start, jnp.arange(num_blocks)
    )
    key_partial = key_blocks.reshape(seqlen, model_width)
    value_partial = value_blocks.reshape(seqlen, model_width)
    grad_keys, grad_values = (
        lax.psum_scatter(
            key_partial.astype(jnp.bfloat16), "narrow", scatter_dimension=0, tiled=True
        ).astype(jnp.float32),
        lax.psum_scatter(
            value_partial.astype(jnp.bfloat16), "narrow", scatter_dimension=0, tiled=True
        ).astype(jnp.float32),
    )
    grad_query_raw = rotate_back(grad_query, cosine, sine_table) * query_scale
    grad_key_raw = rotate_back(grad_keys.reshape(row_count, HEADS, HEAD_DIM), cosine, sine_table)
    grad_projected = jnp.concatenate(
        [
            grad_query_raw.reshape(row_count, model_width),
            grad_key_raw.reshape(row_count, model_width),
            grad_values,
        ],
        axis=1,
    ).astype(jnp.bfloat16)
    grad_qkv_weight = jnp.einsum(
        "td,tf->df", first_in, grad_projected, preferred_element_type=jnp.float32
    )
    grad_first = jnp.einsum(
        "tf,df->td", grad_projected, qkv_weight, preferred_element_type=jnp.float32
    )
    grad_normed_one = grad_first * gain_one.astype(jnp.float32)
    grad_gain_one = jnp.sum(grad_first * normed_one, axis=0)
    grad_inputs = grad_middle + inverse_one * (
        grad_normed_one
        - normed_one * jnp.mean(grad_normed_one * normed_one, axis=-1, keepdims=True)
    )
    dense_parts = (
        lax.psum_scatter(
            grad_gain_one.astype(jnp.bfloat16), "narrow", scatter_dimension=0, tiled=True
        ).astype(jnp.float32),
        lax.psum_scatter(
            grad_qkv_weight.astype(jnp.bfloat16), "narrow", scatter_dimension=0, tiled=True
        ).astype(jnp.float32),
        lax.psum_scatter(
            grad_out_weight.astype(jnp.bfloat16), "narrow", scatter_dimension=0, tiled=True
        ).astype(jnp.float32),
        lax.psum_scatter(
            grad_gain_two.astype(jnp.bfloat16), "narrow", scatter_dimension=0, tiled=True
        ).astype(jnp.float32),
        lax.psum_scatter(
            grad_router.astype(jnp.bfloat16), "narrow", scatter_dimension=0, tiled=True
        ).astype(jnp.float32),
    )
    summed = jax.tree.map(
        lambda part: part.astype(jnp.float32),
        lax.psum(shortened((expert_grads,) + tuple(dense_parts)), "wide"),
    )
    expert_grads = summed[0]
    dense_parts = summed[1:]
    gain_one_sum, qkv_sum, out_sum, gain_two_sum, router_sum = dense_parts
    expert_table = expert_grads.reshape(narrow_rows, up_weight.shape[1], 3 * hidden)
    up_sum = expert_table[:, :, : 2 * hidden]
    down_sum = expert_table[:, :, 2 * hidden :]
    return (
        output,
        grad_inputs.astype(jnp.bfloat16),
        gain_one_sum,
        qkv_sum,
        out_sum,
        gain_two_sum,
        router_sum,
        up_sum,
        down_sum,
    )


PLANES = 4
WINDOW = 3
STARTS = (0, 3, 6, 7)
KEEP = ((0, 3), (0, 3), (0, 2), (1, 3))
MESH_IDS = pl.DeviceIdType.MESH
BF16 = jnp.bfloat16
F32 = jnp.float32


def place():
    w = lax.axis_index("wide")
    z = lax.axis_index("narrow")
    return w, z


def other_plane(z, step):
    return lax.rem(z + step, PLANES), lax.rem(z + PLANES - step, PLANES)


class Net:
    def __init__(self, send_sems, recv_sems):
        self.send_sems, self.recv_sems, self.used, self.started = send_sems, recv_sems, 0, []

    def send(self, src, dst, device):
        copy = pltpu.make_async_remote_copy(
            src_ref=src,
            dst_ref=dst,
            send_sem=self.send_sems.at[self.used],
            recv_sem=self.recv_sems.at[self.used],
            device_id=device,
            device_id_type=MESH_IDS,
        )
        self.used += 1
        copy.start()
        self.started.append(copy)
        return copy

    def keep(self, src, dst):
        copy = pltpu.make_async_copy(src, dst, self.send_sems.at[self.used])
        self.used += 1
        copy.start()
        return copy

    def finish(self):
        for copy in self.started:
            copy.wait_send()


def greet(w, z):
    barrier = pltpu.get_barrier_semaphore()
    peers = [(w, lax.rem(z + step, PLANES)) for step in (1, 2, 3)]
    peers += [(w ^ flip, z) for flip in (1, 2, 4, 6)]
    for peer in peers:
        pl.semaphore_signal(barrier, inc=1, device_id=peer, device_id_type=MESH_IDS)
    pl.semaphore_wait(barrier, len(peers))


class PlaneGather:
    def __init__(self, net, w, z, slot, number, cores):
        self.net, self.w, self.z, self.slot, self.cores = net, w, z, slot, cores
        self.first, self.second = (2, 4) if number % 2 == 0 else (4, 2)

    def push(self, slot_of, flip):
        ref = self.slot(slot_of)
        return self.net.send(ref, ref, (self.w ^ flip, self.z))

    def begin(self):
        self.direct = {flip: self.push(self.w, flip) for flip in (2, 4)}
        self.core = [self.push(self.w, 1)] if self.cores else []

    def relay(self):
        self.direct[self.first].wait_recv()
        self.across = self.push(self.w ^ self.first, self.second)
        if self.cores:
            self.core.append(self.push(self.w ^ self.first, 1))
        self.direct[self.second].wait_recv()
        if self.cores:
            self.core.append(self.push(self.w ^ self.second, 1))

    def end(self):
        self.across.wait_recv()
        if self.cores:
            self.core.append(self.push(self.w ^ 6, 1))

    def settle(self):
        for copy in self.core:
            copy.wait_recv()


def comm_call(kernel, name, collective, out_shape, in_spaces, out_spaces, sems, scratch=(), moved=0):
    return pl.pallas_call(
        kernel,
        out_shape=out_shape,
        in_specs=[pl.BlockSpec(memory_space=space) for space in in_spaces],
        out_specs=[pl.BlockSpec(memory_space=space) for space in out_spaces],
        scratch_shapes=[
            *scratch,
            pltpu.SemaphoreType.DMA((sems,)),
            pltpu.SemaphoreType.DMA((sems,)),
        ],
        compiler_params=pltpu.CompilerParams(
            collective_id=collective, has_side_effects=True, vmem_limit_bytes=62 * 2**20
        ),
        name=name,
    )


def spread_inputs_kernel(
    tok, ids, wq, wo, we, cot, tok_o, ids_o, wq_o, wo_o, we_o, cot_o, hop, send_sems, recv_sems
):
    w, z = place()
    chip = w // 2
    greet(w, z)
    net = Net(send_sems, recv_sems)
    own = [
        net.keep(tok, tok_o.at[z]),
        net.keep(ids, ids_o.at[z]),
        net.keep(wq.at[z], wq_o.at[w, z]),
        net.keep(wo, wo_o.at[w, z]),
        net.keep(we.at[z, chip], we_o.at[w, z]),
        net.keep(cot, cot_o.at[chip, z]),
    ]
    ring, gathers = {}, {}
    for step in (1, 2, 3):
        to, _ = other_plane(z, step)
        ring["tok", step] = net.send(tok, tok_o.at[z], (w, to))
        ring["ids", step] = net.send(ids, ids_o.at[z], (w, to))
        ring["wq", step] = net.send(wq.at[to], wq_o.at[w, z], (w, to))
    for step in (1, 2, 3):
        to, _ = other_plane(z, step)
        for flip in (1, 2, 3):
            ring["we", step, flip] = net.send(
                we.at[to, chip ^ flip], hop.at[step - 1, flip - 1], (w, to)
            )
        ring["we", step, 0] = net.send(we.at[to, chip], we_o.at[w, z], (w, to))
        ring["cot", step] = net.send(cot, cot_o.at[chip, z], (w, to))
        ring["wo", step] = net.send(wo, wo_o.at[w, z], (w, to))
    for copy in own:
        copy.wait()
    weights = {}
    for flip in (1, 2, 3):
        weights[0, flip] = net.send(
            we.at[z, chip ^ flip], we_o.at[w, z], (w ^ (2 * flip), z)
        )
    core = [net.send(we_o.at[w, z], we_o.at[w, z], (w ^ 1, z))]

    def start_gather(kind, step):
        _, source = other_plane(z, step)
        slot = {
            "wq": lambda i: wq_o.at[i, source],
            "wo": lambda i: wo_o.at[i, source],
            "cot": lambda i: cot_o.at[i // 2, source],
        }[kind]
        gathers[kind, step] = PlaneGather(net, w, z, slot, step, kind != "cot")
        gathers[kind, step].begin()

    start_gather("wq", 0)
    start_gather("wo", 0)
    start_gather("cot", 0)
    for step in (1, 2, 3):
        ring["wq", step].wait_recv()
        start_gather("wq", step)
    for step in (0, 1, 2, 3):
        gathers["wq", step].relay()
    gathers["wo", 0].relay()
    gathers["cot", 0].relay()
    for step in (0, 1, 2, 3):
        gathers["wq", step].end()
    gathers["wo", 0].end()
    gathers["cot", 0].end()
    for step in (1, 2, 3):
        _, source = other_plane(z, step)
        for flip in (1, 2, 3):
            ring["we", step, flip].wait_recv()
            weights[step, flip] = net.send(
                hop.at[step - 1, flip - 1], we_o.at[w, source], (w ^ (2 * flip), z)
            )
        ring["we", step, 0].wait_recv()
        core.append(net.send(we_o.at[w, source], we_o.at[w, source], (w ^ 1, z)))
        for kind in ("cot", "wo"):
            ring[kind, step].wait_recv()
            start_gather(kind, step)
        ring["tok", step].wait_recv()
        ring["ids", step].wait_recv()
    for step in (0, 1, 2, 3):
        _, source = other_plane(z, step)
        for flip in (1, 2, 3):
            weights[step, flip].wait_recv()
            peer = w ^ (2 * flip)
            core.append(net.send(we_o.at[peer, source], we_o.at[peer, source], (w ^ 1, z)))
        if step:
            for kind in ("cot", "wo"):
                gathers[kind, step].relay()
    for step in (1, 2, 3):
        for kind in ("cot", "wo"):
            gathers[kind, step].end()
    for gather in gathers.values():
        gather.settle()
    for copy in core:
        copy.wait_recv()
    net.finish()


def spread_inputs(tok, ids, wq, wo, we, cot):
    rows, width = tok.shape
    own = wo.shape[0]
    hidden3 = we.shape[-1]
    shapes = [
        (PLANES, rows, width),
        (PLANES,) + ids.shape,
        (8, PLANES) + wq.shape[1:],
        (8, PLANES) + wo.shape,
        (8, PLANES, own, hidden3),
        (4, PLANES) + cot.shape,
        (3, 3, own, hidden3),
    ]
    out = comm_call(
        spread_inputs_kernel,
        "spread_inputs",
        1,
        [jax.ShapeDtypeStruct(shape, BF16) for shape in shapes],
        [pl.ANY] * 6,
        [pl.ANY] * 7,
        160,
    )(tok, ids, wq, wo, we, cot)
    return out[:6]


def swap_planes_kernel(x, out, send_sems, recv_sems):
    w, z = place()
    greet(w, z)
    net = Net(send_sems, recv_sems)
    own = net.keep(x.at[z], out.at[z])
    copies = []
    for step in (1, 2, 3):
        to, _ = other_plane(z, step)
        copies.append(net.send(x.at[to], out.at[z], (w, to)))
    own.wait()
    for copy in copies:
        copy.wait_recv()
    net.finish()


def swap_planes(x, collective):
    return comm_call(
        swap_planes_kernel,
        "swap_planes",
        collective,
        [jax.ShapeDtypeStruct(x.shape, x.dtype)],
        [pl.ANY],
        [pl.ANY],
        8,
    )(x)[0]


def add_blocks(out, *terms):
    rows = out.shape[0]

    def body(i, carry):
        part = pl.ds(pl.multiple_of(i * 16, 16), 16)
        total = terms[0][part, :].astype(F32)
        for term in terms[1:]:
            total = total + term[part, :].astype(F32)
        out[part, :] = total.astype(out.dtype)
        return carry

    lax.fori_loop(0, rows // 16, body, 0)


def mul(a, b, over_a, over_b):
    return lax.dot_general(a, b, (((over_a,), (over_b,)), ((), ())), preferred_element_type=F32)


def at(start, size):
    return pl.ds(pl.multiple_of(start, 128), size)


def loop(first, last, body):
    def step(i, carry):
        body(i)
        return carry

    lax.fori_loop(first, last, step, 0)


def experts_kernel(
    x_in, cot_in, weights_in, misc_in, grads_o, outs_o, sums_o,
    x, cot, weights, misc, act, scaled, slopes, gate, outs, parts, got_one, got_two, got_far, stage,
    load_sems, send_sems, recv_sems,
):
    w, z = place()
    chip = w // 2
    expert = chip * PLANES + z
    rows, width = x_in.shape
    hidden = weights.shape[1] // 3
    group_rows = 4 * rows

    def remote(kind, step, src, dst, device):
        return pltpu.make_async_remote_copy(
            src_ref=src,
            dst_ref=dst,
            send_sem=send_sems.at[kind, step],
            recv_sem=recv_sems.at[kind, step],
            device_id=device,
            device_id_type=MESH_IDS,
        )

    def plane_of(step, sign):
        return lax.rem(z + PLANES + sign * step, PLANES)

    def step_at(turn):
        step = 0
        for plane, steps in enumerate(((3, 2, 1, 0), (1, 3, 2, 0), (3, 1, 2, 0), (1, 2, 3, 0))):
            for number, value in enumerate(steps):
                step = jnp.where((z == plane) & (turn == number), value, step)
        return step

    def axes(turn):
        first = 1 + lax.rem(turn, 2)
        return first, 3 - first

    def ring(step, up):
        to = lax.rem(step + 1, 4) if up else lax.rem(step + 3, 4)
        return pltpu.make_async_remote_copy(
            src_ref=x.at[step, chip],
            dst_ref=x.at[to, chip],
            send_sem=send_sems.at[0 if up else 8, step],
            recv_sem=recv_sems.at[0, to],
            device_id=(w, z + 1 if up else z - 1),
            device_id_type=MESH_IDS,
        )

    def goes(step, up):
        if up:
            return (z >= step) & (z < PLANES - 1)
        return ((z < step) | (step == 0)) & (z > 0)

    def pass_on(step):
        for up in (True, False):

            @pl.when(goes(step, up))
            def _():
                ring(step, up).start()

    def arrive(step):
        pltpu.make_async_remote_copy(
            src_ref=x.at[step, chip],
            dst_ref=x.at[step, chip],
            send_sem=send_sems.at[0, step],
            recv_sem=recv_sems.at[0, step],
            device_id=(w, z),
            device_id_type=MESH_IDS,
        ).wait_recv()

    def direct(step, flip):
        block = x.at[step, chip]
        return remote(flip, step, block, block, (w ^ (2 * flip), z))

    def across(turn):
        first, second = axes(turn)
        step = step_at(turn)
        block = x.at[step, chip ^ first]
        return remote(3, step, block, block, (w ^ (2 * second), z))

    def near(turn, which):
        first, _ = axes(turn)
        step = step_at(turn)
        block = chip ^ 3 if which else chip ^ first
        return remote(
            4 + which, step, parts.at[step, block], got_one.at[step, which], (w ^ (2 * first), z)
        )

    def cross(turn):
        _, second = axes(turn)
        step = step_at(turn)
        return remote(
            6, step, parts.at[step, chip ^ second], got_two.at[step], (w ^ (2 * second), z)
        )

    def far(step):
        return remote(7, step, parts.at[step, chip], got_far.at[step - 1], (w, plane_of(step, -1)))

    def cot_load(step):
        return pltpu.make_async_copy(
            cot_in.at[:, plane_of(step, -1)], cot.at[step], load_sems.at[step]
        )

    def outs_out(turn):
        return pltpu.make_async_copy(
            outs.at[lax.rem(turn, 2)], outs_o.at[step_at(turn)], load_sems.at[9 + lax.rem(turn, 2)]
        )

    def grads_out(low, size, slot):
        return pltpu.make_async_copy(
            stage.at[slot, :, pl.ds(0, size)], grads_o.at[:, low], load_sems.at[4 + slot]
        )

    loads = [
        pltpu.make_async_copy(src, dst, load_sems.at[6 + i])
        for i, (src, dst) in enumerate(((x_in, x.at[0, chip]), (misc_in, misc), (weights_in, weights)))
    ]
    for load in loads:
        load.start()
    loop(0, 4, lambda step: cot_load(step).start())
    greet(w, z)
    loads[0].wait()
    pass_on(0)

    def begin(turn):
        step = step_at(turn)

        @pl.when(turn < 3)
        def _():
            arrive(step)
            pass_on(step)

        direct(step, 1).start()
        direct(step, 2).start()

    def relay(turn):
        step = step_at(turn)
        direct(step, 1).wait_recv()
        direct(step, 2).wait_recv()
        across(turn).start()

    begin(0)
    begin(1)
    relay(0)
    begin(2)
    begin(3)
    loads[1].wait()
    loads[2].wait()

    def first_half(step):
        cot_load(step).wait()
        rows_in = x[step].reshape(group_rows, width)
        members = cot[step, :, :, width:].reshape(group_rows, 128).astype(F32)
        logits = mul(rows_in, misc[...], 1, 0)
        lane = lax.broadcasted_iota(jnp.int32, logits.shape, 1)
        routed = (lane > 0) & (lane < 16)
        top = jnp.max(jnp.where(routed, logits, -1e30), axis=1, keepdims=True)
        powers = jnp.where(routed, jnp.exp(logits - top), 0.0)
        probs = jnp.where(lane == 0, 1.0, powers / jnp.sum(powers, axis=1, keepdims=True))
        own = jnp.where(lane == expert, members, 0.0)
        gate[0] = jnp.broadcast_to(jnp.sum(probs * own, axis=1, keepdims=True), gate.shape[1:])
        gate[1] = own

        def hidden_chunk(low, size):
            here = x[step].reshape(group_rows, width)
            gate_part = mul(here, weights[:, at(low, size)], 1, 0)
            up_part = mul(here, weights[:, at(hidden + low, size)], 1, 0)
            grad_act = mul(
                cot[step, :, :, :width].reshape(group_rows, width),
                weights[:, at(2 * hidden + low, size)],
                1,
                0,
            )
            scale = gate[0][:, :1]
            grad_act = grad_act * scale
            sigmoid = 1.0 / (1.0 + jnp.exp(-gate_part))
            silu = gate_part * sigmoid
            activated = (silu * up_part).astype(BF16)
            act[:, at(low, size)] = activated
            scaled[step, :, at(low, size)] = (activated.astype(F32) * scale).astype(BF16)
            slopes[step, :, at(low, size)] = (
                grad_act * up_part * (sigmoid + silu * (1.0 - sigmoid))
            ).astype(BF16)
            slopes[step, :, at(hidden + low, size)] = (grad_act * silu).astype(BF16)

        loop(0, hidden // 256, lambda i: hidden_chunk(i * 256, 256))
        if hidden % 256:
            hidden_chunk(hidden // 256 * 256, hidden % 256)

    def second_half(turn, step):
        def width_body(i, total):
            low = i * 256
            expert_rows = mul(act[...], weights[at(low, 256), 2 * hidden :], 1, 1)
            expert_rows = expert_rows.astype(BF16).astype(F32)
            outs[lax.rem(turn, 2), :, :, at(low, 256)] = (
                (expert_rows * gate[0][:, :1]).astype(BF16).reshape(4, rows, 256)
            )
            product = expert_rows * cot[step, :, :, at(low, 256)].reshape(group_rows, 256).astype(F32)
            grad_in = mul(slopes[step], weights[at(low, 256), : 2 * hidden], 1, 1)
            parts[step, :, :, at(low, 256)] = grad_in.astype(BF16).reshape(4, rows, 256)
            return total + product[:, :128] + product[:, 128:]

        total = lax.fori_loop(0, width // 256, width_body, jnp.zeros((group_rows, 128), F32))
        prob = jnp.sum(total, axis=1, keepdims=True) * gate[1]
        high = prob.astype(BF16)
        low = (prob - high.astype(F32)).astype(BF16)
        low = pltpu.roll(low.astype(F32), 32, 1).astype(BF16)
        parts[step, :, :, width:] = (high + low).reshape(4, rows, 128)

    def send_cross(turn):
        _, second = axes(turn)
        step = step_at(turn)
        near(turn, 1).wait_recv()
        block = parts.at[step, chip ^ second]
        add_blocks(block, block, got_one.at[step, 1])
        cross(turn).start()

    def send_far(turn):
        step = step_at(turn)
        near(turn, 0).wait_recv()
        cross(turn).wait_recv()
        block = parts.at[step, chip]
        add_blocks(block, block, got_one.at[step, 0], got_two.at[step])
        far(step).start()

    def group(turn):
        step = step_at(turn)
        across(turn).wait_recv()
        first_half(step)

        @pl.when(turn < 2)
        def _():
            relay(2 * turn + 1)

        @pl.when(turn > 1)
        def _():
            outs_out(turn - 2).wait()

        second_half(turn, step)
        near(turn, 1).start()
        near(turn, 0).start()
        outs_out(turn).start()

        @pl.when(turn == 0)
        def _():
            relay(2)

        @pl.when(turn > 0)
        def _():
            send_cross(turn - 1)

        @pl.when(turn > 1)
        def _():
            send_far(turn - 2)

    loop(0, 4, group)

    def weight_chunk(left, right, low, size, offset, i):
        slot = lax.rem(i, 2)

        @pl.when(i >= 2)
        def _():
            grads_out(pl.ds(0, 256), 256, slot).wait()

        total = None
        for step in range(4):
            term = mul(
                left[step, :, :, :width].reshape(group_rows, width), right[step, :, at(low, size)], 0, 0
            )
            total = term if total is None else total + term
        stage[slot, :, :size] = total.astype(BF16)
        grads_out(at(offset + low, size), size, slot).start()

    ups, downs = 2 * hidden // 256, hidden // 256

    def up_chunk(i):
        weight_chunk(x, slopes, i * 256, 256, 0, i)

    def down_chunk(i):
        weight_chunk(cot, scaled, (i - ups) * 256, 256, 2 * hidden, i)

    loop(0, 3, up_chunk)
    send_cross(3)
    send_far(2)
    loop(3, ups, up_chunk)
    loop(ups, ups + downs, down_chunk)
    last = ups + downs
    if hidden % 256:
        weight_chunk(cot, scaled, downs * 256, hidden % 256, 2 * hidden, jnp.int32(last))
        grads_out(pl.ds(0, 256), 256, (last - 1) % 2).wait()
        grads_out(pl.ds(0, hidden % 256), hidden % 256, last % 2).wait()
    else:
        grads_out(pl.ds(0, 256), 256, last % 2).wait()
        grads_out(pl.ds(0, 256), 256, (last - 1) % 2).wait()
    outs_out(2).wait()
    outs_out(3).wait()
    near(3, 0).wait_recv()
    cross(3).wait_recv()
    loop(1, 4, lambda step: far(step).wait_recv())
    add_blocks(
        sums_o,
        parts.at[0, chip],
        got_one.at[0, 0],
        got_two.at[0],
        got_far.at[0],
        got_far.at[1],
        got_far.at[2],
    )

    def settle(turn):
        step = step_at(turn)
        direct(step, 1).wait_send()
        direct(step, 2).wait_send()
        across(turn).wait_send()
        near(turn, 0).wait_send()
        near(turn, 1).wait_send()
        cross(turn).wait_send()

        @pl.when(turn < 3)
        def _():
            far(step).wait_send()

        for up in (True, False):

            @pl.when(goes(step, up))
            def _():
                ring(step, up).wait_send()

    loop(0, 4, settle)


def run_experts(second_in, cot_all, weights, misc, collective):
    rows, width = second_in.shape
    hidden = weights.shape[1] // 3
    sums_width = width + 128
    block = (rows, sums_width)
    return pl.pallas_call(
        experts_kernel,
        out_shape=[
            jax.ShapeDtypeStruct((width, 3 * hidden), BF16),
            jax.ShapeDtypeStruct((4, 4, rows, width), BF16),
            jax.ShapeDtypeStruct((rows, sums_width), F32),
        ],
        in_specs=[pl.BlockSpec(memory_space=pl.ANY)] * 4,
        out_specs=[
            pl.BlockSpec(memory_space=pl.ANY),
            pl.BlockSpec(memory_space=pl.ANY),
            pl.BlockSpec(memory_space=pltpu.VMEM),
        ],
        scratch_shapes=[
            pltpu.VMEM((4, 4, rows, width), BF16),
            pltpu.VMEM((4, 4, rows, width + 128), BF16),
            pltpu.VMEM((width, 3 * hidden), BF16),
            pltpu.VMEM((width, 128), BF16),
            pltpu.VMEM((4 * rows, hidden), BF16),
            pltpu.VMEM((4, 4 * rows, hidden), BF16),
            pltpu.VMEM((4, 4 * rows, 2 * hidden), BF16),
            pltpu.VMEM((2, 4 * rows, 128), F32),
            pltpu.VMEM((2, 4, rows, width), BF16),
            pltpu.VMEM((4, 4) + block, BF16),
            pltpu.VMEM((4, 2) + block, BF16),
            pltpu.VMEM((4,) + block, BF16),
            pltpu.VMEM((3,) + block, BF16),
            pltpu.VMEM((2, width, 256), BF16),
            pltpu.SemaphoreType.DMA((11,)),
            pltpu.SemaphoreType.DMA((9, 4)),
            pltpu.SemaphoreType.DMA((8, 4)),
        ],
        compiler_params=pltpu.CompilerParams(
            collective_id=collective, has_side_effects=True, vmem_limit_bytes=62 * 2**20
        ),
        name="experts",
    )(second_in, cot_all, weights, misc)


def finish_kernel(
    outs_in, grads_in, first_in, dense_q, dense_o, sums_o, table_o, first_o, q_o, o_o,
    outs, outs_one, outs_two, outs_far, grads_own, grads_got, dense, dense_got, dense_one,
    dense_two, dense_far, dense_sum, load_sems, send_sems, recv_sems,
):
    w, z = place()
    chip, core = w // 2, w % 2
    steps = (1, 2, 3, 0)
    block_rows = o_o.shape[0] // 4
    half = o_o.shape[1] // 2
    plane_rows = o_o.shape[0]

    def remote(kind, step, src, dst, device):
        return pltpu.make_async_remote_copy(
            src_ref=src,
            dst_ref=dst,
            send_sem=send_sems.at[kind, step],
            recv_sem=recv_sems.at[kind, step],
            device_id=device,
            device_id_type=MESH_IDS,
        )

    def plane_of(step, sign):
        return lax.rem(z + PLANES + sign * step, PLANES)

    def axes(step):
        first = 1 + lax.rem(step, 2)
        return first, 3 - first

    class Gather:
        def __init__(self, base, step, turn, slot):
            self.base, self.step, self.slot = base, step, slot
            self.first, self.second = axes(turn)

        def copy(self, kind, owner, flip):
            ref = self.slot(owner)
            return remote(self.base + kind, self.step, ref, ref, (w ^ flip, z))

        def begin(self):
            self.copy(0, w, 2).start()
            self.copy(1, w, 4).start()
            self.copy(2, w, 1).start()

        def relay(self):
            self.copy(0, w, 2).wait_recv()
            self.copy(1, w, 4).wait_recv()
            self.across().start()
            self.copy(4, w ^ 2, 1).start()
            self.copy(5, w ^ 4, 1).start()

        def across(self):
            return self.copy(3, w ^ (2 * self.first), 2 * self.second)

        def end(self):
            self.across().wait_recv()
            self.copy(6, w ^ 6, 1).start()

        def settle(self):
            for copy in (
                self.copy(0, w, 2),
                self.copy(1, w, 4),
                self.copy(2, w, 1),
                self.across(),
                self.copy(4, w ^ 2, 1),
                self.copy(5, w ^ 4, 1),
                self.copy(6, w ^ 6, 1),
            ):
                copy.wait_send()
            for kind in (2, 4, 5, 6):
                self.copy(kind, w, 1).wait_recv()

    def grads_load(step):
        return pltpu.make_async_copy(
            grads_in.at[plane_of(step, 1), core], grads_own.at[step], load_sems.at[0, step]
        )

    def grads_swap(step):
        return remote(
            0, step, grads_in.at[plane_of(step, 1), 1 - core], grads_got.at[step], (w ^ 1, z)
        )

    def grads_ring(step):
        return remote(1, step, grads_own.at[step], table_o.at[chip, z, core], (w, plane_of(step, 1)))

    def grads_keep():
        return pltpu.make_async_copy(
            grads_own.at[0], table_o.at[chip, z, core], load_sems.at[1, 0]
        )

    def grads_gather(step):
        source = plane_of(step, -1)
        return Gather(2, step, step, lambda i: table_o.at[i // 2, source, i % 2])

    def outs_load(step):
        return pltpu.make_async_copy(outs_in.at[step], outs.at[step], load_sems.at[2, step])

    def near(step, which):
        first, _ = axes(step)
        block = chip ^ 3 if which else chip ^ first
        return remote(
            9 + which, step, outs.at[step, block], outs_one.at[step, which], (w ^ (2 * first), z)
        )

    def cross(step):
        _, second = axes(step)
        return remote(
            11, step, outs.at[step, chip ^ second], outs_two.at[step], (w ^ (2 * second), z)
        )

    def far(step):
        return remote(12, step, outs.at[step, chip], outs_far.at[step - 1], (w, plane_of(step, -1)))

    def dense_part(kind, step, side):
        rows = pl.ds(pl.multiple_of(plane_of(step, 1) * plane_rows, 16), plane_rows)
        return (dense_q, dense_o)[kind].at[rows, at(side * half, half)]

    def dense_load(kind, step):
        return pltpu.make_async_copy(
            dense_part(kind, step, core), dense.at[kind, step], load_sems.at[3 + kind, step]
        )

    def dense_swap(kind, step):
        return remote(
            13 + 4 * kind, step, dense_part(kind, step, 1 - core), dense_got.at[kind, step], (w ^ 1, z)
        )

    def rows_of(block):
        return pl.ds(pl.multiple_of(block * block_rows, 16), block_rows)

    def dense_axes(kind):
        return 1 + kind, 2 - kind

    def dense_near(kind, step, which):
        first, _ = dense_axes(kind)
        block = chip ^ 3 if which else chip ^ first
        return remote(
            14 + 4 * kind + which,
            step,
            dense.at[kind, step, rows_of(block)],
            dense_one.at[kind, step, which],
            (w ^ (2 * first), z),
        )

    def dense_cross(kind, step):
        _, second = dense_axes(kind)
        return remote(
            16 + 4 * kind,
            step,
            dense.at[kind, step, rows_of(chip ^ second)],
            dense_two.at[kind, step],
            (w ^ (2 * second), z),
        )

    def place_of(owner):
        return rows_of(owner // 2), at(lax.rem(owner, 2) * half, half)

    def dense_ring(kind, step):
        own = dense.at[kind, step, rows_of(chip)]
        rows, columns = place_of(w)
        to = q_o.at[z, rows, columns] if kind == 0 else dense_far.at[step - 1]
        return remote(21 + kind, step, own, to, (w, plane_of(step, 1)))

    def dense_keep():
        rows, columns = place_of(w)
        return pltpu.make_async_copy(
            dense.at[0, 0, rows_of(chip)], q_o.at[z, rows, columns], load_sems.at[1, 1]
        )

    def dense_last():
        rows, columns = place_of(w)
        return pltpu.make_async_copy(dense_sum, o_o.at[rows, columns], load_sems.at[1, 2])

    def q_slot(step):
        source = plane_of(step, -1)

        def slot(owner):
            rows, columns = place_of(owner)
            return q_o.at[source, rows, columns]

        return slot

    def o_slot(owner):
        rows, columns = place_of(owner)
        return o_o.at[rows, columns]

    def q_gather(step):
        return Gather(23, step, step, q_slot(step))

    def o_gather():
        return Gather(30, 0, 0, o_slot)

    def first_ring(step):
        return remote(37, step, first_in.at[plane_of(step, 1)], first_o.at[z], (w, plane_of(step, 1)))

    def first_keep():
        return pltpu.make_async_copy(first_in.at[z], first_o.at[z], load_sems.at[1, 3])

    for step in steps:
        grads_load(step).start()
    for step in steps:
        outs_load(step).start()
        for kind in (0, 1):
            dense_load(kind, step).start()
    first_keep().start()
    greet(w, z)
    for step in steps:
        grads_swap(step).start()
    for step in steps:
        for kind in (0, 1):
            dense_swap(kind, step).start()
    for step in (1, 2, 3):
        first_ring(step).start()

    def grads_ready(step):
        grads_load(step).wait()
        grads_swap(step).wait_recv()
        add_blocks(grads_own.at[step], grads_own.at[step], grads_got.at[step])

    def dense_ready(kind, step):
        dense_load(kind, step).wait()
        dense_swap(kind, step).wait_recv()
        add_blocks(dense.at[kind, step], dense.at[kind, step], dense_got.at[kind, step])
        dense_near(kind, step, 1).start()
        dense_near(kind, step, 0).start()

    loop(1, 4, lambda step: (grads_ready(step), grads_ring(step).start()))
    grads_ready(0)
    keep = grads_keep()
    keep.start()

    def dense_start(step):
        dense_ready(0, step)
        dense_ready(1, step)

    loop(0, 4, dense_start)
    keep.wait()
    grads_gather(0).begin()

    def outs_start(step):
        outs_load(step).wait()
        near(step, 1).start()
        near(step, 0).start()

    loop(0, 4, outs_start)

    def dense_cross_start(step):
        for kind in (0, 1):
            _, second = dense_axes(kind)
            dense_near(kind, step, 1).wait_recv()
            block = dense.at[kind, step, rows_of(chip ^ second)]
            add_blocks(block, block, dense_one.at[kind, step, 1])
            dense_cross(kind, step).start()

    loop(0, 4, dense_cross_start)

    def grads_next(step):
        grads_ring(step).wait_recv()
        grads_gather(step).begin()

    loop(1, 2, grads_next)

    def outs_cross(step):
        _, second = axes(step)
        near(step, 1).wait_recv()
        block = outs.at[step, chip ^ second]
        add_blocks(block, block, outs_one.at[step, 1])
        cross(step).start()

    loop(0, 4, outs_cross)

    def dense_finish(step):
        for kind in (0, 1):
            dense_near(kind, step, 0).wait_recv()
            dense_cross(kind, step).wait_recv()
            block = dense.at[kind, step, rows_of(chip)]
            add_blocks(block, block, dense_one.at[kind, step, 0], dense_two.at[kind, step])

    loop(0, 4, dense_finish)

    def dense_ring_start(step):
        dense_ring(0, step).start()
        dense_ring(1, step).start()

    loop(1, 4, dense_ring_start)
    keep = dense_keep()
    keep.start()
    loop(2, 3, grads_next)
    loop(0, 1, lambda step: grads_gather(step).relay())
    keep.wait()
    q_gather(0).begin()

    def outs_finish(step):
        near(step, 0).wait_recv()
        cross(step).wait_recv()
        block = outs.at[step, chip]
        add_blocks(block, block, outs_one.at[step, 0], outs_two.at[step])

        @pl.when(step > 0)
        def _():
            far(step).start()

    loop(0, 4, outs_finish)
    loop(3, 4, grads_next)

    def q_next(step):
        dense_ring(0, step).wait_recv()
        q_gather(step).begin()
        dense_ring(1, step).wait_recv()

    loop(1, 4, q_next)
    add_blocks(
        dense_sum, dense.at[1, 0, rows_of(chip)], dense_far.at[0], dense_far.at[1], dense_far.at[2]
    )
    keep = dense_last()
    keep.start()
    keep.wait()
    o_gather().begin()
    loop(1, 4, lambda step: grads_gather(step).relay())
    loop(0, 4, lambda step: q_gather(step).relay())
    o_gather().relay()
    loop(1, 4, lambda step: far(step).wait_recv())
    add_blocks(sums_o, outs.at[0, chip], outs_far.at[0], outs_far.at[1], outs_far.at[2])
    loop(0, 4, lambda step: grads_gather(step).end())
    loop(0, 4, lambda step: q_gather(step).end())
    o_gather().end()
    loop(0, 4, lambda step: grads_gather(step).settle())
    loop(0, 4, lambda step: q_gather(step).settle())
    o_gather().settle()
    first_keep().wait()

    def settle(step):
        grads_swap(step).wait_send()
        near(step, 0).wait_send()
        near(step, 1).wait_send()
        cross(step).wait_send()
        for kind in (0, 1):
            dense_swap(kind, step).wait_send()
            dense_near(kind, step, 0).wait_send()
            dense_near(kind, step, 1).wait_send()
            dense_cross(kind, step).wait_send()

    loop(0, 4, settle)

    def settle_rings(step):
        first_ring(step).wait_recv()
        first_ring(step).wait_send()
        grads_ring(step).wait_send()
        far(step).wait_send()
        dense_ring(0, step).wait_send()
        dense_ring(1, step).wait_send()

    loop(1, 4, settle_rings)


def finish(outs, grads, first, dense_q, dense_o, collective):
    rows, width = first.shape[1:]
    plane_rows = width // PLANES
    block = (plane_rows // 4, width // 2)
    return pl.pallas_call(
        finish_kernel,
        out_shape=[
            jax.ShapeDtypeStruct((rows, width), F32),
            jax.ShapeDtypeStruct((4, PLANES) + grads.shape[1:], BF16),
            jax.ShapeDtypeStruct(first.shape, BF16),
            jax.ShapeDtypeStruct((PLANES, plane_rows, width), BF16),
            jax.ShapeDtypeStruct((plane_rows, width), BF16),
        ],
        in_specs=[pl.BlockSpec(memory_space=pl.ANY)] * 5,
        out_specs=[pl.BlockSpec(memory_space=pltpu.VMEM)] + [pl.BlockSpec(memory_space=pl.ANY)] * 4,
        scratch_shapes=[
            pltpu.VMEM((4, 4, rows, width), BF16),
            pltpu.VMEM((4, 2, rows, width), BF16),
            pltpu.VMEM((4, rows, width), BF16),
            pltpu.VMEM((3, rows, width), BF16),
            pltpu.VMEM((4,) + grads.shape[2:], BF16),
            pltpu.VMEM((4,) + grads.shape[2:], BF16),
            pltpu.VMEM((2, 4, plane_rows, width // 2), BF16),
            pltpu.VMEM((2, 4, plane_rows, width // 2), BF16),
            pltpu.VMEM((2, 4, 2) + block, BF16),
            pltpu.VMEM((2, 4) + block, BF16),
            pltpu.VMEM((3,) + block, BF16),
            pltpu.VMEM(block, BF16),
            pltpu.SemaphoreType.DMA((5, 4)),
            pltpu.SemaphoreType.DMA((38, 4)),
            pltpu.SemaphoreType.DMA((38, 4)),
        ],
        compiler_params=pltpu.CompilerParams(
            collective_id=collective, has_side_effects=True, vmem_limit_bytes=60 * 2**20
        ),
        name="finish",
    )(outs, grads, first, dense_q, dense_o)


def widen_kernel(table, up_o, down_o):
    columns = table.shape[2]
    split = up_o.shape[2]
    for low in range(0, columns, 128):
        part = jnp.swapaxes(table[:, :, low : low + 128].astype(F32), 0, 1)
        if low < split:
            up_o[:, :, low : low + 128] = part
        else:
            down_o[:, :, low - split : low - split + 128] = part


def widen(table):
    experts, rows, columns = table.shape
    split = columns // 3 * 2
    step = 16
    return pl.pallas_call(
        widen_kernel,
        grid=(rows // step,),
        out_shape=[
            jax.ShapeDtypeStruct((rows, experts, split), F32),
            jax.ShapeDtypeStruct((rows, experts, columns - split), F32),
        ],
        in_specs=[pl.BlockSpec((experts, step, columns), lambda i: (0, i, 0))],
        out_specs=[
            pl.BlockSpec((step, experts, split), lambda i: (i, 0, 0)),
            pl.BlockSpec((step, experts, columns - split), lambda i: (i, 0, 0)),
        ],
        compiler_params=pltpu.CompilerParams(vmem_limit_bytes=48 * 2**20),
        name="widen",
    )(table)


def windows(x):
    size = WINDOW * HEAD_DIM
    return jnp.stack([x[:, s * HEAD_DIM : s * HEAD_DIM + size] for s in STARTS])


def from_windows(x):
    return jnp.concatenate(
        [x[p, :, a * HEAD_DIM : b * HEAD_DIM] for p, (a, b) in enumerate(KEEP)], axis=1
    )


def dot(a, b, dims, out=F32):
    return lax.dot_general(a, b, ((dims[0], dims[1]), ((), ())), preferred_element_type=F32).astype(out)


def expert_local(
    tokens, seq_ids, routes, cotangent, gain_attn, w_qkv, w_out, gain_ffn, w_router, w_up, w_down
):
    rows, width = tokens.shape
    own = w_out.shape[0]
    experts = w_router.shape[1]
    seqlen = PLANES * rows
    size = WINDOW * HEAD_DIM
    scale = HEAD_DIM ** (-0.5)
    z = lax.axis_index("narrow")

    misc = jnp.concatenate(
        [
            jnp.zeros((own, 1), BF16),
            w_router,
            gain_attn[:, None],
            gain_ffn[:, None],
            jnp.zeros((own, 128 - experts - 3), BF16),
        ],
        axis=1,
    )
    wq_send = jnp.concatenate(
        [windows(w_qkv[:, i * width : (i + 1) * width]) for i in range(3)]
        + [jnp.broadcast_to(misc[None], (PLANES, own, 128))],
        axis=2,
    )
    we_send = jnp.concatenate([w_up, w_down], axis=2).reshape(own, 4, PLANES, 3 * FF)
    we_send = jnp.transpose(we_send, (2, 1, 0, 3))
    choose = routes[:, :, None] == jnp.arange(experts, dtype=jnp.int32)[None, None, :]
    member = jnp.any(choose, axis=1)
    member_cols = jnp.concatenate(
        [jnp.ones((rows, 1), BF16), member.astype(BF16), jnp.zeros((rows, 127 - experts), BF16)],
        axis=1,
    )
    cot_send = jnp.concatenate([cotangent, member_cols], axis=1)
    ids_send = jnp.broadcast_to(seq_ids.astype(BF16)[None, :], (16, rows))
    tok_all, ids_all, wq_all, wo_all, we_all, cot_all = spread_inputs(
        tokens, ids_send, wq_send, w_out, we_send, cot_send
    )
    wq_all = wq_all.reshape(width, 3 * size + 128)
    misc_all = wq_all[:, 3 * size :]
    wq = wq_all[:, : 3 * size]
    router = misc_all[:, 1 : experts + 1]
    gain_one = misc_all[:, experts + 1].astype(F32)
    gain_two = misc_all[:, experts + 2].astype(F32)
    out_weight = wo_all.reshape(width, width)

    seq_in = tok_all.reshape(seqlen, width).astype(F32)
    seq_normed = seq_in * rms_inverse(seq_in)
    first_in = (seq_normed * gain_one).astype(BF16)
    projected = dot(first_in, wq, ((1,), (0,)))
    cosine, sine_table = rotary(jnp.arange(seqlen, dtype=F32), HEAD_DIM)
    pq, pk, pv = (
        projected[:, i * size : (i + 1) * size].reshape(seqlen, WINDOW, HEAD_DIM) for i in range(3)
    )
    query_rows = (rotate(pq, cosine, sine_table) * scale).astype(BF16)
    key_rows = rotate(pk, cosine, sine_table).astype(BF16)
    value_rows = pv.astype(BF16)
    ids = ids_all[:, 0, :].reshape(seqlen)
    at = jnp.arange(seqlen, dtype=jnp.int32)
    allowed = ((at[None, :] <= at[:, None]) & (ids[None, :] == ids[:, None]))[None]
    scores = jnp.einsum("qhd,khd->hqk", query_rows, key_rows, preferred_element_type=F32)
    masked = jnp.where(allowed, scores, -1e30)
    top = jnp.max(masked, axis=2, keepdims=True)
    powers = jnp.where(allowed, jnp.exp(masked - top), 0.0)
    weights_exact = powers * (1.0 / jnp.sum(powers, axis=2, keepdims=True))
    weights_low = weights_exact.astype(BF16)
    mixed_exact = jnp.einsum("hqk,khd->qhd", weights_low, value_rows, preferred_element_type=F32)
    mixed_send = mixed_exact.astype(BF16).reshape(PLANES, rows, size)
    mixed = from_windows(swap_planes(mixed_send, 2))
    middle = tokens.astype(F32) + dot(mixed, out_weight, ((1,), (0,)))
    inverse_two = rms_inverse(middle)
    normed_two = middle * inverse_two
    second_in = (normed_two * gain_two).astype(BF16)

    weights = we_all.reshape(width, 3 * FF)
    grads, outs, sums = run_experts(second_in, cot_all, weights, misc_all, 3)

    hi = sums[:, width + 1 : width + 1 + experts]
    lo = sums[:, width + 33 : width + 33 + experts]
    grad_probs = hi + lo
    probs = jax.nn.softmax(dot(second_in, router, ((1,), (0,))), axis=-1)
    grad_logits = (
        probs * (grad_probs - jnp.sum(probs * grad_probs, axis=1, keepdims=True))
    ).astype(BF16)
    grad_second = sums[:, :width] + dot(grad_logits, router, ((1,), (1,)))
    grad_output = cotangent.astype(F32)
    grad_normed_two = grad_second * gain_two
    gain_two_part = jnp.sum(grad_second * normed_two, axis=0)
    grad_middle = grad_output + inverse_two * (
        grad_normed_two
        - normed_two * jnp.mean(grad_normed_two * normed_two, axis=-1, keepdims=True)
    )
    router_part = dot(second_in, grad_logits, ((0,), (0,)))
    grad_attention = grad_middle.astype(BF16)
    grad_out_part = dot(mixed, grad_attention, ((0,), (0,)), BF16)
    grad_mixed = dot(grad_attention, out_weight, ((1,), (1,)), BF16)

    valid = jnp.array(
        [[a <= i < b for i in range(WINDOW)] for a, b in KEEP], dtype=BF16
    )[z]
    grad_heads = swap_planes(windows(grad_mixed), 5).reshape(seqlen, WINDOW, HEAD_DIM)
    grad_heads = grad_heads * valid[None, :, None]
    row_delta = jnp.sum(grad_heads.astype(F32) * mixed_exact, axis=2).T
    grad_values = jnp.einsum("hqk,qhd->khd", weights_low, grad_heads, preferred_element_type=F32)
    grad_weights = jnp.einsum("qhd,khd->hqk", grad_heads, value_rows, preferred_element_type=F32)
    grad_scores = (weights_exact * (grad_weights - row_delta[..., None])).astype(BF16)
    grad_query = jnp.einsum("hqk,khd->qhd", grad_scores, key_rows, preferred_element_type=F32)
    grad_keys = jnp.einsum("hqk,qhd->khd", grad_scores, query_rows, preferred_element_type=F32)
    grad_projected = jnp.concatenate(
        [
            (rotate_back(grad_query, cosine, sine_table) * scale).reshape(seqlen, size),
            rotate_back(grad_keys, cosine, sine_table).reshape(seqlen, size),
            grad_values.reshape(seqlen, size),
        ],
        axis=1,
    ).astype(BF16)
    grad_qkv_part = dot(first_in, grad_projected, ((0,), (0,)), BF16)
    first_part = dot(grad_projected, wq, ((1,), (1,)))
    gain_one_part = jnp.sum(first_part * seq_normed, axis=0)
    misc_part = jnp.concatenate(
        [
            router_part,
            gain_one_part[:, None],
            gain_two_part[:, None],
            jnp.zeros((width, 128 - experts - 2), F32),
        ],
        axis=1,
    ).astype(BF16)
    dense_q = jnp.concatenate([grad_qkv_part, misc_part], axis=1)
    sums, table, first_all, q_all, o_all = finish(
        outs,
        grads.reshape(PLANES, 2, width // PLANES // 2, 3 * FF),
        first_part.astype(BF16).reshape(PLANES, rows, width),
        dense_q,
        grad_out_part,
        6,
    )
    output = (middle + sums).astype(BF16)
    grad_first = jnp.sum(first_all.astype(F32), axis=0)
    inputs = tokens.astype(F32)
    inverse_one = rms_inverse(inputs)
    normed_one = inputs * inverse_one
    grad_normed_one = grad_first * gain_one
    grad_tokens = grad_middle + inverse_one * (
        grad_normed_one
        - normed_one * jnp.mean(grad_normed_one * normed_one, axis=-1, keepdims=True)
    )
    out_sum = o_all.astype(F32)
    qkv_sum = jnp.concatenate(
        [from_windows(q_all[:, :, i * size : (i + 1) * size]) for i in range(3)], axis=1
    ).astype(F32)
    misc_sum = jnp.sum(q_all[:, :, 3 * size :].astype(F32), axis=0)

    up_sum, down_sum = widen(table.reshape(experts + 1, width // PLANES, 3 * FF))
    return (
        output,
        grad_tokens.astype(BF16),
        misc_sum[:, experts],
        qkv_sum,
        out_sum,
        misc_sum[:, experts + 1],
        misc_sum[:, :experts],
        up_sum,
        down_sum,
    )


def solution(mesh):
    fits = mesh.shape["wide"] == 8 and mesh.shape["narrow"] == PLANES
    return jax.shard_map(
        expert_local if fits else local,
        mesh=mesh,
        in_specs=(
            P(("wide", "narrow"), None),
            P(("wide", "narrow")),
            P(("wide", "narrow"), None),
            P(("wide", "narrow"), None),
            P(("wide", "narrow")),
            P(("wide", "narrow"), None),
            P(("wide", "narrow"), None),
            P(("wide", "narrow")),
            P(("wide", "narrow"), None),
            P(("wide", "narrow"), None, None),
            P(("wide", "narrow"), None, None),
        ),
        out_specs=(
            P(("wide", "narrow"), None),
            P(("wide", "narrow"), None),
            P("narrow"),
            P("narrow", None),
            P("narrow", None),
            P("narrow"),
            P("narrow", None),
            P("narrow", None, None),
            P("narrow", None, None),
        ),
        check_vma=False,
    )
```

```python
import jax
import jax.numpy as jnp
from jax import lax
from jax.experimental import pallas as pl
from jax.experimental.pallas import tpu as pltpu
from jax.sharding import PartitionSpec as P

HEADS = 10
HEAD_DIM = 128
FF = 896
CAP = 72


epsilon = 1e-06


def shortened(x):
    return jax.tree.map(lambda a: a.astype(jnp.bfloat16) if a.dtype == jnp.float32 else a, x)


def rms_inverse(values):
    return lax.rsqrt(jnp.mean(values * values, axis=-1, keepdims=True) + epsilon)


def rotary(positions, head_size):
    half_dim = head_size // 2
    frequency = 10000.0 ** (-jnp.arange(half_dim, dtype=jnp.float32) / half_dim)
    angles = positions[:, None] * frequency[None, :]
    cosine = jnp.concatenate([jnp.cos(angles), jnp.cos(angles)], axis=1)[:, None, :]
    sine_table = jnp.concatenate([jnp.sin(angles), jnp.sin(angles)], axis=1)[:, None, :]
    return (cosine, sine_table)


def rotate(values, cosine, sine_table):
    half_dim = values.shape[-1] // 2
    turned = jnp.concatenate([-values[..., half_dim:], values[..., :half_dim]], axis=-1)
    return values * cosine + turned * sine_table


def rotate_back(grads, cosine, sine_table):
    half_dim = grads.shape[-1] // 2
    scaled = grads * sine_table
    turned = jnp.concatenate([scaled[..., half_dim:], -scaled[..., :half_dim]], axis=-1)
    return grads * cosine + turned


def expert_weight_terms(
    routed_in, routed_grad, shared_in, shared_grad, slot_grads, slot_acts, shared_grads, shared_acts
):
    up_routed = jnp.einsum(
        "ecd,ecf->def", routed_in, slot_grads, preferred_element_type=jnp.float32
    )
    up_shared = jnp.einsum("td,tf->df", shared_in, shared_grads, preferred_element_type=jnp.float32)
    down_routed = jnp.einsum(
        "ecd,ecf->def", routed_grad, slot_acts, preferred_element_type=jnp.float32
    )
    down_shared = jnp.einsum(
        "td,tf->df", shared_grad, shared_acts, preferred_element_type=jnp.float32
    )
    up_all = jnp.concatenate([up_shared[:, None], up_routed], axis=1)
    down_all = jnp.concatenate([down_shared[:, None], down_routed], axis=1)
    combined = jnp.concatenate([up_all, down_all], axis=2)
    return combined.reshape(combined.shape[0], -1)


def local(
    tokens, seq_ids, routes, cotangent, gain_attn, w_qkv, w_out, gain_ffn, w_router, w_up, w_down
):
    row_count = tokens.shape[0]
    model_width = tokens.shape[1]
    query_scale = HEAD_DIM ** (-0.5)
    hidden = FF
    capacity = CAP
    inputs = tokens.astype(jnp.float32)
    gain_one, qkv_weight, out_weight = (
        lax.all_gather(gain_attn, ("wide", "narrow"), axis=0, tiled=True),
        lax.all_gather(w_qkv, ("wide", "narrow"), axis=0, tiled=True),
        lax.all_gather(w_out, ("wide", "narrow"), axis=0, tiled=True),
    )
    inverse_one = rms_inverse(inputs)
    normed_one = inputs * inverse_one
    first_in = (normed_one * gain_one.astype(jnp.float32)).astype(jnp.bfloat16)
    projected = jnp.dot(first_in, qkv_weight, preferred_element_type=jnp.float32)
    offset = lax.axis_index("narrow") * row_count
    query_pos = offset + jnp.arange(row_count, dtype=jnp.int32)
    cosine, sine_table = rotary(query_pos.astype(jnp.float32), HEAD_DIM)
    query_rows = (
        rotate(projected[:, :model_width].reshape(row_count, HEADS, HEAD_DIM), cosine, sine_table)
        * query_scale
    ).astype(jnp.bfloat16)
    key_rows = (
        rotate(
            projected[:, model_width : 2 * model_width].reshape(row_count, HEADS, HEAD_DIM),
            cosine,
            sine_table,
        )
        .astype(jnp.bfloat16)
        .reshape(row_count, model_width)
    )
    value_rows = projected[:, 2 * model_width :].astype(jnp.bfloat16)
    all_keys, all_values, all_ids = (
        lax.all_gather(key_rows, "narrow", axis=0, tiled=True),
        lax.all_gather(value_rows, "narrow", axis=0, tiled=True),
        lax.all_gather(seq_ids.astype(jnp.bfloat16), "narrow", axis=0, tiled=True),
    )
    seqlen = all_keys.shape[0]
    block_len = min(512, seqlen)
    num_blocks = seqlen // block_len
    own_ids = seq_ids.astype(jnp.float32)

    def block_parts(block_index):
        first_row = block_index * block_len
        key_pos = first_row + jnp.arange(block_len, dtype=jnp.int32)
        key_ids = lax.dynamic_slice_in_dim(all_ids, first_row, block_len, 0).astype(jnp.float32)
        allowed = (key_pos[None, :] <= query_pos[:, None]) & (key_ids[None, :] == own_ids[:, None])
        key_block = lax.dynamic_slice_in_dim(all_keys, first_row, block_len, 0).reshape(
            block_len, HEADS, HEAD_DIM
        )
        value_block = lax.dynamic_slice_in_dim(all_values, first_row, block_len, 0).reshape(
            block_len, HEADS, HEAD_DIM
        )
        scores = jnp.einsum(
            "qhd,khd->hqk", query_rows, key_block, preferred_element_type=jnp.float32
        )
        return (allowed[None], key_block, value_block, scores)

    def max_step(state_pair, block_index):
        running_max, running_sum = state_pair
        allowed, key_block, value_block, scores = block_parts(block_index)
        masked = jnp.where(allowed, scores, -1e30)
        new_max = jnp.maximum(running_max, jnp.max(masked, axis=2))
        added = jnp.sum(jnp.where(allowed, jnp.exp(masked - new_max[..., None]), 0.0), axis=2)
        return ((new_max, running_sum * jnp.exp(running_max - new_max) + added), None)

    start_max = jnp.full((HEADS, row_count), -1e30, jnp.float32)
    start_sum = jnp.zeros((HEADS, row_count), jnp.float32)
    (top_score, exp_total), unused = lax.scan(
        max_step, (start_max, start_sum), jnp.arange(num_blocks)
    )
    log_total = top_score + jnp.log(exp_total)

    def out_step(accum, block_index):
        allowed, key_block, value_block, scores = block_parts(block_index)
        weights_low = jnp.where(allowed, jnp.exp(scores - log_total[..., None]), 0.0).astype(
            jnp.bfloat16
        )
        return (
            accum
            + jnp.einsum(
                "hqk,khd->hqd", weights_low, value_block, preferred_element_type=jnp.float32
            ),
            None,
        )

    accum_start = jnp.zeros((HEADS, row_count, HEAD_DIM), jnp.float32)
    mixed_heads, unused = lax.scan(out_step, accum_start, jnp.arange(num_blocks))
    mixed_exact = jnp.transpose(mixed_heads, (1, 0, 2))
    mixed = mixed_exact.reshape(row_count, model_width).astype(jnp.bfloat16)
    middle = inputs + jnp.dot(mixed, out_weight, preferred_element_type=jnp.float32)
    gain_two, router_weight, up_weight, down_weight = (
        lax.all_gather(gain_ffn, ("wide", "narrow"), axis=0, tiled=True),
        lax.all_gather(w_router, ("wide", "narrow"), axis=0, tiled=True),
        lax.all_gather(w_up, ("wide", "narrow"), axis=0, tiled=True),
        lax.all_gather(w_down, ("wide", "narrow"), axis=0, tiled=True),
    )
    inverse_two = rms_inverse(middle)
    normed_two = middle * inverse_two
    second_in = (normed_two * gain_two.astype(jnp.float32)).astype(jnp.bfloat16)
    logits = jnp.dot(second_in, router_weight, preferred_element_type=jnp.float32)
    router_probs = jax.nn.softmax(logits, axis=-1)
    experts = logits.shape[1]
    choose = routes[:, :, None] == jnp.arange(experts, dtype=jnp.int32)[None, None, :]
    member = jnp.sum(choose.astype(jnp.float32), axis=1)
    earlier = (jnp.arange(row_count)[:, None] > jnp.arange(row_count)[None, :]).astype(jnp.bfloat16)
    before = jnp.dot(earlier, member.astype(jnp.bfloat16), preferred_element_type=jnp.float32)
    slot_hit = (member.T[:, None, :] > 0.5) & (
        before.T[:, None, :] == jnp.arange(capacity, dtype=jnp.float32)[None, :, None]
    )
    dispatch = slot_hit.astype(jnp.bfloat16)
    gathered_in = jnp.einsum(
        "ect,td->ecd", dispatch, second_in, preferred_element_type=jnp.float32
    ).astype(jnp.bfloat16)
    gate_weights = router_probs * member
    gate_up = jnp.einsum(
        "ecd,def->ecf", gathered_in, up_weight[:, 1:], preferred_element_type=jnp.float32
    )
    gate_part = gate_up[..., :hidden]
    up_part = gate_up[..., hidden:]
    activated = (jax.nn.silu(gate_part) * up_part).astype(jnp.bfloat16)
    expert_rows = jnp.einsum(
        "ecf,def->ecd", activated, down_weight[:, 1:], preferred_element_type=jnp.float32
    ).astype(jnp.bfloat16)
    selected = jnp.einsum("ect,ecd->etd", dispatch, expert_rows, preferred_element_type=jnp.float32)
    routed = jnp.sum(gate_weights.T[:, :, None] * selected, axis=0)
    shared_up = jnp.dot(second_in, up_weight[:, 0], preferred_element_type=jnp.float32)
    shared_gate = shared_up[:, :hidden]
    shared_lin = shared_up[:, hidden:]
    shared_act = (jax.nn.silu(shared_gate) * shared_lin).astype(jnp.bfloat16)
    shared_out = jnp.einsum(
        "tf,df->td", shared_act, down_weight[:, 0], preferred_element_type=jnp.float32
    )
    output = (middle + shared_out + routed).astype(jnp.bfloat16)
    gain_two, router_weight, up_weight, down_weight = (
        lax.all_gather(gain_ffn, ("wide", "narrow"), axis=0, tiled=True),
        lax.all_gather(w_router, ("wide", "narrow"), axis=0, tiled=True),
        lax.all_gather(w_up, ("wide", "narrow"), axis=0, tiled=True),
        lax.all_gather(w_down, ("wide", "narrow"), axis=0, tiled=True),
    )
    grad_output = cotangent.astype(jnp.float32)
    slot_token = jnp.sum(
        jnp.where(slot_hit, jnp.arange(row_count, dtype=jnp.int32)[None, None, :], 0), axis=2
    )
    slot_gate = jnp.sum(jnp.where(slot_hit, gate_weights.T[:, None, :], 0.0), axis=2)
    grad_rows = (slot_gate[..., None] * grad_output[slot_token]).astype(jnp.bfloat16)
    grad_probs = jnp.sum(selected * grad_output[None], axis=2).T * member
    grad_logits = (
        router_probs * (grad_probs - jnp.sum(router_probs * grad_probs, axis=1, keepdims=True))
    ).astype(jnp.bfloat16)
    grad_act = jnp.einsum(
        "ecd,def->ecf", grad_rows, down_weight[:, 1:], preferred_element_type=jnp.float32
    )
    sigmoid_gate = jax.nn.sigmoid(gate_part)
    grad_gate_up = jnp.concatenate(
        [
            grad_act * up_part * sigmoid_gate * (1.0 + gate_part * (1.0 - sigmoid_gate)),
            grad_act * jax.nn.silu(gate_part),
        ],
        axis=-1,
    ).astype(jnp.bfloat16)
    grad_gathered = jnp.einsum(
        "ecf,def->ecd", grad_gate_up, up_weight[:, 1:], preferred_element_type=jnp.float32
    )
    slot_index = jnp.sum(jnp.where(choose, before[:, None, :], 0.0), axis=2).astype(jnp.int32)
    flat_index = routes * capacity + slot_index
    grad_second = jnp.sum(grad_gathered.reshape(-1, model_width)[flat_index], axis=1)
    grad_shared_act = jnp.einsum(
        "td,df->tf", cotangent, down_weight[:, 0], preferred_element_type=jnp.float32
    )
    sigmoid_shared = jax.nn.sigmoid(shared_gate)
    grad_shared_up = jnp.concatenate(
        [
            grad_shared_act
            * shared_lin
            * sigmoid_shared
            * (1.0 + shared_gate * (1.0 - sigmoid_shared)),
            grad_shared_act * jax.nn.silu(shared_gate),
        ],
        axis=-1,
    ).astype(jnp.bfloat16)
    grad_second = grad_second + jnp.einsum(
        "tf,df->td", grad_shared_up, up_weight[:, 0], preferred_element_type=jnp.float32
    )
    grad_second = grad_second + jnp.einsum(
        "te,de->td", grad_logits, router_weight, preferred_element_type=jnp.float32
    )
    grad_normed_two = grad_second * gain_two.astype(jnp.float32)
    grad_gain_two = jnp.sum(grad_second * normed_two, axis=0)
    grad_middle = grad_output + inverse_two * (
        grad_normed_two
        - normed_two * jnp.mean(grad_normed_two * normed_two, axis=-1, keepdims=True)
    )
    grad_router = jnp.einsum(
        "td,te->de", second_in, grad_logits, preferred_element_type=jnp.float32
    )
    narrow_rows = model_width // lax.axis_size("narrow")
    routed_cols, grad_cols, shared_cols, cotangent_cols = (
        lax.all_to_all(gathered_in, "narrow", split_axis=2, concat_axis=1, tiled=True),
        lax.all_to_all(grad_rows, "narrow", split_axis=2, concat_axis=1, tiled=True),
        lax.all_to_all(second_in[None], "narrow", split_axis=2, concat_axis=1, tiled=True),
        lax.all_to_all(cotangent[None], "narrow", split_axis=2, concat_axis=1, tiled=True),
    )
    slot_grads, slot_acts, shared_grads, shared_acts = (
        lax.all_gather(grad_gate_up, "narrow", axis=1, tiled=True),
        lax.all_gather(activated, "narrow", axis=1, tiled=True),
        lax.all_gather(grad_shared_up[None], "narrow", axis=1, tiled=True),
        lax.all_gather(shared_act[None], "narrow", axis=1, tiled=True),
    )
    expert_grads = expert_weight_terms(
        routed_cols,
        grad_cols,
        shared_cols[0],
        cotangent_cols[0],
        slot_grads,
        slot_acts,
        shared_grads[0],
        shared_acts[0],
    )
    gain_one, qkv_weight, out_weight = (
        lax.all_gather(gain_attn, ("wide", "narrow"), axis=0, tiled=True),
        lax.all_gather(w_qkv, ("wide", "narrow"), axis=0, tiled=True),
        lax.all_gather(w_out, ("wide", "narrow"), axis=0, tiled=True),
    )
    grad_attention = grad_middle.astype(jnp.bfloat16)
    grad_out_weight = jnp.einsum(
        "td,te->de", mixed, grad_attention, preferred_element_type=jnp.float32
    )
    grad_mixed = jnp.einsum(
        "te,de->td", grad_attention, out_weight, preferred_element_type=jnp.float32
    ).astype(jnp.bfloat16)
    grad_heads = grad_mixed.reshape(row_count, HEADS, HEAD_DIM)
    row_delta = jnp.sum(grad_heads.astype(jnp.float32) * mixed_exact, axis=2).T

    def back_step(grad_query, block_index):
        allowed, key_block, value_block, scores = block_parts(block_index)
        weights_exact = jnp.where(allowed, jnp.exp(scores - log_total[..., None]), 0.0)
        weights_low = weights_exact.astype(jnp.bfloat16)
        grad_value = jnp.einsum(
            "hqk,qhd->khd", weights_low, grad_heads, preferred_element_type=jnp.float32
        )
        grad_weights = jnp.einsum(
            "qhd,khd->hqk", grad_heads, value_block, preferred_element_type=jnp.float32
        )
        grad_scores = (weights_exact * (grad_weights - row_delta[..., None])).astype(jnp.bfloat16)
        grad_query = grad_query + jnp.einsum(
            "hqk,khd->qhd", grad_scores, key_block, preferred_element_type=jnp.float32
        )
        grad_key = jnp.einsum(
            "hqk,qhd->khd", grad_scores, query_rows, preferred_element_type=jnp.float32
        )
        return (
            grad_query,
            (grad_key.reshape(block_len, model_width), grad_value.reshape(block_len, model_width)),
        )

    query_start = jnp.zeros((row_count, HEADS, HEAD_DIM), jnp.float32)
    grad_query, (key_blocks, value_blocks) = lax.scan(
        back_step, query_start, jnp.arange(num_blocks)
    )
    key_partial = key_blocks.reshape(seqlen, model_width)
    value_partial = value_blocks.reshape(seqlen, model_width)
    grad_keys, grad_values = (
        lax.psum_scatter(
            key_partial.astype(jnp.bfloat16), "narrow", scatter_dimension=0, tiled=True
        ).astype(jnp.float32),
        lax.psum_scatter(
            value_partial.astype(jnp.bfloat16), "narrow", scatter_dimension=0, tiled=True
        ).astype(jnp.float32),
    )
    grad_query_raw = rotate_back(grad_query, cosine, sine_table) * query_scale
    grad_key_raw = rotate_back(grad_keys.reshape(row_count, HEADS, HEAD_DIM), cosine, sine_table)
    grad_projected = jnp.concatenate(
        [
            grad_query_raw.reshape(row_count, model_width),
            grad_key_raw.reshape(row_count, model_width),
            grad_values,
        ],
        axis=1,
    ).astype(jnp.bfloat16)
    grad_qkv_weight = jnp.einsum(
        "td,tf->df", first_in, grad_projected, preferred_element_type=jnp.float32
    )
    grad_first = jnp.einsum(
        "tf,df->td", grad_projected, qkv_weight, preferred_element_type=jnp.float32
    )
    grad_normed_one = grad_first * gain_one.astype(jnp.float32)
    grad_gain_one = jnp.sum(grad_first * normed_one, axis=0)
    grad_inputs = grad_middle + inverse_one * (
        grad_normed_one
        - normed_one * jnp.mean(grad_normed_one * normed_one, axis=-1, keepdims=True)
    )
    dense_parts = (
        lax.psum_scatter(
            grad_gain_one.astype(jnp.bfloat16), "narrow", scatter_dimension=0, tiled=True
        ).astype(jnp.float32),
        lax.psum_scatter(
            grad_qkv_weight.astype(jnp.bfloat16), "narrow", scatter_dimension=0, tiled=True
        ).astype(jnp.float32),
        lax.psum_scatter(
            grad_out_weight.astype(jnp.bfloat16), "narrow", scatter_dimension=0, tiled=True
        ).astype(jnp.float32),
        lax.psum_scatter(
            grad_gain_two.astype(jnp.bfloat16), "narrow", scatter_dimension=0, tiled=True
        ).astype(jnp.float32),
        lax.psum_scatter(
            grad_router.astype(jnp.bfloat16), "narrow", scatter_dimension=0, tiled=True
        ).astype(jnp.float32),
    )
    summed = jax.tree.map(
        lambda part: part.astype(jnp.float32),
        lax.psum(shortened((expert_grads,) + tuple(dense_parts)), "wide"),
    )
    expert_grads = summed[0]
    dense_parts = summed[1:]
    gain_one_sum, qkv_sum, out_sum, gain_two_sum, router_sum = dense_parts
    expert_table = expert_grads.reshape(narrow_rows, up_weight.shape[1], 3 * hidden)
    up_sum = expert_table[:, :, : 2 * hidden]
    down_sum = expert_table[:, :, 2 * hidden :]
    return (
        output,
        grad_inputs.astype(jnp.bfloat16),
        gain_one_sum,
        qkv_sum,
        out_sum,
        gain_two_sum,
        router_sum,
        up_sum,
        down_sum,
    )


PLANES = 4
WINDOW = 3
STARTS = (0, 3, 6, 7)
KEEP = ((0, 3), (0, 3), (0, 2), (1, 3))
MESH_IDS = pl.DeviceIdType.MESH
BF16 = jnp.bfloat16
F32 = jnp.float32


def place():
    w = lax.axis_index("wide")
    z = lax.axis_index("narrow")
    return w, z


def other_plane(z, step):
    return lax.rem(z + step, PLANES), lax.rem(z + PLANES - step, PLANES)


class Net:
    def __init__(self, send_sems, recv_sems):
        self.send_sems, self.recv_sems, self.used, self.started = send_sems, recv_sems, 0, []

    def send(self, src, dst, device):
        copy = pltpu.make_async_remote_copy(
            src_ref=src,
            dst_ref=dst,
            send_sem=self.send_sems.at[self.used],
            recv_sem=self.recv_sems.at[self.used],
            device_id=device,
            device_id_type=MESH_IDS,
        )
        self.used += 1
        copy.start()
        self.started.append(copy)
        return copy

    def keep(self, src, dst):
        copy = pltpu.make_async_copy(src, dst, self.send_sems.at[self.used])
        self.used += 1
        copy.start()
        return copy

    def finish(self):
        for copy in self.started:
            copy.wait_send()


def greet(w, z):
    barrier = pltpu.get_barrier_semaphore()
    peers = [(w, lax.rem(z + step, PLANES)) for step in (1, 2, 3)]
    peers += [(w ^ flip, z) for flip in (1, 2, 4, 6)]
    for peer in peers:
        pl.semaphore_signal(barrier, inc=1, device_id=peer, device_id_type=MESH_IDS)
    pl.semaphore_wait(barrier, len(peers))


def comm_call(kernel, name, collective, out_shape, in_spaces, out_spaces, sems, scratch=(), moved=0):
    return pl.pallas_call(
        kernel,
        out_shape=out_shape,
        in_specs=[pl.BlockSpec(memory_space=space) for space in in_spaces],
        out_specs=[pl.BlockSpec(memory_space=space) for space in out_spaces],
        scratch_shapes=[
            *scratch,
            pltpu.SemaphoreType.DMA((sems,)),
            pltpu.SemaphoreType.DMA((sems,)),
        ],
        compiler_params=pltpu.CompilerParams(
            collective_id=collective, has_side_effects=True, vmem_limit_bytes=62 * 2**20
        ),
        name=name,
    )


def mul(a, b, over_a, over_b):
    return lax.dot_general(a, b, (((over_a,), (over_b,)), ((), ())), preferred_element_type=F32)


def at(start, size):
    return pl.ds(pl.multiple_of(start, 128), size)


def loop(first, last, body):
    def step(i, carry):
        body(i)
        return carry

    lax.fori_loop(first, last, step, 0)


def swap_planes_kernel(x, out, send_sems, recv_sems):
    w, z = place()
    greet(w, z)
    net = Net(send_sems, recv_sems)
    own = net.keep(x.at[z], out.at[z])
    copies = []
    for step in (1, 2, 3):
        to, _ = other_plane(z, step)
        copies.append(net.send(x.at[to], out.at[z], (w, to)))
    own.wait()
    for copy in copies:
        copy.wait_recv()
    net.finish()


def swap_planes(x, collective):
    return comm_call(
        swap_planes_kernel,
        "swap_planes",
        collective,
        [jax.ShapeDtypeStruct(x.shape, x.dtype)],
        [pl.ANY],
        [pl.ANY],
        8,
    )(x)[0]


class Links:
    def __init__(self, send_sems, recv_sems):
        self.w, self.z = place()
        self.send_sems, self.recv_sems = send_sems, recv_sems

    def copy(self, kind, step, src, dst, device):
        return pltpu.make_async_remote_copy(
            src_ref=src,
            dst_ref=dst,
            send_sem=self.send_sems.at[kind, step],
            recv_sem=self.recv_sems.at[kind, step],
            device_id=device,
            device_id_type=MESH_IDS,
        )

    def plane(self, step, sign):
        return lax.rem(self.z + PLANES + sign * step, PLANES)


def step_at(z, turn):
    step = 0
    for plane, steps in enumerate(((3, 2, 1, 0), (1, 3, 2, 0), (3, 1, 2, 0), (1, 2, 3, 0))):
        for number, value in enumerate(steps):
            step = jnp.where((z == plane) & (turn == number), value, step)
    return step


class Chain:
    def __init__(self, links, base, own, slot):
        self.links, self.base, self.own, self.slot = links, base, own, slot

    def goes(self, step, up):
        z = self.links.z
        if up:
            return (z >= step) & (z < PLANES - 1)
        return ((z < step) | (step == 0)) & (z > 0)

    def ring(self, step, up, own=False):
        links = self.links
        to = lax.rem(step + 1, 4) if up else lax.rem(step + 3, 4)
        ref = self.slot(links.plane(step, -1))
        return pltpu.make_async_remote_copy(
            src_ref=self.own if own else ref,
            dst_ref=ref,
            send_sem=links.send_sems.at[self.base if up else self.base + 1, step],
            recv_sem=links.recv_sems.at[self.base, to],
            device_id=(links.w, links.z + 1 if up else links.z - 1),
            device_id_type=MESH_IDS,
        )

    def hand_on(self, step, own=False):
        for up in (True, False):

            @pl.when(self.goes(step, up))
            def _():
                self.ring(step, up, own).start()

    def begin(self):
        self.hand_on(0, True)

    def arrive(self, turn):
        step = step_at(self.links.z, turn)
        ref = self.slot(self.links.plane(step, -1))
        self.links.copy(self.base, step, ref, ref, (self.links.w, self.links.z)).wait_recv()
        self.hand_on(step)

    def settle(self):
        def body(step):
            for up in (True, False):

                @pl.when(self.goes(step, up))
                def _():
                    self.ring(step, up).wait_send()

        loop(0, 4, body)


class Gather:
    def __init__(self, links, base, step, turn, slot, cores=True):
        self.links, self.base, self.step, self.slot, self.cores = links, base, step, slot, cores
        self.first = 1 + lax.rem(turn, 2)
        self.second = 3 - self.first

    def copy(self, kind, owner, flip):
        ref = self.slot(owner)
        return self.links.copy(
            self.base + kind, self.step, ref, ref, (self.links.w ^ flip, self.links.z)
        )

    def begin(self):
        w = self.links.w
        self.copy(0, w, 2).start()
        self.copy(1, w, 4).start()
        if self.cores:
            self.copy(4, w, 1).start()

    def relay(self):
        w = self.links.w
        self.copy(0, w, 2).wait_recv()
        self.copy(1, w, 4).wait_recv()
        self.across().start()
        if self.cores:
            self.copy(3, w ^ 2, 1).start()
            self.copy(5, w ^ 4, 1).start()

    def across(self):
        return self.copy(2, self.links.w ^ (2 * self.first), 2 * self.second)

    def end(self):
        self.across().wait_recv()
        if self.cores:
            self.copy(6, self.links.w ^ 6, 1).start()

    def settle(self):
        w = self.links.w
        self.copy(0, w, 2).wait_send()
        self.copy(1, w, 4).wait_send()
        self.across().wait_send()
        if self.cores:
            for kind, owner in ((4, w), (3, w ^ 2), (5, w ^ 4), (6, w ^ 6)):
                copy = self.copy(kind, owner, 1)
                copy.wait_send()
                copy.wait_recv()


def softmax_rows(scores, mask):
    masked = scores + mask
    powers = jnp.exp(masked - jnp.max(masked, axis=1, keepdims=True))
    return powers * (1.0 / jnp.sum(powers, axis=1, keepdims=True))


def start_kernel(
    tok_in, ids_in, wq_in, wo_in, we_in, cot_in, cos_in, sin_in,
    we_o, cot_o, wq_o, wo_o, first_o, qkv_o, exact_o, mixed_o, mixed_rows_o, middle_o, second_o, hop,
    tok, ids, wq_blocks, wo_blocks, staged, mask, mixed_got, mixed_send,
    load_sems, send_sems, recv_sems,
):
    links = Links(send_sems, recv_sems)
    w, z = links.w, links.z
    chip = w // 2
    rows, width = tok_in.shape
    seqlen = PLANES * rows
    size = WINDOW * HEAD_DIM
    own = wo_in.shape[0]
    keeps = [
        pltpu.make_async_copy(src, dst, load_sems.at[i])
        for i, (src, dst) in enumerate(
            (
                (tok_in, tok.at[z]),
                (ids_in, ids.at[z]),
                (wq_in.at[z], wq_blocks.at[w, z]),
                (wo_in, wo_blocks.at[w, z]),
                (cot_in, cot_o.at[chip, z]),
            )
        )
    ]
    for keep in keeps:
        keep.start()
    greet(w, z)

    tok_chain = Chain(links, 0, tok_in, lambda p: tok.at[p])
    ids_chain = Chain(links, 2, ids_in, lambda p: ids.at[p])
    wo_chain = Chain(links, 4, wo_in, lambda p: wo_blocks.at[w, p])
    cot_chain = Chain(links, 6, cot_in, lambda p: cot_o.at[chip, p])

    def wq_ring(step):
        to = links.plane(step, 1)
        return links.copy(8, step, wq_in.at[to], wq_blocks.at[w, z], (w, to))

    def wq_gather(step):
        source = links.plane(step, -1)
        return Gather(links, 9, step, step, lambda i: wq_blocks.at[i, source])

    def wo_gather(turn):
        step = step_at(z, turn)
        source = links.plane(step, -1)
        return Gather(links, 16, step, turn, lambda i: wo_blocks.at[i, source])

    def cot_gather(turn):
        step = step_at(z, turn)
        source = links.plane(step, -1)
        return Gather(links, 23, step, turn, lambda i: cot_o.at[i // 2, source], False)

    def weights_ring(step, flip):
        to = links.plane(step, 1)
        return links.copy(
            26 + flip, step, we_in.at[to, chip ^ flip], hop.at[step - 1, chip ^ flip], (w, to)
        )

    def weights_block(step, flip):
        return hop.at[step - 1, chip ^ flip] if step else we_in.at[z, chip ^ flip]

    def weights_plane(step, flip):
        to = we_o.at[w, links.plane(step, -1)]
        return links.copy(29 + flip, step, weights_block(step, flip), to, (w ^ (2 * flip), z))

    def weights_keep(step):
        return pltpu.make_async_copy(
            weights_block(step, 0), we_o.at[w, links.plane(step, -1)], load_sems.at[6 + step]
        )

    def weights_core(step, flip):
        block = we_o.at[w ^ (2 * flip), links.plane(step, -1)]
        return links.copy(
            34 + flip, step, block if flip else weights_block(step, 0), block, (w ^ 1, z)
        )

    def weights_send(step):
        for flip in (3, 1, 2, 0):
            weights_ring(step, flip).start()

    def weights_next(step):
        for flip in (3, 1, 2):
            if step:
                weights_ring(step, flip).wait_recv()
            weights_plane(step, flip).start()
        if step:
            weights_ring(step, 0).wait_recv()
        weights_core(step, 0).start()
        weights_keep(step).start()

    def weights_end(step):
        for flip in (1, 2, 3):
            weights_plane(step, flip).wait_recv()
            weights_core(step, flip).start()

    def mixed_ring(step):
        to = links.plane(step, 1)
        return links.copy(38, step, mixed_send.at[to], mixed_got.at[z], (w, to))

    tok_chain.begin()
    ids_chain.begin()
    for step in (1, 2, 3):
        wq_ring(step).start()
    for keep in keeps:
        keep.wait()
    wq_gather(0).begin()
    tok_chain.arrive(0)
    ids_chain.arrive(0)
    for step in (1, 2, 3):
        wq_ring(step).wait_recv()
        wq_gather(step).begin()
    wo_chain.begin()
    tok_chain.arrive(1)
    ids_chain.arrive(1)
    cot_chain.begin()
    end_plane = (z == 0) | (z == PLANES - 1)

    @pl.when(jnp.logical_not(end_plane))
    def _():
        tok_chain.arrive(2)
        ids_chain.arrive(2)

    loop(0, 4, lambda step: wq_gather(step).relay())

    @pl.when(end_plane)
    def _():
        tok_chain.arrive(2)
        ids_chain.arrive(2)
        weights_send(1)
        weights_send(3)

    wo_chain.arrive(0)
    wo_gather(0).begin()
    wo_gather(3).begin()
    cot_gather(3).begin()
    weights_next(0)
    for i in range(PLANES):
        for j in range(PLANES):
            here = (slice(i * rows, (i + 1) * rows), slice(j * rows, (j + 1) * rows))
            if j > i:
                mask[here] = jnp.full((rows, rows), -1e30, F32)
            else:
                same = ids[i, rows:, :].astype(F32) == ids[j, :rows, :].astype(F32)
                if i == j:
                    same = same & (
                        lax.broadcasted_iota(jnp.int32, (rows, rows), 1)
                        <= lax.broadcasted_iota(jnp.int32, (rows, rows), 0)
                    )
                mask[here] = jnp.where(same, 0.0, -1e30)
    loop(0, 4, lambda step: wq_gather(step).end())
    loop(0, 4, lambda step: wq_gather(step).settle())

    def assemble(blocks, to):
        def body(i):
            for p in range(PLANES):
                staged[p * own : (p + 1) * own, :] = blocks[i, p].astype(F32)
            span = PLANES * own
            to[pl.ds(pl.multiple_of(i * span, 16), span), :] = staged[...].astype(BF16)

        loop(0, blocks.shape[0], body)

    cot_chain.arrive(0)
    cot_gather(0).begin()
    assemble(wq_blocks, wq_o)
    gains = jnp.transpose(wq_o[:, size * 3 :].astype(F32))
    gain_one = gains[16:17, :]
    gain_two = gains[17:18, :]

    def normalise(p):
        block = tok[p].astype(F32)
        inverse = lax.rsqrt(jnp.mean(block * block, axis=1, keepdims=True) + epsilon)
        first_o[p] = (block * inverse * gain_one).astype(BF16)

    loop(0, PLANES, normalise)
    wo_chain.arrive(1)
    wo_gather(1).begin()
    cot_chain.arrive(1)
    cot_gather(1).begin()

    def project(p):
        span = pl.ds(pl.multiple_of(p * rows, 128), rows)
        cosine, sine = cos_in[span, :], sin_in[span, :]
        for kind in range(3):
            part = mul(first_o[p], wq_o[:, kind * size : (kind + 1) * size], 1, 0)
            for head in range(WINDOW):
                here = part[:, head * HEAD_DIM : (head + 1) * HEAD_DIM]
                if kind < 2:
                    here = here * cosine + pltpu.roll(here, HEAD_DIM // 2, 1) * sine
                if kind == 0:
                    here = here * (HEAD_DIM ** (-0.5))
                qkv_o[kind, head, span, :] = here.astype(BF16)

    loop(0, PLANES, project)
    wo_chain.arrive(2)
    wo_gather(2).begin()
    cot_chain.arrive(2)
    cot_gather(2).begin()

    @pl.when(jnp.logical_not(end_plane))
    def _():
        weights_send(1)
        weights_send(3)

    def attend(head):
        exact = softmax_rows(mul(qkv_o[0, head], qkv_o[1, head], 1, 1), mask[...])
        exact_o[head] = exact
        mixed_o[head] = mul(exact.astype(BF16), qkv_o[2, head], 1, 0)

    loop(0, WINDOW, attend)
    for p in range(PLANES):
        for head in range(WINDOW):
            mixed_send[p, :, head * HEAD_DIM : (head + 1) * HEAD_DIM] = mixed_o[
                head, p * rows : (p + 1) * rows, :
            ].astype(BF16)
    for step in (1, 2, 3):
        mixed_ring(step).start()
    mixed_got[z] = mixed_send[z]
    weights_send(2)
    loop(0, 4, lambda turn: wo_gather(turn).relay())
    loop(0, 4, lambda turn: wo_gather(turn).end())
    weights_next(1)
    loop(0, 4, lambda turn: cot_gather(turn).relay())
    weights_end(0)
    weights_next(3)
    loop(0, 4, lambda turn: wo_gather(turn).settle())
    assemble(wo_blocks, wo_o)
    for step in (1, 2, 3):
        mixed_ring(step).wait_recv()
    column = 0
    for p, (a, b) in enumerate(KEEP):
        span = (b - a) * HEAD_DIM
        mixed_rows_o[:, column : column + span] = mixed_got[p, :, a * HEAD_DIM : b * HEAD_DIM]
        column += span

    def out_project(i):
        here = at(i * 256, 256)
        middle_o[:, here] = tok_in_f32(tok, z, here) + mul(mixed_rows_o[...], wo_o[:, here], 1, 0)

    loop(0, width // 256, out_project)
    middle = middle_o[...]
    inverse = lax.rsqrt(jnp.mean(middle * middle, axis=1, keepdims=True) + epsilon)
    second_o[...] = (middle * inverse * gain_two).astype(BF16)
    weights_end(1)
    loop(0, 4, lambda turn: cot_gather(turn).end())
    weights_end(3)
    weights_next(2)
    weights_end(2)
    loop(0, 4, lambda turn: cot_gather(turn).settle())
    for chain in (tok_chain, ids_chain, wo_chain, cot_chain):
        chain.settle()
    for step in (0, 1, 2, 3):
        weights_keep(step).wait()
        for flip in (0, 1, 2, 3):
            if step:
                weights_ring(step, flip).wait_send()
            if flip:
                weights_plane(step, flip).wait_send()
            weights_core(step, flip).wait_send()
            weights_core(step, flip).wait_recv()
        if step:
            wq_ring(step).wait_send()
            mixed_ring(step).wait_send()


def tok_in_f32(tok, z, here):
    return tok[z, :, here].astype(F32)


def start(tok, ids, wq, wo, we, cot, cosine, sine, collective):
    rows, width = tok.shape
    own = wo.shape[0]
    hidden3 = we.shape[-1]
    seqlen = PLANES * rows
    size = WINDOW * HEAD_DIM
    blocks = (8, PLANES, own, width)
    any_out = pl.BlockSpec(memory_space=pl.ANY)
    vmem_out = pl.BlockSpec(memory_space=pltpu.VMEM)
    shapes = [
        ((8, PLANES, own, hidden3), BF16, any_out),
        ((4, PLANES) + cot.shape, BF16, any_out),
        ((width, width), BF16, vmem_out),
        ((width, width), BF16, vmem_out),
        ((PLANES, rows, width), BF16, vmem_out),
        ((3, WINDOW, seqlen, HEAD_DIM), BF16, vmem_out),
        ((WINDOW, seqlen, seqlen), F32, vmem_out),
        ((WINDOW, seqlen, HEAD_DIM), F32, vmem_out),
        ((rows, width), BF16, vmem_out),
        ((rows, width), F32, vmem_out),
        ((rows, width), BF16, vmem_out),
        ((3, 4, own, hidden3), BF16, any_out),
    ]
    return pl.pallas_call(
        start_kernel,
        out_shape=[jax.ShapeDtypeStruct(shape, kind) for shape, kind, _ in shapes],
        in_specs=[any_out] * 6 + [vmem_out] * 2,
        out_specs=[spec for _, _, spec in shapes],
        scratch_shapes=[
            pltpu.VMEM((PLANES, rows, width), BF16),
            pltpu.VMEM((PLANES,) + ids.shape, BF16),
            pltpu.VMEM(blocks, BF16),
            pltpu.VMEM(blocks, BF16),
            pltpu.VMEM((PLANES * own, width), F32),
            pltpu.VMEM((seqlen, seqlen), F32),
            pltpu.VMEM((PLANES, rows, size), BF16),
            pltpu.VMEM((PLANES, rows, size), BF16),
            pltpu.SemaphoreType.DMA((10,)),
            pltpu.SemaphoreType.DMA((39, 4)),
            pltpu.SemaphoreType.DMA((39, 4)),
        ],
        compiler_params=pltpu.CompilerParams(
            collective_id=collective, has_side_effects=True, vmem_limit_bytes=56 * 2**20
        ),
        name="start",
    )(tok, ids, wq, wo, we, cot, cosine, sine)[:-1]


def add_blocks(out, *terms):
    rows = out.shape[0]

    def body(i, carry):
        part = pl.ds(pl.multiple_of(i * 16, 16), 16)
        total = terms[0][part, :].astype(F32)
        for term in terms[1:]:
            total = total + term[part, :].astype(F32)
        out[part, :] = total.astype(out.dtype)
        return carry

    lax.fori_loop(0, rows // 16, body, 0)


def experts_kernel(
    x_in, cot_in, weights_in, misc_in, grads_o, outs_o, sums_o,
    x, cot, weights, misc, act, scaled, slopes, gate, outs, parts, got_one, got_two, got_far, stage,
    load_sems, send_sems, recv_sems,
):
    w, z = place()
    chip = w // 2
    expert = chip * PLANES + z
    rows, width = x_in.shape
    hidden = weights.shape[1] // 3
    group_rows = 4 * rows

    def remote(kind, step, src, dst, device):
        return pltpu.make_async_remote_copy(
            src_ref=src,
            dst_ref=dst,
            send_sem=send_sems.at[kind, step],
            recv_sem=recv_sems.at[kind, step],
            device_id=device,
            device_id_type=MESH_IDS,
        )

    def plane_of(step, sign):
        return lax.rem(z + PLANES + sign * step, PLANES)

    def step_at(turn):
        step = 0
        for plane, steps in enumerate(((3, 2, 1, 0), (1, 3, 2, 0), (3, 1, 2, 0), (1, 2, 3, 0))):
            for number, value in enumerate(steps):
                step = jnp.where((z == plane) & (turn == number), value, step)
        return step

    def axes(turn):
        first = 1 + lax.rem(turn, 2)
        return first, 3 - first

    def ring(step, up):
        to = lax.rem(step + 1, 4) if up else lax.rem(step + 3, 4)
        return pltpu.make_async_remote_copy(
            src_ref=x.at[step, chip],
            dst_ref=x.at[to, chip],
            send_sem=send_sems.at[0 if up else 8, step],
            recv_sem=recv_sems.at[0, to],
            device_id=(w, z + 1 if up else z - 1),
            device_id_type=MESH_IDS,
        )

    def goes(step, up):
        if up:
            return (z >= step) & (z < PLANES - 1)
        return ((z < step) | (step == 0)) & (z > 0)

    def pass_on(step):
        for up in (True, False):

            @pl.when(goes(step, up))
            def _():
                ring(step, up).start()

    def arrive(step):
        pltpu.make_async_remote_copy(
            src_ref=x.at[step, chip],
            dst_ref=x.at[step, chip],
            send_sem=send_sems.at[0, step],
            recv_sem=recv_sems.at[0, step],
            device_id=(w, z),
            device_id_type=MESH_IDS,
        ).wait_recv()

    def direct(step, flip):
        block = x.at[step, chip]
        return remote(flip, step, block, block, (w ^ (2 * flip), z))

    def across(turn):
        first, second = axes(turn)
        step = step_at(turn)
        block = x.at[step, chip ^ first]
        return remote(3, step, block, block, (w ^ (2 * second), z))

    def near(turn, which):
        first, _ = axes(turn)
        step = step_at(turn)
        block = chip ^ 3 if which else chip ^ first
        return remote(
            4 + which, step, parts.at[step, block], got_one.at[step, which], (w ^ (2 * first), z)
        )

    def cross(turn):
        _, second = axes(turn)
        step = step_at(turn)
        return remote(
            6, step, parts.at[step, chip ^ second], got_two.at[step], (w ^ (2 * second), z)
        )

    def far(step):
        return remote(7, step, parts.at[step, chip], got_far.at[step - 1], (w, plane_of(step, -1)))

    def cot_load(step):
        return pltpu.make_async_copy(
            cot_in.at[:, plane_of(step, -1)], cot.at[step], load_sems.at[step]
        )

    def outs_out(turn):
        return pltpu.make_async_copy(
            outs.at[lax.rem(turn, 2)], outs_o.at[step_at(turn)], load_sems.at[9 + lax.rem(turn, 2)]
        )

    def grads_out(low, size, slot):
        return pltpu.make_async_copy(
            stage.at[slot, :, pl.ds(0, size)], grads_o.at[:, low], load_sems.at[4 + slot]
        )

    loads = [
        pltpu.make_async_copy(src, dst, load_sems.at[6 + i])
        for i, (src, dst) in enumerate(
            (
                (x_in, x.at[0, chip]),
                (misc_in.at[:, pl.ds(misc_in.shape[1] - 128, 128)], misc),
                (weights_in, weights),
            )
        )
    ]
    for load in loads:
        load.start()
    loop(0, 4, lambda step: cot_load(step).start())
    greet(w, z)
    loads[0].wait()
    pass_on(0)

    def begin(turn):
        step = step_at(turn)

        @pl.when(turn < 3)
        def _():
            arrive(step)
            pass_on(step)

        direct(step, 1).start()
        direct(step, 2).start()

    def relay(turn):
        step = step_at(turn)
        direct(step, 1).wait_recv()
        direct(step, 2).wait_recv()
        across(turn).start()

    begin(0)
    begin(1)
    relay(0)
    begin(2)
    begin(3)
    loads[1].wait()
    loads[2].wait()

    def first_half(step):
        cot_load(step).wait()
        rows_in = x[step].reshape(group_rows, width)
        members = cot[step, :, :, width:].reshape(group_rows, 128).astype(F32)
        logits = mul(rows_in, misc[...], 1, 0)
        lane = lax.broadcasted_iota(jnp.int32, logits.shape, 1)
        routed = (lane > 0) & (lane < 16)
        top = jnp.max(jnp.where(routed, logits, -1e30), axis=1, keepdims=True)
        powers = jnp.where(routed, jnp.exp(logits - top), 0.0)
        probs = jnp.where(lane == 0, 1.0, powers / jnp.sum(powers, axis=1, keepdims=True))
        own = jnp.where(lane == expert, members, 0.0)
        gate[0] = jnp.broadcast_to(jnp.sum(probs * own, axis=1, keepdims=True), gate.shape[1:])
        gate[1] = own

        def hidden_chunk(low, size):
            here = x[step].reshape(group_rows, width)
            gate_part = mul(here, weights[:, at(low, size)], 1, 0)
            up_part = mul(here, weights[:, at(hidden + low, size)], 1, 0)
            grad_act = mul(
                cot[step, :, :, :width].reshape(group_rows, width),
                weights[:, at(2 * hidden + low, size)],
                1,
                0,
            )
            scale = gate[0][:, :1]
            grad_act = grad_act * scale
            sigmoid = 1.0 / (1.0 + jnp.exp(-gate_part))
            silu = gate_part * sigmoid
            activated = (silu * up_part).astype(BF16)
            act[:, at(low, size)] = activated
            scaled[step, :, at(low, size)] = (activated.astype(F32) * scale).astype(BF16)
            slopes[step, :, at(low, size)] = (
                grad_act * up_part * (sigmoid + silu * (1.0 - sigmoid))
            ).astype(BF16)
            slopes[step, :, at(hidden + low, size)] = (grad_act * silu).astype(BF16)

        loop(0, hidden // 256, lambda i: hidden_chunk(i * 256, 256))
        if hidden % 256:
            hidden_chunk(hidden // 256 * 256, hidden % 256)

    def second_half(turn, step):
        def width_body(i, total):
            low = i * 256
            expert_rows = mul(act[...], weights[at(low, 256), 2 * hidden :], 1, 1)
            expert_rows = expert_rows.astype(BF16).astype(F32)
            outs[lax.rem(turn, 2), :, :, at(low, 256)] = (
                (expert_rows * gate[0][:, :1]).astype(BF16).reshape(4, rows, 256)
            )
            product = expert_rows * cot[step, :, :, at(low, 256)].reshape(group_rows, 256).astype(F32)
            grad_in = mul(slopes[step], weights[at(low, 256), : 2 * hidden], 1, 1)
            parts[step, :, :, at(low, 256)] = grad_in.astype(BF16).reshape(4, rows, 256)
            return total + product[:, :128] + product[:, 128:]

        total = lax.fori_loop(0, width // 256, width_body, jnp.zeros((group_rows, 128), F32))
        prob = jnp.sum(total, axis=1, keepdims=True) * gate[1]
        high = prob.astype(BF16)
        low = (prob - high.astype(F32)).astype(BF16)
        low = pltpu.roll(low.astype(F32), 32, 1).astype(BF16)
        parts[step, :, :, width:] = (high + low).reshape(4, rows, 128)

    def send_cross(turn):
        _, second = axes(turn)
        step = step_at(turn)
        near(turn, 1).wait_recv()
        block = parts.at[step, chip ^ second]
        add_blocks(block, block, got_one.at[step, 1])
        cross(turn).start()

    def send_far(turn):
        step = step_at(turn)
        near(turn, 0).wait_recv()
        cross(turn).wait_recv()
        block = parts.at[step, chip]
        add_blocks(block, block, got_one.at[step, 0], got_two.at[step])
        far(step).start()

    def group(turn):
        step = step_at(turn)
        across(turn).wait_recv()
        first_half(step)

        @pl.when(turn < 2)
        def _():
            relay(2 * turn + 1)

        @pl.when(turn > 1)
        def _():
            outs_out(turn - 2).wait()

        second_half(turn, step)
        near(turn, 1).start()
        near(turn, 0).start()
        outs_out(turn).start()

        @pl.when(turn == 0)
        def _():
            relay(2)

        @pl.when(turn > 0)
        def _():
            send_cross(turn - 1)

        @pl.when(turn > 1)
        def _():
            send_far(turn - 2)

    loop(0, 4, group)

    def weight_chunk(left, right, low, size, offset, i):
        slot = lax.rem(i, 2)

        @pl.when(i >= 2)
        def _():
            grads_out(pl.ds(0, 256), 256, slot).wait()

        total = None
        for step in range(4):
            term = mul(
                left[step, :, :, :width].reshape(group_rows, width), right[step, :, at(low, size)], 0, 0
            )
            total = term if total is None else total + term
        stage[slot, :, :size] = total.astype(BF16)
        grads_out(at(offset + low, size), size, slot).start()

    ups, downs = 2 * hidden // 256, hidden // 256

    def up_chunk(i):
        weight_chunk(x, slopes, i * 256, 256, 0, i)

    def down_chunk(i):
        weight_chunk(cot, scaled, (i - ups) * 256, 256, 2 * hidden, i)

    loop(0, 3, up_chunk)
    send_cross(3)
    send_far(2)
    loop(3, ups, up_chunk)
    loop(ups, ups + downs, down_chunk)
    last = ups + downs
    if hidden % 256:
        weight_chunk(cot, scaled, downs * 256, hidden % 256, 2 * hidden, jnp.int32(last))
        grads_out(pl.ds(0, 256), 256, (last - 1) % 2).wait()
        grads_out(pl.ds(0, hidden % 256), hidden % 256, last % 2).wait()
    else:
        grads_out(pl.ds(0, 256), 256, last % 2).wait()
        grads_out(pl.ds(0, 256), 256, (last - 1) % 2).wait()
    outs_out(2).wait()
    outs_out(3).wait()
    near(3, 0).wait_recv()
    cross(3).wait_recv()
    loop(1, 4, lambda step: far(step).wait_recv())
    add_blocks(
        sums_o,
        parts.at[0, chip],
        got_one.at[0, 0],
        got_two.at[0],
        got_far.at[0],
        got_far.at[1],
        got_far.at[2],
    )

    def settle(turn):
        step = step_at(turn)
        direct(step, 1).wait_send()
        direct(step, 2).wait_send()
        across(turn).wait_send()
        near(turn, 0).wait_send()
        near(turn, 1).wait_send()
        cross(turn).wait_send()

        @pl.when(turn < 3)
        def _():
            far(step).wait_send()

        for up in (True, False):

            @pl.when(goes(step, up))
            def _():
                ring(step, up).wait_send()

    loop(0, 4, settle)


def run_experts(second_in, cot_all, weights, misc, collective):
    rows, width = second_in.shape
    hidden = weights.shape[1] // 3
    sums_width = width + 128
    block = (rows, sums_width)
    return pl.pallas_call(
        experts_kernel,
        out_shape=[
            jax.ShapeDtypeStruct((width, 3 * hidden), BF16),
            jax.ShapeDtypeStruct((4, 4, rows, width), BF16),
            jax.ShapeDtypeStruct((rows, sums_width), F32),
        ],
        in_specs=[pl.BlockSpec(memory_space=pl.ANY)] * 4,
        out_specs=[
            pl.BlockSpec(memory_space=pl.ANY),
            pl.BlockSpec(memory_space=pl.ANY),
            pl.BlockSpec(memory_space=pltpu.VMEM),
        ],
        scratch_shapes=[
            pltpu.VMEM((4, 4, rows, width), BF16),
            pltpu.VMEM((4, 4, rows, width + 128), BF16),
            pltpu.VMEM((width, 3 * hidden), BF16),
            pltpu.VMEM((width, 128), BF16),
            pltpu.VMEM((4 * rows, hidden), BF16),
            pltpu.VMEM((4, 4 * rows, hidden), BF16),
            pltpu.VMEM((4, 4 * rows, 2 * hidden), BF16),
            pltpu.VMEM((2, 4 * rows, 128), F32),
            pltpu.VMEM((2, 4, rows, width), BF16),
            pltpu.VMEM((4, 4) + block, BF16),
            pltpu.VMEM((4, 2) + block, BF16),
            pltpu.VMEM((4,) + block, BF16),
            pltpu.VMEM((3,) + block, BF16),
            pltpu.VMEM((2, width, 256), BF16),
            pltpu.SemaphoreType.DMA((11,)),
            pltpu.SemaphoreType.DMA((9, 4)),
            pltpu.SemaphoreType.DMA((8, 4)),
        ],
        compiler_params=pltpu.CompilerParams(
            collective_id=collective, has_side_effects=True, vmem_limit_bytes=62 * 2**20
        ),
        name="experts",
    )(second_in, cot_all, weights, misc)


def finish_kernel(
    outs_in, grads_in, first_in, dense_q, dense_o, sums_o, table_o, first_o, q_o, o_o,
    outs, outs_one, outs_two, outs_far, grads_own, grads_got, dense, dense_got, dense_one,
    dense_two, dense_far, dense_sum, load_sems, send_sems, recv_sems,
):
    w, z = place()
    chip, core = w // 2, w % 2
    steps = (1, 2, 3, 0)
    block_rows = o_o.shape[0] // 4
    half = o_o.shape[1] // 2
    plane_rows = o_o.shape[0]

    def remote(kind, step, src, dst, device):
        return pltpu.make_async_remote_copy(
            src_ref=src,
            dst_ref=dst,
            send_sem=send_sems.at[kind, step],
            recv_sem=recv_sems.at[kind, step],
            device_id=device,
            device_id_type=MESH_IDS,
        )

    def plane_of(step, sign):
        return lax.rem(z + PLANES + sign * step, PLANES)

    def axes(step):
        first = 1 + lax.rem(step, 2)
        return first, 3 - first

    class Gather:
        def __init__(self, base, step, turn, slot):
            self.base, self.step, self.slot = base, step, slot
            self.first, self.second = axes(turn)

        def copy(self, kind, owner, flip):
            ref = self.slot(owner)
            return remote(self.base + kind, self.step, ref, ref, (w ^ flip, z))

        def begin(self):
            self.copy(0, w, 2).start()
            self.copy(1, w, 4).start()
            self.copy(2, w, 1).start()

        def relay(self):
            self.copy(0, w, 2).wait_recv()
            self.copy(1, w, 4).wait_recv()
            self.across().start()
            self.copy(4, w ^ 2, 1).start()
            self.copy(5, w ^ 4, 1).start()

        def across(self):
            return self.copy(3, w ^ (2 * self.first), 2 * self.second)

        def end(self):
            self.across().wait_recv()
            self.copy(6, w ^ 6, 1).start()

        def settle(self):
            for copy in (
                self.copy(0, w, 2),
                self.copy(1, w, 4),
                self.copy(2, w, 1),
                self.across(),
                self.copy(4, w ^ 2, 1),
                self.copy(5, w ^ 4, 1),
                self.copy(6, w ^ 6, 1),
            ):
                copy.wait_send()
            for kind in (2, 4, 5, 6):
                self.copy(kind, w, 1).wait_recv()

    def grads_load(step):
        return pltpu.make_async_copy(
            grads_in.at[plane_of(step, 1), core], grads_own.at[step], load_sems.at[0, step]
        )

    def grads_swap(step):
        return remote(
            0, step, grads_in.at[plane_of(step, 1), 1 - core], grads_got.at[step], (w ^ 1, z)
        )

    def grads_ring(step):
        return remote(1, step, grads_own.at[step], table_o.at[chip, z, core], (w, plane_of(step, 1)))

    def grads_keep():
        return pltpu.make_async_copy(
            grads_own.at[0], table_o.at[chip, z, core], load_sems.at[1, 0]
        )

    def grads_gather(step):
        source = plane_of(step, -1)
        return Gather(2, step, step, lambda i: table_o.at[i // 2, source, i % 2])

    def outs_load(step):
        return pltpu.make_async_copy(outs_in.at[step], outs.at[step], load_sems.at[2, step])

    def near(step, which):
        first, _ = axes(step)
        block = chip ^ 3 if which else chip ^ first
        return remote(
            9 + which, step, outs.at[step, block], outs_one.at[step, which], (w ^ (2 * first), z)
        )

    def cross(step):
        _, second = axes(step)
        return remote(
            11, step, outs.at[step, chip ^ second], outs_two.at[step], (w ^ (2 * second), z)
        )

    def far(step):
        return remote(12, step, outs.at[step, chip], outs_far.at[step - 1], (w, plane_of(step, -1)))

    def dense_part(kind, step, side):
        rows = pl.ds(pl.multiple_of(plane_of(step, 1) * plane_rows, 16), plane_rows)
        return (dense_q, dense_o)[kind].at[rows, at(side * half, half)]

    def dense_load(kind, step):
        return pltpu.make_async_copy(
            dense_part(kind, step, core), dense.at[kind, step], load_sems.at[3 + kind, step]
        )

    def dense_swap(kind, step):
        return remote(
            13 + 4 * kind, step, dense_part(kind, step, 1 - core), dense_got.at[kind, step], (w ^ 1, z)
        )

    def rows_of(block):
        return pl.ds(pl.multiple_of(block * block_rows, 16), block_rows)

    def dense_axes(kind):
        return 1 + kind, 2 - kind

    def dense_near(kind, step, which):
        first, _ = dense_axes(kind)
        block = chip ^ 3 if which else chip ^ first
        return remote(
            14 + 4 * kind + which,
            step,
            dense.at[kind, step, rows_of(block)],
            dense_one.at[kind, step, which],
            (w ^ (2 * first), z),
        )

    def dense_cross(kind, step):
        _, second = dense_axes(kind)
        return remote(
            16 + 4 * kind,
            step,
            dense.at[kind, step, rows_of(chip ^ second)],
            dense_two.at[kind, step],
            (w ^ (2 * second), z),
        )

    def place_of(owner):
        return rows_of(owner // 2), at(lax.rem(owner, 2) * half, half)

    def dense_ring(kind, step):
        own = dense.at[kind, step, rows_of(chip)]
        rows, columns = place_of(w)
        to = q_o.at[z, rows, columns] if kind == 0 else dense_far.at[step - 1]
        return remote(21 + kind, step, own, to, (w, plane_of(step, 1)))

    def dense_keep():
        rows, columns = place_of(w)
        return pltpu.make_async_copy(
            dense.at[0, 0, rows_of(chip)], q_o.at[z, rows, columns], load_sems.at[1, 1]
        )

    def dense_last():
        rows, columns = place_of(w)
        return pltpu.make_async_copy(dense_sum, o_o.at[rows, columns], load_sems.at[1, 2])

    def q_slot(step):
        source = plane_of(step, -1)

        def slot(owner):
            rows, columns = place_of(owner)
            return q_o.at[source, rows, columns]

        return slot

    def o_slot(owner):
        rows, columns = place_of(owner)
        return o_o.at[rows, columns]

    def q_gather(step):
        return Gather(23, step, step, q_slot(step))

    def o_gather():
        return Gather(30, 0, 0, o_slot)

    def first_ring(step):
        return remote(37, step, first_in.at[plane_of(step, 1)], first_o.at[z], (w, plane_of(step, 1)))

    def first_keep():
        return pltpu.make_async_copy(first_in.at[z], first_o.at[z], load_sems.at[1, 3])

    for step in steps:
        grads_load(step).start()
    for step in steps:
        outs_load(step).start()
        for kind in (0, 1):
            dense_load(kind, step).start()
    first_keep().start()
    greet(w, z)
    for step in steps:
        grads_swap(step).start()
    for step in steps:
        for kind in (0, 1):
            dense_swap(kind, step).start()
    for step in (1, 2, 3):
        first_ring(step).start()

    def grads_ready(step):
        grads_load(step).wait()
        grads_swap(step).wait_recv()
        add_blocks(grads_own.at[step], grads_own.at[step], grads_got.at[step])

    def dense_ready(kind, step):
        dense_load(kind, step).wait()
        dense_swap(kind, step).wait_recv()
        add_blocks(dense.at[kind, step], dense.at[kind, step], dense_got.at[kind, step])
        dense_near(kind, step, 1).start()
        dense_near(kind, step, 0).start()

    loop(1, 4, lambda step: (grads_ready(step), grads_ring(step).start()))
    grads_ready(0)
    keep = grads_keep()
    keep.start()

    def dense_start(step):
        dense_ready(0, step)
        dense_ready(1, step)

    loop(0, 4, dense_start)
    keep.wait()
    grads_gather(0).begin()

    def outs_start(step):
        outs_load(step).wait()
        near(step, 1).start()
        near(step, 0).start()

    loop(0, 4, outs_start)

    def dense_cross_start(step):
        for kind in (0, 1):
            _, second = dense_axes(kind)
            dense_near(kind, step, 1).wait_recv()
            block = dense.at[kind, step, rows_of(chip ^ second)]
            add_blocks(block, block, dense_one.at[kind, step, 1])
            dense_cross(kind, step).start()

    loop(0, 4, dense_cross_start)

    def grads_next(step):
        grads_ring(step).wait_recv()
        grads_gather(step).begin()

    loop(1, 2, grads_next)

    def outs_cross(step):
        _, second = axes(step)
        near(step, 1).wait_recv()
        block = outs.at[step, chip ^ second]
        add_blocks(block, block, outs_one.at[step, 1])
        cross(step).start()

    loop(0, 4, outs_cross)

    def dense_finish(step):
        for kind in (0, 1):
            dense_near(kind, step, 0).wait_recv()
            dense_cross(kind, step).wait_recv()
            block = dense.at[kind, step, rows_of(chip)]
            add_blocks(block, block, dense_one.at[kind, step, 0], dense_two.at[kind, step])

    loop(0, 4, dense_finish)

    def dense_ring_start(step):
        dense_ring(0, step).start()
        dense_ring(1, step).start()

    loop(1, 4, dense_ring_start)
    keep = dense_keep()
    keep.start()
    loop(2, 3, grads_next)
    loop(0, 1, lambda step: grads_gather(step).relay())
    keep.wait()
    q_gather(0).begin()

    def outs_finish(step):
        near(step, 0).wait_recv()
        cross(step).wait_recv()
        block = outs.at[step, chip]
        add_blocks(block, block, outs_one.at[step, 0], outs_two.at[step])

        @pl.when(step > 0)
        def _():
            far(step).start()

    loop(0, 4, outs_finish)
    loop(3, 4, grads_next)

    def q_next(step):
        dense_ring(0, step).wait_recv()
        q_gather(step).begin()
        dense_ring(1, step).wait_recv()

    loop(1, 4, q_next)
    add_blocks(
        dense_sum, dense.at[1, 0, rows_of(chip)], dense_far.at[0], dense_far.at[1], dense_far.at[2]
    )
    keep = dense_last()
    keep.start()
    keep.wait()
    o_gather().begin()
    loop(1, 4, lambda step: grads_gather(step).relay())
    loop(0, 4, lambda step: q_gather(step).relay())
    o_gather().relay()
    loop(1, 4, lambda step: far(step).wait_recv())
    add_blocks(sums_o, outs.at[0, chip], outs_far.at[0], outs_far.at[1], outs_far.at[2])
    loop(0, 4, lambda step: grads_gather(step).end())
    loop(0, 4, lambda step: q_gather(step).end())
    o_gather().end()
    loop(0, 4, lambda step: grads_gather(step).settle())
    loop(0, 4, lambda step: q_gather(step).settle())
    o_gather().settle()
    first_keep().wait()

    def settle(step):
        grads_swap(step).wait_send()
        near(step, 0).wait_send()
        near(step, 1).wait_send()
        cross(step).wait_send()
        for kind in (0, 1):
            dense_swap(kind, step).wait_send()
            dense_near(kind, step, 0).wait_send()
            dense_near(kind, step, 1).wait_send()
            dense_cross(kind, step).wait_send()

    loop(0, 4, settle)

    def settle_rings(step):
        first_ring(step).wait_recv()
        first_ring(step).wait_send()
        grads_ring(step).wait_send()
        far(step).wait_send()
        dense_ring(0, step).wait_send()
        dense_ring(1, step).wait_send()

    loop(1, 4, settle_rings)


def finish(outs, grads, first, dense_q, dense_o, collective):
    rows, width = first.shape[1:]
    plane_rows = width // PLANES
    block = (plane_rows // 4, width // 2)
    return pl.pallas_call(
        finish_kernel,
        out_shape=[
            jax.ShapeDtypeStruct((rows, width), F32),
            jax.ShapeDtypeStruct((4, PLANES) + grads.shape[1:], BF16),
            jax.ShapeDtypeStruct(first.shape, BF16),
            jax.ShapeDtypeStruct((PLANES, plane_rows, width), BF16),
            jax.ShapeDtypeStruct((plane_rows, width), BF16),
        ],
        in_specs=[pl.BlockSpec(memory_space=pl.ANY)] * 5,
        out_specs=[pl.BlockSpec(memory_space=pltpu.VMEM)] + [pl.BlockSpec(memory_space=pl.ANY)] * 4,
        scratch_shapes=[
            pltpu.VMEM((4, 4, rows, width), BF16),
            pltpu.VMEM((4, 2, rows, width), BF16),
            pltpu.VMEM((4, rows, width), BF16),
            pltpu.VMEM((3, rows, width), BF16),
            pltpu.VMEM((4,) + grads.shape[2:], BF16),
            pltpu.VMEM((4,) + grads.shape[2:], BF16),
            pltpu.VMEM((2, 4, plane_rows, width // 2), BF16),
            pltpu.VMEM((2, 4, plane_rows, width // 2), BF16),
            pltpu.VMEM((2, 4, 2) + block, BF16),
            pltpu.VMEM((2, 4) + block, BF16),
            pltpu.VMEM((3,) + block, BF16),
            pltpu.VMEM(block, BF16),
            pltpu.SemaphoreType.DMA((5, 4)),
            pltpu.SemaphoreType.DMA((38, 4)),
            pltpu.SemaphoreType.DMA((38, 4)),
        ],
        compiler_params=pltpu.CompilerParams(
            collective_id=collective, has_side_effects=True, vmem_limit_bytes=60 * 2**20
        ),
        name="finish",
    )(outs, grads, first, dense_q, dense_o)


def widen_kernel(table, up_o, down_o):
    columns = table.shape[2]
    split = up_o.shape[2]
    for low in range(0, columns, 128):
        part = jnp.swapaxes(table[:, :, low : low + 128].astype(F32), 0, 1)
        if low < split:
            up_o[:, :, low : low + 128] = part
        else:
            down_o[:, :, low - split : low - split + 128] = part


def widen(table):
    experts, rows, columns = table.shape
    split = columns // 3 * 2
    step = 16
    return pl.pallas_call(
        widen_kernel,
        grid=(rows // step,),
        out_shape=[
            jax.ShapeDtypeStruct((rows, experts, split), F32),
            jax.ShapeDtypeStruct((rows, experts, columns - split), F32),
        ],
        in_specs=[pl.BlockSpec((experts, step, columns), lambda i: (0, i, 0))],
        out_specs=[
            pl.BlockSpec((step, experts, split), lambda i: (i, 0, 0)),
            pl.BlockSpec((step, experts, columns - split), lambda i: (i, 0, 0)),
        ],
        compiler_params=pltpu.CompilerParams(vmem_limit_bytes=48 * 2**20),
        name="widen",
    )(table)


def windows(x):
    size = WINDOW * HEAD_DIM
    return jnp.stack([x[:, s * HEAD_DIM : s * HEAD_DIM + size] for s in STARTS])


def from_windows(x):
    return jnp.concatenate(
        [x[p, :, a * HEAD_DIM : b * HEAD_DIM] for p, (a, b) in enumerate(KEEP)], axis=1
    )


def dot(a, b, dims, out=F32):
    return lax.dot_general(a, b, ((dims[0], dims[1]), ((), ())), preferred_element_type=F32).astype(out)


def expert_local(
    tokens, seq_ids, routes, cotangent, gain_attn, w_qkv, w_out, gain_ffn, w_router, w_up, w_down
):
    rows, width = tokens.shape
    own = w_out.shape[0]
    experts = w_router.shape[1]
    seqlen = PLANES * rows
    size = WINDOW * HEAD_DIM
    scale = HEAD_DIM ** (-0.5)
    z = lax.axis_index("narrow")

    misc = jnp.concatenate(
        [
            jnp.zeros((own, 1), BF16),
            w_router,
            gain_attn[:, None],
            gain_ffn[:, None],
            jnp.zeros((own, 128 - experts - 3), BF16),
        ],
        axis=1,
    )
    wq_send = jnp.concatenate(
        [windows(w_qkv[:, i * width : (i + 1) * width]) for i in range(3)]
        + [jnp.broadcast_to(misc[None], (PLANES, own, 128))],
        axis=2,
    )
    we_send = jnp.concatenate([w_up, w_down], axis=2).reshape(own, 4, PLANES, 3 * FF)
    we_send = jnp.transpose(we_send, (2, 1, 0, 3))
    choose = routes[:, :, None] == jnp.arange(experts, dtype=jnp.int32)[None, None, :]
    member = jnp.any(choose, axis=1)
    member_cols = jnp.concatenate(
        [jnp.ones((rows, 1), BF16), member.astype(BF16), jnp.zeros((rows, 127 - experts), BF16)],
        axis=1,
    )
    cot_send = jnp.concatenate([cotangent, member_cols], axis=1)
    ids_f = seq_ids.astype(BF16)
    ids_send = jnp.concatenate(
        [
            jnp.broadcast_to(ids_f[None, :], (rows, rows)),
            jnp.broadcast_to(ids_f[:, None], (rows, rows)),
        ]
    )
    half_dim = HEAD_DIM // 2
    cosine, sine_table = rotary(jnp.arange(seqlen, dtype=F32), HEAD_DIM)
    sine_signed = sine_table[:, 0, :] * jnp.where(jnp.arange(HEAD_DIM) < half_dim, -1.0, 1.0)
    we_all, cot_all, wq_all, out_weight, first_in, qkv, weights_exact, mixed_exact, mixed, middle, second_in = start(
        tokens, ids_send, wq_send, w_out, we_send, cot_send, cosine[:, 0, :], sine_signed, 1
    )
    misc_all = wq_all[:, 3 * size :]
    wq = wq_all[:, : 3 * size]
    router = misc_all[:, 1 : experts + 1]
    gain_one = misc_all[:, experts + 1].astype(F32)
    gain_two = misc_all[:, experts + 2].astype(F32)
    first_in = first_in.reshape(seqlen, width)
    inverse_two = rms_inverse(middle)
    normed_two = middle * inverse_two

    weights = we_all.reshape(width, 3 * FF)
    grads, outs, sums = run_experts(second_in, cot_all, weights, wq_all, 3)

    hi = sums[:, width + 1 : width + 1 + experts]
    lo = sums[:, width + 33 : width + 33 + experts]
    grad_probs = hi + lo
    probs = jax.nn.softmax(dot(second_in, router, ((1,), (0,))), axis=-1)
    grad_logits = (
        probs * (grad_probs - jnp.sum(probs * grad_probs, axis=1, keepdims=True))
    ).astype(BF16)
    grad_second = sums[:, :width] + dot(grad_logits, router, ((1,), (1,)))
    grad_output = cotangent.astype(F32)
    grad_normed_two = grad_second * gain_two
    gain_two_part = jnp.sum(grad_second * normed_two, axis=0)
    grad_middle = grad_output + inverse_two * (
        grad_normed_two
        - normed_two * jnp.mean(grad_normed_two * normed_two, axis=-1, keepdims=True)
    )
    router_part = dot(second_in, grad_logits, ((0,), (0,)))
    grad_attention = grad_middle.astype(BF16)
    grad_out_part = dot(mixed, grad_attention, ((0,), (0,)), BF16)
    grad_mixed = dot(grad_attention, out_weight, ((1,), (1,)), BF16)

    valid = jnp.array(
        [[a <= i < b for i in range(WINDOW)] for a, b in KEEP], dtype=BF16
    )[z]
    grad_heads = swap_planes(windows(grad_mixed), 5).reshape(seqlen, WINDOW, HEAD_DIM)
    grad_heads = grad_heads * valid[None, :, None]
    query_rows, key_rows, value_rows = qkv[0], qkv[1], qkv[2]
    weights_low = weights_exact.astype(BF16)
    row_delta = jnp.einsum("qhd,hqd->hq", grad_heads.astype(F32), mixed_exact)
    grad_values = jnp.einsum("hqk,qhd->khd", weights_low, grad_heads, preferred_element_type=F32)
    grad_weights = jnp.einsum("qhd,hkd->hqk", grad_heads, value_rows, preferred_element_type=F32)
    grad_scores = (weights_exact * (grad_weights - row_delta[..., None])).astype(BF16)
    grad_query = jnp.einsum("hqk,hkd->qhd", grad_scores, key_rows, preferred_element_type=F32)
    grad_keys = jnp.einsum("hqk,hqd->khd", grad_scores, query_rows, preferred_element_type=F32)
    grad_projected = jnp.concatenate(
        [
            (rotate_back(grad_query, cosine, sine_table) * scale).reshape(seqlen, size),
            rotate_back(grad_keys, cosine, sine_table).reshape(seqlen, size),
            grad_values.reshape(seqlen, size),
        ],
        axis=1,
    ).astype(BF16)
    grad_qkv_part = dot(first_in, grad_projected, ((0,), (0,)), BF16)
    first_part = dot(grad_projected, wq, ((1,), (1,)))
    gain_one_part = jnp.sum(first_part * first_in.astype(F32), axis=0) / gain_one
    misc_part = jnp.concatenate(
        [
            router_part,
            gain_one_part[:, None],
            gain_two_part[:, None],
            jnp.zeros((width, 128 - experts - 2), F32),
        ],
        axis=1,
    ).astype(BF16)
    dense_q = jnp.concatenate([grad_qkv_part, misc_part], axis=1)
    sums, table, first_all, q_all, o_all = finish(
        outs,
        grads.reshape(PLANES, 2, width // PLANES // 2, 3 * FF),
        first_part.astype(BF16).reshape(PLANES, rows, width),
        dense_q,
        grad_out_part,
        6,
    )
    output = (middle + sums).astype(BF16)
    grad_first = jnp.sum(first_all.astype(F32), axis=0)
    inputs = tokens.astype(F32)
    inverse_one = rms_inverse(inputs)
    normed_one = inputs * inverse_one
    grad_normed_one = grad_first * gain_one
    grad_tokens = grad_middle + inverse_one * (
        grad_normed_one
        - normed_one * jnp.mean(grad_normed_one * normed_one, axis=-1, keepdims=True)
    )
    out_sum = o_all.astype(F32)
    qkv_sum = jnp.concatenate(
        [from_windows(q_all[:, :, i * size : (i + 1) * size]) for i in range(3)], axis=1
    ).astype(F32)
    misc_sum = jnp.sum(q_all[:, :, 3 * size :].astype(F32), axis=0)

    up_sum, down_sum = widen(table.reshape(experts + 1, width // PLANES, 3 * FF))
    return (
        output,
        grad_tokens.astype(BF16),
        misc_sum[:, experts],
        qkv_sum,
        out_sum,
        misc_sum[:, experts + 1],
        misc_sum[:, :experts],
        up_sum,
        down_sum,
    )


def solution(mesh):
    fits = mesh.shape["wide"] == 8 and mesh.shape["narrow"] == PLANES
    return jax.shard_map(
        expert_local if fits else local,
        mesh=mesh,
        in_specs=(
            P(("wide", "narrow"), None),
            P(("wide", "narrow")),
            P(("wide", "narrow"), None),
            P(("wide", "narrow"), None),
            P(("wide", "narrow")),
            P(("wide", "narrow"), None),
            P(("wide", "narrow"), None),
            P(("wide", "narrow")),
            P(("wide", "narrow"), None),
            P(("wide", "narrow"), None, None),
            P(("wide", "narrow"), None, None),
        ),
        out_specs=(
            P(("wide", "narrow"), None),
            P(("wide", "narrow"), None),
            P("narrow"),
            P("narrow", None),
            P("narrow", None),
            P("narrow"),
            P("narrow", None),
            P("narrow", None, None),
            P("narrow", None, None),
        ),
        check_vma=False,
    )
```

```python
import jax
import jax.numpy as jnp
from jax import lax
from jax.experimental import pallas as pl
from jax.experimental.pallas import tpu as pltpu
from jax.sharding import PartitionSpec as P

HEADS = 10
HEAD_DIM = 128
FF = 896
CAP = 72


epsilon = 1e-06


def shortened(x):
    return jax.tree.map(lambda a: a.astype(jnp.bfloat16) if a.dtype == jnp.float32 else a, x)


def rms_inverse(values):
    return lax.rsqrt(jnp.mean(values * values, axis=-1, keepdims=True) + epsilon)


def rotary(positions, head_size):
    half_dim = head_size // 2
    frequency = 10000.0 ** (-jnp.arange(half_dim, dtype=jnp.float32) / half_dim)
    angles = positions[:, None] * frequency[None, :]
    cosine = jnp.concatenate([jnp.cos(angles), jnp.cos(angles)], axis=1)[:, None, :]
    sine_table = jnp.concatenate([jnp.sin(angles), jnp.sin(angles)], axis=1)[:, None, :]
    return (cosine, sine_table)


def rotate(values, cosine, sine_table):
    half_dim = values.shape[-1] // 2
    turned = jnp.concatenate([-values[..., half_dim:], values[..., :half_dim]], axis=-1)
    return values * cosine + turned * sine_table


def rotate_back(grads, cosine, sine_table):
    half_dim = grads.shape[-1] // 2
    scaled = grads * sine_table
    turned = jnp.concatenate([scaled[..., half_dim:], -scaled[..., :half_dim]], axis=-1)
    return grads * cosine + turned


def expert_weight_terms(
    routed_in, routed_grad, shared_in, shared_grad, slot_grads, slot_acts, shared_grads, shared_acts
):
    up_routed = jnp.einsum(
        "ecd,ecf->def", routed_in, slot_grads, preferred_element_type=jnp.float32
    )
    up_shared = jnp.einsum("td,tf->df", shared_in, shared_grads, preferred_element_type=jnp.float32)
    down_routed = jnp.einsum(
        "ecd,ecf->def", routed_grad, slot_acts, preferred_element_type=jnp.float32
    )
    down_shared = jnp.einsum(
        "td,tf->df", shared_grad, shared_acts, preferred_element_type=jnp.float32
    )
    up_all = jnp.concatenate([up_shared[:, None], up_routed], axis=1)
    down_all = jnp.concatenate([down_shared[:, None], down_routed], axis=1)
    combined = jnp.concatenate([up_all, down_all], axis=2)
    return combined.reshape(combined.shape[0], -1)


def local(
    tokens, seq_ids, routes, cotangent, gain_attn, w_qkv, w_out, gain_ffn, w_router, w_up, w_down
):
    row_count = tokens.shape[0]
    model_width = tokens.shape[1]
    query_scale = HEAD_DIM ** (-0.5)
    hidden = FF
    capacity = CAP
    inputs = tokens.astype(jnp.float32)
    gain_one, qkv_weight, out_weight = (
        lax.all_gather(gain_attn, ("wide", "narrow"), axis=0, tiled=True),
        lax.all_gather(w_qkv, ("wide", "narrow"), axis=0, tiled=True),
        lax.all_gather(w_out, ("wide", "narrow"), axis=0, tiled=True),
    )
    inverse_one = rms_inverse(inputs)
    normed_one = inputs * inverse_one
    first_in = (normed_one * gain_one.astype(jnp.float32)).astype(jnp.bfloat16)
    projected = jnp.dot(first_in, qkv_weight, preferred_element_type=jnp.float32)
    offset = lax.axis_index("narrow") * row_count
    query_pos = offset + jnp.arange(row_count, dtype=jnp.int32)
    cosine, sine_table = rotary(query_pos.astype(jnp.float32), HEAD_DIM)
    query_rows = (
        rotate(projected[:, :model_width].reshape(row_count, HEADS, HEAD_DIM), cosine, sine_table)
        * query_scale
    ).astype(jnp.bfloat16)
    key_rows = (
        rotate(
            projected[:, model_width : 2 * model_width].reshape(row_count, HEADS, HEAD_DIM),
            cosine,
            sine_table,
        )
        .astype(jnp.bfloat16)
        .reshape(row_count, model_width)
    )
    value_rows = projected[:, 2 * model_width :].astype(jnp.bfloat16)
    all_keys, all_values, all_ids = (
        lax.all_gather(key_rows, "narrow", axis=0, tiled=True),
        lax.all_gather(value_rows, "narrow", axis=0, tiled=True),
        lax.all_gather(seq_ids.astype(jnp.bfloat16), "narrow", axis=0, tiled=True),
    )
    seqlen = all_keys.shape[0]
    block_len = min(512, seqlen)
    num_blocks = seqlen // block_len
    own_ids = seq_ids.astype(jnp.float32)

    def block_parts(block_index):
        first_row = block_index * block_len
        key_pos = first_row + jnp.arange(block_len, dtype=jnp.int32)
        key_ids = lax.dynamic_slice_in_dim(all_ids, first_row, block_len, 0).astype(jnp.float32)
        allowed = (key_pos[None, :] <= query_pos[:, None]) & (key_ids[None, :] == own_ids[:, None])
        key_block = lax.dynamic_slice_in_dim(all_keys, first_row, block_len, 0).reshape(
            block_len, HEADS, HEAD_DIM
        )
        value_block = lax.dynamic_slice_in_dim(all_values, first_row, block_len, 0).reshape(
            block_len, HEADS, HEAD_DIM
        )
        scores = jnp.einsum(
            "qhd,khd->hqk", query_rows, key_block, preferred_element_type=jnp.float32
        )
        return (allowed[None], key_block, value_block, scores)

    def max_step(state_pair, block_index):
        running_max, running_sum = state_pair
        allowed, key_block, value_block, scores = block_parts(block_index)
        masked = jnp.where(allowed, scores, -1e30)
        new_max = jnp.maximum(running_max, jnp.max(masked, axis=2))
        added = jnp.sum(jnp.where(allowed, jnp.exp(masked - new_max[..., None]), 0.0), axis=2)
        return ((new_max, running_sum * jnp.exp(running_max - new_max) + added), None)

    start_max = jnp.full((HEADS, row_count), -1e30, jnp.float32)
    start_sum = jnp.zeros((HEADS, row_count), jnp.float32)
    (top_score, exp_total), unused = lax.scan(
        max_step, (start_max, start_sum), jnp.arange(num_blocks)
    )
    log_total = top_score + jnp.log(exp_total)

    def out_step(accum, block_index):
        allowed, key_block, value_block, scores = block_parts(block_index)
        weights_low = jnp.where(allowed, jnp.exp(scores - log_total[..., None]), 0.0).astype(
            jnp.bfloat16
        )
        return (
            accum
            + jnp.einsum(
                "hqk,khd->hqd", weights_low, value_block, preferred_element_type=jnp.float32
            ),
            None,
        )

    accum_start = jnp.zeros((HEADS, row_count, HEAD_DIM), jnp.float32)
    mixed_heads, unused = lax.scan(out_step, accum_start, jnp.arange(num_blocks))
    mixed_exact = jnp.transpose(mixed_heads, (1, 0, 2))
    mixed = mixed_exact.reshape(row_count, model_width).astype(jnp.bfloat16)
    middle = inputs + jnp.dot(mixed, out_weight, preferred_element_type=jnp.float32)
    gain_two, router_weight, up_weight, down_weight = (
        lax.all_gather(gain_ffn, ("wide", "narrow"), axis=0, tiled=True),
        lax.all_gather(w_router, ("wide", "narrow"), axis=0, tiled=True),
        lax.all_gather(w_up, ("wide", "narrow"), axis=0, tiled=True),
        lax.all_gather(w_down, ("wide", "narrow"), axis=0, tiled=True),
    )
    inverse_two = rms_inverse(middle)
    normed_two = middle * inverse_two
    second_in = (normed_two * gain_two.astype(jnp.float32)).astype(jnp.bfloat16)
    logits = jnp.dot(second_in, router_weight, preferred_element_type=jnp.float32)
    router_probs = jax.nn.softmax(logits, axis=-1)
    experts = logits.shape[1]
    choose = routes[:, :, None] == jnp.arange(experts, dtype=jnp.int32)[None, None, :]
    member = jnp.sum(choose.astype(jnp.float32), axis=1)
    earlier = (jnp.arange(row_count)[:, None] > jnp.arange(row_count)[None, :]).astype(jnp.bfloat16)
    before = jnp.dot(earlier, member.astype(jnp.bfloat16), preferred_element_type=jnp.float32)
    slot_hit = (member.T[:, None, :] > 0.5) & (
        before.T[:, None, :] == jnp.arange(capacity, dtype=jnp.float32)[None, :, None]
    )
    dispatch = slot_hit.astype(jnp.bfloat16)
    gathered_in = jnp.einsum(
        "ect,td->ecd", dispatch, second_in, preferred_element_type=jnp.float32
    ).astype(jnp.bfloat16)
    gate_weights = router_probs * member
    gate_up = jnp.einsum(
        "ecd,def->ecf", gathered_in, up_weight[:, 1:], preferred_element_type=jnp.float32
    )
    gate_part = gate_up[..., :hidden]
    up_part = gate_up[..., hidden:]
    activated = (jax.nn.silu(gate_part) * up_part).astype(jnp.bfloat16)
    expert_rows = jnp.einsum(
        "ecf,def->ecd", activated, down_weight[:, 1:], preferred_element_type=jnp.float32
    ).astype(jnp.bfloat16)
    selected = jnp.einsum("ect,ecd->etd", dispatch, expert_rows, preferred_element_type=jnp.float32)
    routed = jnp.sum(gate_weights.T[:, :, None] * selected, axis=0)
    shared_up = jnp.dot(second_in, up_weight[:, 0], preferred_element_type=jnp.float32)
    shared_gate = shared_up[:, :hidden]
    shared_lin = shared_up[:, hidden:]
    shared_act = (jax.nn.silu(shared_gate) * shared_lin).astype(jnp.bfloat16)
    shared_out = jnp.einsum(
        "tf,df->td", shared_act, down_weight[:, 0], preferred_element_type=jnp.float32
    )
    output = (middle + shared_out + routed).astype(jnp.bfloat16)
    gain_two, router_weight, up_weight, down_weight = (
        lax.all_gather(gain_ffn, ("wide", "narrow"), axis=0, tiled=True),
        lax.all_gather(w_router, ("wide", "narrow"), axis=0, tiled=True),
        lax.all_gather(w_up, ("wide", "narrow"), axis=0, tiled=True),
        lax.all_gather(w_down, ("wide", "narrow"), axis=0, tiled=True),
    )
    grad_output = cotangent.astype(jnp.float32)
    slot_token = jnp.sum(
        jnp.where(slot_hit, jnp.arange(row_count, dtype=jnp.int32)[None, None, :], 0), axis=2
    )
    slot_gate = jnp.sum(jnp.where(slot_hit, gate_weights.T[:, None, :], 0.0), axis=2)
    grad_rows = (slot_gate[..., None] * grad_output[slot_token]).astype(jnp.bfloat16)
    grad_probs = jnp.sum(selected * grad_output[None], axis=2).T * member
    grad_logits = (
        router_probs * (grad_probs - jnp.sum(router_probs * grad_probs, axis=1, keepdims=True))
    ).astype(jnp.bfloat16)
    grad_act = jnp.einsum(
        "ecd,def->ecf", grad_rows, down_weight[:, 1:], preferred_element_type=jnp.float32
    )
    sigmoid_gate = jax.nn.sigmoid(gate_part)
    grad_gate_up = jnp.concatenate(
        [
            grad_act * up_part * sigmoid_gate * (1.0 + gate_part * (1.0 - sigmoid_gate)),
            grad_act * jax.nn.silu(gate_part),
        ],
        axis=-1,
    ).astype(jnp.bfloat16)
    grad_gathered = jnp.einsum(
        "ecf,def->ecd", grad_gate_up, up_weight[:, 1:], preferred_element_type=jnp.float32
    )
    slot_index = jnp.sum(jnp.where(choose, before[:, None, :], 0.0), axis=2).astype(jnp.int32)
    flat_index = routes * capacity + slot_index
    grad_second = jnp.sum(grad_gathered.reshape(-1, model_width)[flat_index], axis=1)
    grad_shared_act = jnp.einsum(
        "td,df->tf", cotangent, down_weight[:, 0], preferred_element_type=jnp.float32
    )
    sigmoid_shared = jax.nn.sigmoid(shared_gate)
    grad_shared_up = jnp.concatenate(
        [
            grad_shared_act
            * shared_lin
            * sigmoid_shared
            * (1.0 + shared_gate * (1.0 - sigmoid_shared)),
            grad_shared_act * jax.nn.silu(shared_gate),
        ],
        axis=-1,
    ).astype(jnp.bfloat16)
    grad_second = grad_second + jnp.einsum(
        "tf,df->td", grad_shared_up, up_weight[:, 0], preferred_element_type=jnp.float32
    )
    grad_second = grad_second + jnp.einsum(
        "te,de->td", grad_logits, router_weight, preferred_element_type=jnp.float32
    )
    grad_normed_two = grad_second * gain_two.astype(jnp.float32)
    grad_gain_two = jnp.sum(grad_second * normed_two, axis=0)
    grad_middle = grad_output + inverse_two * (
        grad_normed_two
        - normed_two * jnp.mean(grad_normed_two * normed_two, axis=-1, keepdims=True)
    )
    grad_router = jnp.einsum(
        "td,te->de", second_in, grad_logits, preferred_element_type=jnp.float32
    )
    narrow_rows = model_width // lax.axis_size("narrow")
    routed_cols, grad_cols, shared_cols, cotangent_cols = (
        lax.all_to_all(gathered_in, "narrow", split_axis=2, concat_axis=1, tiled=True),
        lax.all_to_all(grad_rows, "narrow", split_axis=2, concat_axis=1, tiled=True),
        lax.all_to_all(second_in[None], "narrow", split_axis=2, concat_axis=1, tiled=True),
        lax.all_to_all(cotangent[None], "narrow", split_axis=2, concat_axis=1, tiled=True),
    )
    slot_grads, slot_acts, shared_grads, shared_acts = (
        lax.all_gather(grad_gate_up, "narrow", axis=1, tiled=True),
        lax.all_gather(activated, "narrow", axis=1, tiled=True),
        lax.all_gather(grad_shared_up[None], "narrow", axis=1, tiled=True),
        lax.all_gather(shared_act[None], "narrow", axis=1, tiled=True),
    )
    expert_grads = expert_weight_terms(
        routed_cols,
        grad_cols,
        shared_cols[0],
        cotangent_cols[0],
        slot_grads,
        slot_acts,
        shared_grads[0],
        shared_acts[0],
    )
    gain_one, qkv_weight, out_weight = (
        lax.all_gather(gain_attn, ("wide", "narrow"), axis=0, tiled=True),
        lax.all_gather(w_qkv, ("wide", "narrow"), axis=0, tiled=True),
        lax.all_gather(w_out, ("wide", "narrow"), axis=0, tiled=True),
    )
    grad_attention = grad_middle.astype(jnp.bfloat16)
    grad_out_weight = jnp.einsum(
        "td,te->de", mixed, grad_attention, preferred_element_type=jnp.float32
    )
    grad_mixed = jnp.einsum(
        "te,de->td", grad_attention, out_weight, preferred_element_type=jnp.float32
    ).astype(jnp.bfloat16)
    grad_heads = grad_mixed.reshape(row_count, HEADS, HEAD_DIM)
    row_delta = jnp.sum(grad_heads.astype(jnp.float32) * mixed_exact, axis=2).T

    def back_step(grad_query, block_index):
        allowed, key_block, value_block, scores = block_parts(block_index)
        weights_exact = jnp.where(allowed, jnp.exp(scores - log_total[..., None]), 0.0)
        weights_low = weights_exact.astype(jnp.bfloat16)
        grad_value = jnp.einsum(
            "hqk,qhd->khd", weights_low, grad_heads, preferred_element_type=jnp.float32
        )
        grad_weights = jnp.einsum(
            "qhd,khd->hqk", grad_heads, value_block, preferred_element_type=jnp.float32
        )
        grad_scores = (weights_exact * (grad_weights - row_delta[..., None])).astype(jnp.bfloat16)
        grad_query = grad_query + jnp.einsum(
            "hqk,khd->qhd", grad_scores, key_block, preferred_element_type=jnp.float32
        )
        grad_key = jnp.einsum(
            "hqk,qhd->khd", grad_scores, query_rows, preferred_element_type=jnp.float32
        )
        return (
            grad_query,
            (grad_key.reshape(block_len, model_width), grad_value.reshape(block_len, model_width)),
        )

    query_start = jnp.zeros((row_count, HEADS, HEAD_DIM), jnp.float32)
    grad_query, (key_blocks, value_blocks) = lax.scan(
        back_step, query_start, jnp.arange(num_blocks)
    )
    key_partial = key_blocks.reshape(seqlen, model_width)
    value_partial = value_blocks.reshape(seqlen, model_width)
    grad_keys, grad_values = (
        lax.psum_scatter(
            key_partial.astype(jnp.bfloat16), "narrow", scatter_dimension=0, tiled=True
        ).astype(jnp.float32),
        lax.psum_scatter(
            value_partial.astype(jnp.bfloat16), "narrow", scatter_dimension=0, tiled=True
        ).astype(jnp.float32),
    )
    grad_query_raw = rotate_back(grad_query, cosine, sine_table) * query_scale
    grad_key_raw = rotate_back(grad_keys.reshape(row_count, HEADS, HEAD_DIM), cosine, sine_table)
    grad_projected = jnp.concatenate(
        [
            grad_query_raw.reshape(row_count, model_width),
            grad_key_raw.reshape(row_count, model_width),
            grad_values,
        ],
        axis=1,
    ).astype(jnp.bfloat16)
    grad_qkv_weight = jnp.einsum(
        "td,tf->df", first_in, grad_projected, preferred_element_type=jnp.float32
    )
    grad_first = jnp.einsum(
        "tf,df->td", grad_projected, qkv_weight, preferred_element_type=jnp.float32
    )
    grad_normed_one = grad_first * gain_one.astype(jnp.float32)
    grad_gain_one = jnp.sum(grad_first * normed_one, axis=0)
    grad_inputs = grad_middle + inverse_one * (
        grad_normed_one
        - normed_one * jnp.mean(grad_normed_one * normed_one, axis=-1, keepdims=True)
    )
    dense_parts = (
        lax.psum_scatter(
            grad_gain_one.astype(jnp.bfloat16), "narrow", scatter_dimension=0, tiled=True
        ).astype(jnp.float32),
        lax.psum_scatter(
            grad_qkv_weight.astype(jnp.bfloat16), "narrow", scatter_dimension=0, tiled=True
        ).astype(jnp.float32),
        lax.psum_scatter(
            grad_out_weight.astype(jnp.bfloat16), "narrow", scatter_dimension=0, tiled=True
        ).astype(jnp.float32),
        lax.psum_scatter(
            grad_gain_two.astype(jnp.bfloat16), "narrow", scatter_dimension=0, tiled=True
        ).astype(jnp.float32),
        lax.psum_scatter(
            grad_router.astype(jnp.bfloat16), "narrow", scatter_dimension=0, tiled=True
        ).astype(jnp.float32),
    )
    summed = jax.tree.map(
        lambda part: part.astype(jnp.float32),
        lax.psum(shortened((expert_grads,) + tuple(dense_parts)), "wide"),
    )
    expert_grads = summed[0]
    dense_parts = summed[1:]
    gain_one_sum, qkv_sum, out_sum, gain_two_sum, router_sum = dense_parts
    expert_table = expert_grads.reshape(narrow_rows, up_weight.shape[1], 3 * hidden)
    up_sum = expert_table[:, :, : 2 * hidden]
    down_sum = expert_table[:, :, 2 * hidden :]
    return (
        output,
        grad_inputs.astype(jnp.bfloat16),
        gain_one_sum,
        qkv_sum,
        out_sum,
        gain_two_sum,
        router_sum,
        up_sum,
        down_sum,
    )


PLANES = 4
WINDOW = 3
STARTS = (0, 3, 6, 7)
KEEP = ((0, 3), (0, 3), (0, 2), (1, 3))
MESH_IDS = pl.DeviceIdType.MESH
BF16 = jnp.bfloat16
F32 = jnp.float32


def place():
    w = lax.axis_index("wide")
    z = lax.axis_index("narrow")
    return w, z


def greet(w, z):
    barrier = pltpu.get_barrier_semaphore()
    peers = [(w, lax.rem(z + step, PLANES)) for step in (1, 2, 3)]
    peers += [(w ^ flip, z) for flip in (1, 2, 4, 6)]
    for peer in peers:
        pl.semaphore_signal(barrier, inc=1, device_id=peer, device_id_type=MESH_IDS)
    pl.semaphore_wait(barrier, len(peers))


def mul(a, b, over_a, over_b):
    return lax.dot_general(a, b, (((over_a,), (over_b,)), ((), ())), preferred_element_type=F32)


def at(start, size):
    return pl.ds(pl.multiple_of(start, 128), size)


def loop(first, last, body):
    def step(i, carry):
        body(i)
        return carry

    lax.fori_loop(first, last, step, 0)


class Links:
    def __init__(self, send_sems, recv_sems):
        self.w, self.z = place()
        self.send_sems, self.recv_sems = send_sems, recv_sems

    def copy(self, kind, step, src, dst, device):
        return pltpu.make_async_remote_copy(
            src_ref=src,
            dst_ref=dst,
            send_sem=self.send_sems.at[kind, step],
            recv_sem=self.recv_sems.at[kind, step],
            device_id=device,
            device_id_type=MESH_IDS,
        )

    def plane(self, step, sign):
        return lax.rem(self.z + PLANES + sign * step, PLANES)


def step_at(z, turn):
    step = 0
    for plane, steps in enumerate(((3, 2, 1, 0), (1, 3, 2, 0), (3, 1, 2, 0), (1, 2, 3, 0))):
        for number, value in enumerate(steps):
            step = jnp.where((z == plane) & (turn == number), value, step)
    return step


class Chain:
    def __init__(self, links, base, own, slot):
        self.links, self.base, self.own, self.slot = links, base, own, slot

    def goes(self, step, up):
        z = self.links.z
        if up:
            return (z >= step) & (z < PLANES - 1)
        return ((z < step) | (step == 0)) & (z > 0)

    def ring(self, step, up, own=False):
        links = self.links
        to = lax.rem(step + 1, 4) if up else lax.rem(step + 3, 4)
        ref = self.slot(links.plane(step, -1))
        return pltpu.make_async_remote_copy(
            src_ref=self.own if own else ref,
            dst_ref=ref,
            send_sem=links.send_sems.at[self.base if up else self.base + 1, step],
            recv_sem=links.recv_sems.at[self.base, to],
            device_id=(links.w, links.z + 1 if up else links.z - 1),
            device_id_type=MESH_IDS,
        )

    def hand_on(self, step, own=False):
        for up in (True, False):

            @pl.when(self.goes(step, up))
            def _():
                self.ring(step, up, own).start()

    def begin(self):
        self.hand_on(0, True)

    def arrive(self, turn):
        step = step_at(self.links.z, turn)
        ref = self.slot(self.links.plane(step, -1))
        self.links.copy(self.base, step, ref, ref, (self.links.w, self.links.z)).wait_recv()
        self.hand_on(step)

    def settle(self):
        def body(step):
            for up in (True, False):

                @pl.when(self.goes(step, up))
                def _():
                    self.ring(step, up).wait_send()

        loop(0, 4, body)


class Gather:
    def __init__(self, links, base, step, turn, slot, cores=True):
        self.links, self.base, self.step, self.slot, self.cores = links, base, step, slot, cores
        self.first = 1 + lax.rem(turn, 2)
        self.second = 3 - self.first

    def copy(self, kind, owner, flip):
        ref = self.slot(owner)
        return self.links.copy(
            self.base + kind, self.step, ref, ref, (self.links.w ^ flip, self.links.z)
        )

    def begin(self):
        w = self.links.w
        self.copy(0, w, 2).start()
        self.copy(1, w, 4).start()
        if self.cores:
            self.copy(4, w, 1).start()

    def relay(self):
        w = self.links.w
        self.copy(0, w, 2).wait_recv()
        self.copy(1, w, 4).wait_recv()
        self.across().start()
        if self.cores:
            self.copy(3, w ^ 2, 1).start()
            self.copy(5, w ^ 4, 1).start()

    def across(self):
        return self.copy(2, self.links.w ^ (2 * self.first), 2 * self.second)

    def end(self):
        self.across().wait_recv()
        if self.cores:
            self.copy(6, self.links.w ^ 6, 1).start()

    def settle(self):
        w = self.links.w
        self.copy(0, w, 2).wait_send()
        self.copy(1, w, 4).wait_send()
        self.across().wait_send()
        if self.cores:
            for kind, owner in ((4, w), (3, w ^ 2), (5, w ^ 4), (6, w ^ 6)):
                copy = self.copy(kind, owner, 1)
                copy.wait_send()
                copy.wait_recv()


def softmax_rows(scores, mask):
    masked = scores + mask
    powers = jnp.exp(masked - jnp.max(masked, axis=1, keepdims=True))
    return powers * (1.0 / jnp.sum(powers, axis=1, keepdims=True))


def start_kernel(
    tok_in, ids_in, wq_in, wo_in, we_in, cot_in, cos_in, sin_in,
    we_o, cot_o, wq_o, wo_o, first_o, qkv_o, exact_o, mixed_o, mixed_rows_o, middle_o, second_o, hop,
    tok, ids, wq_blocks, wo_blocks, staged, mask, mixed_got, mixed_send,
    load_sems, send_sems, recv_sems,
):
    links = Links(send_sems, recv_sems)
    w, z = links.w, links.z
    chip = w // 2
    rows, width = tok_in.shape
    seqlen = PLANES * rows
    size = WINDOW * HEAD_DIM
    own = wo_in.shape[0]
    keeps = [
        pltpu.make_async_copy(src, dst, load_sems.at[i])
        for i, (src, dst) in enumerate(
            (
                (tok_in, tok.at[z]),
                (ids_in, ids.at[z]),
                (wq_in.at[z], wq_blocks.at[w, z]),
                (wo_in, wo_blocks.at[w, z]),
                (cot_in, cot_o.at[chip, z]),
            )
        )
    ]
    for keep in keeps:
        keep.start()
    greet(w, z)

    tok_chain = Chain(links, 0, tok_in, lambda p: tok.at[p])
    ids_chain = Chain(links, 2, ids_in, lambda p: ids.at[p])
    wo_chain = Chain(links, 4, wo_in, lambda p: wo_blocks.at[w, p])
    cot_chain = Chain(links, 6, cot_in, lambda p: cot_o.at[chip, p])

    def wq_ring(step):
        to = links.plane(step, 1)
        return links.copy(8, step, wq_in.at[to], wq_blocks.at[w, z], (w, to))

    def wq_gather(step):
        source = links.plane(step, -1)
        return Gather(links, 9, step, step, lambda i: wq_blocks.at[i, source])

    def wo_gather(turn):
        step = step_at(z, turn)
        source = links.plane(step, -1)
        return Gather(links, 16, step, turn, lambda i: wo_blocks.at[i, source])

    def cot_gather(turn):
        step = step_at(z, turn)
        source = links.plane(step, -1)
        return Gather(links, 23, step, turn, lambda i: cot_o.at[i // 2, source], False)

    def weights_ring(step, flip):
        to = links.plane(step, 1)
        return links.copy(
            26 + flip, step, we_in.at[to, chip ^ flip], hop.at[step - 1, chip ^ flip], (w, to)
        )

    def weights_block(step, flip):
        return hop.at[step - 1, chip ^ flip] if step else we_in.at[z, chip ^ flip]

    def weights_plane(step, flip):
        to = we_o.at[w, links.plane(step, -1)]
        return links.copy(29 + flip, step, weights_block(step, flip), to, (w ^ (2 * flip), z))

    def weights_keep(step):
        return pltpu.make_async_copy(
            weights_block(step, 0), we_o.at[w, links.plane(step, -1)], load_sems.at[6 + step]
        )

    def weights_core(step, flip):
        block = we_o.at[w ^ (2 * flip), links.plane(step, -1)]
        return links.copy(
            34 + flip, step, block if flip else weights_block(step, 0), block, (w ^ 1, z)
        )

    def weights_send(step):
        for flip in (3, 1, 2, 0):
            weights_ring(step, flip).start()

    def weights_next(step):
        for flip in (3, 1, 2):
            if step:
                weights_ring(step, flip).wait_recv()
            weights_plane(step, flip).start()
        if step:
            weights_ring(step, 0).wait_recv()
        weights_core(step, 0).start()
        weights_keep(step).start()

    def weights_end(step):
        for flip in (1, 2, 3):
            weights_plane(step, flip).wait_recv()
            weights_core(step, flip).start()

    def mixed_ring(step):
        to = links.plane(step, 1)
        return links.copy(38, step, mixed_send.at[to], mixed_got.at[z], (w, to))

    tok_chain.begin()
    ids_chain.begin()
    for step in (1, 2, 3):
        wq_ring(step).start()
    for keep in keeps:
        keep.wait()
    wq_gather(0).begin()
    tok_chain.arrive(0)
    ids_chain.arrive(0)
    for step in (1, 2, 3):
        wq_ring(step).wait_recv()
        wq_gather(step).begin()
    wo_chain.begin()
    tok_chain.arrive(1)
    ids_chain.arrive(1)
    cot_chain.begin()
    end_plane = (z == 0) | (z == PLANES - 1)

    @pl.when(jnp.logical_not(end_plane))
    def _():
        tok_chain.arrive(2)
        ids_chain.arrive(2)

    loop(0, 4, lambda step: wq_gather(step).relay())

    @pl.when(end_plane)
    def _():
        tok_chain.arrive(2)
        ids_chain.arrive(2)
        weights_send(1)
        weights_send(3)

    wo_chain.arrive(0)
    wo_gather(0).begin()
    wo_gather(3).begin()
    cot_gather(3).begin()
    weights_next(0)
    for i in range(PLANES):
        for j in range(PLANES):
            here = (slice(i * rows, (i + 1) * rows), slice(j * rows, (j + 1) * rows))
            if j > i:
                mask[here] = jnp.full((rows, rows), -1e30, F32)
            else:
                same = ids[i, rows:, :].astype(F32) == ids[j, :rows, :].astype(F32)
                if i == j:
                    same = same & (
                        lax.broadcasted_iota(jnp.int32, (rows, rows), 1)
                        <= lax.broadcasted_iota(jnp.int32, (rows, rows), 0)
                    )
                mask[here] = jnp.where(same, 0.0, -1e30)
    loop(0, 4, lambda step: wq_gather(step).end())
    loop(0, 4, lambda step: wq_gather(step).settle())

    def assemble(blocks, to):
        def body(i):
            for p in range(PLANES):
                staged[p * own : (p + 1) * own, :] = blocks[i, p].astype(F32)
            span = PLANES * own
            to[pl.ds(pl.multiple_of(i * span, 16), span), :] = staged[...].astype(BF16)

        loop(0, blocks.shape[0], body)

    cot_chain.arrive(0)
    cot_gather(0).begin()
    assemble(wq_blocks, wq_o)
    gains = jnp.transpose(wq_o[:, size * 3 :].astype(F32))
    gain_one = gains[16:17, :]
    gain_two = gains[17:18, :]

    def normalise(p):
        block = tok[p].astype(F32)
        inverse = lax.rsqrt(jnp.mean(block * block, axis=1, keepdims=True) + epsilon)
        first_o[p] = (block * inverse * gain_one).astype(BF16)

    loop(0, PLANES, normalise)
    wo_chain.arrive(1)
    wo_gather(1).begin()
    cot_chain.arrive(1)
    cot_gather(1).begin()

    def project(p):
        span = pl.ds(pl.multiple_of(p * rows, 128), rows)
        cosine, sine = cos_in[span, :], sin_in[span, :]
        for kind in range(3):
            part = mul(first_o[p], wq_o[:, kind * size : (kind + 1) * size], 1, 0)
            for head in range(WINDOW):
                here = part[:, head * HEAD_DIM : (head + 1) * HEAD_DIM]
                if kind < 2:
                    here = here * cosine + pltpu.roll(here, HEAD_DIM // 2, 1) * sine
                if kind == 0:
                    here = here * (HEAD_DIM ** (-0.5))
                qkv_o[kind, head, span, :] = here.astype(BF16)

    loop(0, PLANES, project)
    wo_chain.arrive(2)
    wo_gather(2).begin()
    cot_chain.arrive(2)
    cot_gather(2).begin()

    @pl.when(jnp.logical_not(end_plane))
    def _():
        weights_send(1)
        weights_send(3)

    def attend(head):
        exact = softmax_rows(mul(qkv_o[0, head], qkv_o[1, head], 1, 1), mask[...])
        exact_o[head] = exact
        mixed_o[head] = mul(exact.astype(BF16), qkv_o[2, head], 1, 0)

    loop(0, WINDOW, attend)
    for p in range(PLANES):
        for head in range(WINDOW):
            mixed_send[p, :, head * HEAD_DIM : (head + 1) * HEAD_DIM] = mixed_o[
                head, p * rows : (p + 1) * rows, :
            ].astype(BF16)
    for step in (1, 2, 3):
        mixed_ring(step).start()
    mixed_got[z] = mixed_send[z]
    weights_send(2)
    loop(0, 4, lambda turn: wo_gather(turn).relay())
    loop(0, 4, lambda turn: wo_gather(turn).end())
    weights_next(1)
    loop(0, 4, lambda turn: cot_gather(turn).relay())
    weights_end(0)
    weights_next(3)
    loop(0, 4, lambda turn: wo_gather(turn).settle())
    assemble(wo_blocks, wo_o)
    for step in (1, 2, 3):
        mixed_ring(step).wait_recv()
    column = 0
    for p, (a, b) in enumerate(KEEP):
        span = (b - a) * HEAD_DIM
        mixed_rows_o[:, column : column + span] = mixed_got[p, :, a * HEAD_DIM : b * HEAD_DIM]
        column += span

    def out_project(i):
        here = at(i * 256, 256)
        middle_o[:, here] = tok_in_f32(tok, z, here) + mul(mixed_rows_o[...], wo_o[:, here], 1, 0)

    loop(0, width // 256, out_project)
    middle = middle_o[...]
    inverse = lax.rsqrt(jnp.mean(middle * middle, axis=1, keepdims=True) + epsilon)
    second_o[...] = (middle * inverse * gain_two).astype(BF16)
    weights_end(1)
    loop(0, 4, lambda turn: cot_gather(turn).end())
    weights_end(3)
    weights_next(2)
    weights_end(2)
    loop(0, 4, lambda turn: cot_gather(turn).settle())
    for chain in (tok_chain, ids_chain, wo_chain, cot_chain):
        chain.settle()
    for step in (0, 1, 2, 3):
        weights_keep(step).wait()
        for flip in (0, 1, 2, 3):
            if step:
                weights_ring(step, flip).wait_send()
            if flip:
                weights_plane(step, flip).wait_send()
            weights_core(step, flip).wait_send()
            weights_core(step, flip).wait_recv()
        if step:
            wq_ring(step).wait_send()
            mixed_ring(step).wait_send()


def tok_in_f32(tok, z, here):
    return tok[z, :, here].astype(F32)


def start(tok, ids, wq, wo, we, cot, cosine, sine, collective):
    rows, width = tok.shape
    own = wo.shape[0]
    hidden3 = we.shape[-1]
    seqlen = PLANES * rows
    size = WINDOW * HEAD_DIM
    blocks = (8, PLANES, own, width)
    any_out = pl.BlockSpec(memory_space=pl.ANY)
    vmem_out = pl.BlockSpec(memory_space=pltpu.VMEM)
    shapes = [
        ((8, PLANES, own, hidden3), BF16, any_out),
        ((4, PLANES) + cot.shape, BF16, any_out),
        ((width, width), BF16, vmem_out),
        ((width, width), BF16, vmem_out),
        ((PLANES, rows, width), BF16, vmem_out),
        ((3, WINDOW, seqlen, HEAD_DIM), BF16, vmem_out),
        ((WINDOW, seqlen, seqlen), F32, vmem_out),
        ((WINDOW, seqlen, HEAD_DIM), F32, vmem_out),
        ((rows, width), BF16, vmem_out),
        ((rows, width), F32, vmem_out),
        ((rows, width), BF16, vmem_out),
        ((3, 4, own, hidden3), BF16, any_out),
    ]
    return pl.pallas_call(
        start_kernel,
        out_shape=[jax.ShapeDtypeStruct(shape, kind) for shape, kind, _ in shapes],
        in_specs=[any_out] * 6 + [vmem_out] * 2,
        out_specs=[spec for _, _, spec in shapes],
        scratch_shapes=[
            pltpu.VMEM((PLANES, rows, width), BF16),
            pltpu.VMEM((PLANES,) + ids.shape, BF16),
            pltpu.VMEM(blocks, BF16),
            pltpu.VMEM(blocks, BF16),
            pltpu.VMEM((PLANES * own, width), F32),
            pltpu.VMEM((seqlen, seqlen), F32),
            pltpu.VMEM((PLANES, rows, size), BF16),
            pltpu.VMEM((PLANES, rows, size), BF16),
            pltpu.SemaphoreType.DMA((10,)),
            pltpu.SemaphoreType.DMA((39, 4)),
            pltpu.SemaphoreType.DMA((39, 4)),
        ],
        compiler_params=pltpu.CompilerParams(
            collective_id=collective, has_side_effects=True, vmem_limit_bytes=56 * 2**20
        ),
        name="start",
    )(tok, ids, wq, wo, we, cot, cosine, sine)[:-1]


def add_blocks(out, *terms):
    rows = out.shape[0]

    def body(i, carry):
        part = pl.ds(pl.multiple_of(i * 16, 16), 16)
        total = terms[0][part, :].astype(F32)
        for term in terms[1:]:
            total = total + term[part, :].astype(F32)
        out[part, :] = total.astype(out.dtype)
        return carry

    lax.fori_loop(0, rows // 16, body, 0)


def experts_kernel(
    x_in, cot_in, weights_in, misc_in, grads_o, outs_o, outs_one_o, sums_o,
    x, cot, weights, misc, act, scaled, slopes, gate, outs, parts, got_one, got_two, got_far, stage,
    load_sems, send_sems, recv_sems,
):
    w, z = place()
    chip = w // 2
    expert = chip * PLANES + z
    rows, width = x_in.shape
    hidden = weights.shape[1] // 3
    group_rows = 4 * rows

    def remote(kind, step, src, dst, device):
        return pltpu.make_async_remote_copy(
            src_ref=src,
            dst_ref=dst,
            send_sem=send_sems.at[kind, step],
            recv_sem=recv_sems.at[kind, step],
            device_id=device,
            device_id_type=MESH_IDS,
        )

    def plane_of(step, sign):
        return lax.rem(z + PLANES + sign * step, PLANES)

    def step_at(turn):
        step = 0
        for plane, steps in enumerate(((3, 2, 1, 0), (1, 3, 2, 0), (3, 1, 2, 0), (1, 2, 3, 0))):
            for number, value in enumerate(steps):
                step = jnp.where((z == plane) & (turn == number), value, step)
        return step

    def axes(turn):
        first = 1 + lax.rem(turn, 2)
        return first, 3 - first

    def ring(step, up):
        to = lax.rem(step + 1, 4) if up else lax.rem(step + 3, 4)
        return pltpu.make_async_remote_copy(
            src_ref=x.at[step, chip],
            dst_ref=x.at[to, chip],
            send_sem=send_sems.at[0 if up else 8, step],
            recv_sem=recv_sems.at[0, to],
            device_id=(w, z + 1 if up else z - 1),
            device_id_type=MESH_IDS,
        )

    def goes(step, up):
        if up:
            return (z >= step) & (z < PLANES - 1)
        return ((z < step) | (step == 0)) & (z > 0)

    def pass_on(step):
        for up in (True, False):

            @pl.when(goes(step, up))
            def _():
                ring(step, up).start()

    def arrive(step):
        pltpu.make_async_remote_copy(
            src_ref=x.at[step, chip],
            dst_ref=x.at[step, chip],
            send_sem=send_sems.at[0, step],
            recv_sem=recv_sems.at[0, step],
            device_id=(w, z),
            device_id_type=MESH_IDS,
        ).wait_recv()

    def direct(step, flip):
        block = x.at[step, chip]
        return remote(flip, step, block, block, (w ^ (2 * flip), z))

    def across(turn):
        first, second = axes(turn)
        step = step_at(turn)
        block = x.at[step, chip ^ first]
        return remote(3, step, block, block, (w ^ (2 * second), z))

    def near(turn, which):
        first, _ = axes(turn)
        step = step_at(turn)
        block = chip ^ 3 if which else chip ^ first
        return remote(
            4 + which, step, parts.at[step, block], got_one.at[step, which], (w ^ (2 * first), z)
        )

    def cross(turn):
        _, second = axes(turn)
        step = step_at(turn)
        return remote(
            6, step, parts.at[step, chip ^ second], got_two.at[step], (w ^ (2 * second), z)
        )

    def far(step):
        return remote(7, step, parts.at[step, chip], got_far.at[step - 1], (w, plane_of(step, -1)))

    def outs_near(step, which):
        first, _ = axes(step)
        block = chip ^ 3 if which else chip ^ first
        return remote(
            9 + which, step, outs_o.at[step, block], outs_one_o.at[step, which], (w ^ (2 * first), z)
        )

    def cot_load(step):
        return pltpu.make_async_copy(
            cot_in.at[:, plane_of(step, -1)], cot.at[step], load_sems.at[step]
        )

    def outs_out(turn):
        return pltpu.make_async_copy(
            outs.at[lax.rem(turn, 2)], outs_o.at[step_at(turn)], load_sems.at[9 + lax.rem(turn, 2)]
        )

    def grads_out(low, size, slot):
        return pltpu.make_async_copy(
            stage.at[slot, :, pl.ds(0, size)], grads_o.at[:, low], load_sems.at[4 + slot]
        )

    loads = [
        pltpu.make_async_copy(src, dst, load_sems.at[6 + i])
        for i, (src, dst) in enumerate(
            (
                (x_in, x.at[0, chip]),
                (misc_in.at[:, pl.ds(misc_in.shape[1] - 128, 128)], misc),
                (weights_in, weights),
            )
        )
    ]
    for load in loads:
        load.start()
    loop(0, 4, lambda step: cot_load(step).start())
    greet(w, z)
    loads[0].wait()
    pass_on(0)

    def begin(turn):
        step = step_at(turn)

        @pl.when(turn < 3)
        def _():
            arrive(step)
            pass_on(step)

        direct(step, 1).start()
        direct(step, 2).start()

    def relay(turn):
        step = step_at(turn)
        direct(step, 1).wait_recv()
        direct(step, 2).wait_recv()
        across(turn).start()

    begin(0)
    begin(1)
    relay(0)
    begin(2)
    begin(3)
    loads[1].wait()
    loads[2].wait()

    def first_half(step):
        cot_load(step).wait()
        rows_in = x[step].reshape(group_rows, width)
        members = cot[step, :, :, width:].reshape(group_rows, 128).astype(F32)
        logits = mul(rows_in, misc[...], 1, 0)
        lane = lax.broadcasted_iota(jnp.int32, logits.shape, 1)
        routed = (lane > 0) & (lane < 16)
        top = jnp.max(jnp.where(routed, logits, -1e30), axis=1, keepdims=True)
        powers = jnp.where(routed, jnp.exp(logits - top), 0.0)
        probs = jnp.where(lane == 0, 1.0, powers / jnp.sum(powers, axis=1, keepdims=True))
        own = jnp.where(lane == expert, members, 0.0)
        gate[0] = jnp.broadcast_to(jnp.sum(probs * own, axis=1, keepdims=True), gate.shape[1:])
        gate[1] = own

        def hidden_chunk(low, size):
            here = x[step].reshape(group_rows, width)
            gate_part = mul(here, weights[:, at(low, size)], 1, 0)
            up_part = mul(here, weights[:, at(hidden + low, size)], 1, 0)
            grad_act = mul(
                cot[step, :, :, :width].reshape(group_rows, width),
                weights[:, at(2 * hidden + low, size)],
                1,
                0,
            )
            scale = gate[0][:, :1]
            grad_act = grad_act * scale
            sigmoid = 1.0 / (1.0 + jnp.exp(-gate_part))
            silu = gate_part * sigmoid
            activated = (silu * up_part).astype(BF16)
            act[:, at(low, size)] = activated
            scaled[step, :, at(low, size)] = (activated.astype(F32) * scale).astype(BF16)
            slopes[step, :, at(low, size)] = (
                grad_act * up_part * (sigmoid + silu * (1.0 - sigmoid))
            ).astype(BF16)
            slopes[step, :, at(hidden + low, size)] = (grad_act * silu).astype(BF16)

        loop(0, hidden // 256, lambda i: hidden_chunk(i * 256, 256))
        if hidden % 256:
            hidden_chunk(hidden // 256 * 256, hidden % 256)

    def second_half(turn, step):
        def width_body(i, total):
            low = i * 256
            expert_rows = mul(act[...], weights[at(low, 256), 2 * hidden :], 1, 1)
            expert_rows = expert_rows.astype(BF16).astype(F32)
            outs[lax.rem(turn, 2), :, :, at(low, 256)] = (
                (expert_rows * gate[0][:, :1]).astype(BF16).reshape(4, rows, 256)
            )
            product = expert_rows * cot[step, :, :, at(low, 256)].reshape(group_rows, 256).astype(F32)
            grad_in = mul(slopes[step], weights[at(low, 256), : 2 * hidden], 1, 1)
            parts[step, :, :, at(low, 256)] = grad_in.astype(BF16).reshape(4, rows, 256)
            return total + product[:, :128] + product[:, 128:]

        total = lax.fori_loop(0, width // 256, width_body, jnp.zeros((group_rows, 128), F32))
        prob = jnp.sum(total, axis=1, keepdims=True) * gate[1]
        high = prob.astype(BF16)
        low = (prob - high.astype(F32)).astype(BF16)
        low = pltpu.roll(low.astype(F32), 32, 1).astype(BF16)
        parts[step, :, :, width:] = (high + low).reshape(4, rows, 128)

    def send_cross(turn):
        _, second = axes(turn)
        step = step_at(turn)
        near(turn, 1).wait_recv()
        block = parts.at[step, chip ^ second]
        add_blocks(block, block, got_one.at[step, 1])
        cross(turn).start()

    def send_far(turn):
        step = step_at(turn)
        near(turn, 0).wait_recv()
        cross(turn).wait_recv()
        block = parts.at[step, chip]
        add_blocks(block, block, got_one.at[step, 0], got_two.at[step])
        far(step).start()

    def group(turn):
        step = step_at(turn)
        across(turn).wait_recv()
        first_half(step)

        @pl.when(turn < 2)
        def _():
            relay(2 * turn + 1)

        @pl.when(turn > 1)
        def _():
            outs_out(turn - 2).wait()

        second_half(turn, step)
        outs_out(turn).start()

        @pl.when(turn == 0)
        def _():
            relay(2)

        @pl.when(turn > 0)
        def _():
            send_cross(turn - 1)

        near(turn, 1).start()
        near(turn, 0).start()

        @pl.when(turn > 1)
        def _():
            send_far(turn - 2)

    loop(0, 4, group)

    def weight_chunk(left, right, low, size, offset, i):
        slot = lax.rem(i, 2)

        @pl.when(i >= 2)
        def _():
            grads_out(pl.ds(0, 256), 256, slot).wait()

        total = None
        for step in range(4):
            term = mul(
                left[step, :, :, :width].reshape(group_rows, width), right[step, :, at(low, size)], 0, 0
            )
            total = term if total is None else total + term
        stage[slot, :, :size] = total.astype(BF16)
        grads_out(at(offset + low, size), size, slot).start()

    ups, downs = 2 * hidden // 256, hidden // 256

    def up_chunk(i):
        weight_chunk(x, slopes, i * 256, 256, 0, i)

    def down_chunk(i):
        weight_chunk(cot, scaled, (i - ups) * 256, 256, 2 * hidden, i)

    loop(0, 3, up_chunk)
    send_cross(3)
    outs_out(2).wait()
    outs_out(3).wait()
    loop(0, 4, lambda step: (outs_near(step, 1).start(), outs_near(step, 0).start()))
    loop(3, 5, up_chunk)
    send_far(2)
    loop(5, ups, up_chunk)
    loop(ups, ups + downs, down_chunk)
    last = ups + downs
    if hidden % 256:
        weight_chunk(cot, scaled, downs * 256, hidden % 256, 2 * hidden, jnp.int32(last))
        grads_out(pl.ds(0, 256), 256, (last - 1) % 2).wait()
        grads_out(pl.ds(0, hidden % 256), hidden % 256, last % 2).wait()
    else:
        grads_out(pl.ds(0, 256), 256, last % 2).wait()
        grads_out(pl.ds(0, 256), 256, (last - 1) % 2).wait()
    near(3, 0).wait_recv()
    cross(3).wait_recv()
    loop(1, 4, lambda step: far(step).wait_recv())
    add_blocks(
        sums_o,
        parts.at[0, chip],
        got_one.at[0, 0],
        got_two.at[0],
        got_far.at[0],
        got_far.at[1],
        got_far.at[2],
    )

    def settle(turn):
        step = step_at(turn)
        direct(step, 1).wait_send()
        direct(step, 2).wait_send()
        across(turn).wait_send()
        near(turn, 0).wait_send()
        near(turn, 1).wait_send()
        cross(turn).wait_send()
        for which in (0, 1):
            outs_near(turn, which).wait_send()
            outs_near(turn, which).wait_recv()

        @pl.when(turn < 3)
        def _():
            far(step).wait_send()

        for up in (True, False):

            @pl.when(goes(step, up))
            def _():
                ring(step, up).wait_send()

    loop(0, 4, settle)


def run_experts(second_in, cot_all, weights, misc, collective):
    rows, width = second_in.shape
    hidden = weights.shape[1] // 3
    sums_width = width + 128
    block = (rows, sums_width)
    return pl.pallas_call(
        experts_kernel,
        out_shape=[
            jax.ShapeDtypeStruct((width, 3 * hidden), BF16),
            jax.ShapeDtypeStruct((4, 4, rows, width), BF16),
            jax.ShapeDtypeStruct((4, 2, rows, width), BF16),
            jax.ShapeDtypeStruct((rows, sums_width), F32),
        ],
        in_specs=[pl.BlockSpec(memory_space=pl.ANY)] * 4,
        out_specs=[
            pl.BlockSpec(memory_space=pl.ANY),
            pl.BlockSpec(memory_space=pl.ANY),
            pl.BlockSpec(memory_space=pl.ANY),
            pl.BlockSpec(memory_space=pltpu.VMEM),
        ],
        scratch_shapes=[
            pltpu.VMEM((4, 4, rows, width), BF16),
            pltpu.VMEM((4, 4, rows, width + 128), BF16),
            pltpu.VMEM((width, 3 * hidden), BF16),
            pltpu.VMEM((width, 128), BF16),
            pltpu.VMEM((4 * rows, hidden), BF16),
            pltpu.VMEM((4, 4 * rows, hidden), BF16),
            pltpu.VMEM((4, 4 * rows, 2 * hidden), BF16),
            pltpu.VMEM((2, 4 * rows, 128), F32),
            pltpu.VMEM((2, 4, rows, width), BF16),
            pltpu.VMEM((4, 4) + block, BF16),
            pltpu.VMEM((4, 2) + block, BF16),
            pltpu.VMEM((4,) + block, BF16),
            pltpu.VMEM((3,) + block, BF16),
            pltpu.VMEM((2, width, 256), BF16),
            pltpu.SemaphoreType.DMA((11,)),
            pltpu.SemaphoreType.DMA((11, 4)),
            pltpu.SemaphoreType.DMA((11, 4)),
        ],
        compiler_params=pltpu.CompilerParams(
            collective_id=collective, has_side_effects=True, vmem_limit_bytes=62 * 2**20
        ),
        name="experts",
    )(second_in, cot_all, weights, misc)


def finish_kernel(
    outs_in, outs_one_in, grads_in, heads_in, exact_in, mixed_in, qkv_in, first_in, wq_in, cos_in, sin_in,
    rows_in, attn_in, misc_in, gain_in,
    sums_o, table_o, first_o, q_o, o_o,
    outs, outs_one, outs_two, outs_far, grads_own, grads_got, heads, exact, mixed, qkv, first, wq,
    projected, first_part, dense, dense_got, dense_one, dense_two, dense_far, dense_sum,
    load_sems, send_sems, recv_sems,
):
    links = Links(send_sems, recv_sems)
    w, z = links.w, links.z
    chip, core = w // 2, w % 2
    rows = outs.shape[2]
    width = outs.shape[3]
    size = WINDOW * HEAD_DIM
    steps = (1, 2, 3, 0)
    block_rows = o_o.shape[0] // 4
    half = o_o.shape[1] // 2
    plane_rows = o_o.shape[0]
    remote, plane_of = links.copy, links.plane

    def axes(step):
        one = 1 + lax.rem(step, 2)
        return one, 3 - one

    def heads_ring(step):
        to = plane_of(step, 1)
        return remote(37, step, heads_in.at[to], heads.at[z], (w, to))

    def grads_load(step):
        return pltpu.make_async_copy(
            grads_in.at[plane_of(step, 1), core], grads_own.at[step], load_sems.at[0, step]
        )

    def grads_swap(step):
        return remote(
            0, step, grads_in.at[plane_of(step, 1), 1 - core], grads_got.at[step], (w ^ 1, z)
        )

    def grads_ring(step):
        return remote(1, step, grads_own.at[step], table_o.at[chip, z, core], (w, plane_of(step, 1)))

    def grads_keep():
        return pltpu.make_async_copy(
            grads_own.at[0], table_o.at[chip, z, core], load_sems.at[1, 0]
        )

    def grads_gather(step):
        source = plane_of(step, -1)
        return Gather(links, 2, step, step, lambda i: table_o.at[i // 2, source, i % 2])

    def outs_loads(step):
        _, two = axes(step)
        return [
            pltpu.make_async_copy(src, dst, load_sems.at[2 + 3 * (i > 0) + (i > 1), step])
            for i, (src, dst) in enumerate(
                (
                    (outs_in.at[step, chip], outs.at[step, 0]),
                    (outs_in.at[step, chip ^ two], outs.at[step, 1]),
                    (outs_one_in.at[step], outs_one.at[step]),
                )
            )
        ]

    def cross(step):
        _, two = axes(step)
        return remote(11, step, outs.at[step, 1], outs_two.at[step], (w ^ (2 * two), z))

    def far(step):
        return remote(12, step, outs.at[step, 0], outs_far.at[step - 1], (w, plane_of(step, -1)))

    def part(kind, step):
        return dense.at[0, kind, plane_of(step, 1)]

    def dense_swap(kind, step):
        to = plane_of(step, 1)
        return remote(
            13 + 4 * kind, step, dense.at[1, kind, to], dense_got.at[kind, step], (w ^ 1, z)
        )

    def rows_of(block):
        return pl.ds(pl.multiple_of(block * block_rows, 16), block_rows)

    def dense_axes(kind):
        return 1 + kind, 2 - kind

    def dense_near(kind, step, which):
        one, _ = dense_axes(kind)
        block = chip ^ 3 if which else chip ^ one
        return remote(
            14 + 4 * kind + which,
            step,
            part(kind, step).at[rows_of(block)],
            dense_one.at[kind, step, which],
            (w ^ (2 * one), z),
        )

    def dense_cross(kind, step):
        _, two = dense_axes(kind)
        return remote(
            16 + 4 * kind,
            step,
            part(kind, step).at[rows_of(chip ^ two)],
            dense_two.at[kind, step],
            (w ^ (2 * two), z),
        )

    def place_of(owner):
        return rows_of(owner // 2), at(lax.rem(owner, 2) * half, half)

    def dense_ring(kind, step):
        own = part(kind, step).at[rows_of(chip)]
        here, columns = place_of(w)
        to = q_o.at[z, here, columns] if kind == 0 else dense_far.at[step - 1]
        return remote(21 + kind, step, own, to, (w, plane_of(step, 1)))

    def dense_keep():
        here, columns = place_of(w)
        return pltpu.make_async_copy(
            part(0, 0).at[rows_of(chip)], q_o.at[z, here, columns], load_sems.at[1, 1]
        )

    def dense_last():
        here, columns = place_of(w)
        return pltpu.make_async_copy(dense_sum, o_o.at[here, columns], load_sems.at[1, 2])

    def q_slot(step):
        source = plane_of(step, -1)

        def slot(owner):
            here, columns = place_of(owner)
            return q_o.at[source, here, columns]

        return slot

    def o_slot(owner):
        here, columns = place_of(owner)
        return o_o.at[here, columns]

    def q_gather(step):
        return Gather(links, 23, step, step, q_slot(step))

    def o_gather():
        return Gather(links, 30, 0, 0, o_slot)

    def first_ring(step):
        to = plane_of(step, 1)
        return remote(38, step, first_part.at[to], first_o.at[z], (w, to))

    def first_keep():
        return pltpu.make_async_copy(first_part.at[z], first_o.at[z], load_sems.at[1, 3])

    loads = [
        pltpu.make_async_copy(src, dst, load_sems.at[3 + i // 4, i % 4])
        for i, (src, dst) in enumerate(
            (
                (heads_in.at[z], heads.at[z]),
                (exact_in, exact),
                (mixed_in, mixed),
                (qkv_in, qkv),
                (first_in, first),
                (wq_in, wq),
            )
        )
    ]
    for step in steps:
        grads_load(step).start()
    for step in steps:
        for load in outs_loads(step):
            load.start()
    for load in loads:
        load.start()
    greet(w, z)
    for step in (1, 2, 3):
        heads_ring(step).start()
    for step in steps:
        grads_swap(step).start()

    def grads_ready(step):
        grads_load(step).wait()
        grads_swap(step).wait_recv()
        add_blocks(grads_own.at[step], grads_own.at[step], grads_got.at[step])

    grads_ready(0)
    keep = grads_keep()
    keep.start()

    def outs_cross(step):
        for load in outs_loads(step):
            load.wait()
        add_blocks(outs.at[step, 1], outs.at[step, 1], outs_one.at[step, 1])
        cross(step).start()

    keep.wait()
    grads_gather(0).begin()
    loop(1, 4, grads_ready)
    loop(0, 4, outs_cross)
    for step in (1, 2, 3):
        heads_ring(step).wait_recv()
    grads_ring(1).start()
    grads_ring(3).start()

    def out_weight(i):
        side = i // (half // 128)
        low = at((i - side * (half // 128)) * 128, 128)
        total = mul(rows_in[...], attn_in[:, at(i * 128, 128)], 0, 0).astype(BF16)
        dense[side ^ core, 1, :, :, low] = total.reshape(PLANES, plane_rows, 128)

    loop(0, width // 128, out_weight)
    for step in steps:
        dense_swap(1, step).start()
    for load in loads:
        load.wait()

    def head_back(head):
        keep_head = jnp.float32(0)
        for plane, (a, b) in enumerate(KEEP):
            keep_head = jnp.where((z == plane) & (head >= a) & (head < b), 1.0, keep_head)
        columns = at(head * HEAD_DIM, HEAD_DIM)
        grad_rows = heads[:, :, columns].reshape(PLANES * rows, HEAD_DIM).astype(F32) * keep_head
        delta = jnp.sum(grad_rows * mixed[head], axis=1, keepdims=True)
        grad_rows = grad_rows.astype(BF16)
        weights = exact[head]
        grad_value = mul(weights.astype(BF16), grad_rows, 0, 0)
        grad_scores = mul(grad_rows, qkv[2, head], 1, 1)
        grad_scores = (weights * (grad_scores - delta)).astype(BF16)
        grad_query = mul(grad_scores, qkv[1, head], 1, 0) * (HEAD_DIM ** (-0.5))
        grad_key = mul(grad_scores, qkv[0, head], 0, 0)

        def back(grads):
            return grads * cos_in[...] + pltpu.roll(grads * sin_in[...], HEAD_DIM // 2, 1)

        projected[:, columns] = back(grad_query).astype(BF16)
        projected[:, at(size + head * HEAD_DIM, HEAD_DIM)] = back(grad_key).astype(BF16)
        projected[:, at(2 * size + head * HEAD_DIM, HEAD_DIM)] = grad_value.astype(BF16)

    loop(0, WINDOW, head_back)

    def grads_next(step):
        grads_ring(step).wait_recv()
        grads_gather(step).begin()

    grads_gather(0).relay()

    def qkv_weight(i):
        side = i // (half // 128)
        low = at((i - side * (half // 128)) * 128, 128)
        total = mul(first[...].reshape(PLANES * rows, width), projected[:, at(i * 128, 128)], 0, 0)
        dense[side ^ core, 0, :, :, low] = total.astype(BF16).reshape(PLANES, plane_rows, 128)

    loop(0, 3 * size // 128, qkv_weight)
    gain_parts = []
    for i in range(width // 256):
        here = slice(i * 256, (i + 1) * 256)
        total = mul(projected[...], wq[here, : 3 * size], 1, 1)
        first_part[:, :, here] = total.astype(BF16).reshape(PLANES, rows, 256)
        scaled = total * first[:, :, here].reshape(PLANES * rows, 256).astype(F32)
        gain_parts.append(jnp.sum(scaled, axis=0, keepdims=True))
    gain_row = jnp.concatenate(gain_parts, axis=1) / gain_in[0:1, :]
    gain_columns = jnp.transpose(jnp.broadcast_to(gain_row, (128, width)))
    lane = lax.broadcasted_iota(jnp.int32, gain_columns.shape, 1)
    misc = jnp.where(lane == 15, gain_columns, misc_in[...])
    dense[1 ^ core, 0, :, :, half - 128 :] = misc.astype(BF16).reshape(PLANES, plane_rows, 128)
    for step in steps:
        dense_swap(0, step).start()

    keep_first = first_keep()
    keep_first.start()
    for step in (1, 2, 3):
        first_ring(step).start()
    grads_ring(2).start()
    loop(1, 2, grads_next)

    def dense_ready(step):
        for kind in (0, 1):
            dense_swap(kind, step).wait_recv()
            block = part(kind, step)
            add_blocks(block, block, dense_got.at[kind, step])
            dense_near(kind, step, 1).start()
            dense_near(kind, step, 0).start()

    loop(0, 4, dense_ready)

    def outs_finish(step):
        cross(step).wait_recv()
        block = outs.at[step, 0]
        add_blocks(block, block, outs_one.at[step, 0], outs_two.at[step])

        @pl.when(step > 0)
        def _():
            far(step).start()

    loop(0, 4, outs_finish)
    grads_gather(0).end()
    loop(3, 4, grads_next)
    grads_gather(1).relay()

    def dense_cross_start(step):
        for kind in (0, 1):
            _, two = dense_axes(kind)
            dense_near(kind, step, 1).wait_recv()
            block = part(kind, step).at[rows_of(chip ^ two)]
            add_blocks(block, block, dense_one.at[kind, step, 1])
            dense_cross(kind, step).start()

    loop(0, 4, dense_cross_start)
    grads_gather(1).end()
    grads_gather(3).relay()

    def dense_finish(step):
        for kind in (0, 1):
            dense_near(kind, step, 0).wait_recv()
            dense_cross(kind, step).wait_recv()
            block = part(kind, step).at[rows_of(chip)]
            add_blocks(block, block, dense_one.at[kind, step, 0], dense_two.at[kind, step])

        @pl.when(step > 0)
        def _():
            dense_ring(0, step).start()
            dense_ring(1, step).start()

    loop(0, 4, dense_finish)
    keep = dense_keep()
    keep.start()
    keep.wait()
    q_gather(0).begin()
    loop(2, 3, grads_next)
    grads_gather(3).end()

    def q_next(step):
        dense_ring(0, step).wait_recv()
        q_gather(step).begin()
        dense_ring(1, step).wait_recv()

    loop(1, 4, q_next)
    add_blocks(
        dense_sum, part(1, 0).at[rows_of(chip)], dense_far.at[0], dense_far.at[1], dense_far.at[2]
    )
    keep = dense_last()
    keep.start()
    keep.wait()
    o_gather().begin()
    grads_gather(2).relay()
    loop(0, 4, lambda step: q_gather(step).relay())
    o_gather().relay()
    loop(1, 4, lambda step: far(step).wait_recv())
    add_blocks(sums_o, outs.at[0, 0], outs_far.at[0], outs_far.at[1], outs_far.at[2])
    grads_gather(2).end()
    loop(0, 4, lambda step: q_gather(step).end())
    o_gather().end()
    loop(0, 4, lambda step: grads_gather(step).settle())
    loop(0, 4, lambda step: q_gather(step).settle())
    o_gather().settle()
    keep_first.wait()

    def settle(step):
        grads_swap(step).wait_send()
        cross(step).wait_send()
        for kind in (0, 1):
            dense_swap(kind, step).wait_send()
            dense_near(kind, step, 0).wait_send()
            dense_near(kind, step, 1).wait_send()
            dense_cross(kind, step).wait_send()

    loop(0, 4, settle)

    def settle_rings(step):
        first_ring(step).wait_recv()
        first_ring(step).wait_send()
        heads_ring(step).wait_send()
        grads_ring(step).wait_send()
        far(step).wait_send()
        dense_ring(0, step).wait_send()
        dense_ring(1, step).wait_send()

    loop(1, 4, settle_rings)


def finish(
    outs, outs_one, grads, heads, exact, mixed, qkv, first, wq, tables, rows_attn, misc, gain, collective
):
    rows, width = first.shape[1:]
    seqlen = PLANES * rows
    size = WINDOW * HEAD_DIM
    plane_rows = width // PLANES
    block = (plane_rows // 4, width // 2)
    any_spec = pl.BlockSpec(memory_space=pl.ANY)
    vmem_spec = pl.BlockSpec(memory_space=pltpu.VMEM)
    return pl.pallas_call(
        finish_kernel,
        out_shape=[
            jax.ShapeDtypeStruct((rows, width), F32),
            jax.ShapeDtypeStruct((4, PLANES) + grads.shape[1:], BF16),
            jax.ShapeDtypeStruct(first.shape, BF16),
            jax.ShapeDtypeStruct((PLANES, plane_rows, width), BF16),
            jax.ShapeDtypeStruct((plane_rows, width), BF16),
        ],
        in_specs=[any_spec] * 9 + [vmem_spec] * 6,
        out_specs=[vmem_spec] + [any_spec] * 4,
        scratch_shapes=[
            pltpu.VMEM((4, 2, rows, width), BF16),
            pltpu.VMEM((4, 2, rows, width), BF16),
            pltpu.VMEM((4, rows, width), BF16),
            pltpu.VMEM((3, rows, width), BF16),
            pltpu.VMEM((4,) + grads.shape[2:], BF16),
            pltpu.VMEM((4,) + grads.shape[2:], BF16),
            pltpu.VMEM(heads.shape, BF16),
            pltpu.VMEM(exact.shape, F32),
            pltpu.VMEM(mixed.shape, F32),
            pltpu.VMEM(qkv.shape, BF16),
            pltpu.VMEM(first.shape, BF16),
            pltpu.VMEM(wq.shape, BF16),
            pltpu.VMEM((seqlen, 3 * size), BF16),
            pltpu.VMEM(first.shape, BF16),
            pltpu.VMEM((2, 2, PLANES, plane_rows, width // 2), BF16),
            pltpu.VMEM((2, 4, plane_rows, width // 2), BF16),
            pltpu.VMEM((2, 4, 2) + block, BF16),
            pltpu.VMEM((2, 4) + block, BF16),
            pltpu.VMEM((3,) + block, BF16),
            pltpu.VMEM(block, BF16),
            pltpu.SemaphoreType.DMA((7, 4)),
            pltpu.SemaphoreType.DMA((39, 4)),
            pltpu.SemaphoreType.DMA((39, 4)),
        ],
        compiler_params=pltpu.CompilerParams(
            collective_id=collective, has_side_effects=True, vmem_limit_bytes=62 * 2**20
        ),
        name="finish",
    )(outs, outs_one, grads, heads, exact, mixed, qkv, first, wq, *tables, *rows_attn, misc, gain)


def widen_kernel(table, up_o, down_o):
    columns = table.shape[2]
    split = up_o.shape[2]
    for low in range(0, columns, 128):
        part = jnp.swapaxes(table[:, :, low : low + 128].astype(F32), 0, 1)
        if low < split:
            up_o[:, :, low : low + 128] = part
        else:
            down_o[:, :, low - split : low - split + 128] = part


def widen(table):
    experts, rows, columns = table.shape
    split = columns // 3 * 2
    step = rows // 4
    return pl.pallas_call(
        widen_kernel,
        grid=(rows // step,),
        out_shape=[
            jax.ShapeDtypeStruct((rows, experts, split), F32),
            jax.ShapeDtypeStruct((rows, experts, columns - split), F32),
        ],
        in_specs=[pl.BlockSpec((experts, step, columns), lambda i: (0, i, 0))],
        out_specs=[
            pl.BlockSpec((step, experts, split), lambda i: (i, 0, 0)),
            pl.BlockSpec((step, experts, columns - split), lambda i: (i, 0, 0)),
        ],
        compiler_params=pltpu.CompilerParams(vmem_limit_bytes=60 * 2**20),
        name="widen",
    )(table)


def windows(x):
    size = WINDOW * HEAD_DIM
    return jnp.stack([x[:, s * HEAD_DIM : s * HEAD_DIM + size] for s in STARTS])


def from_windows(x):
    return jnp.concatenate(
        [x[p, :, a * HEAD_DIM : b * HEAD_DIM] for p, (a, b) in enumerate(KEEP)], axis=1
    )


def dot(a, b, dims, out=F32):
    return lax.dot_general(a, b, ((dims[0], dims[1]), ((), ())), preferred_element_type=F32).astype(out)


def expert_local(
    tokens, seq_ids, routes, cotangent, gain_attn, w_qkv, w_out, gain_ffn, w_router, w_up, w_down
):
    rows, width = tokens.shape
    own = w_out.shape[0]
    experts = w_router.shape[1]
    seqlen = PLANES * rows
    size = WINDOW * HEAD_DIM

    misc = jnp.concatenate(
        [
            jnp.zeros((own, 1), BF16),
            w_router,
            gain_attn[:, None],
            gain_ffn[:, None],
            jnp.zeros((own, 128 - experts - 3), BF16),
        ],
        axis=1,
    )
    wq_send = jnp.concatenate(
        [windows(w_qkv[:, i * width : (i + 1) * width]) for i in range(3)]
        + [jnp.broadcast_to(misc[None], (PLANES, own, 128))],
        axis=2,
    )
    we_send = jnp.concatenate([w_up, w_down], axis=2).reshape(own, 4, PLANES, 3 * FF)
    we_send = jnp.transpose(we_send, (2, 1, 0, 3))
    choose = routes[:, :, None] == jnp.arange(experts, dtype=jnp.int32)[None, None, :]
    member = jnp.any(choose, axis=1)
    member_cols = jnp.concatenate(
        [jnp.ones((rows, 1), BF16), member.astype(BF16), jnp.zeros((rows, 127 - experts), BF16)],
        axis=1,
    )
    cot_send = jnp.concatenate([cotangent, member_cols], axis=1)
    ids_f = seq_ids.astype(BF16)
    ids_send = jnp.concatenate(
        [
            jnp.broadcast_to(ids_f[None, :], (rows, rows)),
            jnp.broadcast_to(ids_f[:, None], (rows, rows)),
        ]
    )
    half_dim = HEAD_DIM // 2
    cosine, sine_table = rotary(jnp.arange(seqlen, dtype=F32), HEAD_DIM)
    sine_signed = sine_table[:, 0, :] * jnp.where(jnp.arange(HEAD_DIM) < half_dim, -1.0, 1.0)
    we_all, cot_all, wq_all, out_weight, first_in, qkv, weights_exact, mixed_exact, mixed, middle, second_in = start(
        tokens, ids_send, wq_send, w_out, we_send, cot_send, cosine[:, 0, :], sine_signed, 1
    )
    misc_all = wq_all[:, 3 * size :]
    router = misc_all[:, 1 : experts + 1]
    gain_one = misc_all[:, experts + 1].astype(F32)
    gain_two = misc_all[:, experts + 2].astype(F32)
    inverse_two = rms_inverse(middle)
    normed_two = middle * inverse_two

    weights = we_all.reshape(width, 3 * FF)
    grads, outs, outs_one, sums = run_experts(second_in, cot_all, weights, wq_all, 3)

    hi = sums[:, width + 1 : width + 1 + experts]
    lo = sums[:, width + 33 : width + 33 + experts]
    grad_probs = hi + lo
    probs = jax.nn.softmax(dot(second_in, router, ((1,), (0,))), axis=-1)
    grad_logits = (
        probs * (grad_probs - jnp.sum(probs * grad_probs, axis=1, keepdims=True))
    ).astype(BF16)
    grad_second = sums[:, :width] + dot(grad_logits, router, ((1,), (1,)))
    grad_output = cotangent.astype(F32)
    grad_normed_two = grad_second * gain_two
    gain_two_part = jnp.sum(grad_second * normed_two, axis=0)
    grad_middle = grad_output + inverse_two * (
        grad_normed_two
        - normed_two * jnp.mean(grad_normed_two * normed_two, axis=-1, keepdims=True)
    )
    router_part = dot(second_in, grad_logits, ((0,), (0,)))
    grad_attention = grad_middle.astype(BF16)
    grad_mixed = dot(grad_attention, out_weight, ((1,), (1,)), BF16)
    misc_part = jnp.concatenate(
        [
            router_part,
            jnp.zeros((width, 1), F32),
            gain_two_part[:, None],
            jnp.zeros((width, 128 - experts - 2), F32),
        ],
        axis=1,
    )
    sums, table, first_all, q_all, o_all = finish(
        outs,
        outs_one,
        grads.reshape(PLANES, 2, width // PLANES // 2, 3 * FF),
        windows(grad_mixed),
        weights_exact,
        mixed_exact,
        qkv,
        first_in,
        wq_all,
        (cosine[:, 0, :], sine_signed),
        (mixed, grad_attention),
        misc_part,
        jnp.broadcast_to(gain_one[None, :], (8, width)),
        6,
    )
    output = (middle + sums).astype(BF16)
    grad_first = jnp.sum(first_all.astype(F32), axis=0)
    inputs = tokens.astype(F32)
    inverse_one = rms_inverse(inputs)
    normed_one = inputs * inverse_one
    grad_normed_one = grad_first * gain_one
    grad_tokens = grad_middle + inverse_one * (
        grad_normed_one
        - normed_one * jnp.mean(grad_normed_one * normed_one, axis=-1, keepdims=True)
    )
    out_sum = o_all.astype(F32)
    qkv_sum = jnp.concatenate(
        [from_windows(q_all[:, :, i * size : (i + 1) * size]) for i in range(3)], axis=1
    ).astype(F32)
    misc_sum = jnp.sum(q_all[:, :, 3 * size :].astype(F32), axis=0)

    up_sum, down_sum = widen(table.reshape(experts + 1, width // PLANES, 3 * FF))
    return (
        output,
        grad_tokens.astype(BF16),
        misc_sum[:, experts],
        qkv_sum,
        out_sum,
        misc_sum[:, experts + 1],
        misc_sum[:, :experts],
        up_sum,
        down_sum,
    )


def solution(mesh):
    fits = mesh.shape["wide"] == 8 and mesh.shape["narrow"] == PLANES
    return jax.shard_map(
        expert_local if fits else local,
        mesh=mesh,
        in_specs=(
            P(("wide", "narrow"), None),
            P(("wide", "narrow")),
            P(("wide", "narrow"), None),
            P(("wide", "narrow"), None),
            P(("wide", "narrow")),
            P(("wide", "narrow"), None),
            P(("wide", "narrow"), None),
            P(("wide", "narrow")),
            P(("wide", "narrow"), None),
            P(("wide", "narrow"), None, None),
            P(("wide", "narrow"), None, None),
        ),
        out_specs=(
            P(("wide", "narrow"), None),
            P(("wide", "narrow"), None),
            P("narrow"),
            P("narrow", None),
            P("narrow", None),
            P("narrow"),
            P("narrow", None),
            P("narrow", None, None),
            P("narrow", None, None),
        ),
        check_vma=False,
    )
```

```python
import jax
import jax.numpy as jnp
from jax import lax
from jax.experimental import pallas as pl
from jax.experimental.pallas import tpu as pltpu
from jax.sharding import PartitionSpec as P

HEADS = 10
HEAD_DIM = 128
FF = 896
CAP = 72


epsilon = 1e-06


def shortened(x):
    return jax.tree.map(lambda a: a.astype(jnp.bfloat16) if a.dtype == jnp.float32 else a, x)


def rms_inverse(values):
    return lax.rsqrt(jnp.mean(values * values, axis=-1, keepdims=True) + epsilon)


def rotary(positions, head_size):
    half_dim = head_size // 2
    frequency = 10000.0 ** (-jnp.arange(half_dim, dtype=jnp.float32) / half_dim)
    angles = positions[:, None] * frequency[None, :]
    cosine = jnp.concatenate([jnp.cos(angles), jnp.cos(angles)], axis=1)[:, None, :]
    sine_table = jnp.concatenate([jnp.sin(angles), jnp.sin(angles)], axis=1)[:, None, :]
    return (cosine, sine_table)


def rotate(values, cosine, sine_table):
    half_dim = values.shape[-1] // 2
    turned = jnp.concatenate([-values[..., half_dim:], values[..., :half_dim]], axis=-1)
    return values * cosine + turned * sine_table


def rotate_back(grads, cosine, sine_table):
    half_dim = grads.shape[-1] // 2
    scaled = grads * sine_table
    turned = jnp.concatenate([scaled[..., half_dim:], -scaled[..., :half_dim]], axis=-1)
    return grads * cosine + turned


def expert_weight_terms(
    routed_in, routed_grad, shared_in, shared_grad, slot_grads, slot_acts, shared_grads, shared_acts
):
    up_routed = jnp.einsum(
        "ecd,ecf->def", routed_in, slot_grads, preferred_element_type=jnp.float32
    )
    up_shared = jnp.einsum("td,tf->df", shared_in, shared_grads, preferred_element_type=jnp.float32)
    down_routed = jnp.einsum(
        "ecd,ecf->def", routed_grad, slot_acts, preferred_element_type=jnp.float32
    )
    down_shared = jnp.einsum(
        "td,tf->df", shared_grad, shared_acts, preferred_element_type=jnp.float32
    )
    up_all = jnp.concatenate([up_shared[:, None], up_routed], axis=1)
    down_all = jnp.concatenate([down_shared[:, None], down_routed], axis=1)
    combined = jnp.concatenate([up_all, down_all], axis=2)
    return combined.reshape(combined.shape[0], -1)


def local(
    tokens, seq_ids, routes, cotangent, gain_attn, w_qkv, w_out, gain_ffn, w_router, w_up, w_down
):
    row_count = tokens.shape[0]
    model_width = tokens.shape[1]
    query_scale = HEAD_DIM ** (-0.5)
    hidden = FF
    capacity = CAP
    inputs = tokens.astype(jnp.float32)
    gain_one, qkv_weight, out_weight = (
        lax.all_gather(gain_attn, ("wide", "narrow"), axis=0, tiled=True),
        lax.all_gather(w_qkv, ("wide", "narrow"), axis=0, tiled=True),
        lax.all_gather(w_out, ("wide", "narrow"), axis=0, tiled=True),
    )
    inverse_one = rms_inverse(inputs)
    normed_one = inputs * inverse_one
    first_in = (normed_one * gain_one.astype(jnp.float32)).astype(jnp.bfloat16)
    projected = jnp.dot(first_in, qkv_weight, preferred_element_type=jnp.float32)
    offset = lax.axis_index("narrow") * row_count
    query_pos = offset + jnp.arange(row_count, dtype=jnp.int32)
    cosine, sine_table = rotary(query_pos.astype(jnp.float32), HEAD_DIM)
    query_rows = (
        rotate(projected[:, :model_width].reshape(row_count, HEADS, HEAD_DIM), cosine, sine_table)
        * query_scale
    ).astype(jnp.bfloat16)
    key_rows = (
        rotate(
            projected[:, model_width : 2 * model_width].reshape(row_count, HEADS, HEAD_DIM),
            cosine,
            sine_table,
        )
        .astype(jnp.bfloat16)
        .reshape(row_count, model_width)
    )
    value_rows = projected[:, 2 * model_width :].astype(jnp.bfloat16)
    all_keys, all_values, all_ids = (
        lax.all_gather(key_rows, "narrow", axis=0, tiled=True),
        lax.all_gather(value_rows, "narrow", axis=0, tiled=True),
        lax.all_gather(seq_ids.astype(jnp.bfloat16), "narrow", axis=0, tiled=True),
    )
    seqlen = all_keys.shape[0]
    block_len = min(512, seqlen)
    num_blocks = seqlen // block_len
    own_ids = seq_ids.astype(jnp.float32)

    def block_parts(block_index):
        first_row = block_index * block_len
        key_pos = first_row + jnp.arange(block_len, dtype=jnp.int32)
        key_ids = lax.dynamic_slice_in_dim(all_ids, first_row, block_len, 0).astype(jnp.float32)
        allowed = (key_pos[None, :] <= query_pos[:, None]) & (key_ids[None, :] == own_ids[:, None])
        key_block = lax.dynamic_slice_in_dim(all_keys, first_row, block_len, 0).reshape(
            block_len, HEADS, HEAD_DIM
        )
        value_block = lax.dynamic_slice_in_dim(all_values, first_row, block_len, 0).reshape(
            block_len, HEADS, HEAD_DIM
        )
        scores = jnp.einsum(
            "qhd,khd->hqk", query_rows, key_block, preferred_element_type=jnp.float32
        )
        return (allowed[None], key_block, value_block, scores)

    def max_step(state_pair, block_index):
        running_max, running_sum = state_pair
        allowed, key_block, value_block, scores = block_parts(block_index)
        masked = jnp.where(allowed, scores, -1e30)
        new_max = jnp.maximum(running_max, jnp.max(masked, axis=2))
        added = jnp.sum(jnp.where(allowed, jnp.exp(masked - new_max[..., None]), 0.0), axis=2)
        return ((new_max, running_sum * jnp.exp(running_max - new_max) + added), None)

    start_max = jnp.full((HEADS, row_count), -1e30, jnp.float32)
    start_sum = jnp.zeros((HEADS, row_count), jnp.float32)
    (top_score, exp_total), unused = lax.scan(
        max_step, (start_max, start_sum), jnp.arange(num_blocks)
    )
    log_total = top_score + jnp.log(exp_total)

    def out_step(accum, block_index):
        allowed, key_block, value_block, scores = block_parts(block_index)
        weights_low = jnp.where(allowed, jnp.exp(scores - log_total[..., None]), 0.0).astype(
            jnp.bfloat16
        )
        return (
            accum
            + jnp.einsum(
                "hqk,khd->hqd", weights_low, value_block, preferred_element_type=jnp.float32
            ),
            None,
        )

    accum_start = jnp.zeros((HEADS, row_count, HEAD_DIM), jnp.float32)
    mixed_heads, unused = lax.scan(out_step, accum_start, jnp.arange(num_blocks))
    mixed_exact = jnp.transpose(mixed_heads, (1, 0, 2))
    mixed = mixed_exact.reshape(row_count, model_width).astype(jnp.bfloat16)
    middle = inputs + jnp.dot(mixed, out_weight, preferred_element_type=jnp.float32)
    gain_two, router_weight, up_weight, down_weight = (
        lax.all_gather(gain_ffn, ("wide", "narrow"), axis=0, tiled=True),
        lax.all_gather(w_router, ("wide", "narrow"), axis=0, tiled=True),
        lax.all_gather(w_up, ("wide", "narrow"), axis=0, tiled=True),
        lax.all_gather(w_down, ("wide", "narrow"), axis=0, tiled=True),
    )
    inverse_two = rms_inverse(middle)
    normed_two = middle * inverse_two
    second_in = (normed_two * gain_two.astype(jnp.float32)).astype(jnp.bfloat16)
    logits = jnp.dot(second_in, router_weight, preferred_element_type=jnp.float32)
    router_probs = jax.nn.softmax(logits, axis=-1)
    experts = logits.shape[1]
    choose = routes[:, :, None] == jnp.arange(experts, dtype=jnp.int32)[None, None, :]
    member = jnp.sum(choose.astype(jnp.float32), axis=1)
    earlier = (jnp.arange(row_count)[:, None] > jnp.arange(row_count)[None, :]).astype(jnp.bfloat16)
    before = jnp.dot(earlier, member.astype(jnp.bfloat16), preferred_element_type=jnp.float32)
    slot_hit = (member.T[:, None, :] > 0.5) & (
        before.T[:, None, :] == jnp.arange(capacity, dtype=jnp.float32)[None, :, None]
    )
    dispatch = slot_hit.astype(jnp.bfloat16)
    gathered_in = jnp.einsum(
        "ect,td->ecd", dispatch, second_in, preferred_element_type=jnp.float32
    ).astype(jnp.bfloat16)
    gate_weights = router_probs * member
    gate_up = jnp.einsum(
        "ecd,def->ecf", gathered_in, up_weight[:, 1:], preferred_element_type=jnp.float32
    )
    gate_part = gate_up[..., :hidden]
    up_part = gate_up[..., hidden:]
    activated = (jax.nn.silu(gate_part) * up_part).astype(jnp.bfloat16)
    expert_rows = jnp.einsum(
        "ecf,def->ecd", activated, down_weight[:, 1:], preferred_element_type=jnp.float32
    ).astype(jnp.bfloat16)
    selected = jnp.einsum("ect,ecd->etd", dispatch, expert_rows, preferred_element_type=jnp.float32)
    routed = jnp.sum(gate_weights.T[:, :, None] * selected, axis=0)
    shared_up = jnp.dot(second_in, up_weight[:, 0], preferred_element_type=jnp.float32)
    shared_gate = shared_up[:, :hidden]
    shared_lin = shared_up[:, hidden:]
    shared_act = (jax.nn.silu(shared_gate) * shared_lin).astype(jnp.bfloat16)
    shared_out = jnp.einsum(
        "tf,df->td", shared_act, down_weight[:, 0], preferred_element_type=jnp.float32
    )
    output = (middle + shared_out + routed).astype(jnp.bfloat16)
    gain_two, router_weight, up_weight, down_weight = (
        lax.all_gather(gain_ffn, ("wide", "narrow"), axis=0, tiled=True),
        lax.all_gather(w_router, ("wide", "narrow"), axis=0, tiled=True),
        lax.all_gather(w_up, ("wide", "narrow"), axis=0, tiled=True),
        lax.all_gather(w_down, ("wide", "narrow"), axis=0, tiled=True),
    )
    grad_output = cotangent.astype(jnp.float32)
    slot_token = jnp.sum(
        jnp.where(slot_hit, jnp.arange(row_count, dtype=jnp.int32)[None, None, :], 0), axis=2
    )
    slot_gate = jnp.sum(jnp.where(slot_hit, gate_weights.T[:, None, :], 0.0), axis=2)
    grad_rows = (slot_gate[..., None] * grad_output[slot_token]).astype(jnp.bfloat16)
    grad_probs = jnp.sum(selected * grad_output[None], axis=2).T * member
    grad_logits = (
        router_probs * (grad_probs - jnp.sum(router_probs * grad_probs, axis=1, keepdims=True))
    ).astype(jnp.bfloat16)
    grad_act = jnp.einsum(
        "ecd,def->ecf", grad_rows, down_weight[:, 1:], preferred_element_type=jnp.float32
    )
    sigmoid_gate = jax.nn.sigmoid(gate_part)
    grad_gate_up = jnp.concatenate(
        [
            grad_act * up_part * sigmoid_gate * (1.0 + gate_part * (1.0 - sigmoid_gate)),
            grad_act * jax.nn.silu(gate_part),
        ],
        axis=-1,
    ).astype(jnp.bfloat16)
    grad_gathered = jnp.einsum(
        "ecf,def->ecd", grad_gate_up, up_weight[:, 1:], preferred_element_type=jnp.float32
    )
    slot_index = jnp.sum(jnp.where(choose, before[:, None, :], 0.0), axis=2).astype(jnp.int32)
    flat_index = routes * capacity + slot_index
    grad_second = jnp.sum(grad_gathered.reshape(-1, model_width)[flat_index], axis=1)
    grad_shared_act = jnp.einsum(
        "td,df->tf", cotangent, down_weight[:, 0], preferred_element_type=jnp.float32
    )
    sigmoid_shared = jax.nn.sigmoid(shared_gate)
    grad_shared_up = jnp.concatenate(
        [
            grad_shared_act
            * shared_lin
            * sigmoid_shared
            * (1.0 + shared_gate * (1.0 - sigmoid_shared)),
            grad_shared_act * jax.nn.silu(shared_gate),
        ],
        axis=-1,
    ).astype(jnp.bfloat16)
    grad_second = grad_second + jnp.einsum(
        "tf,df->td", grad_shared_up, up_weight[:, 0], preferred_element_type=jnp.float32
    )
    grad_second = grad_second + jnp.einsum(
        "te,de->td", grad_logits, router_weight, preferred_element_type=jnp.float32
    )
    grad_normed_two = grad_second * gain_two.astype(jnp.float32)
    grad_gain_two = jnp.sum(grad_second * normed_two, axis=0)
    grad_middle = grad_output + inverse_two * (
        grad_normed_two
        - normed_two * jnp.mean(grad_normed_two * normed_two, axis=-1, keepdims=True)
    )
    grad_router = jnp.einsum(
        "td,te->de", second_in, grad_logits, preferred_element_type=jnp.float32
    )
    narrow_rows = model_width // lax.axis_size("narrow")
    routed_cols, grad_cols, shared_cols, cotangent_cols = (
        lax.all_to_all(gathered_in, "narrow", split_axis=2, concat_axis=1, tiled=True),
        lax.all_to_all(grad_rows, "narrow", split_axis=2, concat_axis=1, tiled=True),
        lax.all_to_all(second_in[None], "narrow", split_axis=2, concat_axis=1, tiled=True),
        lax.all_to_all(cotangent[None], "narrow", split_axis=2, concat_axis=1, tiled=True),
    )
    slot_grads, slot_acts, shared_grads, shared_acts = (
        lax.all_gather(grad_gate_up, "narrow", axis=1, tiled=True),
        lax.all_gather(activated, "narrow", axis=1, tiled=True),
        lax.all_gather(grad_shared_up[None], "narrow", axis=1, tiled=True),
        lax.all_gather(shared_act[None], "narrow", axis=1, tiled=True),
    )
    expert_grads = expert_weight_terms(
        routed_cols,
        grad_cols,
        shared_cols[0],
        cotangent_cols[0],
        slot_grads,
        slot_acts,
        shared_grads[0],
        shared_acts[0],
    )
    gain_one, qkv_weight, out_weight = (
        lax.all_gather(gain_attn, ("wide", "narrow"), axis=0, tiled=True),
        lax.all_gather(w_qkv, ("wide", "narrow"), axis=0, tiled=True),
        lax.all_gather(w_out, ("wide", "narrow"), axis=0, tiled=True),
    )
    grad_attention = grad_middle.astype(jnp.bfloat16)
    grad_out_weight = jnp.einsum(
        "td,te->de", mixed, grad_attention, preferred_element_type=jnp.float32
    )
    grad_mixed = jnp.einsum(
        "te,de->td", grad_attention, out_weight, preferred_element_type=jnp.float32
    ).astype(jnp.bfloat16)
    grad_heads = grad_mixed.reshape(row_count, HEADS, HEAD_DIM)
    row_delta = jnp.sum(grad_heads.astype(jnp.float32) * mixed_exact, axis=2).T

    def back_step(grad_query, block_index):
        allowed, key_block, value_block, scores = block_parts(block_index)
        weights_exact = jnp.where(allowed, jnp.exp(scores - log_total[..., None]), 0.0)
        weights_low = weights_exact.astype(jnp.bfloat16)
        grad_value = jnp.einsum(
            "hqk,qhd->khd", weights_low, grad_heads, preferred_element_type=jnp.float32
        )
        grad_weights = jnp.einsum(
            "qhd,khd->hqk", grad_heads, value_block, preferred_element_type=jnp.float32
        )
        grad_scores = (weights_exact * (grad_weights - row_delta[..., None])).astype(jnp.bfloat16)
        grad_query = grad_query + jnp.einsum(
            "hqk,khd->qhd", grad_scores, key_block, preferred_element_type=jnp.float32
        )
        grad_key = jnp.einsum(
            "hqk,qhd->khd", grad_scores, query_rows, preferred_element_type=jnp.float32
        )
        return (
            grad_query,
            (grad_key.reshape(block_len, model_width), grad_value.reshape(block_len, model_width)),
        )

    query_start = jnp.zeros((row_count, HEADS, HEAD_DIM), jnp.float32)
    grad_query, (key_blocks, value_blocks) = lax.scan(
        back_step, query_start, jnp.arange(num_blocks)
    )
    key_partial = key_blocks.reshape(seqlen, model_width)
    value_partial = value_blocks.reshape(seqlen, model_width)
    grad_keys, grad_values = (
        lax.psum_scatter(
            key_partial.astype(jnp.bfloat16), "narrow", scatter_dimension=0, tiled=True
        ).astype(jnp.float32),
        lax.psum_scatter(
            value_partial.astype(jnp.bfloat16), "narrow", scatter_dimension=0, tiled=True
        ).astype(jnp.float32),
    )
    grad_query_raw = rotate_back(grad_query, cosine, sine_table) * query_scale
    grad_key_raw = rotate_back(grad_keys.reshape(row_count, HEADS, HEAD_DIM), cosine, sine_table)
    grad_projected = jnp.concatenate(
        [
            grad_query_raw.reshape(row_count, model_width),
            grad_key_raw.reshape(row_count, model_width),
            grad_values,
        ],
        axis=1,
    ).astype(jnp.bfloat16)
    grad_qkv_weight = jnp.einsum(
        "td,tf->df", first_in, grad_projected, preferred_element_type=jnp.float32
    )
    grad_first = jnp.einsum(
        "tf,df->td", grad_projected, qkv_weight, preferred_element_type=jnp.float32
    )
    grad_normed_one = grad_first * gain_one.astype(jnp.float32)
    grad_gain_one = jnp.sum(grad_first * normed_one, axis=0)
    grad_inputs = grad_middle + inverse_one * (
        grad_normed_one
        - normed_one * jnp.mean(grad_normed_one * normed_one, axis=-1, keepdims=True)
    )
    dense_parts = (
        lax.psum_scatter(
            grad_gain_one.astype(jnp.bfloat16), "narrow", scatter_dimension=0, tiled=True
        ).astype(jnp.float32),
        lax.psum_scatter(
            grad_qkv_weight.astype(jnp.bfloat16), "narrow", scatter_dimension=0, tiled=True
        ).astype(jnp.float32),
        lax.psum_scatter(
            grad_out_weight.astype(jnp.bfloat16), "narrow", scatter_dimension=0, tiled=True
        ).astype(jnp.float32),
        lax.psum_scatter(
            grad_gain_two.astype(jnp.bfloat16), "narrow", scatter_dimension=0, tiled=True
        ).astype(jnp.float32),
        lax.psum_scatter(
            grad_router.astype(jnp.bfloat16), "narrow", scatter_dimension=0, tiled=True
        ).astype(jnp.float32),
    )
    summed = jax.tree.map(
        lambda part: part.astype(jnp.float32),
        lax.psum(shortened((expert_grads,) + tuple(dense_parts)), "wide"),
    )
    expert_grads = summed[0]
    dense_parts = summed[1:]
    gain_one_sum, qkv_sum, out_sum, gain_two_sum, router_sum = dense_parts
    expert_table = expert_grads.reshape(narrow_rows, up_weight.shape[1], 3 * hidden)
    up_sum = expert_table[:, :, : 2 * hidden]
    down_sum = expert_table[:, :, 2 * hidden :]
    return (
        output,
        grad_inputs.astype(jnp.bfloat16),
        gain_one_sum,
        qkv_sum,
        out_sum,
        gain_two_sum,
        router_sum,
        up_sum,
        down_sum,
    )


PLANES = 4
WINDOW = 3
STARTS = (0, 3, 6, 7)
KEEP = ((0, 3), (0, 3), (0, 2), (1, 3))
MESH_IDS = pl.DeviceIdType.MESH
BF16 = jnp.bfloat16
F32 = jnp.float32


def place():
    w = lax.axis_index("wide")
    z = lax.axis_index("narrow")
    return w, z


def greet(w, z):
    barrier = pltpu.get_barrier_semaphore()
    peers = [(w, lax.rem(z + step, PLANES)) for step in (1, 2, 3)]
    peers += [(w ^ flip, z) for flip in (1, 2, 4, 6)]
    for peer in peers:
        pl.semaphore_signal(barrier, inc=1, device_id=peer, device_id_type=MESH_IDS)
    pl.semaphore_wait(barrier, len(peers))


def mul(a, b, over_a, over_b):
    return lax.dot_general(a, b, (((over_a,), (over_b,)), ((), ())), preferred_element_type=F32)


def at(start, size):
    return pl.ds(pl.multiple_of(start, 128), size)


def loop(first, last, body):
    def step(i, carry):
        body(i)
        return carry

    lax.fori_loop(first, last, step, 0)


class Links:
    def __init__(self, send_sems, recv_sems):
        self.w, self.z = place()
        self.send_sems, self.recv_sems = send_sems, recv_sems

    def copy(self, kind, step, src, dst, device):
        return pltpu.make_async_remote_copy(
            src_ref=src,
            dst_ref=dst,
            send_sem=self.send_sems.at[kind, step],
            recv_sem=self.recv_sems.at[kind, step],
            device_id=device,
            device_id_type=MESH_IDS,
        )

    def plane(self, step, sign):
        return lax.rem(self.z + PLANES + sign * step, PLANES)


def step_at(z, turn):
    step = 0
    for plane, steps in enumerate(((3, 2, 1, 0), (1, 3, 2, 0), (3, 1, 2, 0), (1, 2, 3, 0))):
        for number, value in enumerate(steps):
            step = jnp.where((z == plane) & (turn == number), value, step)
    return step


def direct_at(z, turn):
    even = lax.rem(z, 2) == 0
    first, second = jnp.where(even, 3, 1), jnp.where(even, 1, 3)
    return jnp.where(turn == 0, first, jnp.where(turn == 1, second, jnp.where(turn == 2, 2, 0)))


def send_next(z, send):
    @pl.when(z < PLANES - 1)
    def _():
        send(1)

    @pl.when(z > 0)
    def _():
        send(3)


def send_beyond(z, send):
    @pl.when(z == 0)
    def _():
        send(3)

    @pl.when(z == PLANES - 1)
    def _():
        send(1)

    send(2)


class Chain:
    def __init__(self, links, base, own, slot):
        self.links, self.base, self.own, self.slot = links, base, own, slot

    def goes(self, step, up):
        z = self.links.z
        if up:
            return (z >= step) & (z < PLANES - 1)
        return ((z < step) | (step == 0)) & (z > 0)

    def ring(self, step, up, own=False):
        links = self.links
        to = lax.rem(step + 1, 4) if up else lax.rem(step + 3, 4)
        ref = self.slot(links.plane(step, -1))
        return pltpu.make_async_remote_copy(
            src_ref=self.own if own else ref,
            dst_ref=ref,
            send_sem=links.send_sems.at[self.base if up else self.base + 1, step],
            recv_sem=links.recv_sems.at[self.base, to],
            device_id=(links.w, links.z + 1 if up else links.z - 1),
            device_id_type=MESH_IDS,
        )

    def hand_on(self, step, own=False):
        for up in (True, False):

            @pl.when(self.goes(step, up))
            def _():
                self.ring(step, up, own).start()

    def begin(self):
        self.hand_on(0, True)

    def arrive(self, turn):
        step = step_at(self.links.z, turn)
        ref = self.slot(self.links.plane(step, -1))
        self.links.copy(self.base, step, ref, ref, (self.links.w, self.links.z)).wait_recv()
        self.hand_on(step)

    def settle(self):
        def body(step):
            for up in (True, False):

                @pl.when(self.goes(step, up))
                def _():
                    self.ring(step, up).wait_send()

        loop(0, 4, body)


class Gather:
    def __init__(self, links, base, step, turn, slot, cores=True, half=0):
        self.links, self.base, self.step, self.slot, self.cores = links, base, step, slot, cores
        self.half = half
        self.first = 1 + lax.rem(turn, 2)
        self.second = 3 - self.first

    def copy(self, kind, owner, flip):
        ref = self.slot(owner)
        return self.links.copy(
            self.base + kind, self.step, ref, ref, (self.links.w ^ flip, self.links.z)
        )

    def begin(self):
        w = self.links.w
        self.copy(0, w, 2).start()
        self.copy(1, w, 4).start()
        if self.cores:
            self.copy(4, w, 1).start()

    def relay(self):
        w = self.links.w
        self.copy(0, w, 2).wait_recv()
        self.copy(1, w, 4).wait_recv()
        for copy in self.across():
            copy.start()
        if self.cores:
            self.copy(3, w ^ 2, 1).start()
            self.copy(5, w ^ 4, 1).start()

    def across(self):
        if not self.half:
            return [self.copy(2, self.links.w ^ (2 * self.first), 2 * self.second)]
        copies = []
        for kind, flip in ((2, 2), (7, 4)):
            ref = self.slot(self.links.w ^ flip).at[pl.ds((kind == 7) * self.half, self.half)]
            copies.append(
                self.links.copy(
                    self.base + kind, self.step, ref, ref, (self.links.w ^ (6 - flip), self.links.z)
                )
            )
        return copies

    def end(self):
        for copy in self.across():
            copy.wait_recv()
        if self.cores:
            self.copy(6, self.links.w ^ 6, 1).start()

    def settle(self):
        w = self.links.w
        self.copy(0, w, 2).wait_send()
        self.copy(1, w, 4).wait_send()
        for copy in self.across():
            copy.wait_send()
        if self.cores:
            for kind, owner in ((4, w), (3, w ^ 2), (5, w ^ 4), (6, w ^ 6)):
                copy = self.copy(kind, owner, 1)
                copy.wait_send()
                copy.wait_recv()


def softmax_rows(scores, mask):
    masked = scores + mask
    powers = jnp.exp(masked - jnp.max(masked, axis=1, keepdims=True))
    return powers * (1.0 / jnp.sum(powers, axis=1, keepdims=True))


def start_kernel(
    tok_in, ids_in, wq_in, wo_in, we_in, cot_in, cos_in, sin_in,
    we_o, cot_o, wq_o, wo_o, first_o, qkv_o, exact_o, mixed_o, mixed_rows_o, middle_o, second_o, hop,
    tok, ids, wq_blocks, wo_blocks, staged, mask, mixed_got, mixed_send,
    load_sems, send_sems, recv_sems,
):
    links = Links(send_sems, recv_sems)
    w, z = links.w, links.z
    chip = w // 2
    rows, width = tok_in.shape
    seqlen = PLANES * rows
    size = WINDOW * HEAD_DIM
    own = wo_in.shape[0]
    keeps = [
        pltpu.make_async_copy(src, dst, load_sems.at[i])
        for i, (src, dst) in enumerate(
            (
                (tok_in, tok.at[z]),
                (ids_in, ids.at[z]),
                (wq_in.at[z], wq_blocks.at[w, z]),
                (wo_in, wo_blocks.at[w, z]),
                (cot_in, cot_o.at[chip, z]),
            )
        )
    ]
    for keep in keeps:
        keep.start()
    greet(w, z)

    tok_chain = Chain(links, 0, tok_in, lambda p: tok.at[p])
    ids_chain = Chain(links, 2, ids_in, lambda p: ids.at[p])
    wo_chain = Chain(links, 4, wo_in, lambda p: wo_blocks.at[w, p])
    cot_chain = Chain(links, 6, cot_in, lambda p: cot_o.at[chip, p])

    def wq_ring(step):
        to = links.plane(step, 1)
        return links.copy(8, step, wq_in.at[to], wq_blocks.at[w, z], (w, to))

    def wq_gather(step):
        source = links.plane(step, -1)
        return Gather(links, 9, step, step, lambda i: wq_blocks.at[i, source])

    def wo_gather(turn):
        step = step_at(z, turn)
        source = links.plane(step, -1)
        return Gather(links, 16, step, turn, lambda i: wo_blocks.at[i, source])

    def cot_gather(turn):
        step = step_at(z, turn)
        source = links.plane(step, -1)
        return Gather(links, 23, step, turn, lambda i: cot_o.at[i // 2, source], False)

    def weights_ring(step, flip):
        to = links.plane(step, 1)
        return links.copy(
            26 + flip, step, we_in.at[to, chip ^ flip], hop.at[step - 1, chip ^ flip], (w, to)
        )

    def weights_step(turn):
        return 0 if turn == 3 else direct_at(z, turn)

    def weights_block(turn, flip):
        if turn == 3:
            return we_in.at[z, chip ^ flip]
        return hop.at[weights_step(turn) - 1, chip ^ flip]

    def weights_place(turn, owner):
        return we_o.at[owner, links.plane(weights_step(turn), -1)]

    def weights_plane(turn, flip):
        to = (w ^ (2 * flip), z)
        return links.copy(
            29 + flip, turn, weights_block(turn, flip), weights_place(turn, w), to
        )

    def weights_keep(turn):
        return pltpu.make_async_copy(
            weights_block(turn, 0), weights_place(turn, w), load_sems.at[6 + turn]
        )

    def weights_core(turn, flip):
        block = weights_place(turn, w ^ (2 * flip))
        return links.copy(
            34 + flip, turn, block if flip else weights_block(turn, 0), block, (w ^ 1, z)
        )

    def weights_send(step):
        for flip in (3, 1, 2, 0):
            weights_ring(step, flip).start()

    def weights_next(turn):
        for flip in (3, 1, 2):
            if turn < 3:
                weights_ring(weights_step(turn), flip).wait_recv()
            weights_plane(turn, flip).start()
        if turn < 3:
            weights_ring(weights_step(turn), 0).wait_recv()
        weights_core(turn, 0).start()
        weights_keep(turn).start()

    def weights_end(turn):
        for flip in (1, 2, 3):
            weights_plane(turn, flip).wait_recv()
            weights_core(turn, flip).start()

    def mixed_ring(step):
        to = links.plane(step, 1)
        return links.copy(38, step, mixed_send.at[to], mixed_got.at[z], (w, to))

    tok_chain.begin()
    ids_chain.begin()
    for step in (1, 2, 3):
        wq_ring(step).start()
    for keep in keeps:
        keep.wait()
    wq_gather(0).begin()
    tok_chain.arrive(0)
    ids_chain.arrive(0)
    for step in (1, 2, 3):
        wq_ring(step).wait_recv()
        wq_gather(step).begin()
    wo_chain.begin()
    tok_chain.arrive(1)
    ids_chain.arrive(1)
    cot_chain.begin()
    end_plane = (z == 0) | (z == PLANES - 1)

    @pl.when(jnp.logical_not(end_plane))
    def _():
        tok_chain.arrive(2)
        ids_chain.arrive(2)

    loop(0, 4, lambda step: wq_gather(step).relay())

    @pl.when(end_plane)
    def _():
        tok_chain.arrive(2)
        ids_chain.arrive(2)
        send_next(z, weights_send)

    wo_chain.arrive(0)
    wo_gather(0).begin()
    wo_gather(3).begin()
    cot_gather(3).begin()
    weights_next(3)
    for i in range(PLANES):
        for j in range(PLANES):
            here = (slice(i * rows, (i + 1) * rows), slice(j * rows, (j + 1) * rows))
            if j > i:
                mask[here] = jnp.full((rows, rows), -1e30, F32)
            else:
                same = ids[i, rows:, :].astype(F32) == ids[j, :rows, :].astype(F32)
                if i == j:
                    same = same & (
                        lax.broadcasted_iota(jnp.int32, (rows, rows), 1)
                        <= lax.broadcasted_iota(jnp.int32, (rows, rows), 0)
                    )
                mask[here] = jnp.where(same, 0.0, -1e30)
    loop(0, 4, lambda step: wq_gather(step).end())
    loop(0, 4, lambda step: wq_gather(step).settle())

    def assemble(blocks, to):
        def body(i):
            for p in range(PLANES):
                staged[p * own : (p + 1) * own, :] = blocks[i, p].astype(F32)
            span = PLANES * own
            to[pl.ds(pl.multiple_of(i * span, 16), span), :] = staged[...].astype(BF16)

        loop(0, blocks.shape[0], body)

    cot_chain.arrive(0)
    cot_gather(0).begin()
    assemble(wq_blocks, wq_o)
    gains = jnp.transpose(wq_o[:, size * 3 :].astype(F32))
    gain_one = gains[16:17, :]
    gain_two = gains[17:18, :]

    def normalise(p):
        block = tok[p].astype(F32)
        inverse = lax.rsqrt(jnp.mean(block * block, axis=1, keepdims=True) + epsilon)
        first_o[p] = (block * inverse * gain_one).astype(BF16)

    loop(0, PLANES, normalise)
    wo_chain.arrive(1)
    wo_gather(1).begin()
    cot_chain.arrive(1)
    cot_gather(1).begin()

    def project(p):
        span = pl.ds(pl.multiple_of(p * rows, 128), rows)
        cosine, sine = cos_in[span, :], sin_in[span, :]
        for kind in range(3):
            part = mul(first_o[p], wq_o[:, kind * size : (kind + 1) * size], 1, 0)
            for head in range(WINDOW):
                here = part[:, head * HEAD_DIM : (head + 1) * HEAD_DIM]
                if kind < 2:
                    here = here * cosine + pltpu.roll(here, HEAD_DIM // 2, 1) * sine
                if kind == 0:
                    here = here * (HEAD_DIM ** (-0.5))
                qkv_o[kind, head, span, :] = here.astype(BF16)

    loop(0, PLANES, project)
    wo_chain.arrive(2)
    wo_gather(2).begin()
    cot_chain.arrive(2)
    cot_gather(2).begin()

    @pl.when(jnp.logical_not(end_plane))
    def _():
        send_next(z, weights_send)

    def attend(head):
        exact = softmax_rows(mul(qkv_o[0, head], qkv_o[1, head], 1, 1), mask[...])
        exact_o[head] = exact
        mixed_o[head] = mul(exact.astype(BF16), qkv_o[2, head], 1, 0)

    loop(0, WINDOW, attend)
    for p in range(PLANES):
        for head in range(WINDOW):
            mixed_send[p, :, head * HEAD_DIM : (head + 1) * HEAD_DIM] = mixed_o[
                head, p * rows : (p + 1) * rows, :
            ].astype(BF16)
    for step in (1, 2, 3):
        mixed_ring(step).start()
    mixed_got[z] = mixed_send[z]
    send_beyond(z, weights_send)
    loop(0, 4, lambda turn: wo_gather(turn).relay())
    weights_next(0)
    loop(0, 4, lambda turn: wo_gather(turn).end())
    loop(0, 4, lambda turn: cot_gather(turn).relay())
    weights_end(3)
    weights_end(0)
    loop(0, 4, lambda turn: wo_gather(turn).settle())
    assemble(wo_blocks, wo_o)
    for step in (1, 2, 3):
        mixed_ring(step).wait_recv()
    column = 0
    for p, (a, b) in enumerate(KEEP):
        span = (b - a) * HEAD_DIM
        mixed_rows_o[:, column : column + span] = mixed_got[p, :, a * HEAD_DIM : b * HEAD_DIM]
        column += span

    def out_project(i):
        here = at(i * 256, 256)
        middle_o[:, here] = tok_in_f32(tok, z, here) + mul(mixed_rows_o[...], wo_o[:, here], 1, 0)

    loop(0, width // 256, out_project)
    middle = middle_o[...]
    inverse = lax.rsqrt(jnp.mean(middle * middle, axis=1, keepdims=True) + epsilon)
    second_o[...] = (middle * inverse * gain_two).astype(BF16)
    loop(0, 4, lambda turn: cot_gather(turn).end())
    weights_next(1)
    weights_next(2)
    weights_end(1)
    weights_end(2)
    loop(0, 4, lambda turn: cot_gather(turn).settle())
    for chain in (tok_chain, ids_chain, wo_chain, cot_chain):
        chain.settle()
    for step in (0, 1, 2, 3):
        weights_keep(step).wait()
        for flip in (0, 1, 2, 3):
            if step:
                weights_ring(step, flip).wait_send()
            if flip:
                weights_plane(step, flip).wait_send()
            weights_core(step, flip).wait_send()
            weights_core(step, flip).wait_recv()
        if step:
            wq_ring(step).wait_send()
            mixed_ring(step).wait_send()


def tok_in_f32(tok, z, here):
    return tok[z, :, here].astype(F32)


def start(tok, ids, wq, wo, we, cot, cosine, sine, collective):
    rows, width = tok.shape
    own = wo.shape[0]
    hidden3 = we.shape[-1]
    seqlen = PLANES * rows
    size = WINDOW * HEAD_DIM
    blocks = (8, PLANES, own, width)
    any_out = pl.BlockSpec(memory_space=pl.ANY)
    vmem_out = pl.BlockSpec(memory_space=pltpu.VMEM)
    shapes = [
        ((8, PLANES, own, hidden3), BF16, any_out),
        ((4, PLANES) + cot.shape, BF16, any_out),
        ((width, width), BF16, vmem_out),
        ((width, width), BF16, vmem_out),
        ((PLANES, rows, width), BF16, vmem_out),
        ((3, WINDOW, seqlen, HEAD_DIM), BF16, vmem_out),
        ((WINDOW, seqlen, seqlen), F32, vmem_out),
        ((WINDOW, seqlen, HEAD_DIM), F32, vmem_out),
        ((rows, width), BF16, vmem_out),
        ((rows, width), F32, vmem_out),
        ((rows, width), BF16, vmem_out),
        ((3, 4, own, hidden3), BF16, any_out),
    ]
    return pl.pallas_call(
        start_kernel,
        out_shape=[jax.ShapeDtypeStruct(shape, kind) for shape, kind, _ in shapes],
        in_specs=[any_out] * 6 + [vmem_out] * 2,
        out_specs=[spec for _, _, spec in shapes],
        scratch_shapes=[
            pltpu.VMEM((PLANES, rows, width), BF16),
            pltpu.VMEM((PLANES,) + ids.shape, BF16),
            pltpu.VMEM(blocks, BF16),
            pltpu.VMEM(blocks, BF16),
            pltpu.VMEM((PLANES * own, width), F32),
            pltpu.VMEM((seqlen, seqlen), F32),
            pltpu.VMEM((PLANES, rows, size), BF16),
            pltpu.VMEM((PLANES, rows, size), BF16),
            pltpu.SemaphoreType.DMA((10,)),
            pltpu.SemaphoreType.DMA((39, 4)),
            pltpu.SemaphoreType.DMA((39, 4)),
        ],
        compiler_params=pltpu.CompilerParams(
            collective_id=collective, has_side_effects=True, vmem_limit_bytes=56 * 2**20
        ),
        name="start",
    )(tok, ids, wq, wo, we, cot, cosine, sine)[:-1]


def add_blocks(out, *terms):
    rows = out.shape[0]

    def body(i, carry):
        part = pl.ds(pl.multiple_of(i * 16, 16), 16)
        total = terms[0][part, :].astype(F32)
        for term in terms[1:]:
            total = total + term[part, :].astype(F32)
        out[part, :] = total.astype(out.dtype)
        return carry

    lax.fori_loop(0, rows // 16, body, 0)


def experts_kernel(
    x_in, cot_in, weights_in, misc_in, grads_o, outs_o, outs_one_o, sums_o,
    x, cot, weights, misc, act, scaled, slopes, gate, outs, parts, got_one, got_two, got_far, stage,
    load_sems, send_sems, recv_sems,
):
    w, z = place()
    chip = w // 2
    expert = chip * PLANES + z
    rows, width = x_in.shape
    hidden = weights.shape[1] // 3
    group_rows = 4 * rows

    def remote(kind, step, src, dst, device):
        return pltpu.make_async_remote_copy(
            src_ref=src,
            dst_ref=dst,
            send_sem=send_sems.at[kind, step],
            recv_sem=recv_sems.at[kind, step],
            device_id=device,
            device_id_type=MESH_IDS,
        )

    def plane_of(step, sign):
        return lax.rem(z + PLANES + sign * step, PLANES)

    def step_at(turn):
        step = 0
        for plane, steps in enumerate(((3, 2, 1, 0), (1, 3, 2, 0), (3, 1, 2, 0), (1, 2, 3, 0))):
            for number, value in enumerate(steps):
                step = jnp.where((z == plane) & (turn == number), value, step)
        return step

    def axes(turn):
        first = 1 + lax.rem(turn, 2)
        return first, 3 - first

    def ring(step, up):
        to = lax.rem(step + 1, 4) if up else lax.rem(step + 3, 4)
        return pltpu.make_async_remote_copy(
            src_ref=x.at[step, chip],
            dst_ref=x.at[to, chip],
            send_sem=send_sems.at[0 if up else 8, step],
            recv_sem=recv_sems.at[0, to],
            device_id=(w, z + 1 if up else z - 1),
            device_id_type=MESH_IDS,
        )

    def goes(step, up):
        if up:
            return (z >= step) & (z < PLANES - 1)
        return ((z < step) | (step == 0)) & (z > 0)

    def pass_on(step):
        for up in (True, False):

            @pl.when(goes(step, up))
            def _():
                ring(step, up).start()

    def arrive(step):
        pltpu.make_async_remote_copy(
            src_ref=x.at[step, chip],
            dst_ref=x.at[step, chip],
            send_sem=send_sems.at[0, step],
            recv_sem=recv_sems.at[0, step],
            device_id=(w, z),
            device_id_type=MESH_IDS,
        ).wait_recv()

    def direct(step, flip):
        block = x.at[step, chip]
        return remote(flip, step, block, block, (w ^ (2 * flip), z))

    def across(turn):
        first, second = axes(turn)
        step = step_at(turn)
        block = x.at[step, chip ^ first]
        return remote(3, step, block, block, (w ^ (2 * second), z))

    def near(turn, which):
        first, _ = axes(turn)
        step = step_at(turn)
        block = chip ^ 3 if which else chip ^ first
        return remote(
            4 + which, step, parts.at[step, block], got_one.at[step, which], (w ^ (2 * first), z)
        )

    def cross(turn):
        _, second = axes(turn)
        step = step_at(turn)
        return remote(
            6, step, parts.at[step, chip ^ second], got_two.at[step], (w ^ (2 * second), z)
        )

    def far(step):
        return remote(7, step, parts.at[step, chip], got_far.at[step - 1], (w, plane_of(step, -1)))

    def outs_near(step, which):
        first, _ = axes(step)
        block = chip ^ 3 if which else chip ^ first
        return remote(
            9 + which, step, outs_o.at[step, block], outs_one_o.at[step, which], (w ^ (2 * first), z)
        )

    def cot_load(step):
        return pltpu.make_async_copy(
            cot_in.at[:, plane_of(step, -1)], cot.at[step], load_sems.at[step]
        )

    def outs_out(turn):
        return pltpu.make_async_copy(
            outs.at[lax.rem(turn, 2)], outs_o.at[step_at(turn)], load_sems.at[9 + lax.rem(turn, 2)]
        )

    def grads_out(low, size, slot):
        return pltpu.make_async_copy(
            stage.at[slot, :, pl.ds(0, size)], grads_o.at[:, low], load_sems.at[4 + slot]
        )

    loads = [
        pltpu.make_async_copy(src, dst, load_sems.at[6 + i])
        for i, (src, dst) in enumerate(
            (
                (x_in, x.at[0, chip]),
                (misc_in.at[:, pl.ds(misc_in.shape[1] - 128, 128)], misc),
                (weights_in, weights),
            )
        )
    ]
    for load in loads:
        load.start()
    loop(0, 4, lambda step: cot_load(step).start())
    greet(w, z)
    loads[0].wait()
    pass_on(0)

    def begin(turn):
        step = step_at(turn)

        @pl.when(turn < 3)
        def _():
            arrive(step)
            pass_on(step)

        direct(step, 1).start()
        direct(step, 2).start()

    def relay(turn):
        step = step_at(turn)
        direct(step, 1).wait_recv()
        direct(step, 2).wait_recv()
        across(turn).start()

    begin(0)
    begin(1)
    relay(0)
    begin(2)
    relay(1)
    loads[1].wait()
    loads[2].wait()

    def first_half(step):
        cot_load(step).wait()
        rows_in = x[step].reshape(group_rows, width)
        members = cot[step, :, :, width:].reshape(group_rows, 128).astype(F32)
        logits = mul(rows_in, misc[...], 1, 0)
        lane = lax.broadcasted_iota(jnp.int32, logits.shape, 1)
        routed = (lane > 0) & (lane < 16)
        top = jnp.max(jnp.where(routed, logits, -1e30), axis=1, keepdims=True)
        powers = jnp.where(routed, jnp.exp(logits - top), 0.0)
        probs = jnp.where(lane == 0, 1.0, powers / jnp.sum(powers, axis=1, keepdims=True))
        own = jnp.where(lane == expert, members, 0.0)
        gate[0] = jnp.broadcast_to(jnp.sum(probs * own, axis=1, keepdims=True), gate.shape[1:])
        gate[1] = own

        def hidden_chunk(low, size):
            here = x[step].reshape(group_rows, width)
            gate_part = mul(here, weights[:, at(low, size)], 1, 0)
            up_part = mul(here, weights[:, at(hidden + low, size)], 1, 0)
            grad_act = mul(
                cot[step, :, :, :width].reshape(group_rows, width),
                weights[:, at(2 * hidden + low, size)],
                1,
                0,
            )
            scale = gate[0][:, :1]
            grad_act = grad_act * scale
            sigmoid = 1.0 / (1.0 + jnp.exp(-gate_part))
            silu = gate_part * sigmoid
            activated = (silu * up_part).astype(BF16)
            act[:, at(low, size)] = activated
            scaled[step, :, at(low, size)] = (activated.astype(F32) * scale).astype(BF16)
            slopes[step, :, at(low, size)] = (
                grad_act * up_part * (sigmoid + silu * (1.0 - sigmoid))
            ).astype(BF16)
            slopes[step, :, at(hidden + low, size)] = (grad_act * silu).astype(BF16)

        loop(0, hidden // 256, lambda i: hidden_chunk(i * 256, 256))
        if hidden % 256:
            hidden_chunk(hidden // 256 * 256, hidden % 256)

    def second_half(turn, step):
        def width_body(i, total):
            low = i * 256
            expert_rows = mul(act[...], weights[at(low, 256), 2 * hidden :], 1, 1)
            expert_rows = expert_rows.astype(BF16).astype(F32)
            outs[lax.rem(turn, 2), :, :, at(low, 256)] = (
                (expert_rows * gate[0][:, :1]).astype(BF16).reshape(4, rows, 256)
            )
            product = expert_rows * cot[step, :, :, at(low, 256)].reshape(group_rows, 256).astype(F32)
            grad_in = mul(slopes[step], weights[at(low, 256), : 2 * hidden], 1, 1)
            parts[step, :, :, at(low, 256)] = grad_in.astype(BF16).reshape(4, rows, 256)
            return total + product[:, :128] + product[:, 128:]

        total = lax.fori_loop(0, width // 256, width_body, jnp.zeros((group_rows, 128), F32))
        prob = jnp.sum(total, axis=1, keepdims=True) * gate[1]
        high = prob.astype(BF16)
        low = (prob - high.astype(F32)).astype(BF16)
        low = pltpu.roll(low.astype(F32), 32, 1).astype(BF16)
        parts[step, :, :, width:] = (high + low).reshape(4, rows, 128)

    def send_cross(turn):
        _, second = axes(turn)
        step = step_at(turn)
        near(turn, 1).wait_recv()
        block = parts.at[step, chip ^ second]
        add_blocks(block, block, got_one.at[step, 1])
        cross(turn).start()

    def send_far(turn):
        step = step_at(turn)
        near(turn, 0).wait_recv()
        cross(turn).wait_recv()
        block = parts.at[step, chip]
        add_blocks(block, block, got_one.at[step, 0], got_two.at[step])
        far(step).start()

    def group(turn):
        step = step_at(turn)
        across(turn).wait_recv()
        first_half(step)

        @pl.when(turn == 0)
        def _():
            begin(3)

        @pl.when(turn < 2)
        def _():
            relay(turn + 2)

        @pl.when(turn > 1)
        def _():
            outs_out(turn - 2).wait()

        second_half(turn, step)
        outs_out(turn).start()

        @pl.when(turn > 0)
        def _():
            send_cross(turn - 1)

        near(turn, 1).start()
        near(turn, 0).start()

        @pl.when(turn > 1)
        def _():
            send_far(turn - 2)

    loop(0, 4, group)

    def weight_chunk(left, right, low, size, offset, i):
        slot = lax.rem(i, 2)

        @pl.when(i >= 2)
        def _():
            grads_out(pl.ds(0, 256), 256, slot).wait()

        total = None
        for step in range(4):
            term = mul(
                left[step, :, :, :width].reshape(group_rows, width), right[step, :, at(low, size)], 0, 0
            )
            total = term if total is None else total + term
        stage[slot, :, :size] = total.astype(BF16)
        grads_out(at(offset + low, size), size, slot).start()

    ups, downs = 2 * hidden // 256, hidden // 256

    def up_chunk(i):
        weight_chunk(x, slopes, i * 256, 256, 0, i)

    def down_chunk(i):
        weight_chunk(cot, scaled, (i - ups) * 256, 256, 2 * hidden, i)

    loop(0, 4, up_chunk)
    send_cross(3)
    outs_out(2).wait()
    outs_out(3).wait()
    loop(0, 4, lambda step: (outs_near(step, 1).start(), outs_near(step, 0).start()))
    loop(4, 6, up_chunk)
    send_far(2)
    loop(6, ups, up_chunk)
    loop(ups, ups + downs, down_chunk)
    last = ups + downs
    if hidden % 256:
        weight_chunk(cot, scaled, downs * 256, hidden % 256, 2 * hidden, jnp.int32(last))
        grads_out(pl.ds(0, 256), 256, (last - 1) % 2).wait()
        grads_out(pl.ds(0, hidden % 256), hidden % 256, last % 2).wait()
    else:
        grads_out(pl.ds(0, 256), 256, last % 2).wait()
        grads_out(pl.ds(0, 256), 256, (last - 1) % 2).wait()
    near(3, 0).wait_recv()
    cross(3).wait_recv()
    loop(1, 4, lambda step: far(step).wait_recv())
    add_blocks(
        sums_o,
        parts.at[0, chip],
        got_one.at[0, 0],
        got_two.at[0],
        got_far.at[0],
        got_far.at[1],
        got_far.at[2],
    )

    def settle(turn):
        step = step_at(turn)
        direct(step, 1).wait_send()
        direct(step, 2).wait_send()
        across(turn).wait_send()
        near(turn, 0).wait_send()
        near(turn, 1).wait_send()
        cross(turn).wait_send()
        for which in (0, 1):
            outs_near(turn, which).wait_send()
            outs_near(turn, which).wait_recv()

        @pl.when(turn < 3)
        def _():
            far(step).wait_send()

        for up in (True, False):

            @pl.when(goes(step, up))
            def _():
                ring(step, up).wait_send()

    loop(0, 4, settle)


def run_experts(second_in, cot_all, weights, misc, collective):
    rows, width = second_in.shape
    hidden = weights.shape[1] // 3
    sums_width = width + 128
    block = (rows, sums_width)
    return pl.pallas_call(
        experts_kernel,
        out_shape=[
            jax.ShapeDtypeStruct((width, 3 * hidden), BF16),
            jax.ShapeDtypeStruct((4, 4, rows, width), BF16),
            jax.ShapeDtypeStruct((4, 2, rows, width), BF16),
            jax.ShapeDtypeStruct((rows, sums_width), F32),
        ],
        in_specs=[pl.BlockSpec(memory_space=pl.ANY)] * 4,
        out_specs=[
            pl.BlockSpec(memory_space=pl.ANY),
            pl.BlockSpec(memory_space=pl.ANY),
            pl.BlockSpec(memory_space=pl.ANY),
            pl.BlockSpec(memory_space=pltpu.VMEM),
        ],
        scratch_shapes=[
            pltpu.VMEM((4, 4, rows, width), BF16),
            pltpu.VMEM((4, 4, rows, width + 128), BF16),
            pltpu.VMEM((width, 3 * hidden), BF16),
            pltpu.VMEM((width, 128), BF16),
            pltpu.VMEM((4 * rows, hidden), BF16),
            pltpu.VMEM((4, 4 * rows, hidden), BF16),
            pltpu.VMEM((4, 4 * rows, 2 * hidden), BF16),
            pltpu.VMEM((2, 4 * rows, 128), F32),
            pltpu.VMEM((2, 4, rows, width), BF16),
            pltpu.VMEM((4, 4) + block, BF16),
            pltpu.VMEM((4, 2) + block, BF16),
            pltpu.VMEM((4,) + block, BF16),
            pltpu.VMEM((3,) + block, BF16),
            pltpu.VMEM((2, width, 256), BF16),
            pltpu.SemaphoreType.DMA((11,)),
            pltpu.SemaphoreType.DMA((11, 4)),
            pltpu.SemaphoreType.DMA((11, 4)),
        ],
        compiler_params=pltpu.CompilerParams(
            collective_id=collective, has_side_effects=True, vmem_limit_bytes=62 * 2**20
        ),
        name="experts",
    )(second_in, cot_all, weights, misc)


def finish_kernel(
    outs_in, outs_one_in, grads_in, exact_in, mixed_in, qkv_in, first_in, wq_in, wo_in,
    cos_in, sin_in, rows_in, sums_in, second_in, middle_in, cot_in, tok_in,
    output_o, grad_o, table_o, q_o, o_o,
    outs, outs_one, outs_two, outs_far, grads_own, grads_got, heads, exact, mixed, qkv, first, wq,
    wo, heads_send, attn, grad_middle, first_got, projected, first_part, dense, dense_got, dense_one,
    dense_two, dense_far, dense_sum, load_sems, send_sems, recv_sems,
):
    links = Links(send_sems, recv_sems)
    w, z = links.w, links.z
    chip, core = w // 2, w % 2
    rows = outs.shape[2]
    width = outs.shape[3]
    size = WINDOW * HEAD_DIM
    steps = (1, 2, 3, 0)
    block_rows = o_o.shape[0] // 4
    half = o_o.shape[1] // 2
    plane_rows = o_o.shape[0]
    remote, plane_of = links.copy, links.plane

    def axes(step):
        one = 1 + lax.rem(step, 2)
        return one, 3 - one

    def heads_ring(step):
        to = plane_of(step, 1)
        return remote(37, step, heads_send.at[to], heads.at[z], (w, to))

    def grads_load(step):
        return pltpu.make_async_copy(
            grads_in.at[plane_of(step, 1), core], grads_own.at[step], load_sems.at[0, step]
        )

    def grads_swap(step):
        return remote(
            0, step, grads_in.at[plane_of(step, 1), 1 - core], grads_got.at[step], (w ^ 1, z)
        )

    def grads_ring(step):
        return remote(1, step, grads_own.at[step], table_o.at[chip, z, core], (w, plane_of(step, 1)))

    def grads_keep():
        return pltpu.make_async_copy(
            grads_own.at[0], table_o.at[chip, z, core], load_sems.at[1, 0]
        )

    def grads_gather(turn):
        step = direct_at(z, turn)
        source = plane_of(step, -1)
        half = grads_own.shape[1] // 2
        return Gather(
            links, 2, step, turn, lambda i: table_o.at[i // 2, source, i % 2], True, half
        )

    def outs_loads(step):
        _, two = axes(step)
        return [
            pltpu.make_async_copy(src, dst, load_sems.at[2 + 3 * (i > 0) + (i > 1), step])
            for i, (src, dst) in enumerate(
                (
                    (outs_in.at[step, chip], outs.at[step, 0]),
                    (outs_in.at[step, chip ^ two], outs.at[step, 1]),
                    (outs_one_in.at[step], outs_one.at[step]),
                )
            )
        ]

    def cross(step):
        _, two = axes(step)
        return remote(11, step, outs.at[step, 1], outs_two.at[step], (w ^ (2 * two), z))

    def far(step):
        return remote(12, step, outs.at[step, 0], outs_far.at[step - 1], (w, plane_of(step, -1)))

    def part(kind, step):
        return dense.at[0, kind, plane_of(step, 1)]

    def dense_swap(kind, step):
        to = plane_of(step, 1)
        return remote(
            13 + 4 * kind, step, dense.at[1, kind, to], dense_got.at[kind, step], (w ^ 1, z)
        )

    def rows_of(block):
        return pl.ds(pl.multiple_of(block * block_rows, 16), block_rows)

    def dense_axes(kind):
        return 1 + kind, 2 - kind

    def dense_near(kind, step, which):
        one, _ = dense_axes(kind)
        block = chip ^ 3 if which else chip ^ one
        return remote(
            14 + 4 * kind + which,
            step,
            part(kind, step).at[rows_of(block)],
            dense_one.at[kind, step, which],
            (w ^ (2 * one), z),
        )

    def dense_cross(kind, step):
        _, two = dense_axes(kind)
        return remote(
            16 + 4 * kind,
            step,
            part(kind, step).at[rows_of(chip ^ two)],
            dense_two.at[kind, step],
            (w ^ (2 * two), z),
        )

    def place_of(owner):
        return rows_of(owner // 2), at(lax.rem(owner, 2) * half, half)

    def dense_ring(kind, step):
        own = part(kind, step).at[rows_of(chip)]
        here, columns = place_of(w)
        to = q_o.at[z, here, columns] if kind == 0 else dense_far.at[step - 1]
        return remote(21 + kind, step, own, to, (w, plane_of(step, 1)))

    def dense_keep():
        here, columns = place_of(w)
        return pltpu.make_async_copy(
            part(0, 0).at[rows_of(chip)], q_o.at[z, here, columns], load_sems.at[1, 1]
        )

    def dense_last():
        here, columns = place_of(w)
        return pltpu.make_async_copy(dense_sum, o_o.at[here, columns], load_sems.at[1, 2])

    def q_slot(step):
        source = plane_of(step, -1)

        def slot(owner):
            here, columns = place_of(owner)
            return q_o.at[source, here, columns]

        return slot

    def o_slot(owner):
        here, columns = place_of(owner)
        return o_o.at[here, columns]

    def q_gather(step):
        return Gather(links, 23, step, step, q_slot(step))

    def o_gather():
        return Gather(links, 30, 0, 0, o_slot)

    def first_ring(step):
        to = plane_of(step, 1)
        return remote(38, step, first_part.at[to], first_got.at[step - 1], (w, to))

    loads = [
        pltpu.make_async_copy(src, dst, load_sems.at[3 + i // 4, i % 4])
        for i, (src, dst) in enumerate(
            (
                (wq_in, wq),
                (wo_in, wo),
                (exact_in, exact),
                (mixed_in, mixed),
                (qkv_in, qkv),
                (first_in, first),
            )
        )
    ]
    for load in loads[:2]:
        load.start()
    for step in steps:
        grads_load(step).start()
    for step in steps:
        for load in outs_loads(step):
            load.start()
    for load in loads[2:]:
        load.start()
    greet(w, z)
    for step in steps:
        grads_swap(step).start()

    def grads_ready(step):
        grads_load(step).wait()
        grads_swap(step).wait_recv()
        add_blocks(grads_own.at[step], grads_own.at[step], grads_got.at[step])

    grads_ready(0)
    keep = grads_keep()
    keep.start()

    def outs_cross(step):
        for load in outs_loads(step):
            load.wait()
        add_blocks(outs.at[step, 1], outs.at[step, 1], outs_one.at[step, 1])
        cross(step).start()

    keep.wait()
    grads_gather(3).begin()
    for load in loads[:2]:
        load.wait()

    lane = lax.broadcasted_iota(jnp.int32, (rows, 128), 1)
    routed = (lane > 0) & (lane < 16)
    logits = jnp.where(routed, mul(second_in[...], wq[:, 3 * size :], 1, 0), -1e30)
    powers = jnp.where(routed, jnp.exp(logits - jnp.max(logits, axis=1, keepdims=True)), 0.0)
    probs = powers / jnp.sum(powers, axis=1, keepdims=True)
    high_low = sums_in[:, width:]
    grad_probs = jnp.where(routed, high_low + pltpu.roll(high_low, 96, 1), 0.0)
    grad_logits = probs * (grad_probs - jnp.sum(probs * grad_probs, axis=1, keepdims=True))
    grad_logits = grad_logits.astype(BF16)
    gains = jnp.transpose(wq[:, 3 * size :].astype(F32))
    gain_one, gain_two = gains[16:17, :], gains[17:18, :]
    grad_second = sums_in[:, :width] + mul(grad_logits, wq[:, 3 * size :], 1, 1)
    middle = middle_in[...]
    inverse = lax.rsqrt(jnp.mean(middle * middle, axis=1, keepdims=True) + epsilon)
    normed = middle * inverse
    grad_normed = grad_second * gain_two
    grad_here = cot_in[...].astype(F32) + inverse * (
        grad_normed - normed * jnp.mean(grad_normed * normed, axis=1, keepdims=True)
    )
    grad_middle[...] = grad_here
    attn[...] = grad_here.astype(BF16)
    gain_two_row = jnp.sum(grad_second * normed, axis=0, keepdims=True)
    router_part = mul(second_in[...], grad_logits, 0, 0)
    for plane, begin in enumerate(STARTS):
        grad_mixed = mul(
            attn[...], wo[begin * HEAD_DIM : begin * HEAD_DIM + size, :], 1, 1
        )
        heads_send[plane] = grad_mixed.astype(BF16)
    for step in (1, 2, 3):
        heads_ring(step).start()
    heads[z] = heads_send[z]
    loop(1, 4, grads_ready)
    loop(0, 4, outs_cross)
    for step in (1, 2, 3):
        heads_ring(step).wait_recv()
    send_next(z, lambda step: grads_ring(step).start())

    def out_weight(i):
        side = i // (half // 128)
        low = at((i - side * (half // 128)) * 128, 128)
        total = mul(rows_in[...], attn[:, at(i * 128, 128)], 0, 0).astype(BF16)
        dense[side ^ core, 1, :, :, low] = total.reshape(PLANES, plane_rows, 128)

    loop(0, width // 128, out_weight)
    for step in steps:
        dense_swap(1, step).start()
    for load in loads[2:]:
        load.wait()

    def head_back(head):
        keep_head = jnp.float32(0)
        for plane, (a, b) in enumerate(KEEP):
            keep_head = jnp.where((z == plane) & (head >= a) & (head < b), 1.0, keep_head)
        columns = at(head * HEAD_DIM, HEAD_DIM)
        grad_rows = heads[:, :, columns].reshape(PLANES * rows, HEAD_DIM).astype(F32) * keep_head
        delta = jnp.sum(grad_rows * mixed[head], axis=1, keepdims=True)
        grad_rows = grad_rows.astype(BF16)
        weights = exact[head]
        grad_value = mul(weights.astype(BF16), grad_rows, 0, 0)
        grad_scores = mul(grad_rows, qkv[2, head], 1, 1)
        grad_scores = (weights * (grad_scores - delta)).astype(BF16)
        grad_query = mul(grad_scores, qkv[1, head], 1, 0) * (HEAD_DIM ** (-0.5))
        grad_key = mul(grad_scores, qkv[0, head], 0, 0)

        def back(grads):
            return grads * cos_in[...] + pltpu.roll(grads * sin_in[...], HEAD_DIM // 2, 1)

        projected[:, columns] = back(grad_query).astype(BF16)
        projected[:, at(size + head * HEAD_DIM, HEAD_DIM)] = back(grad_key).astype(BF16)
        projected[:, at(2 * size + head * HEAD_DIM, HEAD_DIM)] = grad_value.astype(BF16)

    loop(0, WINDOW, head_back)

    def grads_next(turn):
        grads_ring(direct_at(z, turn)).wait_recv()
        grads_gather(turn).begin()

    grads_gather(3).relay()

    def qkv_weight(i):
        side = i // (half // 128)
        low = at((i - side * (half // 128)) * 128, 128)
        total = mul(first[...].reshape(PLANES * rows, width), projected[:, at(i * 128, 128)], 0, 0)
        dense[side ^ core, 0, :, :, low] = total.astype(BF16).reshape(PLANES, plane_rows, 128)

    loop(0, 3 * size // 128, qkv_weight)
    gain_parts = []
    for i in range(width // 256):
        here = slice(i * 256, (i + 1) * 256)
        total = mul(projected[...], wq[here, : 3 * size], 1, 1)
        first_part[:, :, here] = total.astype(BF16).reshape(PLANES, rows, 256)
        scaled = total * first[:, :, here].reshape(PLANES * rows, 256).astype(F32)
        gain_parts.append(jnp.sum(scaled, axis=0, keepdims=True))
    gain_one_row = jnp.concatenate(gain_parts, axis=1) / gain_one
    kind = lax.broadcasted_iota(jnp.int32, (128, width), 0)
    gain_rows = jnp.where(kind == 16, gain_one_row, jnp.where(kind == 17, gain_two_row, 0.0))
    misc = jnp.transpose(gain_rows) + router_part
    dense[1 ^ core, 0, :, :, half - 128 :] = misc.astype(BF16).reshape(PLANES, plane_rows, 128)
    for step in steps:
        dense_swap(0, step).start()

    loop(0, 1, grads_next)
    send_beyond(z, lambda step: grads_ring(step).start())

    def dense_ready(step):
        for kind in (0, 1):
            dense_swap(kind, step).wait_recv()
            block = part(kind, step)
            add_blocks(block, block, dense_got.at[kind, step])
            dense_near(kind, step, 1).start()
            dense_near(kind, step, 0).start()

    loop(0, 4, dense_ready)

    def outs_finish(step):
        cross(step).wait_recv()
        block = outs.at[step, 0]
        add_blocks(block, block, outs_one.at[step, 0], outs_two.at[step])

    loop(0, 4, outs_finish)
    grads_gather(0).relay()

    def dense_cross_start(step):
        for kind in (0, 1):
            _, two = dense_axes(kind)
            dense_near(kind, step, 1).wait_recv()
            block = part(kind, step).at[rows_of(chip ^ two)]
            add_blocks(block, block, dense_one.at[kind, step, 1])
            dense_cross(kind, step).start()

    loop(0, 4, dense_cross_start)
    loop(1, 3, grads_next)
    loop(1, 4, lambda step: far(step).start())

    def dense_finish(step):
        for kind in (0, 1):
            dense_near(kind, step, 0).wait_recv()
            dense_cross(kind, step).wait_recv()
            block = part(kind, step).at[rows_of(chip)]
            add_blocks(block, block, dense_one.at[kind, step, 0], dense_two.at[kind, step])

        @pl.when(step > 0)
        def _():
            dense_ring(0, step).start()
            dense_ring(1, step).start()

    loop(0, 4, dense_finish)
    loop(1, 4, lambda step: first_ring(step).start())
    keep = dense_keep()
    keep.start()
    grads_gather(3).end()
    grads_gather(0).end()
    grads_gather(1).relay()
    keep.wait()
    q_gather(0).begin()

    def q_next(step):
        dense_ring(0, step).wait_recv()
        q_gather(step).begin()
        dense_ring(1, step).wait_recv()

    loop(1, 4, q_next)
    add_blocks(
        dense_sum, part(1, 0).at[rows_of(chip)], dense_far.at[0], dense_far.at[1], dense_far.at[2]
    )
    keep = dense_last()
    keep.start()
    keep.wait()
    o_gather().begin()
    grads_gather(2).relay()
    grads_gather(1).end()
    loop(0, 4, lambda step: q_gather(step).relay())
    o_gather().relay()
    loop(1, 4, lambda step: far(step).wait_recv())

    def output_rows(i):
        here = pl.ds(pl.multiple_of(i * 16, 16), 16)
        total = middle_in[here, :] + outs[0, 0, here, :].astype(F32)
        for step in range(3):
            total = total + outs_far[step, here, :].astype(F32)
        output_o[here, :] = total.astype(BF16)

    loop(0, rows // 16, output_rows)
    for step in (1, 2, 3):
        first_ring(step).wait_recv()
    grad_first = first_part[z].astype(F32)
    for step in range(3):
        grad_first = grad_first + first_got[step].astype(F32)
    tokens = tok_in[...].astype(F32)
    inverse = lax.rsqrt(jnp.mean(tokens * tokens, axis=1, keepdims=True) + epsilon)
    normed = tokens * inverse
    grad_normed = grad_first * gain_one
    grad_o[...] = (
        grad_middle[...]
        + inverse
        * (grad_normed - normed * jnp.mean(grad_normed * normed, axis=1, keepdims=True))
    ).astype(BF16)
    loop(0, 4, lambda step: q_gather(step).end())
    o_gather().end()
    grads_gather(2).end()
    loop(0, 4, lambda turn: grads_gather(turn).settle())
    loop(0, 4, lambda step: q_gather(step).settle())
    o_gather().settle()

    def settle(step):
        grads_swap(step).wait_send()
        cross(step).wait_send()
        for kind in (0, 1):
            dense_swap(kind, step).wait_send()
            dense_near(kind, step, 0).wait_send()
            dense_near(kind, step, 1).wait_send()
            dense_cross(kind, step).wait_send()

    loop(0, 4, settle)

    def settle_rings(step):
        first_ring(step).wait_send()
        heads_ring(step).wait_send()
        grads_ring(step).wait_send()
        far(step).wait_send()
        dense_ring(0, step).wait_send()
        dense_ring(1, step).wait_send()

    loop(1, 4, settle_rings)


def finish(outs, outs_one, grads, saved, tables, at_rows, collective):
    exact, mixed, qkv, first, wq, wo = saved
    rows, width = first.shape[1:]
    seqlen = PLANES * rows
    size = WINDOW * HEAD_DIM
    plane_rows = width // PLANES
    block = (plane_rows // 4, width // 2)
    heads = (PLANES, rows, size)
    any_spec = pl.BlockSpec(memory_space=pl.ANY)
    vmem_spec = pl.BlockSpec(memory_space=pltpu.VMEM)
    return pl.pallas_call(
        finish_kernel,
        out_shape=[
            jax.ShapeDtypeStruct((rows, width), BF16),
            jax.ShapeDtypeStruct((rows, width), BF16),
            jax.ShapeDtypeStruct((4, PLANES) + grads.shape[1:], BF16),
            jax.ShapeDtypeStruct((PLANES, plane_rows, width), BF16),
            jax.ShapeDtypeStruct((plane_rows, width), BF16),
        ],
        in_specs=[any_spec] * 9 + [vmem_spec] * 8,
        out_specs=[vmem_spec] * 2 + [any_spec] * 3,
        scratch_shapes=[
            pltpu.VMEM((4, 2, rows, width), BF16),
            pltpu.VMEM((4, 2, rows, width), BF16),
            pltpu.VMEM((4, rows, width), BF16),
            pltpu.VMEM((3, rows, width), BF16),
            pltpu.VMEM((4,) + grads.shape[2:], BF16),
            pltpu.VMEM((4,) + grads.shape[2:], BF16),
            pltpu.VMEM(heads, BF16),
            pltpu.VMEM(exact.shape, F32),
            pltpu.VMEM(mixed.shape, F32),
            pltpu.VMEM(qkv.shape, BF16),
            pltpu.VMEM(first.shape, BF16),
            pltpu.VMEM(wq.shape, BF16),
            pltpu.VMEM(wo.shape, BF16),
            pltpu.VMEM(heads, BF16),
            pltpu.VMEM((rows, width), BF16),
            pltpu.VMEM((rows, width), F32),
            pltpu.VMEM((3, rows, width), BF16),
            pltpu.VMEM((seqlen, 3 * size), BF16),
            pltpu.VMEM(first.shape, BF16),
            pltpu.VMEM((2, 2, PLANES, plane_rows, width // 2), BF16),
            pltpu.VMEM((2, 4, plane_rows, width // 2), BF16),
            pltpu.VMEM((2, 4, 2) + block, BF16),
            pltpu.VMEM((2, 4) + block, BF16),
            pltpu.VMEM((3,) + block, BF16),
            pltpu.VMEM(block, BF16),
            pltpu.SemaphoreType.DMA((7, 4)),
            pltpu.SemaphoreType.DMA((39, 4)),
            pltpu.SemaphoreType.DMA((39, 4)),
        ],
        compiler_params=pltpu.CompilerParams(
            collective_id=collective, has_side_effects=True, vmem_limit_bytes=62 * 2**20
        ),
        name="finish",
    )(outs, outs_one, grads, *saved, *tables, *at_rows)


def widen_kernel(table, q, o, up_o, down_o, qkv_o, out_o, misc_o):
    columns = table.shape[2]
    split = up_o.shape[2]
    size = WINDOW * HEAD_DIM
    for low in range(0, columns, 128):
        part = jnp.swapaxes(table[:, :, low : low + 128].astype(F32), 0, 1)
        if low < split:
            up_o[:, :, low : low + 128] = part
        else:
            down_o[:, :, low - split : low - split + 128] = part
    out_o[...] = o[...].astype(F32)
    column = 0
    for kind in range(3):
        for plane, (a, b) in enumerate(KEEP):
            span = (b - a) * HEAD_DIM
            begin = kind * size + a * HEAD_DIM
            qkv_o[:, column : column + span] = q[plane, :, begin : begin + span].astype(F32)
            column += span
    total = q[0, :, 3 * size :].astype(F32)
    for plane in range(1, PLANES):
        total = total + q[plane, :, 3 * size :].astype(F32)
    misc_o[...] = total


def widen(table, q, o):
    experts, rows, columns = table.shape
    width = o.shape[1]
    split = columns // 3 * 2
    step = rows // 4
    shapes = [
        (rows, experts, split),
        (rows, experts, columns - split),
        (rows, 3 * width),
        (rows, width),
        (rows, 128),
    ]
    return pl.pallas_call(
        widen_kernel,
        grid=(rows // step,),
        out_shape=[jax.ShapeDtypeStruct(shape, F32) for shape in shapes],
        in_specs=[
            pl.BlockSpec((experts, step, columns), lambda i: (0, i, 0)),
            pl.BlockSpec((PLANES, step, width), lambda i: (0, i, 0)),
            pl.BlockSpec((step, width), lambda i: (i, 0)),
        ],
        out_specs=[
            pl.BlockSpec((step,) + shape[1:], lambda i, n=len(shape): (i,) + (0,) * (n - 1))
            for shape in shapes
        ],
        compiler_params=pltpu.CompilerParams(vmem_limit_bytes=62 * 2**20),
        name="widen",
    )(table, q, o)


def windows(x):
    size = WINDOW * HEAD_DIM
    return jnp.stack([x[:, s * HEAD_DIM : s * HEAD_DIM + size] for s in STARTS])


def from_windows(x):
    return jnp.concatenate(
        [x[p, :, a * HEAD_DIM : b * HEAD_DIM] for p, (a, b) in enumerate(KEEP)], axis=1
    )


def dot(a, b, dims, out=F32):
    return lax.dot_general(a, b, ((dims[0], dims[1]), ((), ())), preferred_element_type=F32).astype(out)


def expert_local(
    tokens, seq_ids, routes, cotangent, gain_attn, w_qkv, w_out, gain_ffn, w_router, w_up, w_down
):
    rows, width = tokens.shape
    own = w_out.shape[0]
    experts = w_router.shape[1]
    seqlen = PLANES * rows
    size = WINDOW * HEAD_DIM

    misc = jnp.concatenate(
        [
            jnp.zeros((own, 1), BF16),
            w_router,
            gain_attn[:, None],
            gain_ffn[:, None],
            jnp.zeros((own, 128 - experts - 3), BF16),
        ],
        axis=1,
    )
    wq_send = jnp.concatenate(
        [windows(w_qkv[:, i * width : (i + 1) * width]) for i in range(3)]
        + [jnp.broadcast_to(misc[None], (PLANES, own, 128))],
        axis=2,
    )
    we_send = jnp.concatenate([w_up, w_down], axis=2).reshape(own, 4, PLANES, 3 * FF)
    we_send = jnp.transpose(we_send, (2, 1, 0, 3))
    choose = routes[:, :, None] == jnp.arange(experts, dtype=jnp.int32)[None, None, :]
    member = jnp.any(choose, axis=1)
    member_cols = jnp.concatenate(
        [jnp.ones((rows, 1), BF16), member.astype(BF16), jnp.zeros((rows, 127 - experts), BF16)],
        axis=1,
    )
    cot_send = jnp.concatenate([cotangent, member_cols], axis=1)
    ids_f = seq_ids.astype(BF16)
    ids_send = jnp.concatenate(
        [
            jnp.broadcast_to(ids_f[None, :], (rows, rows)),
            jnp.broadcast_to(ids_f[:, None], (rows, rows)),
        ]
    )
    half_dim = HEAD_DIM // 2
    cosine, sine_table = rotary(jnp.arange(seqlen, dtype=F32), HEAD_DIM)
    sine_signed = sine_table[:, 0, :] * jnp.where(jnp.arange(HEAD_DIM) < half_dim, -1.0, 1.0)
    we_all, cot_all, wq_all, out_weight, first_in, qkv, weights_exact, mixed_exact, mixed, middle, second_in = start(
        tokens, ids_send, wq_send, w_out, we_send, cot_send, cosine[:, 0, :], sine_signed, 1
    )
    weights = we_all.reshape(width, 3 * FF)
    grads, outs, outs_one, sums = run_experts(second_in, cot_all, weights, wq_all, 3)

    output, grad_tokens, table, q_all, o_all = finish(
        outs,
        outs_one,
        grads.reshape(PLANES, 2, width // PLANES // 2, 3 * FF),
        (weights_exact, mixed_exact, qkv, first_in, wq_all, out_weight),
        (cosine[:, 0, :], sine_signed),
        (mixed, sums, second_in, middle, cotangent, tokens),
        6,
    )
    up_sum, down_sum, qkv_sum, out_sum, misc_sum = widen(
        table.reshape(experts + 1, width // PLANES, 3 * FF), q_all, o_all
    )
    return (
        output,
        grad_tokens,
        misc_sum[:, experts + 1],
        qkv_sum,
        out_sum,
        misc_sum[:, experts + 2],
        misc_sum[:, 1 : experts + 1],
        up_sum,
        down_sum,
    )


def solution(mesh):
    fits = mesh.shape["wide"] == 8 and mesh.shape["narrow"] == PLANES
    return jax.shard_map(
        expert_local if fits else local,
        mesh=mesh,
        in_specs=(
            P(("wide", "narrow"), None),
            P(("wide", "narrow")),
            P(("wide", "narrow"), None),
            P(("wide", "narrow"), None),
            P(("wide", "narrow")),
            P(("wide", "narrow"), None),
            P(("wide", "narrow"), None),
            P(("wide", "narrow")),
            P(("wide", "narrow"), None),
            P(("wide", "narrow"), None, None),
            P(("wide", "narrow"), None, None),
        ),
        out_specs=(
            P(("wide", "narrow"), None),
            P(("wide", "narrow"), None),
            P("narrow"),
            P("narrow", None),
            P("narrow", None),
            P("narrow"),
            P("narrow", None),
            P("narrow", None, None),
            P("narrow", None, None),
        ),
        check_vma=False,
    )
```

```python
import jax
import jax.numpy as jnp
import numpy as np
from jax import lax
from jax.experimental import pallas as pl
from jax.experimental.pallas import tpu as pltpu
from jax.sharding import PartitionSpec as P

HEADS = 10
HEAD_DIM = 128
FF = 896
CAP = 72


epsilon = 1e-06


def shortened(x):
    return jax.tree.map(lambda a: a.astype(jnp.bfloat16) if a.dtype == jnp.float32 else a, x)


def rms_inverse(values):
    return lax.rsqrt(jnp.mean(values * values, axis=-1, keepdims=True) + epsilon)


def rotary(positions, head_size):
    half_dim = head_size // 2
    frequency = 10000.0 ** (-jnp.arange(half_dim, dtype=jnp.float32) / half_dim)
    angles = positions[:, None] * frequency[None, :]
    cosine = jnp.concatenate([jnp.cos(angles), jnp.cos(angles)], axis=1)[:, None, :]
    sine_table = jnp.concatenate([jnp.sin(angles), jnp.sin(angles)], axis=1)[:, None, :]
    return (cosine, sine_table)


def rotate(values, cosine, sine_table):
    half_dim = values.shape[-1] // 2
    turned = jnp.concatenate([-values[..., half_dim:], values[..., :half_dim]], axis=-1)
    return values * cosine + turned * sine_table


def rotate_back(grads, cosine, sine_table):
    half_dim = grads.shape[-1] // 2
    scaled = grads * sine_table
    turned = jnp.concatenate([scaled[..., half_dim:], -scaled[..., :half_dim]], axis=-1)
    return grads * cosine + turned


def expert_weight_terms(
    routed_in, routed_grad, shared_in, shared_grad, slot_grads, slot_acts, shared_grads, shared_acts
):
    up_routed = jnp.einsum(
        "ecd,ecf->def", routed_in, slot_grads, preferred_element_type=jnp.float32
    )
    up_shared = jnp.einsum("td,tf->df", shared_in, shared_grads, preferred_element_type=jnp.float32)
    down_routed = jnp.einsum(
        "ecd,ecf->def", routed_grad, slot_acts, preferred_element_type=jnp.float32
    )
    down_shared = jnp.einsum(
        "td,tf->df", shared_grad, shared_acts, preferred_element_type=jnp.float32
    )
    up_all = jnp.concatenate([up_shared[:, None], up_routed], axis=1)
    down_all = jnp.concatenate([down_shared[:, None], down_routed], axis=1)
    combined = jnp.concatenate([up_all, down_all], axis=2)
    return combined.reshape(combined.shape[0], -1)


def local(
    tokens, seq_ids, routes, cotangent, gain_attn, w_qkv, w_out, gain_ffn, w_router, w_up, w_down
):
    row_count = tokens.shape[0]
    model_width = tokens.shape[1]
    query_scale = HEAD_DIM ** (-0.5)
    hidden = FF
    capacity = CAP
    inputs = tokens.astype(jnp.float32)
    gain_one, qkv_weight, out_weight = (
        lax.all_gather(gain_attn, ("wide", "narrow"), axis=0, tiled=True),
        lax.all_gather(w_qkv, ("wide", "narrow"), axis=0, tiled=True),
        lax.all_gather(w_out, ("wide", "narrow"), axis=0, tiled=True),
    )
    inverse_one = rms_inverse(inputs)
    normed_one = inputs * inverse_one
    first_in = (normed_one * gain_one.astype(jnp.float32)).astype(jnp.bfloat16)
    projected = jnp.dot(first_in, qkv_weight, preferred_element_type=jnp.float32)
    offset = lax.axis_index("narrow") * row_count
    query_pos = offset + jnp.arange(row_count, dtype=jnp.int32)
    cosine, sine_table = rotary(query_pos.astype(jnp.float32), HEAD_DIM)
    query_rows = (
        rotate(projected[:, :model_width].reshape(row_count, HEADS, HEAD_DIM), cosine, sine_table)
        * query_scale
    ).astype(jnp.bfloat16)
    key_rows = (
        rotate(
            projected[:, model_width : 2 * model_width].reshape(row_count, HEADS, HEAD_DIM),
            cosine,
            sine_table,
        )
        .astype(jnp.bfloat16)
        .reshape(row_count, model_width)
    )
    value_rows = projected[:, 2 * model_width :].astype(jnp.bfloat16)
    all_keys, all_values, all_ids = (
        lax.all_gather(key_rows, "narrow", axis=0, tiled=True),
        lax.all_gather(value_rows, "narrow", axis=0, tiled=True),
        lax.all_gather(seq_ids.astype(jnp.bfloat16), "narrow", axis=0, tiled=True),
    )
    seqlen = all_keys.shape[0]
    block_len = min(512, seqlen)
    num_blocks = seqlen // block_len
    own_ids = seq_ids.astype(jnp.float32)

    def block_parts(block_index):
        first_row = block_index * block_len
        key_pos = first_row + jnp.arange(block_len, dtype=jnp.int32)
        key_ids = lax.dynamic_slice_in_dim(all_ids, first_row, block_len, 0).astype(jnp.float32)
        allowed = (key_pos[None, :] <= query_pos[:, None]) & (key_ids[None, :] == own_ids[:, None])
        key_block = lax.dynamic_slice_in_dim(all_keys, first_row, block_len, 0).reshape(
            block_len, HEADS, HEAD_DIM
        )
        value_block = lax.dynamic_slice_in_dim(all_values, first_row, block_len, 0).reshape(
            block_len, HEADS, HEAD_DIM
        )
        scores = jnp.einsum(
            "qhd,khd->hqk", query_rows, key_block, preferred_element_type=jnp.float32
        )
        return (allowed[None], key_block, value_block, scores)

    def max_step(state_pair, block_index):
        running_max, running_sum = state_pair
        allowed, key_block, value_block, scores = block_parts(block_index)
        masked = jnp.where(allowed, scores, -1e30)
        new_max = jnp.maximum(running_max, jnp.max(masked, axis=2))
        added = jnp.sum(jnp.where(allowed, jnp.exp(masked - new_max[..., None]), 0.0), axis=2)
        return ((new_max, running_sum * jnp.exp(running_max - new_max) + added), None)

    start_max = jnp.full((HEADS, row_count), -1e30, jnp.float32)
    start_sum = jnp.zeros((HEADS, row_count), jnp.float32)
    (top_score, exp_total), unused = lax.scan(
        max_step, (start_max, start_sum), jnp.arange(num_blocks)
    )
    log_total = top_score + jnp.log(exp_total)

    def out_step(accum, block_index):
        allowed, key_block, value_block, scores = block_parts(block_index)
        weights_low = jnp.where(allowed, jnp.exp(scores - log_total[..., None]), 0.0).astype(
            jnp.bfloat16
        )
        return (
            accum
            + jnp.einsum(
                "hqk,khd->hqd", weights_low, value_block, preferred_element_type=jnp.float32
            ),
            None,
        )

    accum_start = jnp.zeros((HEADS, row_count, HEAD_DIM), jnp.float32)
    mixed_heads, unused = lax.scan(out_step, accum_start, jnp.arange(num_blocks))
    mixed_exact = jnp.transpose(mixed_heads, (1, 0, 2))
    mixed = mixed_exact.reshape(row_count, model_width).astype(jnp.bfloat16)
    middle = inputs + jnp.dot(mixed, out_weight, preferred_element_type=jnp.float32)
    gain_two, router_weight, up_weight, down_weight = (
        lax.all_gather(gain_ffn, ("wide", "narrow"), axis=0, tiled=True),
        lax.all_gather(w_router, ("wide", "narrow"), axis=0, tiled=True),
        lax.all_gather(w_up, ("wide", "narrow"), axis=0, tiled=True),
        lax.all_gather(w_down, ("wide", "narrow"), axis=0, tiled=True),
    )
    inverse_two = rms_inverse(middle)
    normed_two = middle * inverse_two
    second_in = (normed_two * gain_two.astype(jnp.float32)).astype(jnp.bfloat16)
    logits = jnp.dot(second_in, router_weight, preferred_element_type=jnp.float32)
    router_probs = jax.nn.softmax(logits, axis=-1)
    experts = logits.shape[1]
    choose = routes[:, :, None] == jnp.arange(experts, dtype=jnp.int32)[None, None, :]
    member = jnp.sum(choose.astype(jnp.float32), axis=1)
    earlier = (jnp.arange(row_count)[:, None] > jnp.arange(row_count)[None, :]).astype(jnp.bfloat16)
    before = jnp.dot(earlier, member.astype(jnp.bfloat16), preferred_element_type=jnp.float32)
    slot_hit = (member.T[:, None, :] > 0.5) & (
        before.T[:, None, :] == jnp.arange(capacity, dtype=jnp.float32)[None, :, None]
    )
    dispatch = slot_hit.astype(jnp.bfloat16)
    gathered_in = jnp.einsum(
        "ect,td->ecd", dispatch, second_in, preferred_element_type=jnp.float32
    ).astype(jnp.bfloat16)
    gate_weights = router_probs * member
    gate_up = jnp.einsum(
        "ecd,def->ecf", gathered_in, up_weight[:, 1:], preferred_element_type=jnp.float32
    )
    gate_part = gate_up[..., :hidden]
    up_part = gate_up[..., hidden:]
    activated = (jax.nn.silu(gate_part) * up_part).astype(jnp.bfloat16)
    expert_rows = jnp.einsum(
        "ecf,def->ecd", activated, down_weight[:, 1:], preferred_element_type=jnp.float32
    ).astype(jnp.bfloat16)
    selected = jnp.einsum("ect,ecd->etd", dispatch, expert_rows, preferred_element_type=jnp.float32)
    routed = jnp.sum(gate_weights.T[:, :, None] * selected, axis=0)
    shared_up = jnp.dot(second_in, up_weight[:, 0], preferred_element_type=jnp.float32)
    shared_gate = shared_up[:, :hidden]
    shared_lin = shared_up[:, hidden:]
    shared_act = (jax.nn.silu(shared_gate) * shared_lin).astype(jnp.bfloat16)
    shared_out = jnp.einsum(
        "tf,df->td", shared_act, down_weight[:, 0], preferred_element_type=jnp.float32
    )
    output = (middle + shared_out + routed).astype(jnp.bfloat16)
    gain_two, router_weight, up_weight, down_weight = (
        lax.all_gather(gain_ffn, ("wide", "narrow"), axis=0, tiled=True),
        lax.all_gather(w_router, ("wide", "narrow"), axis=0, tiled=True),
        lax.all_gather(w_up, ("wide", "narrow"), axis=0, tiled=True),
        lax.all_gather(w_down, ("wide", "narrow"), axis=0, tiled=True),
    )
    grad_output = cotangent.astype(jnp.float32)
    slot_token = jnp.sum(
        jnp.where(slot_hit, jnp.arange(row_count, dtype=jnp.int32)[None, None, :], 0), axis=2
    )
    slot_gate = jnp.sum(jnp.where(slot_hit, gate_weights.T[:, None, :], 0.0), axis=2)
    grad_rows = (slot_gate[..., None] * grad_output[slot_token]).astype(jnp.bfloat16)
    grad_probs = jnp.sum(selected * grad_output[None], axis=2).T * member
    grad_logits = (
        router_probs * (grad_probs - jnp.sum(router_probs * grad_probs, axis=1, keepdims=True))
    ).astype(jnp.bfloat16)
    grad_act = jnp.einsum(
        "ecd,def->ecf", grad_rows, down_weight[:, 1:], preferred_element_type=jnp.float32
    )
    sigmoid_gate = jax.nn.sigmoid(gate_part)
    grad_gate_up = jnp.concatenate(
        [
            grad_act * up_part * sigmoid_gate * (1.0 + gate_part * (1.0 - sigmoid_gate)),
            grad_act * jax.nn.silu(gate_part),
        ],
        axis=-1,
    ).astype(jnp.bfloat16)
    grad_gathered = jnp.einsum(
        "ecf,def->ecd", grad_gate_up, up_weight[:, 1:], preferred_element_type=jnp.float32
    )
    slot_index = jnp.sum(jnp.where(choose, before[:, None, :], 0.0), axis=2).astype(jnp.int32)
    flat_index = routes * capacity + slot_index
    grad_second = jnp.sum(grad_gathered.reshape(-1, model_width)[flat_index], axis=1)
    grad_shared_act = jnp.einsum(
        "td,df->tf", cotangent, down_weight[:, 0], preferred_element_type=jnp.float32
    )
    sigmoid_shared = jax.nn.sigmoid(shared_gate)
    grad_shared_up = jnp.concatenate(
        [
            grad_shared_act
            * shared_lin
            * sigmoid_shared
            * (1.0 + shared_gate * (1.0 - sigmoid_shared)),
            grad_shared_act * jax.nn.silu(shared_gate),
        ],
        axis=-1,
    ).astype(jnp.bfloat16)
    grad_second = grad_second + jnp.einsum(
        "tf,df->td", grad_shared_up, up_weight[:, 0], preferred_element_type=jnp.float32
    )
    grad_second = grad_second + jnp.einsum(
        "te,de->td", grad_logits, router_weight, preferred_element_type=jnp.float32
    )
    grad_normed_two = grad_second * gain_two.astype(jnp.float32)
    grad_gain_two = jnp.sum(grad_second * normed_two, axis=0)
    grad_middle = grad_output + inverse_two * (
        grad_normed_two
        - normed_two * jnp.mean(grad_normed_two * normed_two, axis=-1, keepdims=True)
    )
    grad_router = jnp.einsum(
        "td,te->de", second_in, grad_logits, preferred_element_type=jnp.float32
    )
    narrow_rows = model_width // lax.axis_size("narrow")
    routed_cols, grad_cols, shared_cols, cotangent_cols = (
        lax.all_to_all(gathered_in, "narrow", split_axis=2, concat_axis=1, tiled=True),
        lax.all_to_all(grad_rows, "narrow", split_axis=2, concat_axis=1, tiled=True),
        lax.all_to_all(second_in[None], "narrow", split_axis=2, concat_axis=1, tiled=True),
        lax.all_to_all(cotangent[None], "narrow", split_axis=2, concat_axis=1, tiled=True),
    )
    slot_grads, slot_acts, shared_grads, shared_acts = (
        lax.all_gather(grad_gate_up, "narrow", axis=1, tiled=True),
        lax.all_gather(activated, "narrow", axis=1, tiled=True),
        lax.all_gather(grad_shared_up[None], "narrow", axis=1, tiled=True),
        lax.all_gather(shared_act[None], "narrow", axis=1, tiled=True),
    )
    expert_grads = expert_weight_terms(
        routed_cols,
        grad_cols,
        shared_cols[0],
        cotangent_cols[0],
        slot_grads,
        slot_acts,
        shared_grads[0],
        shared_acts[0],
    )
    gain_one, qkv_weight, out_weight = (
        lax.all_gather(gain_attn, ("wide", "narrow"), axis=0, tiled=True),
        lax.all_gather(w_qkv, ("wide", "narrow"), axis=0, tiled=True),
        lax.all_gather(w_out, ("wide", "narrow"), axis=0, tiled=True),
    )
    grad_attention = grad_middle.astype(jnp.bfloat16)
    grad_out_weight = jnp.einsum(
        "td,te->de", mixed, grad_attention, preferred_element_type=jnp.float32
    )
    grad_mixed = jnp.einsum(
        "te,de->td", grad_attention, out_weight, preferred_element_type=jnp.float32
    ).astype(jnp.bfloat16)
    grad_heads = grad_mixed.reshape(row_count, HEADS, HEAD_DIM)
    row_delta = jnp.sum(grad_heads.astype(jnp.float32) * mixed_exact, axis=2).T

    def back_step(grad_query, block_index):
        allowed, key_block, value_block, scores = block_parts(block_index)
        weights_exact = jnp.where(allowed, jnp.exp(scores - log_total[..., None]), 0.0)
        weights_low = weights_exact.astype(jnp.bfloat16)
        grad_value = jnp.einsum(
            "hqk,qhd->khd", weights_low, grad_heads, preferred_element_type=jnp.float32
        )
        grad_weights = jnp.einsum(
            "qhd,khd->hqk", grad_heads, value_block, preferred_element_type=jnp.float32
        )
        grad_scores = (weights_exact * (grad_weights - row_delta[..., None])).astype(jnp.bfloat16)
        grad_query = grad_query + jnp.einsum(
            "hqk,khd->qhd", grad_scores, key_block, preferred_element_type=jnp.float32
        )
        grad_key = jnp.einsum(
            "hqk,qhd->khd", grad_scores, query_rows, preferred_element_type=jnp.float32
        )
        return (
            grad_query,
            (grad_key.reshape(block_len, model_width), grad_value.reshape(block_len, model_width)),
        )

    query_start = jnp.zeros((row_count, HEADS, HEAD_DIM), jnp.float32)
    grad_query, (key_blocks, value_blocks) = lax.scan(
        back_step, query_start, jnp.arange(num_blocks)
    )
    key_partial = key_blocks.reshape(seqlen, model_width)
    value_partial = value_blocks.reshape(seqlen, model_width)
    grad_keys, grad_values = (
        lax.psum_scatter(
            key_partial.astype(jnp.bfloat16), "narrow", scatter_dimension=0, tiled=True
        ).astype(jnp.float32),
        lax.psum_scatter(
            value_partial.astype(jnp.bfloat16), "narrow", scatter_dimension=0, tiled=True
        ).astype(jnp.float32),
    )
    grad_query_raw = rotate_back(grad_query, cosine, sine_table) * query_scale
    grad_key_raw = rotate_back(grad_keys.reshape(row_count, HEADS, HEAD_DIM), cosine, sine_table)
    grad_projected = jnp.concatenate(
        [
            grad_query_raw.reshape(row_count, model_width),
            grad_key_raw.reshape(row_count, model_width),
            grad_values,
        ],
        axis=1,
    ).astype(jnp.bfloat16)
    grad_qkv_weight = jnp.einsum(
        "td,tf->df", first_in, grad_projected, preferred_element_type=jnp.float32
    )
    grad_first = jnp.einsum(
        "tf,df->td", grad_projected, qkv_weight, preferred_element_type=jnp.float32
    )
    grad_normed_one = grad_first * gain_one.astype(jnp.float32)
    grad_gain_one = jnp.sum(grad_first * normed_one, axis=0)
    grad_inputs = grad_middle + inverse_one * (
        grad_normed_one
        - normed_one * jnp.mean(grad_normed_one * normed_one, axis=-1, keepdims=True)
    )
    dense_parts = (
        lax.psum_scatter(
            grad_gain_one.astype(jnp.bfloat16), "narrow", scatter_dimension=0, tiled=True
        ).astype(jnp.float32),
        lax.psum_scatter(
            grad_qkv_weight.astype(jnp.bfloat16), "narrow", scatter_dimension=0, tiled=True
        ).astype(jnp.float32),
        lax.psum_scatter(
            grad_out_weight.astype(jnp.bfloat16), "narrow", scatter_dimension=0, tiled=True
        ).astype(jnp.float32),
        lax.psum_scatter(
            grad_gain_two.astype(jnp.bfloat16), "narrow", scatter_dimension=0, tiled=True
        ).astype(jnp.float32),
        lax.psum_scatter(
            grad_router.astype(jnp.bfloat16), "narrow", scatter_dimension=0, tiled=True
        ).astype(jnp.float32),
    )
    summed = jax.tree.map(
        lambda part: part.astype(jnp.float32),
        lax.psum(shortened((expert_grads,) + tuple(dense_parts)), "wide"),
    )
    expert_grads = summed[0]
    dense_parts = summed[1:]
    gain_one_sum, qkv_sum, out_sum, gain_two_sum, router_sum = dense_parts
    expert_table = expert_grads.reshape(narrow_rows, up_weight.shape[1], 3 * hidden)
    up_sum = expert_table[:, :, : 2 * hidden]
    down_sum = expert_table[:, :, 2 * hidden :]
    return (
        output,
        grad_inputs.astype(jnp.bfloat16),
        gain_one_sum,
        qkv_sum,
        out_sum,
        gain_two_sum,
        router_sum,
        up_sum,
        down_sum,
    )


PLANES = 4
WINDOW = 3
STARTS = (0, 3, 6, 7)
KEEP = ((0, 3), (0, 3), (0, 2), (1, 3))
MESH_IDS = pl.DeviceIdType.MESH
BF16 = jnp.bfloat16
F32 = jnp.float32


def place():
    w = lax.axis_index("wide")
    z = lax.axis_index("narrow")
    return w, z


def greet(w, z):
    barrier = pltpu.get_barrier_semaphore()
    peers = [(w, lax.rem(z + step, PLANES)) for step in (1, 2, 3)]
    peers += [(w ^ flip, z) for flip in (1, 2, 4, 6)]
    for peer in peers:
        pl.semaphore_signal(barrier, inc=1, device_id=peer, device_id_type=MESH_IDS)
    pl.semaphore_wait(barrier, len(peers))


def mul(a, b, over_a, over_b):
    return lax.dot_general(a, b, (((over_a,), (over_b,)), ((), ())), preferred_element_type=F32)


def at(start, size):
    return pl.ds(pl.multiple_of(start, 128), size)


def loop(first, last, body):
    def step(i, carry):
        body(i)
        return carry

    lax.fori_loop(first, last, step, 0)


class Links:
    def __init__(self, send_sems, recv_sems):
        self.w, self.z = place()
        self.send_sems, self.recv_sems = send_sems, recv_sems

    def copy(self, kind, step, src, dst, device):
        return pltpu.make_async_remote_copy(
            src_ref=src,
            dst_ref=dst,
            send_sem=self.send_sems.at[kind, step],
            recv_sem=self.recv_sems.at[kind, step],
            device_id=device,
            device_id_type=MESH_IDS,
        )

    def plane(self, step, sign):
        return lax.rem(self.z + PLANES + sign * step, PLANES)


def step_at(z, turn):
    step = 0
    for plane, steps in enumerate(((3, 2, 1, 0), (1, 3, 2, 0), (3, 1, 2, 0), (1, 2, 3, 0))):
        for number, value in enumerate(steps):
            step = jnp.where((z == plane) & (turn == number), value, step)
    return step


def direct_at(z, turn):
    even = lax.rem(z, 2) == 0
    first, second = jnp.where(even, 3, 1), jnp.where(even, 1, 3)
    return jnp.where(turn == 0, first, jnp.where(turn == 1, second, jnp.where(turn == 2, 2, 0)))


def send_next(z, send):
    @pl.when(z < PLANES - 1)
    def _():
        send(1)

    @pl.when(z > 0)
    def _():
        send(3)


def send_beyond(z, send):
    @pl.when(z == 0)
    def _():
        send(3)

    @pl.when(z == PLANES - 1)
    def _():
        send(1)

    send(2)


class Chain:
    def __init__(self, links, base, own, slot):
        self.links, self.base, self.own, self.slot = links, base, own, slot

    def goes(self, step, up):
        z = self.links.z
        if up:
            return (z >= step) & (z < PLANES - 1)
        return ((z < step) | (step == 0)) & (z > 0)

    def ring(self, step, up, own=False):
        links = self.links
        to = lax.rem(step + 1, 4) if up else lax.rem(step + 3, 4)
        ref = self.slot(links.plane(step, -1))
        return pltpu.make_async_remote_copy(
            src_ref=self.own if own else ref,
            dst_ref=ref,
            send_sem=links.send_sems.at[self.base if up else self.base + 1, step],
            recv_sem=links.recv_sems.at[self.base, to],
            device_id=(links.w, links.z + 1 if up else links.z - 1),
            device_id_type=MESH_IDS,
        )

    def hand_on(self, step, own=False):
        for up in (True, False):

            @pl.when(self.goes(step, up))
            def _():
                self.ring(step, up, own).start()

    def begin(self):
        self.hand_on(0, True)

    def arrive(self, turn):
        step = step_at(self.links.z, turn)
        ref = self.slot(self.links.plane(step, -1))
        self.links.copy(self.base, step, ref, ref, (self.links.w, self.links.z)).wait_recv()
        self.hand_on(step)

    def settle(self):
        def body(step):
            for up in (True, False):

                @pl.when(self.goes(step, up))
                def _():
                    self.ring(step, up).wait_send()

        loop(0, 4, body)


class Gather:
    def __init__(self, links, base, step, turn, slot, cores=True, half=0):
        self.links, self.base, self.step, self.slot, self.cores = links, base, step, slot, cores
        self.half = half
        self.first = 1 + lax.rem(turn, 2)
        self.second = 3 - self.first

    def copy(self, kind, owner, flip):
        ref = self.slot(owner)
        return self.links.copy(
            self.base + kind, self.step, ref, ref, (self.links.w ^ flip, self.links.z)
        )

    def begin(self):
        w = self.links.w
        self.copy(0, w, 2).start()
        self.copy(1, w, 4).start()
        if self.cores:
            self.copy(4, w, 1).start()

    def relay(self):
        w = self.links.w
        self.copy(0, w, 2).wait_recv()
        self.copy(1, w, 4).wait_recv()
        for copy in self.across():
            copy.start()
        if self.cores:
            self.copy(3, w ^ 2, 1).start()
            self.copy(5, w ^ 4, 1).start()

    def across(self):
        if not self.half:
            return [self.copy(2, self.links.w ^ (2 * self.first), 2 * self.second)]
        copies = []
        for kind, flip in ((2, 2), (7, 4)):
            ref = self.slot(self.links.w ^ flip).at[pl.ds((kind == 7) * self.half, self.half)]
            copies.append(
                self.links.copy(
                    self.base + kind, self.step, ref, ref, (self.links.w ^ (6 - flip), self.links.z)
                )
            )
        return copies

    def end(self):
        for copy in self.across():
            copy.wait_recv()
        if self.cores:
            self.copy(6, self.links.w ^ 6, 1).start()

    def settle(self):
        w = self.links.w
        self.copy(0, w, 2).wait_send()
        self.copy(1, w, 4).wait_send()
        for copy in self.across():
            copy.wait_send()
        if self.cores:
            for kind, owner in ((4, w), (3, w ^ 2), (5, w ^ 4), (6, w ^ 6)):
                copy = self.copy(kind, owner, 1)
                copy.wait_send()
                copy.wait_recv()


def softmax_rows(scores, mask):
    masked = scores + mask
    powers = jnp.exp(masked - jnp.max(masked, axis=1, keepdims=True))
    return powers * (1.0 / jnp.sum(powers, axis=1, keepdims=True))


def start_kernel(
    tok_in, wq_in, wo_in, seq_in, routes_in, misc_in, up_in, down_in, cot_in, cos_in, sin_in,
    we_o, cot_o, wq_out, wo_out, first_out, qkv_out, exact_out, mixed_out, mixed_rows_o, middle_o,
    second_o, hop,
    tok, ids, wq_blocks, wo_blocks, staged, mask, mixed_got, mixed_send, ids_in, we_in, cot_full,
    wq_o, wo_o, first_o, qkv_o, exact_o, mixed_o,
    load_sems, out_sems, send_sems, recv_sems,
):
    links = Links(send_sems, recv_sems)
    w, z = links.w, links.z
    chip = w // 2
    rows, width = tok_in.shape
    seqlen = PLANES * rows
    size = WINDOW * HEAD_DIM
    own = wo_in.shape[0]
    keeps = [
        pltpu.make_async_copy(src, dst, load_sems.at[i])
        for i, (src, dst) in enumerate(
            (
                (tok_in, tok.at[z]),
                (wo_in, wo_blocks.at[w, z]),
                (cot_full, cot_o.at[chip, z]),
            )
        )
    ]
    for keep in keeps[:2]:
        keep.start()
    window_starts = [jnp.int32(0)] * 4
    for plane, begin in enumerate(STARTS):
        for step in range(4):
            window_starts[step] = jnp.where(
                lax.rem(z + step, PLANES) == plane, begin, window_starts[step]
            )

    def window(step, kind):
        return wq_in.at[:, at(kind * width + window_starts[step] * HEAD_DIM, size)]

    def wq_own(kind):
        return pltpu.make_async_copy(
            window(0, kind),
            wq_blocks.at[w, z, :, pl.ds(kind * size, size)],
            load_sems.at[3 + kind],
        )

    for kind in range(3):
        wq_own(kind).start()
    wq_blocks[w, z, :, 3 * size :] = misc_in[...]
    row_ids = jnp.broadcast_to(seq_in[...].astype(F32), (rows, rows))
    ids_in[:rows, :] = row_ids.astype(BF16)
    ids_in[rows:, :] = jnp.transpose(row_ids).astype(BF16)
    ids[z] = ids_in[...]
    greet(w, z)

    tok_chain = Chain(links, 0, tok_in, lambda p: tok.at[p])
    ids_chain = Chain(links, 2, ids_in, lambda p: ids.at[p])
    wo_chain = Chain(links, 4, wo_in, lambda p: wo_blocks.at[w, p])
    cot_chain = Chain(links, 6, cot_full, lambda p: cot_o.at[chip, p])

    def wq_ring(step, kind):
        to = links.plane(step, 1)
        here = wq_blocks.at[w, z, :, pl.ds(kind * size, size if kind < 3 else 128)]
        src = window(step, kind) if kind < 3 else misc_in
        return links.copy(39 + kind if kind else 8, step, src, here, (w, to))

    def wq_gather(step):
        source = links.plane(step, -1)
        return Gather(links, 9, step, step, lambda i: wq_blocks.at[i, source])

    def wo_gather(turn):
        step = step_at(z, turn)
        source = links.plane(step, -1)
        return Gather(links, 16, step, turn, lambda i: wo_blocks.at[i, source])

    def cot_gather(turn):
        step = step_at(z, turn)
        source = links.plane(step, -1)
        return Gather(links, 23, step, turn, lambda i: cot_o.at[i // 2, source], False)

    def weights_ring(step, flip):
        to = links.plane(step, 1)
        return links.copy(
            26 + flip, step, we_in.at[to, chip ^ flip], hop.at[step - 1, chip ^ flip], (w, to)
        )

    def weights_step(turn):
        return 0 if turn == 3 else direct_at(z, turn)

    def weights_block(turn, flip):
        if turn == 3:
            return we_in.at[z, chip ^ flip]
        return hop.at[weights_step(turn) - 1, chip ^ flip]

    def weights_place(turn, owner):
        return we_o.at[owner, links.plane(weights_step(turn), -1)]

    def weights_plane(turn, flip):
        to = (w ^ (2 * flip), z)
        return links.copy(
            29 + flip, turn, weights_block(turn, flip), weights_place(turn, w), to
        )

    def weights_keep(turn):
        return pltpu.make_async_copy(
            weights_block(turn, 0), weights_place(turn, w), load_sems.at[6 + turn]
        )

    def weights_core(turn, flip):
        block = weights_place(turn, w ^ (2 * flip))
        return links.copy(
            34 + flip, turn, block if flip else weights_block(turn, 0), block, (w ^ 1, z)
        )

    def weights_send(step):
        for flip in (3, 1, 2, 0):
            weights_ring(step, flip).start()

    def weights_next(turn):
        for flip in (3, 1, 2):
            if turn < 3:
                weights_ring(weights_step(turn), flip).wait_recv()
            weights_plane(turn, flip).start()
        if turn < 3:
            weights_ring(weights_step(turn), 0).wait_recv()
        weights_core(turn, 0).start()
        weights_keep(turn).start()

    def weights_end(turn):
        for flip in (1, 2, 3):
            weights_plane(turn, flip).wait_recv()
            weights_core(turn, flip).start()

    def mixed_ring(step):
        to = links.plane(step, 1)
        return links.copy(38, step, mixed_send.at[to], mixed_got.at[z], (w, to))

    tok_chain.begin()
    ids_chain.begin()
    for step in (1, 2, 3):
        for kind in range(4):
            wq_ring(step, kind).start()
    for kind in range(3):
        wq_own(kind).wait()
    wq_gather(0).begin()
    for keep in keeps[:2]:
        keep.wait()

    lane = lax.broadcasted_iota(jnp.int32, (rows, 128), 1)
    member = lane == 0
    for route in range(routes_in.shape[1]):
        member = member | (lane == routes_in[:, route : route + 1] + 1)
    cot_full[:, :width] = cot_in[...]
    cot_full[:, width:] = member.astype(F32).astype(BF16)
    keeps[2].start()
    tok_chain.arrive(0)
    ids_chain.arrive(0)
    for step in (1, 2, 3):
        for kind in range(4):
            wq_ring(step, kind).wait_recv()
        wq_gather(step).begin()
    wo_chain.begin()
    tok_chain.arrive(1)
    ids_chain.arrive(1)
    cot_chain.begin()

    def experts_first(source, low):
        for i in range(0, source.shape[2], 128):
            part = jnp.swapaxes(source[:, :, i : i + 128].astype(F32), 0, 1).astype(BF16)
            for expert in range(source.shape[1]):
                we_in[expert % PLANES, expert // PLANES, :, low + i : low + i + 128] = part[expert]

    end_plane = (z == 0) | (z == PLANES - 1)

    @pl.when(jnp.logical_not(end_plane))
    def _():
        tok_chain.arrive(2)
        ids_chain.arrive(2)

    loop(0, 4, lambda step: wq_gather(step).relay())
    experts_first(up_in, 0)
    experts_first(down_in, up_in.shape[2])

    @pl.when(end_plane)
    def _():
        tok_chain.arrive(2)
        ids_chain.arrive(2)
        send_next(z, weights_send)

    wo_chain.arrive(0)
    wo_gather(0).begin()
    wo_gather(3).begin()
    keeps[2].wait()
    cot_gather(3).begin()
    weights_next(3)
    for i in range(PLANES):
        for j in range(PLANES):
            here = (slice(i * rows, (i + 1) * rows), slice(j * rows, (j + 1) * rows))
            if j > i:
                mask[here] = jnp.full((rows, rows), -1e30, F32)
            else:
                same = ids[i, rows:, :].astype(F32) == ids[j, :rows, :].astype(F32)
                if i == j:
                    same = same & (
                        lax.broadcasted_iota(jnp.int32, (rows, rows), 1)
                        <= lax.broadcasted_iota(jnp.int32, (rows, rows), 0)
                    )
                mask[here] = jnp.where(same, 0.0, -1e30)
    loop(0, 4, lambda step: wq_gather(step).end())
    loop(0, 4, lambda step: wq_gather(step).settle())

    def assemble(blocks, to):
        def body(i):
            for p in range(PLANES):
                staged[p * own : (p + 1) * own, :] = blocks[i, p].astype(F32)
            span = PLANES * own
            to[pl.ds(pl.multiple_of(i * span, 16), span), :] = staged[...].astype(BF16)

        loop(0, blocks.shape[0], body)

    cot_chain.arrive(0)
    cot_gather(0).begin()
    outputs = [
        pltpu.make_async_copy(src, dst, out_sems.at[i])
        for i, (src, dst) in enumerate(
            (
                (wq_o, wq_out),
                (first_o, first_out),
                (qkv_o, qkv_out),
                (exact_o, exact_out),
                (mixed_o, mixed_out),
                (wo_o, wo_out),
            )
        )
    ]
    assemble(wq_blocks, wq_o)
    outputs[0].start()
    gains = jnp.transpose(wq_o[:, size * 3 :].astype(F32))
    gain_one = gains[16:17, :]
    gain_two = gains[17:18, :]

    def normalise(p):
        block = tok[p].astype(F32)
        inverse = lax.rsqrt(jnp.mean(block * block, axis=1, keepdims=True) + epsilon)
        first_o[p] = (block * inverse * gain_one).astype(BF16)

    loop(0, PLANES, normalise)
    outputs[1].start()
    wo_chain.arrive(1)
    wo_gather(1).begin()
    cot_chain.arrive(1)
    cot_gather(1).begin()

    def project(p):
        span = pl.ds(pl.multiple_of(p * rows, 128), rows)
        cosine, sine = cos_in[span, :], sin_in[span, :]
        for kind in range(3):
            part = mul(first_o[p], wq_o[:, kind * size : (kind + 1) * size], 1, 0)
            for head in range(WINDOW):
                here = part[:, head * HEAD_DIM : (head + 1) * HEAD_DIM]
                if kind < 2:
                    here = here * cosine + pltpu.roll(here, HEAD_DIM // 2, 1) * sine
                if kind == 0:
                    here = here * (HEAD_DIM ** (-0.5))
                qkv_o[kind, head, span, :] = here.astype(BF16)

    loop(0, PLANES, project)
    outputs[2].start()
    wo_chain.arrive(2)
    wo_gather(2).begin()
    cot_chain.arrive(2)
    cot_gather(2).begin()

    @pl.when(jnp.logical_not(end_plane))
    def _():
        send_next(z, weights_send)

    def attend(head):
        exact = softmax_rows(mul(qkv_o[0, head], qkv_o[1, head], 1, 1), mask[...])
        exact_o[head] = exact
        mixed_o[head] = mul(exact.astype(BF16), qkv_o[2, head], 1, 0)

    loop(0, WINDOW, attend)
    outputs[3].start()
    outputs[4].start()
    for p in range(PLANES):
        for head in range(WINDOW):
            mixed_send[p, :, head * HEAD_DIM : (head + 1) * HEAD_DIM] = mixed_o[
                head, p * rows : (p + 1) * rows, :
            ].astype(BF16)
    for step in (1, 2, 3):
        mixed_ring(step).start()
    mixed_got[z] = mixed_send[z]
    send_beyond(z, weights_send)
    loop(0, 4, lambda turn: wo_gather(turn).relay())
    weights_next(0)
    loop(0, 4, lambda turn: wo_gather(turn).end())
    loop(0, 4, lambda turn: cot_gather(turn).relay())
    weights_end(3)
    weights_end(0)
    loop(0, 4, lambda turn: wo_gather(turn).settle())
    assemble(wo_blocks, wo_o)
    outputs[5].start()
    for step in (1, 2, 3):
        mixed_ring(step).wait_recv()
    column = 0
    for p, (a, b) in enumerate(KEEP):
        span = (b - a) * HEAD_DIM
        mixed_rows_o[:, column : column + span] = mixed_got[p, :, a * HEAD_DIM : b * HEAD_DIM]
        column += span

    def out_project(i):
        here = at(i * 256, 256)
        middle_o[:, here] = tok_in_f32(tok, z, here) + mul(mixed_rows_o[...], wo_o[:, here], 1, 0)

    loop(0, width // 256, out_project)
    middle = middle_o[...]
    inverse = lax.rsqrt(jnp.mean(middle * middle, axis=1, keepdims=True) + epsilon)
    second_o[...] = (middle * inverse * gain_two).astype(BF16)
    loop(0, 4, lambda turn: cot_gather(turn).end())
    weights_next(1)
    weights_next(2)
    weights_end(1)
    weights_end(2)
    loop(0, 4, lambda turn: cot_gather(turn).settle())
    for output in outputs:
        output.wait()
    for chain in (tok_chain, ids_chain, wo_chain, cot_chain):
        chain.settle()
    for step in (0, 1, 2, 3):
        weights_keep(step).wait()
        for flip in (0, 1, 2, 3):
            if step:
                weights_ring(step, flip).wait_send()
            if flip:
                weights_plane(step, flip).wait_send()
            weights_core(step, flip).wait_send()
            weights_core(step, flip).wait_recv()
        if step:
            for kind in range(4):
                wq_ring(step, kind).wait_send()
            mixed_ring(step).wait_send()


def tok_in_f32(tok, z, here):
    return tok[z, :, here].astype(F32)


def start(tok, wq, wo, seq, routes, misc, up, down, cot, tables, collective):
    rows, width = tok.shape
    own = wo.shape[0]
    experts = up.shape[1]
    hidden3 = up.shape[2] + down.shape[2]
    seqlen = PLANES * rows
    size = WINDOW * HEAD_DIM
    blocks = (8, PLANES, own, width)
    any_spec = pl.BlockSpec(memory_space=pl.ANY)
    vmem_spec = pl.BlockSpec(memory_space=pltpu.VMEM)
    kept = [
        ((width, width), BF16),
        ((width, width), BF16),
        ((PLANES, rows, width), BF16),
        ((3, WINDOW, seqlen, HEAD_DIM), BF16),
        ((WINDOW, seqlen, seqlen), F32),
        ((WINDOW, seqlen, HEAD_DIM), F32),
    ]
    shapes = [
        ((8, PLANES, own, hidden3), BF16),
        ((4, PLANES, rows, width + 128), BF16),
        *kept,
        ((rows, width), BF16),
        ((rows, width), F32),
        ((rows, width), BF16),
        ((3, 4, own, hidden3), BF16),
    ]
    return pl.pallas_call(
        start_kernel,
        out_shape=[jax.ShapeDtypeStruct(shape, kind) for shape, kind in shapes],
        in_specs=[any_spec] * 3 + [vmem_spec] * 8,
        out_specs=[any_spec] * 8 + [vmem_spec] * 3 + [any_spec],
        scratch_shapes=[
            pltpu.VMEM((PLANES, rows, width), BF16),
            pltpu.VMEM((PLANES, 2 * rows, rows), BF16),
            pltpu.VMEM(blocks, BF16),
            pltpu.VMEM(blocks, BF16),
            pltpu.VMEM((PLANES * own, width), F32),
            pltpu.VMEM((seqlen, seqlen), F32),
            pltpu.VMEM((PLANES, rows, size), BF16),
            pltpu.VMEM((PLANES, rows, size), BF16),
            pltpu.VMEM((2 * rows, rows), BF16),
            pltpu.VMEM((PLANES, experts // PLANES, own, hidden3), BF16),
            pltpu.VMEM((rows, width + 128), BF16),
            *[pltpu.VMEM(shape, kind) for shape, kind in kept],
            pltpu.SemaphoreType.DMA((10,)),
            pltpu.SemaphoreType.DMA((6,)),
            pltpu.SemaphoreType.DMA((43, 4)),
            pltpu.SemaphoreType.DMA((43, 4)),
        ],
        compiler_params=pltpu.CompilerParams(
            collective_id=collective, has_side_effects=True, vmem_limit_bytes=60 * 2**20
        ),
        name="start",
    )(tok, wq, wo, seq, routes, misc, up, down, cot, *tables)[:-1]


def add_blocks(out, *terms):
    rows = out.shape[0]

    def body(i, carry):
        part = pl.ds(pl.multiple_of(i * 16, 16), 16)
        total = terms[0][part, :].astype(F32)
        for term in terms[1:]:
            total = total + term[part, :].astype(F32)
        out[part, :] = total.astype(out.dtype)
        return carry

    lax.fori_loop(0, rows // 16, body, 0)


def experts_kernel(
    x_in, cot_in, weights_in, misc_in, grads_o, outs_o, outs_one_o, sums_o,
    x, cot, weights, misc, act, scaled, slopes, gate, outs, parts, got_one, got_two, got_far, stage,
    load_sems, send_sems, recv_sems,
):
    w, z = place()
    chip = w // 2
    expert = chip * PLANES + z
    rows, width = x_in.shape
    hidden = weights.shape[1] // 3
    group_rows = 4 * rows

    def remote(kind, step, src, dst, device):
        return pltpu.make_async_remote_copy(
            src_ref=src,
            dst_ref=dst,
            send_sem=send_sems.at[kind, step],
            recv_sem=recv_sems.at[kind, step],
            device_id=device,
            device_id_type=MESH_IDS,
        )

    def plane_of(step, sign):
        return lax.rem(z + PLANES + sign * step, PLANES)

    def step_at(turn):
        step = 0
        for plane, steps in enumerate(((3, 2, 1, 0), (1, 3, 2, 0), (3, 1, 2, 0), (1, 2, 3, 0))):
            for number, value in enumerate(steps):
                step = jnp.where((z == plane) & (turn == number), value, step)
        return step

    def axes(turn):
        first = 1 + lax.rem(turn, 2)
        return first, 3 - first

    def ring(step, up):
        to = lax.rem(step + 1, 4) if up else lax.rem(step + 3, 4)
        return pltpu.make_async_remote_copy(
            src_ref=x.at[step, chip],
            dst_ref=x.at[to, chip],
            send_sem=send_sems.at[0 if up else 8, step],
            recv_sem=recv_sems.at[0, to],
            device_id=(w, z + 1 if up else z - 1),
            device_id_type=MESH_IDS,
        )

    def goes(step, up):
        if up:
            return (z >= step) & (z < PLANES - 1)
        return ((z < step) | (step == 0)) & (z > 0)

    def pass_on(step):
        for up in (True, False):

            @pl.when(goes(step, up))
            def _():
                ring(step, up).start()

    def arrive(step):
        pltpu.make_async_remote_copy(
            src_ref=x.at[step, chip],
            dst_ref=x.at[step, chip],
            send_sem=send_sems.at[0, step],
            recv_sem=recv_sems.at[0, step],
            device_id=(w, z),
            device_id_type=MESH_IDS,
        ).wait_recv()

    def direct(step, flip):
        block = x.at[step, chip]
        return remote(flip, step, block, block, (w ^ (2 * flip), z))

    def across(turn):
        first, second = axes(turn)
        step = step_at(turn)
        block = x.at[step, chip ^ first]
        return remote(3, step, block, block, (w ^ (2 * second), z))

    def near(turn, which):
        first, _ = axes(turn)
        step = step_at(turn)
        block = chip ^ 3 if which else chip ^ first
        return remote(
            4 + which, step, parts.at[step, block], got_one.at[step, which], (w ^ (2 * first), z)
        )

    def cross(turn):
        _, second = axes(turn)
        step = step_at(turn)
        return remote(
            6, step, parts.at[step, chip ^ second], got_two.at[step], (w ^ (2 * second), z)
        )

    def far(step):
        return remote(7, step, parts.at[step, chip], got_far.at[step - 1], (w, plane_of(step, -1)))

    def outs_near(step, which):
        first, _ = axes(step)
        block = chip ^ 3 if which else chip ^ first
        return remote(
            9 + which, step, outs_o.at[step, block], outs_one_o.at[step, which], (w ^ (2 * first), z)
        )

    def cot_load(step):
        return pltpu.make_async_copy(
            cot_in.at[:, plane_of(step, -1)], cot.at[step], load_sems.at[step]
        )

    def outs_out(turn):
        return pltpu.make_async_copy(
            outs.at[lax.rem(turn, 2)], outs_o.at[step_at(turn)], load_sems.at[9 + lax.rem(turn, 2)]
        )

    def grads_out(low, size, slot):
        return pltpu.make_async_copy(
            stage.at[slot, :, pl.ds(0, size)], grads_o.at[:, low], load_sems.at[4 + slot]
        )

    loads = [
        pltpu.make_async_copy(src, dst, load_sems.at[6 + i])
        for i, (src, dst) in enumerate(
            (
                (x_in, x.at[0, chip]),
                (misc_in.at[:, pl.ds(misc_in.shape[1] - 128, 128)], misc),
                (weights_in, weights),
            )
        )
    ]
    for load in loads:
        load.start()
    loop(0, 4, lambda step: cot_load(step).start())
    greet(w, z)
    loads[0].wait()
    pass_on(0)

    def begin(turn):
        step = step_at(turn)

        @pl.when(turn < 3)
        def _():
            arrive(step)
            pass_on(step)

        direct(step, 1).start()
        direct(step, 2).start()

    def relay(turn):
        step = step_at(turn)
        direct(step, 1).wait_recv()
        direct(step, 2).wait_recv()
        across(turn).start()

    begin(0)
    begin(1)
    relay(0)
    begin(2)
    relay(1)
    loads[1].wait()
    loads[2].wait()

    def first_half(step):
        cot_load(step).wait()
        rows_in = x[step].reshape(group_rows, width)
        members = cot[step, :, :, width:].reshape(group_rows, 128).astype(F32)
        logits = mul(rows_in, misc[...], 1, 0)
        lane = lax.broadcasted_iota(jnp.int32, logits.shape, 1)
        routed = (lane > 0) & (lane < 16)
        top = jnp.max(jnp.where(routed, logits, -1e30), axis=1, keepdims=True)
        powers = jnp.where(routed, jnp.exp(logits - top), 0.0)
        probs = jnp.where(lane == 0, 1.0, powers / jnp.sum(powers, axis=1, keepdims=True))
        own = jnp.where(lane == expert, members, 0.0)
        gate[0] = jnp.broadcast_to(jnp.sum(probs * own, axis=1, keepdims=True), gate.shape[1:])
        gate[1] = own

        def hidden_chunk(low, size):
            here = x[step].reshape(group_rows, width)
            gate_part = mul(here, weights[:, at(low, size)], 1, 0)
            up_part = mul(here, weights[:, at(hidden + low, size)], 1, 0)
            grad_act = mul(
                cot[step, :, :, :width].reshape(group_rows, width),
                weights[:, at(2 * hidden + low, size)],
                1,
                0,
            )
            scale = gate[0][:, :1]
            grad_act = grad_act * scale
            sigmoid = 1.0 / (1.0 + jnp.exp(-gate_part))
            silu = gate_part * sigmoid
            activated = (silu * up_part).astype(BF16)
            act[:, at(low, size)] = activated
            scaled[step, :, at(low, size)] = (activated.astype(F32) * scale).astype(BF16)
            slopes[step, :, at(low, size)] = (
                grad_act * up_part * (sigmoid + silu * (1.0 - sigmoid))
            ).astype(BF16)
            slopes[step, :, at(hidden + low, size)] = (grad_act * silu).astype(BF16)

        loop(0, hidden // 256, lambda i: hidden_chunk(i * 256, 256))
        if hidden % 256:
            hidden_chunk(hidden // 256 * 256, hidden % 256)

    def second_half(turn, step):
        def width_body(i, total):
            low = i * 256
            expert_rows = mul(act[...], weights[at(low, 256), 2 * hidden :], 1, 1)
            expert_rows = expert_rows.astype(BF16).astype(F32)
            outs[lax.rem(turn, 2), :, :, at(low, 256)] = (
                (expert_rows * gate[0][:, :1]).astype(BF16).reshape(4, rows, 256)
            )
            product = expert_rows * cot[step, :, :, at(low, 256)].reshape(group_rows, 256).astype(F32)
            grad_in = mul(slopes[step], weights[at(low, 256), : 2 * hidden], 1, 1)
            parts[step, :, :, at(low, 256)] = grad_in.astype(BF16).reshape(4, rows, 256)
            return total + product[:, :128] + product[:, 128:]

        total = lax.fori_loop(0, width // 256, width_body, jnp.zeros((group_rows, 128), F32))
        prob = jnp.sum(total, axis=1, keepdims=True) * gate[1]
        high = prob.astype(BF16)
        low = (prob - high.astype(F32)).astype(BF16)
        low = pltpu.roll(low.astype(F32), 32, 1).astype(BF16)
        parts[step, :, :, width:] = (high + low).reshape(4, rows, 128)

    def send_cross(turn):
        _, second = axes(turn)
        step = step_at(turn)
        near(turn, 1).wait_recv()
        block = parts.at[step, chip ^ second]
        add_blocks(block, block, got_one.at[step, 1])
        cross(turn).start()

    def send_far(turn):
        step = step_at(turn)
        near(turn, 0).wait_recv()
        cross(turn).wait_recv()
        block = parts.at[step, chip]
        add_blocks(block, block, got_one.at[step, 0], got_two.at[step])
        far(step).start()

    def group(turn):
        step = step_at(turn)
        across(turn).wait_recv()
        first_half(step)

        @pl.when(turn == 0)
        def _():
            begin(3)

        @pl.when(turn < 2)
        def _():
            relay(turn + 2)

        @pl.when(turn > 1)
        def _():
            outs_out(turn - 2).wait()

        second_half(turn, step)
        outs_out(turn).start()

        @pl.when(turn > 0)
        def _():
            send_cross(turn - 1)

        near(turn, 1).start()
        near(turn, 0).start()

        @pl.when(turn > 1)
        def _():
            send_far(turn - 2)

    loop(0, 4, group)

    def weight_chunk(left, right, low, size, offset, i):
        slot = lax.rem(i, 2)

        @pl.when(i >= 2)
        def _():
            grads_out(pl.ds(0, 256), 256, slot).wait()

        total = None
        for step in range(4):
            term = mul(
                left[step, :, :, :width].reshape(group_rows, width), right[step, :, at(low, size)], 0, 0
            )
            total = term if total is None else total + term
        stage[slot, :, :size] = total.astype(BF16)
        grads_out(at(offset + low, size), size, slot).start()

    ups, downs = 2 * hidden // 256, hidden // 256

    def up_chunk(i):
        weight_chunk(x, slopes, i * 256, 256, 0, i)

    def down_chunk(i):
        weight_chunk(cot, scaled, (i - ups) * 256, 256, 2 * hidden, i)

    loop(0, 4, up_chunk)
    send_cross(3)
    outs_out(2).wait()
    outs_out(3).wait()
    loop(0, 4, lambda step: (outs_near(step, 1).start(), outs_near(step, 0).start()))
    loop(4, 6, up_chunk)
    send_far(2)
    loop(6, ups, up_chunk)
    loop(ups, ups + downs, down_chunk)
    last = ups + downs
    if hidden % 256:
        weight_chunk(cot, scaled, downs * 256, hidden % 256, 2 * hidden, jnp.int32(last))
        grads_out(pl.ds(0, 256), 256, (last - 1) % 2).wait()
        grads_out(pl.ds(0, hidden % 256), hidden % 256, last % 2).wait()
    else:
        grads_out(pl.ds(0, 256), 256, last % 2).wait()
        grads_out(pl.ds(0, 256), 256, (last - 1) % 2).wait()
    near(3, 0).wait_recv()
    cross(3).wait_recv()
    loop(1, 4, lambda step: far(step).wait_recv())
    add_blocks(
        sums_o,
        parts.at[0, chip],
        got_one.at[0, 0],
        got_two.at[0],
        got_far.at[0],
        got_far.at[1],
        got_far.at[2],
    )

    def settle(turn):
        step = step_at(turn)
        direct(step, 1).wait_send()
        direct(step, 2).wait_send()
        across(turn).wait_send()
        near(turn, 0).wait_send()
        near(turn, 1).wait_send()
        cross(turn).wait_send()
        for which in (0, 1):
            outs_near(turn, which).wait_send()
            outs_near(turn, which).wait_recv()

        @pl.when(turn < 3)
        def _():
            far(step).wait_send()

        for up in (True, False):

            @pl.when(goes(step, up))
            def _():
                ring(step, up).wait_send()

    loop(0, 4, settle)


def run_experts(second_in, cot_all, weights, misc, collective):
    rows, width = second_in.shape
    hidden = weights.shape[1] // 3
    sums_width = width + 128
    block = (rows, sums_width)
    return pl.pallas_call(
        experts_kernel,
        out_shape=[
            jax.ShapeDtypeStruct((width, 3 * hidden), BF16),
            jax.ShapeDtypeStruct((4, 4, rows, width), BF16),
            jax.ShapeDtypeStruct((4, 2, rows, width), BF16),
            jax.ShapeDtypeStruct((rows, sums_width), F32),
        ],
        in_specs=[pl.BlockSpec(memory_space=pl.ANY)] * 4,
        out_specs=[
            pl.BlockSpec(memory_space=pl.ANY),
            pl.BlockSpec(memory_space=pl.ANY),
            pl.BlockSpec(memory_space=pl.ANY),
            pl.BlockSpec(memory_space=pltpu.VMEM),
        ],
        scratch_shapes=[
            pltpu.VMEM((4, 4, rows, width), BF16),
            pltpu.VMEM((4, 4, rows, width + 128), BF16),
            pltpu.VMEM((width, 3 * hidden), BF16),
            pltpu.VMEM((width, 128), BF16),
            pltpu.VMEM((4 * rows, hidden), BF16),
            pltpu.VMEM((4, 4 * rows, hidden), BF16),
            pltpu.VMEM((4, 4 * rows, 2 * hidden), BF16),
            pltpu.VMEM((2, 4 * rows, 128), F32),
            pltpu.VMEM((2, 4, rows, width), BF16),
            pltpu.VMEM((4, 4) + block, BF16),
            pltpu.VMEM((4, 2) + block, BF16),
            pltpu.VMEM((4,) + block, BF16),
            pltpu.VMEM((3,) + block, BF16),
            pltpu.VMEM((2, width, 256), BF16),
            pltpu.SemaphoreType.DMA((11,)),
            pltpu.SemaphoreType.DMA((11, 4)),
            pltpu.SemaphoreType.DMA((11, 4)),
        ],
        compiler_params=pltpu.CompilerParams(
            collective_id=collective, has_side_effects=True, vmem_limit_bytes=62 * 2**20
        ),
        name="experts",
    )(second_in, cot_all, weights, misc)


def finish_kernel(
    outs_in, outs_one_in, grads_in, exact_in, mixed_in, qkv_in, first_in, wq_in, wo_in,
    cos_in, sin_in, rows_in, sums_in, second_in, middle_in, cot_in, tok_in,
    output_o, grad_o, table_o, q_o, o_o,
    outs, outs_one, outs_two, outs_far, grads_own, grads_got, heads, exact, mixed, qkv, first, wq,
    wo, heads_send, attn, grad_middle, first_got, projected, first_part, dense, dense_got, dense_one,
    dense_two, dense_far, dense_sum, load_sems, send_sems, recv_sems,
):
    links = Links(send_sems, recv_sems)
    w, z = links.w, links.z
    chip, core = w // 2, w % 2
    rows = outs.shape[2]
    width = outs.shape[3]
    size = WINDOW * HEAD_DIM
    steps = (1, 2, 3, 0)
    block_rows = o_o.shape[0] // 4
    half = o_o.shape[1] // 2
    plane_rows = o_o.shape[0]
    remote, plane_of = links.copy, links.plane

    def axes(step):
        one = 1 + lax.rem(step, 2)
        return one, 3 - one

    def heads_ring(step):
        to = plane_of(step, 1)
        return remote(37, step, heads_send.at[to], heads.at[z], (w, to))

    def grads_load(step):
        return pltpu.make_async_copy(
            grads_in.at[plane_of(step, 1), core], grads_own.at[step], load_sems.at[0, step]
        )

    def grads_swap(step):
        return remote(
            0, step, grads_in.at[plane_of(step, 1), 1 - core], grads_got.at[step], (w ^ 1, z)
        )

    def grads_ring(step):
        return remote(1, step, grads_own.at[step], table_o.at[chip, z, core], (w, plane_of(step, 1)))

    def grads_keep():
        return pltpu.make_async_copy(
            grads_own.at[0], table_o.at[chip, z, core], load_sems.at[1, 0]
        )

    def grads_gather(turn):
        step = direct_at(z, turn)
        source = plane_of(step, -1)
        half = grads_own.shape[1] // 2
        return Gather(
            links, 2, step, turn, lambda i: table_o.at[i // 2, source, i % 2], True, half
        )

    def outs_loads(step):
        _, two = axes(step)
        return [
            pltpu.make_async_copy(src, dst, load_sems.at[2 + 3 * (i > 0) + (i > 1), step])
            for i, (src, dst) in enumerate(
                (
                    (outs_in.at[step, chip], outs.at[step, 0]),
                    (outs_in.at[step, chip ^ two], outs.at[step, 1]),
                    (outs_one_in.at[step], outs_one.at[step]),
                )
            )
        ]

    def cross(step):
        _, two = axes(step)
        return remote(11, step, outs.at[step, 1], outs_two.at[step], (w ^ (2 * two), z))

    def far(step):
        return remote(12, step, outs.at[step, 0], outs_far.at[step - 1], (w, plane_of(step, -1)))

    def part(kind, step):
        return dense.at[0, kind, plane_of(step, 1)]

    def dense_swap(kind, step):
        to = plane_of(step, 1)
        return remote(
            13 + 4 * kind, step, dense.at[1, kind, to], dense_got.at[kind, step], (w ^ 1, z)
        )

    def rows_of(block):
        return pl.ds(pl.multiple_of(block * block_rows, 16), block_rows)

    def dense_axes(kind):
        return 1 + kind, 2 - kind

    def dense_near(kind, step, which):
        one, _ = dense_axes(kind)
        block = chip ^ 3 if which else chip ^ one
        return remote(
            14 + 4 * kind + which,
            step,
            part(kind, step).at[rows_of(block)],
            dense_one.at[kind, step, which],
            (w ^ (2 * one), z),
        )

    def dense_cross(kind, step):
        _, two = dense_axes(kind)
        return remote(
            16 + 4 * kind,
            step,
            part(kind, step).at[rows_of(chip ^ two)],
            dense_two.at[kind, step],
            (w ^ (2 * two), z),
        )

    def place_of(owner):
        return rows_of(owner // 2), at(lax.rem(owner, 2) * half, half)

    def dense_ring(kind, step):
        own = part(kind, step).at[rows_of(chip)]
        here, columns = place_of(w)
        to = q_o.at[z, here, columns] if kind == 0 else dense_far.at[step - 1]
        return remote(21 + kind, step, own, to, (w, plane_of(step, 1)))

    def dense_keep():
        here, columns = place_of(w)
        return pltpu.make_async_copy(
            part(0, 0).at[rows_of(chip)], q_o.at[z, here, columns], load_sems.at[1, 1]
        )

    def dense_last():
        here, columns = place_of(w)
        return pltpu.make_async_copy(dense_sum, o_o.at[here, columns], load_sems.at[1, 2])

    def q_slot(step):
        source = plane_of(step, -1)

        def slot(owner):
            here, columns = place_of(owner)
            return q_o.at[source, here, columns]

        return slot

    def o_slot(owner):
        here, columns = place_of(owner)
        return o_o.at[here, columns]

    def q_gather(step):
        return Gather(links, 23, step, step, q_slot(step))

    def o_gather():
        return Gather(links, 30, 0, 0, o_slot)

    def first_ring(step):
        to = plane_of(step, 1)
        return remote(38, step, first_part.at[to], first_got.at[step - 1], (w, to))

    loads = [
        pltpu.make_async_copy(src, dst, load_sems.at[3 + i // 4, i % 4])
        for i, (src, dst) in enumerate(
            (
                (wq_in, wq),
                (wo_in, wo),
                (exact_in, exact),
                (mixed_in, mixed),
                (qkv_in, qkv),
                (first_in, first),
            )
        )
    ]
    for load in loads[:2]:
        load.start()
    for step in steps:
        grads_load(step).start()
    for step in steps:
        for load in outs_loads(step):
            load.start()
    for load in loads[2:]:
        load.start()
    greet(w, z)
    for step in steps:
        grads_swap(step).start()

    def grads_ready(step):
        grads_load(step).wait()
        grads_swap(step).wait_recv()
        add_blocks(grads_own.at[step], grads_own.at[step], grads_got.at[step])

    grads_ready(0)
    keep = grads_keep()
    keep.start()

    def outs_cross(step):
        for load in outs_loads(step):
            load.wait()
        add_blocks(outs.at[step, 1], outs.at[step, 1], outs_one.at[step, 1])
        cross(step).start()

    keep.wait()
    grads_gather(3).begin()
    for load in loads[:2]:
        load.wait()

    lane = lax.broadcasted_iota(jnp.int32, (rows, 128), 1)
    routed = (lane > 0) & (lane < 16)
    logits = jnp.where(routed, mul(second_in[...], wq[:, 3 * size :], 1, 0), -1e30)
    powers = jnp.where(routed, jnp.exp(logits - jnp.max(logits, axis=1, keepdims=True)), 0.0)
    probs = powers / jnp.sum(powers, axis=1, keepdims=True)
    high_low = sums_in[:, width:]
    grad_probs = jnp.where(routed, high_low + pltpu.roll(high_low, 96, 1), 0.0)
    grad_logits = probs * (grad_probs - jnp.sum(probs * grad_probs, axis=1, keepdims=True))
    grad_logits = grad_logits.astype(BF16)
    gains = jnp.transpose(wq[:, 3 * size :].astype(F32))
    gain_one, gain_two = gains[16:17, :], gains[17:18, :]
    grad_second = sums_in[:, :width] + mul(grad_logits, wq[:, 3 * size :], 1, 1)
    middle = middle_in[...]
    inverse = lax.rsqrt(jnp.mean(middle * middle, axis=1, keepdims=True) + epsilon)
    normed = middle * inverse
    grad_normed = grad_second * gain_two
    grad_here = cot_in[...].astype(F32) + inverse * (
        grad_normed - normed * jnp.mean(grad_normed * normed, axis=1, keepdims=True)
    )
    grad_middle[...] = grad_here
    attn[...] = grad_here.astype(BF16)
    gain_two_row = jnp.sum(grad_second * normed, axis=0, keepdims=True)
    router_part = mul(second_in[...], grad_logits, 0, 0)
    for plane, begin in enumerate(STARTS):
        grad_mixed = mul(
            attn[...], wo[begin * HEAD_DIM : begin * HEAD_DIM + size, :], 1, 1
        )
        heads_send[plane] = grad_mixed.astype(BF16)
    for step in (1, 2, 3):
        heads_ring(step).start()
    heads[z] = heads_send[z]
    loop(1, 4, grads_ready)
    loop(0, 4, outs_cross)
    for step in (1, 2, 3):
        heads_ring(step).wait_recv()
    send_next(z, lambda step: grads_ring(step).start())

    def out_weight(i):
        side = i // (half // 128)
        low = at((i - side * (half // 128)) * 128, 128)
        total = mul(rows_in[...], attn[:, at(i * 128, 128)], 0, 0).astype(BF16)
        dense[side ^ core, 1, :, :, low] = total.reshape(PLANES, plane_rows, 128)

    loop(0, width // 128, out_weight)
    for step in steps:
        dense_swap(1, step).start()
    for load in loads[2:]:
        load.wait()

    def head_back(head):
        keep_head = jnp.float32(0)
        for plane, (a, b) in enumerate(KEEP):
            keep_head = jnp.where((z == plane) & (head >= a) & (head < b), 1.0, keep_head)
        columns = at(head * HEAD_DIM, HEAD_DIM)
        grad_rows = heads[:, :, columns].reshape(PLANES * rows, HEAD_DIM).astype(F32) * keep_head
        delta = jnp.sum(grad_rows * mixed[head], axis=1, keepdims=True)
        grad_rows = grad_rows.astype(BF16)
        weights = exact[head]
        grad_value = mul(weights.astype(BF16), grad_rows, 0, 0)
        grad_scores = mul(grad_rows, qkv[2, head], 1, 1)
        grad_scores = (weights * (grad_scores - delta)).astype(BF16)
        grad_query = mul(grad_scores, qkv[1, head], 1, 0) * (HEAD_DIM ** (-0.5))
        grad_key = mul(grad_scores, qkv[0, head], 0, 0)

        def back(grads):
            return grads * cos_in[...] + pltpu.roll(grads * sin_in[...], HEAD_DIM // 2, 1)

        projected[:, columns] = back(grad_query).astype(BF16)
        projected[:, at(size + head * HEAD_DIM, HEAD_DIM)] = back(grad_key).astype(BF16)
        projected[:, at(2 * size + head * HEAD_DIM, HEAD_DIM)] = grad_value.astype(BF16)

    loop(0, WINDOW, head_back)

    def grads_next(turn):
        grads_ring(direct_at(z, turn)).wait_recv()
        grads_gather(turn).begin()

    grads_gather(3).relay()

    def qkv_weight(i):
        side = i // (half // 128)
        low = at((i - side * (half // 128)) * 128, 128)
        total = mul(first[...].reshape(PLANES * rows, width), projected[:, at(i * 128, 128)], 0, 0)
        dense[side ^ core, 0, :, :, low] = total.astype(BF16).reshape(PLANES, plane_rows, 128)

    loop(0, 3 * size // 128, qkv_weight)
    gain_parts = []
    for i in range(width // 256):
        here = slice(i * 256, (i + 1) * 256)
        total = mul(projected[...], wq[here, : 3 * size], 1, 1)
        first_part[:, :, here] = total.astype(BF16).reshape(PLANES, rows, 256)
        scaled = total * first[:, :, here].reshape(PLANES * rows, 256).astype(F32)
        gain_parts.append(jnp.sum(scaled, axis=0, keepdims=True))
    gain_one_row = jnp.concatenate(gain_parts, axis=1) / gain_one
    kind = lax.broadcasted_iota(jnp.int32, (128, width), 0)
    gain_rows = jnp.where(kind == 16, gain_one_row, jnp.where(kind == 17, gain_two_row, 0.0))
    misc = jnp.transpose(gain_rows) + router_part
    dense[1 ^ core, 0, :, :, half - 128 :] = misc.astype(BF16).reshape(PLANES, plane_rows, 128)
    for step in steps:
        dense_swap(0, step).start()

    loop(0, 1, grads_next)
    send_beyond(z, lambda step: grads_ring(step).start())

    def dense_ready(step):
        for kind in (0, 1):
            dense_swap(kind, step).wait_recv()
            block = part(kind, step)
            add_blocks(block, block, dense_got.at[kind, step])
            dense_near(kind, step, 1).start()
            dense_near(kind, step, 0).start()

    loop(0, 4, dense_ready)

    def outs_finish(step):
        cross(step).wait_recv()
        block = outs.at[step, 0]
        add_blocks(block, block, outs_one.at[step, 0], outs_two.at[step])

    loop(0, 4, outs_finish)
    grads_gather(0).relay()

    def dense_cross_start(step):
        for kind in (0, 1):
            _, two = dense_axes(kind)
            dense_near(kind, step, 1).wait_recv()
            block = part(kind, step).at[rows_of(chip ^ two)]
            add_blocks(block, block, dense_one.at[kind, step, 1])
            dense_cross(kind, step).start()

    loop(0, 4, dense_cross_start)
    loop(1, 3, grads_next)
    loop(1, 4, lambda step: far(step).start())

    def dense_finish(step):
        for kind in (0, 1):
            dense_near(kind, step, 0).wait_recv()
            dense_cross(kind, step).wait_recv()
            block = part(kind, step).at[rows_of(chip)]
            add_blocks(block, block, dense_one.at[kind, step, 0], dense_two.at[kind, step])

        @pl.when(step > 0)
        def _():
            dense_ring(0, step).start()
            dense_ring(1, step).start()

    loop(0, 4, dense_finish)
    loop(1, 4, lambda step: first_ring(step).start())
    keep = dense_keep()
    keep.start()
    grads_gather(3).end()
    grads_gather(0).end()
    grads_gather(1).relay()
    keep.wait()
    q_gather(0).begin()

    def q_next(step):
        dense_ring(0, step).wait_recv()
        q_gather(step).begin()
        dense_ring(1, step).wait_recv()

    loop(1, 4, q_next)
    add_blocks(
        dense_sum, part(1, 0).at[rows_of(chip)], dense_far.at[0], dense_far.at[1], dense_far.at[2]
    )
    keep = dense_last()
    keep.start()
    keep.wait()
    o_gather().begin()
    grads_gather(2).relay()
    grads_gather(1).end()
    loop(0, 4, lambda step: q_gather(step).relay())
    o_gather().relay()
    loop(1, 4, lambda step: far(step).wait_recv())

    def output_rows(i):
        here = pl.ds(pl.multiple_of(i * 16, 16), 16)
        total = middle_in[here, :] + outs[0, 0, here, :].astype(F32)
        for step in range(3):
            total = total + outs_far[step, here, :].astype(F32)
        output_o[here, :] = total.astype(BF16)

    loop(0, rows // 16, output_rows)
    for step in (1, 2, 3):
        first_ring(step).wait_recv()
    grad_first = first_part[z].astype(F32)
    for step in range(3):
        grad_first = grad_first + first_got[step].astype(F32)
    tokens = tok_in[...].astype(F32)
    inverse = lax.rsqrt(jnp.mean(tokens * tokens, axis=1, keepdims=True) + epsilon)
    normed = tokens * inverse
    grad_normed = grad_first * gain_one
    grad_o[...] = (
        grad_middle[...]
        + inverse
        * (grad_normed - normed * jnp.mean(grad_normed * normed, axis=1, keepdims=True))
    ).astype(BF16)
    loop(0, 4, lambda step: q_gather(step).end())
    o_gather().end()
    grads_gather(2).end()
    loop(0, 4, lambda turn: grads_gather(turn).settle())
    loop(0, 4, lambda step: q_gather(step).settle())
    o_gather().settle()

    def settle(step):
        grads_swap(step).wait_send()
        cross(step).wait_send()
        for kind in (0, 1):
            dense_swap(kind, step).wait_send()
            dense_near(kind, step, 0).wait_send()
            dense_near(kind, step, 1).wait_send()
            dense_cross(kind, step).wait_send()

    loop(0, 4, settle)

    def settle_rings(step):
        first_ring(step).wait_send()
        heads_ring(step).wait_send()
        grads_ring(step).wait_send()
        far(step).wait_send()
        dense_ring(0, step).wait_send()
        dense_ring(1, step).wait_send()

    loop(1, 4, settle_rings)


def finish(outs, outs_one, grads, saved, tables, at_rows, collective):
    exact, mixed, qkv, first, wq, wo = saved
    rows, width = first.shape[1:]
    seqlen = PLANES * rows
    size = WINDOW * HEAD_DIM
    plane_rows = width // PLANES
    block = (plane_rows // 4, width // 2)
    heads = (PLANES, rows, size)
    any_spec = pl.BlockSpec(memory_space=pl.ANY)
    vmem_spec = pl.BlockSpec(memory_space=pltpu.VMEM)
    return pl.pallas_call(
        finish_kernel,
        out_shape=[
            jax.ShapeDtypeStruct((rows, width), BF16),
            jax.ShapeDtypeStruct((rows, width), BF16),
            jax.ShapeDtypeStruct((4, PLANES) + grads.shape[1:], BF16),
            jax.ShapeDtypeStruct((PLANES, plane_rows, width), BF16),
            jax.ShapeDtypeStruct((plane_rows, width), BF16),
        ],
        in_specs=[any_spec] * 9 + [vmem_spec] * 8,
        out_specs=[vmem_spec] * 2 + [any_spec] * 3,
        scratch_shapes=[
            pltpu.VMEM((4, 2, rows, width), BF16),
            pltpu.VMEM((4, 2, rows, width), BF16),
            pltpu.VMEM((4, rows, width), BF16),
            pltpu.VMEM((3, rows, width), BF16),
            pltpu.VMEM((4,) + grads.shape[2:], BF16),
            pltpu.VMEM((4,) + grads.shape[2:], BF16),
            pltpu.VMEM(heads, BF16),
            pltpu.VMEM(exact.shape, F32),
            pltpu.VMEM(mixed.shape, F32),
            pltpu.VMEM(qkv.shape, BF16),
            pltpu.VMEM(first.shape, BF16),
            pltpu.VMEM(wq.shape, BF16),
            pltpu.VMEM(wo.shape, BF16),
            pltpu.VMEM(heads, BF16),
            pltpu.VMEM((rows, width), BF16),
            pltpu.VMEM((rows, width), F32),
            pltpu.VMEM((3, rows, width), BF16),
            pltpu.VMEM((seqlen, 3 * size), BF16),
            pltpu.VMEM(first.shape, BF16),
            pltpu.VMEM((2, 2, PLANES, plane_rows, width // 2), BF16),
            pltpu.VMEM((2, 4, plane_rows, width // 2), BF16),
            pltpu.VMEM((2, 4, 2) + block, BF16),
            pltpu.VMEM((2, 4) + block, BF16),
            pltpu.VMEM((3,) + block, BF16),
            pltpu.VMEM(block, BF16),
            pltpu.SemaphoreType.DMA((7, 4)),
            pltpu.SemaphoreType.DMA((39, 4)),
            pltpu.SemaphoreType.DMA((39, 4)),
        ],
        compiler_params=pltpu.CompilerParams(
            collective_id=collective, has_side_effects=True, vmem_limit_bytes=62 * 2**20
        ),
        name="finish",
    )(outs, outs_one, grads, *saved, *tables, *at_rows)


def widen_kernel(table, q, o, up_o, down_o, qkv_o, out_o, misc_o, router_o):
    columns = table.shape[2]
    split = up_o.shape[2]
    size = WINDOW * HEAD_DIM
    for low in range(0, columns, 128):
        part = jnp.swapaxes(table[:, :, low : low + 128].astype(F32), 0, 1)
        if low < split:
            up_o[:, :, low : low + 128] = part
        else:
            down_o[:, :, low - split : low - split + 128] = part
    out_o[...] = o[...].astype(F32)
    column = 0
    for kind in range(3):
        for plane, (a, b) in enumerate(KEEP):
            span = (b - a) * HEAD_DIM
            begin = kind * size + a * HEAD_DIM
            qkv_o[:, column : column + span] = q[plane, :, begin : begin + span].astype(F32)
            column += span
    total = q[0, :, 3 * size :].astype(F32)
    for plane in range(1, PLANES):
        total = total + q[plane, :, 3 * size :].astype(F32)
    misc_o[...] = total
    router_o[...] = total[:, 1 : 1 + router_o.shape[1]]


def widen(table, q, o):
    experts, rows, columns = table.shape
    width = o.shape[1]
    split = columns // 3 * 2
    step = rows // 4
    shapes = [
        (rows, experts, split),
        (rows, experts, columns - split),
        (rows, 3 * width),
        (rows, width),
        (rows, 128),
        (rows, experts - 1),
    ]
    return pl.pallas_call(
        widen_kernel,
        grid=(rows // step,),
        out_shape=[jax.ShapeDtypeStruct(shape, F32) for shape in shapes],
        in_specs=[
            pl.BlockSpec((experts, step, columns), lambda i: (0, i, 0)),
            pl.BlockSpec((PLANES, step, width), lambda i: (0, i, 0)),
            pl.BlockSpec((step, width), lambda i: (i, 0)),
        ],
        out_specs=[
            pl.BlockSpec((step,) + shape[1:], lambda i, n=len(shape): (i,) + (0,) * (n - 1))
            for shape in shapes
        ],
        compiler_params=pltpu.CompilerParams(vmem_limit_bytes=62 * 2**20),
        name="widen",
    )(table, q, o)


def windows(x):
    size = WINDOW * HEAD_DIM
    return jnp.stack([x[:, s * HEAD_DIM : s * HEAD_DIM + size] for s in STARTS])


def from_windows(x):
    return jnp.concatenate(
        [x[p, :, a * HEAD_DIM : b * HEAD_DIM] for p, (a, b) in enumerate(KEEP)], axis=1
    )


def dot(a, b, dims, out=F32):
    return lax.dot_general(a, b, ((dims[0], dims[1]), ((), ())), preferred_element_type=F32).astype(out)


def rotary_tables(seqlen):
    half_dim = HEAD_DIM // 2
    frequency = 10000.0 ** (-np.arange(half_dim, dtype=np.float32) / half_dim)
    angles = np.arange(seqlen, dtype=np.float32)[:, None] * frequency[None, :].astype(np.float32)
    cosine, sine = np.cos(angles), np.sin(angles)
    return (
        jnp.asarray(np.concatenate([cosine, cosine], axis=1), F32),
        jnp.asarray(np.concatenate([-sine, sine], axis=1), F32),
    )


def expert_local(
    tokens, seq_ids, routes, cotangent, gain_attn, w_qkv, w_out, gain_ffn, w_router, w_up, w_down
):
    rows, width = tokens.shape
    own = w_out.shape[0]
    experts = w_router.shape[1]
    seqlen = PLANES * rows
    size = WINDOW * HEAD_DIM

    misc = jnp.concatenate(
        [
            jnp.zeros((own, 1), BF16),
            w_router,
            gain_attn[:, None],
            gain_ffn[:, None],
            jnp.zeros((own, 128 - experts - 3), BF16),
        ],
        axis=1,
    )
    tables = rotary_tables(seqlen)
    (
        we_all, cot_all, wq_all, out_weight, first_in, qkv, weights_exact, mixed_exact, mixed, middle,
        second_in,
    ) = start(
        tokens, w_qkv, w_out, seq_ids[None, :], routes, misc, w_up, w_down, cotangent, tables, 1
    )

    weights = we_all.reshape(width, 3 * FF)
    grads, outs, outs_one, sums = run_experts(second_in, cot_all, weights, wq_all, 3)

    output, grad_tokens, table, q_all, o_all = finish(
        outs,
        outs_one,
        grads.reshape(PLANES, 2, width // PLANES // 2, 3 * FF),
        (weights_exact, mixed_exact, qkv, first_in, wq_all, out_weight),
        tables,
        (mixed, sums, second_in, middle, cotangent, tokens),
        6,
    )
    up_sum, down_sum, qkv_sum, out_sum, misc_sum, router_sum = widen(
        table.reshape(experts + 1, width // PLANES, 3 * FF), q_all, o_all
    )
    return (
        output,
        grad_tokens,
        misc_sum[:, experts + 1],
        qkv_sum,
        out_sum,
        misc_sum[:, experts + 2],
        router_sum,
        up_sum,
        down_sum,
    )


def solution(mesh):
    fits = mesh.shape["wide"] == 8 and mesh.shape["narrow"] == PLANES
    return jax.shard_map(
        expert_local if fits else local,
        mesh=mesh,
        in_specs=(
            P(("wide", "narrow"), None),
            P(("wide", "narrow")),
            P(("wide", "narrow"), None),
            P(("wide", "narrow"), None),
            P(("wide", "narrow")),
            P(("wide", "narrow"), None),
            P(("wide", "narrow"), None),
            P(("wide", "narrow")),
            P(("wide", "narrow"), None),
            P(("wide", "narrow"), None, None),
            P(("wide", "narrow"), None, None),
        ),
        out_specs=(
            P(("wide", "narrow"), None),
            P(("wide", "narrow"), None),
            P("narrow"),
            P("narrow", None),
            P("narrow", None),
            P("narrow"),
            P("narrow", None),
            P("narrow", None, None),
            P("narrow", None, None),
        ),
        check_vma=False,
    )
```

```python
import jax
import jax.numpy as jnp
import numpy as np
from jax import lax
from jax.experimental import pallas as pl
from jax.experimental.pallas import tpu as pltpu
from jax.sharding import PartitionSpec as P

HEADS = 10
HEAD_DIM = 128
FF = 896
CAP = 72


epsilon = 1e-06


def shortened(x):
    return jax.tree.map(lambda a: a.astype(jnp.bfloat16) if a.dtype == jnp.float32 else a, x)


def rms_inverse(values):
    return lax.rsqrt(jnp.mean(values * values, axis=-1, keepdims=True) + epsilon)


def rotary(positions, head_size):
    half_dim = head_size // 2
    frequency = 10000.0 ** (-jnp.arange(half_dim, dtype=jnp.float32) / half_dim)
    angles = positions[:, None] * frequency[None, :]
    cosine = jnp.concatenate([jnp.cos(angles), jnp.cos(angles)], axis=1)[:, None, :]
    sine_table = jnp.concatenate([jnp.sin(angles), jnp.sin(angles)], axis=1)[:, None, :]
    return (cosine, sine_table)


def rotate(values, cosine, sine_table):
    half_dim = values.shape[-1] // 2
    turned = jnp.concatenate([-values[..., half_dim:], values[..., :half_dim]], axis=-1)
    return values * cosine + turned * sine_table


def rotate_back(grads, cosine, sine_table):
    half_dim = grads.shape[-1] // 2
    scaled = grads * sine_table
    turned = jnp.concatenate([scaled[..., half_dim:], -scaled[..., :half_dim]], axis=-1)
    return grads * cosine + turned


def expert_weight_terms(
    routed_in, routed_grad, shared_in, shared_grad, slot_grads, slot_acts, shared_grads, shared_acts
):
    up_routed = jnp.einsum(
        "ecd,ecf->def", routed_in, slot_grads, preferred_element_type=jnp.float32
    )
    up_shared = jnp.einsum("td,tf->df", shared_in, shared_grads, preferred_element_type=jnp.float32)
    down_routed = jnp.einsum(
        "ecd,ecf->def", routed_grad, slot_acts, preferred_element_type=jnp.float32
    )
    down_shared = jnp.einsum(
        "td,tf->df", shared_grad, shared_acts, preferred_element_type=jnp.float32
    )
    up_all = jnp.concatenate([up_shared[:, None], up_routed], axis=1)
    down_all = jnp.concatenate([down_shared[:, None], down_routed], axis=1)
    combined = jnp.concatenate([up_all, down_all], axis=2)
    return combined.reshape(combined.shape[0], -1)


def local(
    tokens, seq_ids, routes, cotangent, gain_attn, w_qkv, w_out, gain_ffn, w_router, w_up, w_down
):
    row_count = tokens.shape[0]
    model_width = tokens.shape[1]
    query_scale = HEAD_DIM ** (-0.5)
    hidden = FF
    capacity = CAP
    inputs = tokens.astype(jnp.float32)
    gain_one, qkv_weight, out_weight = (
        lax.all_gather(gain_attn, ("wide", "narrow"), axis=0, tiled=True),
        lax.all_gather(w_qkv, ("wide", "narrow"), axis=0, tiled=True),
        lax.all_gather(w_out, ("wide", "narrow"), axis=0, tiled=True),
    )
    inverse_one = rms_inverse(inputs)
    normed_one = inputs * inverse_one
    first_in = (normed_one * gain_one.astype(jnp.float32)).astype(jnp.bfloat16)
    projected = jnp.dot(first_in, qkv_weight, preferred_element_type=jnp.float32)
    offset = lax.axis_index("narrow") * row_count
    query_pos = offset + jnp.arange(row_count, dtype=jnp.int32)
    cosine, sine_table = rotary(query_pos.astype(jnp.float32), HEAD_DIM)
    query_rows = (
        rotate(projected[:, :model_width].reshape(row_count, HEADS, HEAD_DIM), cosine, sine_table)
        * query_scale
    ).astype(jnp.bfloat16)
    key_rows = (
        rotate(
            projected[:, model_width : 2 * model_width].reshape(row_count, HEADS, HEAD_DIM),
            cosine,
            sine_table,
        )
        .astype(jnp.bfloat16)
        .reshape(row_count, model_width)
    )
    value_rows = projected[:, 2 * model_width :].astype(jnp.bfloat16)
    all_keys, all_values, all_ids = (
        lax.all_gather(key_rows, "narrow", axis=0, tiled=True),
        lax.all_gather(value_rows, "narrow", axis=0, tiled=True),
        lax.all_gather(seq_ids.astype(jnp.bfloat16), "narrow", axis=0, tiled=True),
    )
    seqlen = all_keys.shape[0]
    block_len = min(512, seqlen)
    num_blocks = seqlen // block_len
    own_ids = seq_ids.astype(jnp.float32)

    def block_parts(block_index):
        first_row = block_index * block_len
        key_pos = first_row + jnp.arange(block_len, dtype=jnp.int32)
        key_ids = lax.dynamic_slice_in_dim(all_ids, first_row, block_len, 0).astype(jnp.float32)
        allowed = (key_pos[None, :] <= query_pos[:, None]) & (key_ids[None, :] == own_ids[:, None])
        key_block = lax.dynamic_slice_in_dim(all_keys, first_row, block_len, 0).reshape(
            block_len, HEADS, HEAD_DIM
        )
        value_block = lax.dynamic_slice_in_dim(all_values, first_row, block_len, 0).reshape(
            block_len, HEADS, HEAD_DIM
        )
        scores = jnp.einsum(
            "qhd,khd->hqk", query_rows, key_block, preferred_element_type=jnp.float32
        )
        return (allowed[None], key_block, value_block, scores)

    def max_step(state_pair, block_index):
        running_max, running_sum = state_pair
        allowed, key_block, value_block, scores = block_parts(block_index)
        masked = jnp.where(allowed, scores, -1e30)
        new_max = jnp.maximum(running_max, jnp.max(masked, axis=2))
        added = jnp.sum(jnp.where(allowed, jnp.exp(masked - new_max[..., None]), 0.0), axis=2)
        return ((new_max, running_sum * jnp.exp(running_max - new_max) + added), None)

    start_max = jnp.full((HEADS, row_count), -1e30, jnp.float32)
    start_sum = jnp.zeros((HEADS, row_count), jnp.float32)
    (top_score, exp_total), unused = lax.scan(
        max_step, (start_max, start_sum), jnp.arange(num_blocks)
    )
    log_total = top_score + jnp.log(exp_total)

    def out_step(accum, block_index):
        allowed, key_block, value_block, scores = block_parts(block_index)
        weights_low = jnp.where(allowed, jnp.exp(scores - log_total[..., None]), 0.0).astype(
            jnp.bfloat16
        )
        return (
            accum
            + jnp.einsum(
                "hqk,khd->hqd", weights_low, value_block, preferred_element_type=jnp.float32
            ),
            None,
        )

    accum_start = jnp.zeros((HEADS, row_count, HEAD_DIM), jnp.float32)
    mixed_heads, unused = lax.scan(out_step, accum_start, jnp.arange(num_blocks))
    mixed_exact = jnp.transpose(mixed_heads, (1, 0, 2))
    mixed = mixed_exact.reshape(row_count, model_width).astype(jnp.bfloat16)
    middle = inputs + jnp.dot(mixed, out_weight, preferred_element_type=jnp.float32)
    gain_two, router_weight, up_weight, down_weight = (
        lax.all_gather(gain_ffn, ("wide", "narrow"), axis=0, tiled=True),
        lax.all_gather(w_router, ("wide", "narrow"), axis=0, tiled=True),
        lax.all_gather(w_up, ("wide", "narrow"), axis=0, tiled=True),
        lax.all_gather(w_down, ("wide", "narrow"), axis=0, tiled=True),
    )
    inverse_two = rms_inverse(middle)
    normed_two = middle * inverse_two
    second_in = (normed_two * gain_two.astype(jnp.float32)).astype(jnp.bfloat16)
    logits = jnp.dot(second_in, router_weight, preferred_element_type=jnp.float32)
    router_probs = jax.nn.softmax(logits, axis=-1)
    experts = logits.shape[1]
    choose = routes[:, :, None] == jnp.arange(experts, dtype=jnp.int32)[None, None, :]
    member = jnp.sum(choose.astype(jnp.float32), axis=1)
    earlier = (jnp.arange(row_count)[:, None] > jnp.arange(row_count)[None, :]).astype(jnp.bfloat16)
    before = jnp.dot(earlier, member.astype(jnp.bfloat16), preferred_element_type=jnp.float32)
    slot_hit = (member.T[:, None, :] > 0.5) & (
        before.T[:, None, :] == jnp.arange(capacity, dtype=jnp.float32)[None, :, None]
    )
    dispatch = slot_hit.astype(jnp.bfloat16)
    gathered_in = jnp.einsum(
        "ect,td->ecd", dispatch, second_in, preferred_element_type=jnp.float32
    ).astype(jnp.bfloat16)
    gate_weights = router_probs * member
    gate_up = jnp.einsum(
        "ecd,def->ecf", gathered_in, up_weight[:, 1:], preferred_element_type=jnp.float32
    )
    gate_part = gate_up[..., :hidden]
    up_part = gate_up[..., hidden:]
    activated = (jax.nn.silu(gate_part) * up_part).astype(jnp.bfloat16)
    expert_rows = jnp.einsum(
        "ecf,def->ecd", activated, down_weight[:, 1:], preferred_element_type=jnp.float32
    ).astype(jnp.bfloat16)
    selected = jnp.einsum("ect,ecd->etd", dispatch, expert_rows, preferred_element_type=jnp.float32)
    routed = jnp.sum(gate_weights.T[:, :, None] * selected, axis=0)
    shared_up = jnp.dot(second_in, up_weight[:, 0], preferred_element_type=jnp.float32)
    shared_gate = shared_up[:, :hidden]
    shared_lin = shared_up[:, hidden:]
    shared_act = (jax.nn.silu(shared_gate) * shared_lin).astype(jnp.bfloat16)
    shared_out = jnp.einsum(
        "tf,df->td", shared_act, down_weight[:, 0], preferred_element_type=jnp.float32
    )
    output = (middle + shared_out + routed).astype(jnp.bfloat16)
    gain_two, router_weight, up_weight, down_weight = (
        lax.all_gather(gain_ffn, ("wide", "narrow"), axis=0, tiled=True),
        lax.all_gather(w_router, ("wide", "narrow"), axis=0, tiled=True),
        lax.all_gather(w_up, ("wide", "narrow"), axis=0, tiled=True),
        lax.all_gather(w_down, ("wide", "narrow"), axis=0, tiled=True),
    )
    grad_output = cotangent.astype(jnp.float32)
    slot_token = jnp.sum(
        jnp.where(slot_hit, jnp.arange(row_count, dtype=jnp.int32)[None, None, :], 0), axis=2
    )
    slot_gate = jnp.sum(jnp.where(slot_hit, gate_weights.T[:, None, :], 0.0), axis=2)
    grad_rows = (slot_gate[..., None] * grad_output[slot_token]).astype(jnp.bfloat16)
    grad_probs = jnp.sum(selected * grad_output[None], axis=2).T * member
    grad_logits = (
        router_probs * (grad_probs - jnp.sum(router_probs * grad_probs, axis=1, keepdims=True))
    ).astype(jnp.bfloat16)
    grad_act = jnp.einsum(
        "ecd,def->ecf", grad_rows, down_weight[:, 1:], preferred_element_type=jnp.float32
    )
    sigmoid_gate = jax.nn.sigmoid(gate_part)
    grad_gate_up = jnp.concatenate(
        [
            grad_act * up_part * sigmoid_gate * (1.0 + gate_part * (1.0 - sigmoid_gate)),
            grad_act * jax.nn.silu(gate_part),
        ],
        axis=-1,
    ).astype(jnp.bfloat16)
    grad_gathered = jnp.einsum(
        "ecf,def->ecd", grad_gate_up, up_weight[:, 1:], preferred_element_type=jnp.float32
    )
    slot_index = jnp.sum(jnp.where(choose, before[:, None, :], 0.0), axis=2).astype(jnp.int32)
    flat_index = routes * capacity + slot_index
    grad_second = jnp.sum(grad_gathered.reshape(-1, model_width)[flat_index], axis=1)
    grad_shared_act = jnp.einsum(
        "td,df->tf", cotangent, down_weight[:, 0], preferred_element_type=jnp.float32
    )
    sigmoid_shared = jax.nn.sigmoid(shared_gate)
    grad_shared_up = jnp.concatenate(
        [
            grad_shared_act
            * shared_lin
            * sigmoid_shared
            * (1.0 + shared_gate * (1.0 - sigmoid_shared)),
            grad_shared_act * jax.nn.silu(shared_gate),
        ],
        axis=-1,
    ).astype(jnp.bfloat16)
    grad_second = grad_second + jnp.einsum(
        "tf,df->td", grad_shared_up, up_weight[:, 0], preferred_element_type=jnp.float32
    )
    grad_second = grad_second + jnp.einsum(
        "te,de->td", grad_logits, router_weight, preferred_element_type=jnp.float32
    )
    grad_normed_two = grad_second * gain_two.astype(jnp.float32)
    grad_gain_two = jnp.sum(grad_second * normed_two, axis=0)
    grad_middle = grad_output + inverse_two * (
        grad_normed_two
        - normed_two * jnp.mean(grad_normed_two * normed_two, axis=-1, keepdims=True)
    )
    grad_router = jnp.einsum(
        "td,te->de", second_in, grad_logits, preferred_element_type=jnp.float32
    )
    narrow_rows = model_width // lax.axis_size("narrow")
    routed_cols, grad_cols, shared_cols, cotangent_cols = (
        lax.all_to_all(gathered_in, "narrow", split_axis=2, concat_axis=1, tiled=True),
        lax.all_to_all(grad_rows, "narrow", split_axis=2, concat_axis=1, tiled=True),
        lax.all_to_all(second_in[None], "narrow", split_axis=2, concat_axis=1, tiled=True),
        lax.all_to_all(cotangent[None], "narrow", split_axis=2, concat_axis=1, tiled=True),
    )
    slot_grads, slot_acts, shared_grads, shared_acts = (
        lax.all_gather(grad_gate_up, "narrow", axis=1, tiled=True),
        lax.all_gather(activated, "narrow", axis=1, tiled=True),
        lax.all_gather(grad_shared_up[None], "narrow", axis=1, tiled=True),
        lax.all_gather(shared_act[None], "narrow", axis=1, tiled=True),
    )
    expert_grads = expert_weight_terms(
        routed_cols,
        grad_cols,
        shared_cols[0],
        cotangent_cols[0],
        slot_grads,
        slot_acts,
        shared_grads[0],
        shared_acts[0],
    )
    gain_one, qkv_weight, out_weight = (
        lax.all_gather(gain_attn, ("wide", "narrow"), axis=0, tiled=True),
        lax.all_gather(w_qkv, ("wide", "narrow"), axis=0, tiled=True),
        lax.all_gather(w_out, ("wide", "narrow"), axis=0, tiled=True),
    )
    grad_attention = grad_middle.astype(jnp.bfloat16)
    grad_out_weight = jnp.einsum(
        "td,te->de", mixed, grad_attention, preferred_element_type=jnp.float32
    )
    grad_mixed = jnp.einsum(
        "te,de->td", grad_attention, out_weight, preferred_element_type=jnp.float32
    ).astype(jnp.bfloat16)
    grad_heads = grad_mixed.reshape(row_count, HEADS, HEAD_DIM)
    row_delta = jnp.sum(grad_heads.astype(jnp.float32) * mixed_exact, axis=2).T

    def back_step(grad_query, block_index):
        allowed, key_block, value_block, scores = block_parts(block_index)
        weights_exact = jnp.where(allowed, jnp.exp(scores - log_total[..., None]), 0.0)
        weights_low = weights_exact.astype(jnp.bfloat16)
        grad_value = jnp.einsum(
            "hqk,qhd->khd", weights_low, grad_heads, preferred_element_type=jnp.float32
        )
        grad_weights = jnp.einsum(
            "qhd,khd->hqk", grad_heads, value_block, preferred_element_type=jnp.float32
        )
        grad_scores = (weights_exact * (grad_weights - row_delta[..., None])).astype(jnp.bfloat16)
        grad_query = grad_query + jnp.einsum(
            "hqk,khd->qhd", grad_scores, key_block, preferred_element_type=jnp.float32
        )
        grad_key = jnp.einsum(
            "hqk,qhd->khd", grad_scores, query_rows, preferred_element_type=jnp.float32
        )
        return (
            grad_query,
            (grad_key.reshape(block_len, model_width), grad_value.reshape(block_len, model_width)),
        )

    query_start = jnp.zeros((row_count, HEADS, HEAD_DIM), jnp.float32)
    grad_query, (key_blocks, value_blocks) = lax.scan(
        back_step, query_start, jnp.arange(num_blocks)
    )
    key_partial = key_blocks.reshape(seqlen, model_width)
    value_partial = value_blocks.reshape(seqlen, model_width)
    grad_keys, grad_values = (
        lax.psum_scatter(
            key_partial.astype(jnp.bfloat16), "narrow", scatter_dimension=0, tiled=True
        ).astype(jnp.float32),
        lax.psum_scatter(
            value_partial.astype(jnp.bfloat16), "narrow", scatter_dimension=0, tiled=True
        ).astype(jnp.float32),
    )
    grad_query_raw = rotate_back(grad_query, cosine, sine_table) * query_scale
    grad_key_raw = rotate_back(grad_keys.reshape(row_count, HEADS, HEAD_DIM), cosine, sine_table)
    grad_projected = jnp.concatenate(
        [
            grad_query_raw.reshape(row_count, model_width),
            grad_key_raw.reshape(row_count, model_width),
            grad_values,
        ],
        axis=1,
    ).astype(jnp.bfloat16)
    grad_qkv_weight = jnp.einsum(
        "td,tf->df", first_in, grad_projected, preferred_element_type=jnp.float32
    )
    grad_first = jnp.einsum(
        "tf,df->td", grad_projected, qkv_weight, preferred_element_type=jnp.float32
    )
    grad_normed_one = grad_first * gain_one.astype(jnp.float32)
    grad_gain_one = jnp.sum(grad_first * normed_one, axis=0)
    grad_inputs = grad_middle + inverse_one * (
        grad_normed_one
        - normed_one * jnp.mean(grad_normed_one * normed_one, axis=-1, keepdims=True)
    )
    dense_parts = (
        lax.psum_scatter(
            grad_gain_one.astype(jnp.bfloat16), "narrow", scatter_dimension=0, tiled=True
        ).astype(jnp.float32),
        lax.psum_scatter(
            grad_qkv_weight.astype(jnp.bfloat16), "narrow", scatter_dimension=0, tiled=True
        ).astype(jnp.float32),
        lax.psum_scatter(
            grad_out_weight.astype(jnp.bfloat16), "narrow", scatter_dimension=0, tiled=True
        ).astype(jnp.float32),
        lax.psum_scatter(
            grad_gain_two.astype(jnp.bfloat16), "narrow", scatter_dimension=0, tiled=True
        ).astype(jnp.float32),
        lax.psum_scatter(
            grad_router.astype(jnp.bfloat16), "narrow", scatter_dimension=0, tiled=True
        ).astype(jnp.float32),
    )
    summed = jax.tree.map(
        lambda part: part.astype(jnp.float32),
        lax.psum(shortened((expert_grads,) + tuple(dense_parts)), "wide"),
    )
    expert_grads = summed[0]
    dense_parts = summed[1:]
    gain_one_sum, qkv_sum, out_sum, gain_two_sum, router_sum = dense_parts
    expert_table = expert_grads.reshape(narrow_rows, up_weight.shape[1], 3 * hidden)
    up_sum = expert_table[:, :, : 2 * hidden]
    down_sum = expert_table[:, :, 2 * hidden :]
    return (
        output,
        grad_inputs.astype(jnp.bfloat16),
        gain_one_sum,
        qkv_sum,
        out_sum,
        gain_two_sum,
        router_sum,
        up_sum,
        down_sum,
    )


PLANES = 4
WINDOW = 3
STARTS = (0, 3, 6, 7)
KEEP = ((0, 3), (0, 3), (0, 2), (1, 3))
MESH_IDS = pl.DeviceIdType.MESH
BF16 = jnp.bfloat16
F32 = jnp.float32


def place():
    w = lax.axis_index("wide")
    z = lax.axis_index("narrow")
    return w, z


def greet(w, z):
    barrier = pltpu.get_barrier_semaphore()
    peers = [(w, lax.rem(z + step, PLANES)) for step in (1, 2, 3)]
    peers += [(w ^ flip, z) for flip in (1, 2, 4, 6)]
    for peer in peers:
        pl.semaphore_signal(barrier, inc=1, device_id=peer, device_id_type=MESH_IDS)
    pl.semaphore_wait(barrier, len(peers))


def mul(a, b, over_a, over_b):
    return lax.dot_general(a, b, (((over_a,), (over_b,)), ((), ())), preferred_element_type=F32)


def at(start, size):
    return pl.ds(pl.multiple_of(start, 128), size)


def loop(first, last, body):
    def step(i, carry):
        body(i)
        return carry

    lax.fori_loop(first, last, step, 0)


class Links:
    def __init__(self, send_sems, recv_sems):
        self.w, self.z = place()
        self.send_sems, self.recv_sems = send_sems, recv_sems

    def copy(self, kind, step, src, dst, device):
        return pltpu.make_async_remote_copy(
            src_ref=src,
            dst_ref=dst,
            send_sem=self.send_sems.at[kind, step],
            recv_sem=self.recv_sems.at[kind, step],
            device_id=device,
            device_id_type=MESH_IDS,
        )

    def plane(self, step, sign):
        return lax.rem(self.z + PLANES + sign * step, PLANES)


def step_at(z, turn):
    step = 0
    for plane, steps in enumerate(((3, 2, 1, 0), (1, 3, 2, 0), (3, 1, 2, 0), (1, 2, 3, 0))):
        for number, value in enumerate(steps):
            step = jnp.where((z == plane) & (turn == number), value, step)
    return step


def direct_at(z, turn):
    even = lax.rem(z, 2) == 0
    first, second = jnp.where(even, 3, 1), jnp.where(even, 1, 3)
    return jnp.where(turn == 0, first, jnp.where(turn == 1, second, jnp.where(turn == 2, 2, 0)))


def send_next(z, send):
    @pl.when(z < PLANES - 1)
    def _():
        send(1)

    @pl.when(z > 0)
    def _():
        send(3)


def send_beyond(z, send):
    @pl.when(z == 0)
    def _():
        send(3)

    @pl.when(z == PLANES - 1)
    def _():
        send(1)

    send(2)


class Chain:
    def __init__(self, links, base, own, slot):
        self.links, self.base, self.own, self.slot = links, base, own, slot

    def goes(self, step, up):
        z = self.links.z
        if up:
            return (z >= step) & (z < PLANES - 1)
        return ((z < step) | (step == 0)) & (z > 0)

    def ring(self, step, up, own=False):
        links = self.links
        to = lax.rem(step + 1, 4) if up else lax.rem(step + 3, 4)
        ref = self.slot(links.plane(step, -1))
        return pltpu.make_async_remote_copy(
            src_ref=self.own if own else ref,
            dst_ref=ref,
            send_sem=links.send_sems.at[self.base if up else self.base + 1, step],
            recv_sem=links.recv_sems.at[self.base, to],
            device_id=(links.w, links.z + 1 if up else links.z - 1),
            device_id_type=MESH_IDS,
        )

    def hand_on(self, step, own=False):
        for up in (True, False):

            @pl.when(self.goes(step, up))
            def _():
                self.ring(step, up, own).start()

    def begin(self):
        self.hand_on(0, True)

    def arrive(self, turn):
        step = step_at(self.links.z, turn)
        ref = self.slot(self.links.plane(step, -1))
        self.links.copy(self.base, step, ref, ref, (self.links.w, self.links.z)).wait_recv()
        self.hand_on(step)

    def settle(self):
        def body(step):
            for up in (True, False):

                @pl.when(self.goes(step, up))
                def _():
                    self.ring(step, up).wait_send()

        loop(0, 4, body)


class Gather:
    def __init__(self, links, base, step, turn, slot, cores=True, half=0):
        self.links, self.base, self.step, self.slot, self.cores = links, base, step, slot, cores
        self.half = half
        self.first = 1 + lax.rem(turn, 2)
        self.second = 3 - self.first

    def copy(self, kind, owner, flip):
        ref = self.slot(owner)
        return self.links.copy(
            self.base + kind, self.step, ref, ref, (self.links.w ^ flip, self.links.z)
        )

    def begin(self):
        w = self.links.w
        self.copy(0, w, 2).start()
        self.copy(1, w, 4).start()
        if self.cores:
            self.copy(4, w, 1).start()

    def relay(self):
        w = self.links.w
        self.copy(0, w, 2).wait_recv()
        self.copy(1, w, 4).wait_recv()
        for copy in self.across():
            copy.start()
        if self.cores:
            self.copy(3, w ^ 2, 1).start()
            self.copy(5, w ^ 4, 1).start()

    def across(self):
        if not self.half:
            return [self.copy(2, self.links.w ^ (2 * self.first), 2 * self.second)]
        copies = []
        for kind, flip in ((2, 2), (7, 4)):
            ref = self.slot(self.links.w ^ flip).at[pl.ds((kind == 7) * self.half, self.half)]
            copies.append(
                self.links.copy(
                    self.base + kind, self.step, ref, ref, (self.links.w ^ (6 - flip), self.links.z)
                )
            )
        return copies

    def end(self):
        for copy in self.across():
            copy.wait_recv()
        if self.cores:
            self.copy(6, self.links.w ^ 6, 1).start()

    def settle(self):
        w = self.links.w
        self.copy(0, w, 2).wait_send()
        self.copy(1, w, 4).wait_send()
        for copy in self.across():
            copy.wait_send()
        if self.cores:
            for kind, owner in ((4, w), (3, w ^ 2), (5, w ^ 4), (6, w ^ 6)):
                copy = self.copy(kind, owner, 1)
                copy.wait_send()
                copy.wait_recv()


def softmax_rows(scores, mask):
    masked = scores + mask
    powers = jnp.exp(masked - jnp.max(masked, axis=1, keepdims=True))
    return powers * (1.0 / jnp.sum(powers, axis=1, keepdims=True))


def start_kernel(
    tok_in, wq_in, wo_in, seq_in, routes_in, router_in, gains_in, up_in, down_in, cot_in, cos_in, sin_in,
    we_o, cot_o, wq_out, wo_out, first_out, qkv_out, exact_out, mixed_out, mixed_rows_o, middle_o,
    second_o, hop,
    tok, ids, wq_blocks, wo_blocks, staged, mask, mixed_got, mixed_send, ids_in, we_in, cot_full,
    columns, misc_in, wq_o, wo_o, first_o, qkv_o, exact_o, mixed_o,
    load_sems, out_sems, send_sems, recv_sems,
):
    links = Links(send_sems, recv_sems)
    w, z = links.w, links.z
    chip = w // 2
    rows, width = tok_in.shape
    seqlen = PLANES * rows
    size = WINDOW * HEAD_DIM
    own = wo_in.shape[0]
    keeps = [
        pltpu.make_async_copy(src, dst, load_sems.at[i])
        for i, (src, dst) in enumerate(
            (
                (tok_in, tok.at[z]),
                (wo_in, wo_blocks.at[w, z]),
                (cot_full, cot_o.at[chip, z]),
            )
        )
    ]
    for keep in keeps[:2]:
        keep.start()
    window_starts = [jnp.int32(0)] * 4
    for plane, begin in enumerate(STARTS):
        for step in range(4):
            window_starts[step] = jnp.where(
                lax.rem(z + step, PLANES) == plane, begin, window_starts[step]
            )

    def window(step, kind):
        return wq_in.at[:, at(kind * width + window_starts[step] * HEAD_DIM, size)]

    def wq_own(kind):
        return pltpu.make_async_copy(
            window(0, kind),
            wq_blocks.at[w, z, :, pl.ds(kind * size, size)],
            load_sems.at[3 + kind],
        )

    for kind in range(3):
        wq_own(kind).start()
    routed = router_in.shape[0]
    columns[...] = jnp.zeros(columns.shape, F32)
    columns[1 : routed + 1, :own] = router_in[...].astype(F32)
    columns[routed + 1 : routed + 3, :own] = gains_in[...].astype(F32)
    misc_in[...] = jnp.transpose(columns[...])[:own, :].astype(BF16)
    wq_blocks[w, z, :, 3 * size :] = misc_in[...]
    row_ids = jnp.broadcast_to(seq_in[...].astype(F32), (rows, rows))
    ids_in[:rows, :] = row_ids.astype(BF16)
    ids_in[rows:, :] = jnp.transpose(row_ids).astype(BF16)
    ids[z] = ids_in[...]
    greet(w, z)

    tok_chain = Chain(links, 0, tok_in, lambda p: tok.at[p])
    ids_chain = Chain(links, 2, ids_in, lambda p: ids.at[p])
    wo_chain = Chain(links, 4, wo_in, lambda p: wo_blocks.at[w, p])
    cot_chain = Chain(links, 6, cot_full, lambda p: cot_o.at[chip, p])

    def wq_ring(step, kind):
        to = links.plane(step, 1)
        here = wq_blocks.at[w, z, :, pl.ds(kind * size, size if kind < 3 else 128)]
        src = window(step, kind) if kind < 3 else misc_in
        return links.copy(39 + kind if kind else 8, step, src, here, (w, to))

    def wq_gather(step):
        source = links.plane(step, -1)
        return Gather(links, 9, step, step, lambda i: wq_blocks.at[i, source])

    def wo_gather(turn):
        step = step_at(z, turn)
        source = links.plane(step, -1)
        return Gather(links, 16, step, turn, lambda i: wo_blocks.at[i, source])

    def cot_gather(turn):
        step = step_at(z, turn)
        source = links.plane(step, -1)
        return Gather(links, 23, step, turn, lambda i: cot_o.at[i // 2, source], False)

    def weights_ring(step, flip):
        to = links.plane(step, 1)
        return links.copy(
            26 + flip, step, we_in.at[to, chip ^ flip], hop.at[step - 1, chip ^ flip], (w, to)
        )

    def weights_step(turn):
        return 0 if turn == 3 else direct_at(z, turn)

    def weights_block(turn, flip):
        if turn == 3:
            return we_in.at[z, chip ^ flip]
        return hop.at[weights_step(turn) - 1, chip ^ flip]

    def weights_place(turn, owner):
        return we_o.at[owner, links.plane(weights_step(turn), -1)]

    def weights_plane(turn, flip):
        to = (w ^ (2 * flip), z)
        return links.copy(
            29 + flip, turn, weights_block(turn, flip), weights_place(turn, w), to
        )

    def weights_keep(turn):
        return pltpu.make_async_copy(
            weights_block(turn, 0), weights_place(turn, w), load_sems.at[6 + turn]
        )

    def weights_core(turn, flip):
        block = weights_place(turn, w ^ (2 * flip))
        return links.copy(
            34 + flip, turn, block if flip else weights_block(turn, 0), block, (w ^ 1, z)
        )

    def weights_send(step):
        for flip in (3, 1, 2, 0):
            weights_ring(step, flip).start()

    def weights_next(turn):
        for flip in (3, 1, 2):
            if turn < 3:
                weights_ring(weights_step(turn), flip).wait_recv()
            weights_plane(turn, flip).start()
        if turn < 3:
            weights_ring(weights_step(turn), 0).wait_recv()
        weights_core(turn, 0).start()
        weights_keep(turn).start()

    def weights_end(turn):
        for flip in (1, 2, 3):
            weights_plane(turn, flip).wait_recv()
            weights_core(turn, flip).start()

    def mixed_ring(step):
        to = links.plane(step, 1)
        return links.copy(38, step, mixed_send.at[to], mixed_got.at[z], (w, to))

    tok_chain.begin()
    ids_chain.begin()
    for step in (1, 2, 3):
        for kind in range(4):
            wq_ring(step, kind).start()
    for kind in range(3):
        wq_own(kind).wait()
    wq_gather(0).begin()
    for keep in keeps[:2]:
        keep.wait()

    expert = lax.broadcasted_iota(jnp.int32, (128, rows), 0)
    member = expert == 0
    for route in range(routes_in.shape[0]):
        member = member | (expert == routes_in[route : route + 1, :] + 1)
    cot_full[:, :width] = cot_in[...]
    cot_full[:, width:] = jnp.transpose(member.astype(F32)).astype(BF16)
    keeps[2].start()
    tok_chain.arrive(0)
    ids_chain.arrive(0)
    for step in (1, 2, 3):
        for kind in range(4):
            wq_ring(step, kind).wait_recv()
        wq_gather(step).begin()
    wo_chain.begin()
    tok_chain.arrive(1)
    ids_chain.arrive(1)
    cot_chain.begin()

    def experts_first(source, low):
        for i in range(0, source.shape[2], 128):
            part = jnp.swapaxes(source[:, :, i : i + 128].astype(F32), 0, 1).astype(BF16)
            for expert in range(source.shape[1]):
                we_in[expert % PLANES, expert // PLANES, :, low + i : low + i + 128] = part[expert]

    end_plane = (z == 0) | (z == PLANES - 1)

    @pl.when(jnp.logical_not(end_plane))
    def _():
        tok_chain.arrive(2)
        ids_chain.arrive(2)

    loop(0, 4, lambda step: wq_gather(step).relay())
    experts_first(up_in, 0)
    experts_first(down_in, up_in.shape[2])

    @pl.when(end_plane)
    def _():
        tok_chain.arrive(2)
        ids_chain.arrive(2)
        send_next(z, weights_send)

    wo_chain.arrive(0)
    wo_gather(0).begin()
    wo_gather(3).begin()
    keeps[2].wait()
    cot_gather(3).begin()
    weights_next(3)
    for i in range(PLANES):
        for j in range(PLANES):
            here = (slice(i * rows, (i + 1) * rows), slice(j * rows, (j + 1) * rows))
            if j > i:
                mask[here] = jnp.full((rows, rows), -1e30, F32)
            else:
                same = ids[i, rows:, :].astype(F32) == ids[j, :rows, :].astype(F32)
                if i == j:
                    same = same & (
                        lax.broadcasted_iota(jnp.int32, (rows, rows), 1)
                        <= lax.broadcasted_iota(jnp.int32, (rows, rows), 0)
                    )
                mask[here] = jnp.where(same, 0.0, -1e30)
    loop(0, 4, lambda step: wq_gather(step).end())
    loop(0, 4, lambda step: wq_gather(step).settle())

    def assemble(blocks, to):
        def body(i):
            for p in range(PLANES):
                staged[p * own : (p + 1) * own, :] = blocks[i, p].astype(F32)
            span = PLANES * own
            to[pl.ds(pl.multiple_of(i * span, 16), span), :] = staged[...].astype(BF16)

        loop(0, blocks.shape[0], body)

    cot_chain.arrive(0)
    cot_gather(0).begin()
    outputs = [
        pltpu.make_async_copy(src, dst, out_sems.at[i])
        for i, (src, dst) in enumerate(
            (
                (wq_o, wq_out),
                (first_o, first_out),
                (qkv_o, qkv_out),
                (exact_o, exact_out),
                (mixed_o, mixed_out),
                (wo_o, wo_out),
            )
        )
    ]
    assemble(wq_blocks, wq_o)
    outputs[0].start()
    gains = jnp.transpose(wq_o[:, size * 3 :].astype(F32))
    gain_one = gains[16:17, :]
    gain_two = gains[17:18, :]

    def normalise(p):
        block = tok[p].astype(F32)
        inverse = lax.rsqrt(jnp.mean(block * block, axis=1, keepdims=True) + epsilon)
        first_o[p] = (block * inverse * gain_one).astype(BF16)

    loop(0, PLANES, normalise)
    outputs[1].start()
    wo_chain.arrive(1)
    wo_gather(1).begin()
    cot_chain.arrive(1)
    cot_gather(1).begin()

    def project(p):
        span = pl.ds(pl.multiple_of(p * rows, 128), rows)
        cosine, sine = cos_in[span, :], sin_in[span, :]
        for kind in range(3):
            part = mul(first_o[p], wq_o[:, kind * size : (kind + 1) * size], 1, 0)
            for head in range(WINDOW):
                here = part[:, head * HEAD_DIM : (head + 1) * HEAD_DIM]
                if kind < 2:
                    here = here * cosine + pltpu.roll(here, HEAD_DIM // 2, 1) * sine
                if kind == 0:
                    here = here * (HEAD_DIM ** (-0.5))
                qkv_o[kind, head, span, :] = here.astype(BF16)

    loop(0, PLANES, project)
    outputs[2].start()
    wo_chain.arrive(2)
    wo_gather(2).begin()
    cot_chain.arrive(2)
    cot_gather(2).begin()

    @pl.when(jnp.logical_not(end_plane))
    def _():
        send_next(z, weights_send)

    def attend(head):
        exact = softmax_rows(mul(qkv_o[0, head], qkv_o[1, head], 1, 1), mask[...])
        exact_o[head] = exact
        mixed_o[head] = mul(exact.astype(BF16), qkv_o[2, head], 1, 0)

    loop(0, WINDOW, attend)
    outputs[3].start()
    outputs[4].start()
    for p in range(PLANES):
        for head in range(WINDOW):
            mixed_send[p, :, head * HEAD_DIM : (head + 1) * HEAD_DIM] = mixed_o[
                head, p * rows : (p + 1) * rows, :
            ].astype(BF16)
    for step in (1, 2, 3):
        mixed_ring(step).start()
    mixed_got[z] = mixed_send[z]
    send_beyond(z, weights_send)
    loop(0, 4, lambda turn: wo_gather(turn).relay())
    weights_next(0)
    loop(0, 4, lambda turn: wo_gather(turn).end())
    loop(0, 4, lambda turn: cot_gather(turn).relay())
    weights_end(3)
    weights_end(0)
    loop(0, 4, lambda turn: wo_gather(turn).settle())
    assemble(wo_blocks, wo_o)
    outputs[5].start()
    for step in (1, 2, 3):
        mixed_ring(step).wait_recv()
    column = 0
    for p, (a, b) in enumerate(KEEP):
        span = (b - a) * HEAD_DIM
        mixed_rows_o[:, column : column + span] = mixed_got[p, :, a * HEAD_DIM : b * HEAD_DIM]
        column += span

    def out_project(i):
        here = at(i * 256, 256)
        middle_o[:, here] = tok_in_f32(tok, z, here) + mul(mixed_rows_o[...], wo_o[:, here], 1, 0)

    loop(0, width // 256, out_project)
    middle = middle_o[...]
    inverse = lax.rsqrt(jnp.mean(middle * middle, axis=1, keepdims=True) + epsilon)
    second_o[...] = (middle * inverse * gain_two).astype(BF16)
    loop(0, 4, lambda turn: cot_gather(turn).end())
    weights_next(1)
    weights_next(2)
    weights_end(1)
    weights_end(2)
    loop(0, 4, lambda turn: cot_gather(turn).settle())
    for output in outputs:
        output.wait()
    for chain in (tok_chain, ids_chain, wo_chain, cot_chain):
        chain.settle()
    for step in (0, 1, 2, 3):
        weights_keep(step).wait()
        for flip in (0, 1, 2, 3):
            if step:
                weights_ring(step, flip).wait_send()
            if flip:
                weights_plane(step, flip).wait_send()
            weights_core(step, flip).wait_send()
            weights_core(step, flip).wait_recv()
        if step:
            for kind in range(4):
                wq_ring(step, kind).wait_send()
            mixed_ring(step).wait_send()


def tok_in_f32(tok, z, here):
    return tok[z, :, here].astype(F32)


def start(tok, wq, wo, seq, routes, router, gains, up, down, cot, tables, collective):
    rows, width = tok.shape
    own = wo.shape[0]
    experts = up.shape[1]
    hidden3 = up.shape[2] + down.shape[2]
    seqlen = PLANES * rows
    size = WINDOW * HEAD_DIM
    blocks = (8, PLANES, own, width)
    any_spec = pl.BlockSpec(memory_space=pl.ANY)
    vmem_spec = pl.BlockSpec(memory_space=pltpu.VMEM)
    kept = [
        ((width, width), BF16),
        ((width, width), BF16),
        ((PLANES, rows, width), BF16),
        ((3, WINDOW, seqlen, HEAD_DIM), BF16),
        ((WINDOW, seqlen, seqlen), F32),
        ((WINDOW, seqlen, HEAD_DIM), F32),
    ]
    shapes = [
        ((8, PLANES, own, hidden3), BF16),
        ((4, PLANES, rows, width + 128), BF16),
        *kept,
        ((rows, width), BF16),
        ((rows, width), F32),
        ((rows, width), BF16),
        ((3, 4, own, hidden3), BF16),
    ]
    return pl.pallas_call(
        start_kernel,
        out_shape=[jax.ShapeDtypeStruct(shape, kind) for shape, kind in shapes],
        in_specs=[any_spec] * 3 + [vmem_spec] * 9,
        out_specs=[any_spec] * 8 + [vmem_spec] * 3 + [any_spec],
        scratch_shapes=[
            pltpu.VMEM((PLANES, rows, width), BF16),
            pltpu.VMEM((PLANES, 2 * rows, rows), BF16),
            pltpu.VMEM(blocks, BF16),
            pltpu.VMEM(blocks, BF16),
            pltpu.VMEM((PLANES * own, width), F32),
            pltpu.VMEM((seqlen, seqlen), F32),
            pltpu.VMEM((PLANES, rows, size), BF16),
            pltpu.VMEM((PLANES, rows, size), BF16),
            pltpu.VMEM((2 * rows, rows), BF16),
            pltpu.VMEM((PLANES, experts // PLANES, own, hidden3), BF16),
            pltpu.VMEM((rows, width + 128), BF16),
            pltpu.VMEM((128, 128), F32),
            pltpu.VMEM((own, 128), BF16),
            *[pltpu.VMEM(shape, kind) for shape, kind in kept],
            pltpu.SemaphoreType.DMA((10,)),
            pltpu.SemaphoreType.DMA((6,)),
            pltpu.SemaphoreType.DMA((43, 4)),
            pltpu.SemaphoreType.DMA((43, 4)),
        ],
        compiler_params=pltpu.CompilerParams(
            collective_id=collective, has_side_effects=True, vmem_limit_bytes=60 * 2**20
        ),
        name="start",
    )(tok, wq, wo, seq, routes, router, gains, up, down, cot, *tables)[:-1]


def add_blocks(out, *terms):
    rows = out.shape[0]

    def body(i, carry):
        part = pl.ds(pl.multiple_of(i * 16, 16), 16)
        total = terms[0][part, :].astype(F32)
        for term in terms[1:]:
            total = total + term[part, :].astype(F32)
        out[part, :] = total.astype(out.dtype)
        return carry

    lax.fori_loop(0, rows // 16, body, 0)


def experts_kernel(
    x_in, cot_in, weights_in, misc_in, grads_o, outs_o, outs_one_o, sums_o,
    x, cot, weights, misc, act, scaled, slopes, gate, outs, parts, got_one, got_two, got_far, stage,
    load_sems, send_sems, recv_sems,
):
    w, z = place()
    chip = w // 2
    expert = chip * PLANES + z
    rows, width = x_in.shape
    hidden = weights.shape[1] // 3
    group_rows = 4 * rows

    def remote(kind, step, src, dst, device):
        return pltpu.make_async_remote_copy(
            src_ref=src,
            dst_ref=dst,
            send_sem=send_sems.at[kind, step],
            recv_sem=recv_sems.at[kind, step],
            device_id=device,
            device_id_type=MESH_IDS,
        )

    def plane_of(step, sign):
        return lax.rem(z + PLANES + sign * step, PLANES)

    def step_at(turn):
        step = 0
        for plane, steps in enumerate(((3, 2, 1, 0), (1, 3, 2, 0), (3, 1, 2, 0), (1, 2, 3, 0))):
            for number, value in enumerate(steps):
                step = jnp.where((z == plane) & (turn == number), value, step)
        return step

    def axes(turn):
        first = 1 + lax.rem(turn, 2)
        return first, 3 - first

    def ring(step, up):
        to = lax.rem(step + 1, 4) if up else lax.rem(step + 3, 4)
        return pltpu.make_async_remote_copy(
            src_ref=x.at[step, chip],
            dst_ref=x.at[to, chip],
            send_sem=send_sems.at[0 if up else 8, step],
            recv_sem=recv_sems.at[0, to],
            device_id=(w, z + 1 if up else z - 1),
            device_id_type=MESH_IDS,
        )

    def goes(step, up):
        if up:
            return (z >= step) & (z < PLANES - 1)
        return ((z < step) | (step == 0)) & (z > 0)

    def pass_on(step):
        for up in (True, False):

            @pl.when(goes(step, up))
            def _():
                ring(step, up).start()

    def arrive(step):
        pltpu.make_async_remote_copy(
            src_ref=x.at[step, chip],
            dst_ref=x.at[step, chip],
            send_sem=send_sems.at[0, step],
            recv_sem=recv_sems.at[0, step],
            device_id=(w, z),
            device_id_type=MESH_IDS,
        ).wait_recv()

    def direct(step, flip):
        block = x.at[step, chip]
        return remote(flip, step, block, block, (w ^ (2 * flip), z))

    def across(turn):
        first, second = axes(turn)
        step = step_at(turn)
        block = x.at[step, chip ^ first]
        return remote(3, step, block, block, (w ^ (2 * second), z))

    def near(turn, which):
        first, _ = axes(turn)
        step = step_at(turn)
        block = chip ^ 3 if which else chip ^ first
        return remote(
            4 + which, step, parts.at[step, block], got_one.at[step, which], (w ^ (2 * first), z)
        )

    def cross(turn):
        _, second = axes(turn)
        step = step_at(turn)
        return remote(
            6, step, parts.at[step, chip ^ second], got_two.at[step], (w ^ (2 * second), z)
        )

    def far(step):
        return remote(7, step, parts.at[step, chip], got_far.at[step - 1], (w, plane_of(step, -1)))

    def outs_near(step, which):
        first, _ = axes(step)
        block = chip ^ 3 if which else chip ^ first
        return remote(
            9 + which, step, outs_o.at[step, block], outs_one_o.at[step, which], (w ^ (2 * first), z)
        )

    def cot_load(step):
        return pltpu.make_async_copy(
            cot_in.at[:, plane_of(step, -1)], cot.at[step], load_sems.at[step]
        )

    def outs_out(turn):
        return pltpu.make_async_copy(
            outs.at[lax.rem(turn, 2)], outs_o.at[step_at(turn)], load_sems.at[9 + lax.rem(turn, 2)]
        )

    def grads_out(low, size, slot):
        return pltpu.make_async_copy(
            stage.at[slot, :, pl.ds(0, size)], grads_o.at[:, low], load_sems.at[4 + slot]
        )

    loads = [
        pltpu.make_async_copy(src, dst, load_sems.at[6 + i])
        for i, (src, dst) in enumerate(
            (
                (x_in, x.at[0, chip]),
                (misc_in.at[:, pl.ds(misc_in.shape[1] - 128, 128)], misc),
                (weights_in, weights),
            )
        )
    ]
    for load in loads:
        load.start()
    loop(0, 4, lambda step: cot_load(step).start())
    greet(w, z)
    loads[0].wait()
    pass_on(0)

    def begin(turn):
        step = step_at(turn)

        @pl.when(turn < 3)
        def _():
            arrive(step)
            pass_on(step)

        direct(step, 1).start()
        direct(step, 2).start()

    def relay(turn):
        step = step_at(turn)
        direct(step, 1).wait_recv()
        direct(step, 2).wait_recv()
        across(turn).start()

    begin(3)
    begin(0)
    begin(1)
    relay(0)
    begin(2)
    relay(1)
    loads[1].wait()
    loads[2].wait()

    def first_half(step):
        cot_load(step).wait()
        rows_in = x[step].reshape(group_rows, width)
        members = cot[step, :, :, width:].reshape(group_rows, 128).astype(F32)
        logits = mul(rows_in, misc[...], 1, 0)
        lane = lax.broadcasted_iota(jnp.int32, logits.shape, 1)
        routed = (lane > 0) & (lane < 16)
        top = jnp.max(jnp.where(routed, logits, -1e30), axis=1, keepdims=True)
        powers = jnp.where(routed, jnp.exp(logits - top), 0.0)
        probs = jnp.where(lane == 0, 1.0, powers / jnp.sum(powers, axis=1, keepdims=True))
        own = jnp.where(lane == expert, members, 0.0)
        gate[0] = jnp.broadcast_to(jnp.sum(probs * own, axis=1, keepdims=True), gate.shape[1:])
        gate[1] = own

        def hidden_chunk(low, size):
            here = x[step].reshape(group_rows, width)
            gate_part = mul(here, weights[:, at(low, size)], 1, 0)
            up_part = mul(here, weights[:, at(hidden + low, size)], 1, 0)
            grad_act = mul(
                cot[step, :, :, :width].reshape(group_rows, width),
                weights[:, at(2 * hidden + low, size)],
                1,
                0,
            )
            scale = gate[0][:, :1]
            grad_act = grad_act * scale
            sigmoid = 1.0 / (1.0 + jnp.exp(-gate_part))
            silu = gate_part * sigmoid
            activated = (silu * up_part).astype(BF16)
            act[:, at(low, size)] = activated
            scaled[step, :, at(low, size)] = (activated.astype(F32) * scale).astype(BF16)
            slopes[step, :, at(low, size)] = (
                grad_act * up_part * (sigmoid + silu * (1.0 - sigmoid))
            ).astype(BF16)
            slopes[step, :, at(hidden + low, size)] = (grad_act * silu).astype(BF16)

        loop(0, hidden // 256, lambda i: hidden_chunk(i * 256, 256))
        if hidden % 256:
            hidden_chunk(hidden // 256 * 256, hidden % 256)

    def second_half(turn, step):
        def width_body(i, total):
            low = i * 256
            expert_rows = mul(act[...], weights[at(low, 256), 2 * hidden :], 1, 1)
            expert_rows = expert_rows.astype(BF16).astype(F32)
            outs[lax.rem(turn, 2), :, :, at(low, 256)] = (
                (expert_rows * gate[0][:, :1]).astype(BF16).reshape(4, rows, 256)
            )
            product = expert_rows * cot[step, :, :, at(low, 256)].reshape(group_rows, 256).astype(F32)
            grad_in = mul(slopes[step], weights[at(low, 256), : 2 * hidden], 1, 1)
            parts[step, :, :, at(low, 256)] = grad_in.astype(BF16).reshape(4, rows, 256)
            return total + product[:, :128] + product[:, 128:]

        total = lax.fori_loop(0, width // 256, width_body, jnp.zeros((group_rows, 128), F32))
        prob = jnp.sum(total, axis=1, keepdims=True) * gate[1]
        high = prob.astype(BF16)
        low = (prob - high.astype(F32)).astype(BF16)
        low = pltpu.roll(low.astype(F32), 32, 1).astype(BF16)
        parts[step, :, :, width:] = (high + low).reshape(4, rows, 128)

    def send_cross(turn):
        _, second = axes(turn)
        step = step_at(turn)
        near(turn, 1).wait_recv()
        block = parts.at[step, chip ^ second]
        add_blocks(block, block, got_one.at[step, 1])
        cross(turn).start()

    def send_far(turn):
        step = step_at(turn)
        near(turn, 0).wait_recv()
        cross(turn).wait_recv()
        block = parts.at[step, chip]
        add_blocks(block, block, got_one.at[step, 0], got_two.at[step])
        far(step).start()

    def group(turn):
        step = step_at(turn)
        across(turn).wait_recv()
        first_half(step)

        @pl.when(turn < 2)
        def _():
            relay(turn + 2)

        @pl.when(turn > 1)
        def _():
            outs_out(turn - 2).wait()

        second_half(turn, step)
        outs_out(turn).start()

        @pl.when(turn > 0)
        def _():
            send_cross(turn - 1)

        near(turn, 1).start()
        near(turn, 0).start()

        @pl.when(turn > 1)
        def _():
            send_far(turn - 2)

    loop(0, 4, group)

    def weight_chunk(left, right, low, size, offset, i):
        slot = lax.rem(i, 2)

        @pl.when(i >= 2)
        def _():
            grads_out(pl.ds(0, 256), 256, slot).wait()

        total = None
        for step in range(4):
            term = mul(
                left[step, :, :, :width].reshape(group_rows, width), right[step, :, at(low, size)], 0, 0
            )
            total = term if total is None else total + term
        stage[slot, :, :size] = total.astype(BF16)
        grads_out(at(offset + low, size), size, slot).start()

    ups, downs = 2 * hidden // 256, hidden // 256

    def up_chunk(i):
        weight_chunk(x, slopes, i * 256, 256, 0, i)

    def down_chunk(i):
        weight_chunk(cot, scaled, (i - ups) * 256, 256, 2 * hidden, i)

    loop(0, 4, up_chunk)
    send_cross(3)
    outs_out(2).wait()
    outs_out(3).wait()
    loop(0, 4, lambda step: (outs_near(step, 1).start(), outs_near(step, 0).start()))
    loop(4, 6, up_chunk)
    send_far(2)
    loop(6, ups, up_chunk)
    loop(ups, ups + downs, down_chunk)
    last = ups + downs
    if hidden % 256:
        weight_chunk(cot, scaled, downs * 256, hidden % 256, 2 * hidden, jnp.int32(last))
        grads_out(pl.ds(0, 256), 256, (last - 1) % 2).wait()
        grads_out(pl.ds(0, hidden % 256), hidden % 256, last % 2).wait()
    else:
        grads_out(pl.ds(0, 256), 256, last % 2).wait()
        grads_out(pl.ds(0, 256), 256, (last - 1) % 2).wait()
    near(3, 0).wait_recv()
    cross(3).wait_recv()
    loop(1, 4, lambda step: far(step).wait_recv())
    add_blocks(
        sums_o,
        parts.at[0, chip],
        got_one.at[0, 0],
        got_two.at[0],
        got_far.at[0],
        got_far.at[1],
        got_far.at[2],
    )

    def settle(turn):
        step = step_at(turn)
        direct(step, 1).wait_send()
        direct(step, 2).wait_send()
        across(turn).wait_send()
        near(turn, 0).wait_send()
        near(turn, 1).wait_send()
        cross(turn).wait_send()
        for which in (0, 1):
            outs_near(turn, which).wait_send()
            outs_near(turn, which).wait_recv()

        @pl.when(turn < 3)
        def _():
            far(step).wait_send()

        for up in (True, False):

            @pl.when(goes(step, up))
            def _():
                ring(step, up).wait_send()

    loop(0, 4, settle)


def run_experts(second_in, cot_all, weights, misc, collective):
    rows, width = second_in.shape
    hidden = weights.shape[1] // 3
    sums_width = width + 128
    block = (rows, sums_width)
    return pl.pallas_call(
        experts_kernel,
        out_shape=[
            jax.ShapeDtypeStruct((width, 3 * hidden), BF16),
            jax.ShapeDtypeStruct((4, 4, rows, width), BF16),
            jax.ShapeDtypeStruct((4, 2, rows, width), BF16),
            jax.ShapeDtypeStruct((rows, sums_width), F32),
        ],
        in_specs=[pl.BlockSpec(memory_space=pl.ANY)] * 4,
        out_specs=[
            pl.BlockSpec(memory_space=pl.ANY),
            pl.BlockSpec(memory_space=pl.ANY),
            pl.BlockSpec(memory_space=pl.ANY),
            pl.BlockSpec(memory_space=pltpu.VMEM),
        ],
        scratch_shapes=[
            pltpu.VMEM((4, 4, rows, width), BF16),
            pltpu.VMEM((4, 4, rows, width + 128), BF16),
            pltpu.VMEM((width, 3 * hidden), BF16),
            pltpu.VMEM((width, 128), BF16),
            pltpu.VMEM((4 * rows, hidden), BF16),
            pltpu.VMEM((4, 4 * rows, hidden), BF16),
            pltpu.VMEM((4, 4 * rows, 2 * hidden), BF16),
            pltpu.VMEM((2, 4 * rows, 128), F32),
            pltpu.VMEM((2, 4, rows, width), BF16),
            pltpu.VMEM((4, 4) + block, BF16),
            pltpu.VMEM((4, 2) + block, BF16),
            pltpu.VMEM((4,) + block, BF16),
            pltpu.VMEM((3,) + block, BF16),
            pltpu.VMEM((2, width, 256), BF16),
            pltpu.SemaphoreType.DMA((11,)),
            pltpu.SemaphoreType.DMA((11, 4)),
            pltpu.SemaphoreType.DMA((11, 4)),
        ],
        compiler_params=pltpu.CompilerParams(
            collective_id=collective, has_side_effects=True, vmem_limit_bytes=62 * 2**20
        ),
        name="experts",
    )(second_in, cot_all, weights, misc)


def finish_kernel(
    outs_in, outs_one_in, grads_in, exact_in, mixed_in, qkv_in, first_in, wq_in, wo_in,
    cos_in, sin_in, rows_in, sums_in, second_in, middle_in, cot_in, tok_in,
    output_o, grad_o, table_o, q_o, o_o,
    outs, outs_one, outs_two, outs_far, grads_own, grads_got, heads, exact, mixed, qkv, first, wq,
    wo, heads_send, attn, grad_middle, first_got, projected, first_part, dense, dense_got, dense_one,
    dense_two, dense_far, dense_sum, load_sems, send_sems, recv_sems,
):
    links = Links(send_sems, recv_sems)
    w, z = links.w, links.z
    chip, core = w // 2, w % 2
    rows = outs.shape[2]
    width = outs.shape[3]
    size = WINDOW * HEAD_DIM
    steps = (1, 2, 3, 0)
    block_rows = o_o.shape[0] // 4
    half = o_o.shape[1] // 2
    plane_rows = o_o.shape[0]
    remote, plane_of = links.copy, links.plane

    def axes(step):
        one = 1 + lax.rem(step, 2)
        return one, 3 - one

    def heads_ring(step):
        to = plane_of(step, 1)
        return remote(37, step, heads_send.at[to], heads.at[z], (w, to))

    def grads_load(step):
        return pltpu.make_async_copy(
            grads_in.at[plane_of(step, 1), core], grads_own.at[step], load_sems.at[0, step]
        )

    def grads_swap(step):
        return remote(
            0, step, grads_in.at[plane_of(step, 1), 1 - core], grads_got.at[step], (w ^ 1, z)
        )

    def grads_ring(step):
        return remote(1, step, grads_own.at[step], table_o.at[chip, z, core], (w, plane_of(step, 1)))

    def grads_keep():
        return pltpu.make_async_copy(
            grads_own.at[0], table_o.at[chip, z, core], load_sems.at[1, 0]
        )

    def grads_gather(turn):
        step = direct_at(z, turn)
        source = plane_of(step, -1)
        half = grads_own.shape[1] // 2
        return Gather(
            links, 2, step, turn, lambda i: table_o.at[i // 2, source, i % 2], True, half
        )

    def outs_loads(step):
        _, two = axes(step)
        return [
            pltpu.make_async_copy(src, dst, load_sems.at[2 + 3 * (i > 0) + (i > 1), step])
            for i, (src, dst) in enumerate(
                (
                    (outs_in.at[step, chip], outs.at[step, 0]),
                    (outs_in.at[step, chip ^ two], outs.at[step, 1]),
                    (outs_one_in.at[step], outs_one.at[step]),
                )
            )
        ]

    def cross(step):
        _, two = axes(step)
        return remote(11, step, outs.at[step, 1], outs_two.at[step], (w ^ (2 * two), z))

    def far(step):
        return remote(12, step, outs.at[step, 0], outs_far.at[step - 1], (w, plane_of(step, -1)))

    def part(kind, step):
        return dense.at[0, kind, plane_of(step, 1)]

    def dense_swap(kind, step):
        to = plane_of(step, 1)
        return remote(
            13 + 4 * kind, step, dense.at[1, kind, to], dense_got.at[kind, step], (w ^ 1, z)
        )

    def rows_of(block):
        return pl.ds(pl.multiple_of(block * block_rows, 16), block_rows)

    def dense_axes(kind):
        return 1 + kind, 2 - kind

    def dense_near(kind, step, which):
        one, _ = dense_axes(kind)
        block = chip ^ 3 if which else chip ^ one
        return remote(
            14 + 4 * kind + which,
            step,
            part(kind, step).at[rows_of(block)],
            dense_one.at[kind, step, which],
            (w ^ (2 * one), z),
        )

    def dense_cross(kind, step):
        _, two = dense_axes(kind)
        return remote(
            16 + 4 * kind,
            step,
            part(kind, step).at[rows_of(chip ^ two)],
            dense_two.at[kind, step],
            (w ^ (2 * two), z),
        )

    def place_of(owner):
        return rows_of(owner // 2), at(lax.rem(owner, 2) * half, half)

    def dense_ring(kind, step):
        own = part(kind, step).at[rows_of(chip)]
        here, columns = place_of(w)
        to = q_o.at[z, here, columns] if kind == 0 else dense_far.at[step - 1]
        return remote(21 + kind, step, own, to, (w, plane_of(step, 1)))

    def dense_keep():
        here, columns = place_of(w)
        return pltpu.make_async_copy(
            part(0, 0).at[rows_of(chip)], q_o.at[z, here, columns], load_sems.at[1, 1]
        )

    def dense_last():
        here, columns = place_of(w)
        return pltpu.make_async_copy(dense_sum, o_o.at[here, columns], load_sems.at[1, 2])

    def q_slot(step):
        source = plane_of(step, -1)

        def slot(owner):
            here, columns = place_of(owner)
            return q_o.at[source, here, columns]

        return slot

    def o_slot(owner):
        here, columns = place_of(owner)
        return o_o.at[here, columns]

    def q_gather(step):
        return Gather(links, 23, step, step, q_slot(step))

    def o_gather():
        return Gather(links, 30, 0, 0, o_slot)

    def first_ring(step):
        to = plane_of(step, 1)
        return remote(38, step, first_part.at[to], first_got.at[step - 1], (w, to))

    loads = [
        pltpu.make_async_copy(src, dst, load_sems.at[3 + i // 4, i % 4])
        for i, (src, dst) in enumerate(
            (
                (wq_in, wq),
                (wo_in, wo),
                (exact_in, exact),
                (mixed_in, mixed),
                (qkv_in, qkv),
                (first_in, first),
            )
        )
    ]
    for step in range(4):
        for load in outs_loads(step):
            load.start()
    for load in loads[:2]:
        load.start()
    for step in steps:
        grads_load(step).start()
    for load in loads[2:]:
        load.start()
    greet(w, z)
    for step in steps:
        grads_swap(step).start()

    def grads_ready(step):
        grads_load(step).wait()
        grads_swap(step).wait_recv()
        add_blocks(grads_own.at[step], grads_own.at[step], grads_got.at[step])

    def outs_cross(step):
        for load in outs_loads(step):
            load.wait()
        add_blocks(outs.at[step, 1], outs.at[step, 1], outs_one.at[step, 1])
        cross(step).start()

    loop(0, 4, outs_cross)
    grads_ready(0)
    keep = grads_keep()
    keep.start()
    keep.wait()
    grads_gather(3).begin()
    for load in loads[:2]:
        load.wait()

    lane = lax.broadcasted_iota(jnp.int32, (rows, 128), 1)
    routed = (lane > 0) & (lane < 16)
    logits = jnp.where(routed, mul(second_in[...], wq[:, 3 * size :], 1, 0), -1e30)
    powers = jnp.where(routed, jnp.exp(logits - jnp.max(logits, axis=1, keepdims=True)), 0.0)
    probs = powers / jnp.sum(powers, axis=1, keepdims=True)
    high_low = sums_in[:, width:]
    grad_probs = jnp.where(routed, high_low + pltpu.roll(high_low, 96, 1), 0.0)
    grad_logits = probs * (grad_probs - jnp.sum(probs * grad_probs, axis=1, keepdims=True))
    grad_logits = grad_logits.astype(BF16)
    gains = jnp.transpose(wq[:, 3 * size :].astype(F32))
    gain_one, gain_two = gains[16:17, :], gains[17:18, :]
    grad_second = sums_in[:, :width] + mul(grad_logits, wq[:, 3 * size :], 1, 1)
    middle = middle_in[...]
    inverse = lax.rsqrt(jnp.mean(middle * middle, axis=1, keepdims=True) + epsilon)
    normed = middle * inverse
    grad_normed = grad_second * gain_two
    grad_here = cot_in[...].astype(F32) + inverse * (
        grad_normed - normed * jnp.mean(grad_normed * normed, axis=1, keepdims=True)
    )
    grad_middle[...] = grad_here
    attn[...] = grad_here.astype(BF16)
    gain_two_row = jnp.sum(grad_second * normed, axis=0, keepdims=True)
    router_part = mul(second_in[...], grad_logits, 0, 0)
    for plane, begin in enumerate(STARTS):
        grad_mixed = mul(
            attn[...], wo[begin * HEAD_DIM : begin * HEAD_DIM + size, :], 1, 1
        )
        heads_send[plane] = grad_mixed.astype(BF16)
    for step in (1, 2, 3):
        heads_ring(step).start()
    heads[z] = heads_send[z]
    loop(1, 4, grads_ready)
    for step in (1, 2, 3):
        heads_ring(step).wait_recv()
    send_next(z, lambda step: grads_ring(step).start())

    def out_weight(i):
        side = i // (half // 128)
        low = at((i - side * (half // 128)) * 128, 128)
        total = mul(rows_in[...], attn[:, at(i * 128, 128)], 0, 0).astype(BF16)
        dense[side ^ core, 1, :, :, low] = total.reshape(PLANES, plane_rows, 128)

    loop(0, width // 128, out_weight)
    for step in steps:
        dense_swap(1, step).start()
    for load in loads[2:]:
        load.wait()

    def head_back(head):
        keep_head = jnp.float32(0)
        for plane, (a, b) in enumerate(KEEP):
            keep_head = jnp.where((z == plane) & (head >= a) & (head < b), 1.0, keep_head)
        columns = at(head * HEAD_DIM, HEAD_DIM)
        grad_rows = heads[:, :, columns].reshape(PLANES * rows, HEAD_DIM).astype(F32) * keep_head
        delta = jnp.sum(grad_rows * mixed[head], axis=1, keepdims=True)
        grad_rows = grad_rows.astype(BF16)
        weights = exact[head]
        grad_value = mul(weights.astype(BF16), grad_rows, 0, 0)
        grad_scores = mul(grad_rows, qkv[2, head], 1, 1)
        grad_scores = (weights * (grad_scores - delta)).astype(BF16)
        grad_query = mul(grad_scores, qkv[1, head], 1, 0) * (HEAD_DIM ** (-0.5))
        grad_key = mul(grad_scores, qkv[0, head], 0, 0)

        def back(grads):
            return grads * cos_in[...] + pltpu.roll(grads * sin_in[...], HEAD_DIM // 2, 1)

        projected[:, columns] = back(grad_query).astype(BF16)
        projected[:, at(size + head * HEAD_DIM, HEAD_DIM)] = back(grad_key).astype(BF16)
        projected[:, at(2 * size + head * HEAD_DIM, HEAD_DIM)] = grad_value.astype(BF16)

    loop(0, WINDOW, head_back)

    def grads_next(turn):
        grads_ring(direct_at(z, turn)).wait_recv()
        grads_gather(turn).begin()

    grads_gather(3).relay()

    def qkv_weight(i):
        side = i // (half // 128)
        low = at((i - side * (half // 128)) * 128, 128)
        total = mul(first[...].reshape(PLANES * rows, width), projected[:, at(i * 128, 128)], 0, 0)
        dense[side ^ core, 0, :, :, low] = total.astype(BF16).reshape(PLANES, plane_rows, 128)

    loop(0, 3 * size // 128, qkv_weight)
    gain_parts = []
    for i in range(width // 256):
        here = slice(i * 256, (i + 1) * 256)
        total = mul(projected[...], wq[here, : 3 * size], 1, 1)
        first_part[:, :, here] = total.astype(BF16).reshape(PLANES, rows, 256)
        scaled = total * first[:, :, here].reshape(PLANES * rows, 256).astype(F32)
        gain_parts.append(jnp.sum(scaled, axis=0, keepdims=True))
    gain_one_row = jnp.concatenate(gain_parts, axis=1) / gain_one
    kind = lax.broadcasted_iota(jnp.int32, (128, width), 0)
    gain_rows = jnp.where(kind == 16, gain_one_row, jnp.where(kind == 17, gain_two_row, 0.0))
    misc = jnp.transpose(gain_rows) + router_part
    dense[1 ^ core, 0, :, :, half - 128 :] = misc.astype(BF16).reshape(PLANES, plane_rows, 128)
    for step in steps:
        dense_swap(0, step).start()

    loop(0, 1, grads_next)
    send_beyond(z, lambda step: grads_ring(step).start())

    def dense_ready(step):
        for kind in (0, 1):
            dense_swap(kind, step).wait_recv()
            block = part(kind, step)
            add_blocks(block, block, dense_got.at[kind, step])
            dense_near(kind, step, 1).start()
            dense_near(kind, step, 0).start()

    loop(0, 4, dense_ready)

    def outs_finish(step):
        cross(step).wait_recv()
        block = outs.at[step, 0]
        add_blocks(block, block, outs_one.at[step, 0], outs_two.at[step])

    loop(0, 4, outs_finish)
    grads_gather(0).relay()

    def dense_cross_start(step):
        for kind in (0, 1):
            _, two = dense_axes(kind)
            dense_near(kind, step, 1).wait_recv()
            block = part(kind, step).at[rows_of(chip ^ two)]
            add_blocks(block, block, dense_one.at[kind, step, 1])
            dense_cross(kind, step).start()

    loop(0, 4, dense_cross_start)
    loop(1, 3, grads_next)

    def dense_finish(step):
        for kind in (0, 1):
            dense_near(kind, step, 0).wait_recv()
            dense_cross(kind, step).wait_recv()
            block = part(kind, step).at[rows_of(chip)]
            add_blocks(block, block, dense_one.at[kind, step, 0], dense_two.at[kind, step])

        @pl.when(step > 0)
        def _():
            dense_ring(0, step).start()
            dense_ring(1, step).start()

    loop(0, 4, dense_finish)
    loop(1, 4, lambda step: far(step).start())
    loop(1, 4, lambda step: first_ring(step).start())
    keep = dense_keep()
    keep.start()
    grads_gather(3).end()
    grads_gather(0).end()
    grads_gather(1).relay()
    keep.wait()
    q_gather(0).begin()

    def q_next(step):
        dense_ring(0, step).wait_recv()
        q_gather(step).begin()
        dense_ring(1, step).wait_recv()

    loop(1, 4, q_next)
    add_blocks(
        dense_sum, part(1, 0).at[rows_of(chip)], dense_far.at[0], dense_far.at[1], dense_far.at[2]
    )
    keep = dense_last()
    keep.start()
    keep.wait()
    o_gather().begin()
    grads_gather(2).relay()
    grads_gather(1).end()
    loop(0, 4, lambda step: q_gather(step).relay())
    o_gather().relay()
    loop(1, 4, lambda step: far(step).wait_recv())

    def output_rows(i):
        here = pl.ds(pl.multiple_of(i * 16, 16), 16)
        total = middle_in[here, :] + outs[0, 0, here, :].astype(F32)
        for step in range(3):
            total = total + outs_far[step, here, :].astype(F32)
        output_o[here, :] = total.astype(BF16)

    loop(0, rows // 16, output_rows)
    for step in (1, 2, 3):
        first_ring(step).wait_recv()
    grad_first = first_part[z].astype(F32)
    for step in range(3):
        grad_first = grad_first + first_got[step].astype(F32)
    tokens = tok_in[...].astype(F32)
    inverse = lax.rsqrt(jnp.mean(tokens * tokens, axis=1, keepdims=True) + epsilon)
    normed = tokens * inverse
    grad_normed = grad_first * gain_one
    grad_o[...] = (
        grad_middle[...]
        + inverse
        * (grad_normed - normed * jnp.mean(grad_normed * normed, axis=1, keepdims=True))
    ).astype(BF16)
    loop(0, 4, lambda step: q_gather(step).end())
    o_gather().end()
    grads_gather(2).end()
    loop(0, 4, lambda turn: grads_gather(turn).settle())
    loop(0, 4, lambda step: q_gather(step).settle())
    o_gather().settle()

    def settle(step):
        grads_swap(step).wait_send()
        cross(step).wait_send()
        for kind in (0, 1):
            dense_swap(kind, step).wait_send()
            dense_near(kind, step, 0).wait_send()
            dense_near(kind, step, 1).wait_send()
            dense_cross(kind, step).wait_send()

    loop(0, 4, settle)

    def settle_rings(step):
        first_ring(step).wait_send()
        heads_ring(step).wait_send()
        grads_ring(step).wait_send()
        far(step).wait_send()
        dense_ring(0, step).wait_send()
        dense_ring(1, step).wait_send()

    loop(1, 4, settle_rings)


def finish(outs, outs_one, grads, saved, tables, at_rows, collective):
    exact, mixed, qkv, first, wq, wo = saved
    rows, width = first.shape[1:]
    seqlen = PLANES * rows
    size = WINDOW * HEAD_DIM
    plane_rows = width // PLANES
    block = (plane_rows // 4, width // 2)
    heads = (PLANES, rows, size)
    any_spec = pl.BlockSpec(memory_space=pl.ANY)
    vmem_spec = pl.BlockSpec(memory_space=pltpu.VMEM)
    return pl.pallas_call(
        finish_kernel,
        out_shape=[
            jax.ShapeDtypeStruct((rows, width), BF16),
            jax.ShapeDtypeStruct((rows, width), BF16),
            jax.ShapeDtypeStruct((4, PLANES) + grads.shape[1:], BF16),
            jax.ShapeDtypeStruct((PLANES, plane_rows, width), BF16),
            jax.ShapeDtypeStruct((plane_rows, width), BF16),
        ],
        in_specs=[any_spec] * 9 + [vmem_spec] * 8,
        out_specs=[vmem_spec] * 2 + [any_spec] * 3,
        scratch_shapes=[
            pltpu.VMEM((4, 2, rows, width), BF16),
            pltpu.VMEM((4, 2, rows, width), BF16),
            pltpu.VMEM((4, rows, width), BF16),
            pltpu.VMEM((3, rows, width), BF16),
            pltpu.VMEM((4,) + grads.shape[2:], BF16),
            pltpu.VMEM((4,) + grads.shape[2:], BF16),
            pltpu.VMEM(heads, BF16),
            pltpu.VMEM(exact.shape, F32),
            pltpu.VMEM(mixed.shape, F32),
            pltpu.VMEM(qkv.shape, BF16),
            pltpu.VMEM(first.shape, BF16),
            pltpu.VMEM(wq.shape, BF16),
            pltpu.VMEM(wo.shape, BF16),
            pltpu.VMEM(heads, BF16),
            pltpu.VMEM((rows, width), BF16),
            pltpu.VMEM((rows, width), F32),
            pltpu.VMEM((3, rows, width), BF16),
            pltpu.VMEM((seqlen, 3 * size), BF16),
            pltpu.VMEM(first.shape, BF16),
            pltpu.VMEM((2, 2, PLANES, plane_rows, width // 2), BF16),
            pltpu.VMEM((2, 4, plane_rows, width // 2), BF16),
            pltpu.VMEM((2, 4, 2) + block, BF16),
            pltpu.VMEM((2, 4) + block, BF16),
            pltpu.VMEM((3,) + block, BF16),
            pltpu.VMEM(block, BF16),
            pltpu.SemaphoreType.DMA((7, 4)),
            pltpu.SemaphoreType.DMA((39, 4)),
            pltpu.SemaphoreType.DMA((39, 4)),
        ],
        compiler_params=pltpu.CompilerParams(
            collective_id=collective, has_side_effects=True, vmem_limit_bytes=62 * 2**20
        ),
        name="finish",
    )(outs, outs_one, grads, *saved, *tables, *at_rows)


def widen_kernel(table, q, o, up_o, down_o, qkv_o, out_o, misc_o, router_o):
    columns = table.shape[2]
    split = up_o.shape[2]
    size = WINDOW * HEAD_DIM
    for low in range(0, columns, 128):
        part = jnp.swapaxes(table[:, :, low : low + 128].astype(F32), 0, 1)
        if low < split:
            up_o[:, :, low : low + 128] = part
        else:
            down_o[:, :, low - split : low - split + 128] = part
    out_o[...] = o[...].astype(F32)
    column = 0
    for kind in range(3):
        for plane, (a, b) in enumerate(KEEP):
            span = (b - a) * HEAD_DIM
            begin = kind * size + a * HEAD_DIM
            qkv_o[:, column : column + span] = q[plane, :, begin : begin + span].astype(F32)
            column += span
    total = q[0, :, 3 * size :].astype(F32)
    for plane in range(1, PLANES):
        total = total + q[plane, :, 3 * size :].astype(F32)
    misc_o[...] = total
    router_o[...] = total[:, 1 : 1 + router_o.shape[1]]


def widen(table, q, o):
    experts, rows, columns = table.shape
    width = o.shape[1]
    split = columns // 3 * 2
    step = rows // 4
    shapes = [
        (rows, experts, split),
        (rows, experts, columns - split),
        (rows, 3 * width),
        (rows, width),
        (rows, 128),
        (rows, experts - 1),
    ]
    return pl.pallas_call(
        widen_kernel,
        grid=(rows // step,),
        out_shape=[jax.ShapeDtypeStruct(shape, F32) for shape in shapes],
        in_specs=[
            pl.BlockSpec((experts, step, columns), lambda i: (0, i, 0)),
            pl.BlockSpec((PLANES, step, width), lambda i: (0, i, 0)),
            pl.BlockSpec((step, width), lambda i: (i, 0)),
        ],
        out_specs=[
            pl.BlockSpec((step,) + shape[1:], lambda i, n=len(shape): (i,) + (0,) * (n - 1))
            for shape in shapes
        ],
        compiler_params=pltpu.CompilerParams(vmem_limit_bytes=62 * 2**20),
        name="widen",
    )(table, q, o)


def windows(x):
    size = WINDOW * HEAD_DIM
    return jnp.stack([x[:, s * HEAD_DIM : s * HEAD_DIM + size] for s in STARTS])


def from_windows(x):
    return jnp.concatenate(
        [x[p, :, a * HEAD_DIM : b * HEAD_DIM] for p, (a, b) in enumerate(KEEP)], axis=1
    )


def dot(a, b, dims, out=F32):
    return lax.dot_general(a, b, ((dims[0], dims[1]), ((), ())), preferred_element_type=F32).astype(out)


def rotary_tables(seqlen):
    half_dim = HEAD_DIM // 2
    frequency = 10000.0 ** (-np.arange(half_dim, dtype=np.float32) / half_dim)
    angles = np.arange(seqlen, dtype=np.float32)[:, None] * frequency[None, :].astype(np.float32)
    cosine, sine = np.cos(angles), np.sin(angles)
    return (
        jnp.asarray(np.concatenate([cosine, cosine], axis=1), F32),
        jnp.asarray(np.concatenate([-sine, sine], axis=1), F32),
    )


def expert_local(
    tokens, seq_ids, routes, cotangent, gain_attn, w_qkv, w_out, gain_ffn, w_router, w_up, w_down
):
    rows, width = tokens.shape
    own = w_out.shape[0]
    experts = w_router.shape[1]
    seqlen = PLANES * rows
    size = WINDOW * HEAD_DIM

    tables = rotary_tables(seqlen)
    (
        we_all, cot_all, wq_all, out_weight, first_in, qkv, weights_exact, mixed_exact, mixed, middle,
        second_in,
    ) = start(
        tokens,
        w_qkv,
        w_out,
        seq_ids[None, :],
        routes.T,
        w_router.T,
        jnp.stack([gain_attn, gain_ffn]),
        w_up,
        w_down,
        cotangent,
        tables,
        1,
    )

    weights = we_all.reshape(width, 3 * FF)
    grads, outs, outs_one, sums = run_experts(second_in, cot_all, weights, wq_all, 3)

    output, grad_tokens, table, q_all, o_all = finish(
        outs,
        outs_one,
        grads.reshape(PLANES, 2, width // PLANES // 2, 3 * FF),
        (weights_exact, mixed_exact, qkv, first_in, wq_all, out_weight),
        tables,
        (mixed, sums, second_in, middle, cotangent, tokens),
        6,
    )
    up_sum, down_sum, qkv_sum, out_sum, misc_sum, router_sum = widen(
        table.reshape(experts + 1, width // PLANES, 3 * FF), q_all, o_all
    )
    return (
        output,
        grad_tokens,
        misc_sum[:, experts + 1],
        qkv_sum,
        out_sum,
        misc_sum[:, experts + 2],
        router_sum,
        up_sum,
        down_sum,
    )


def solution(mesh):
    fits = mesh.shape["wide"] == 8 and mesh.shape["narrow"] == PLANES
    return jax.shard_map(
        expert_local if fits else local,
        mesh=mesh,
        in_specs=(
            P(("wide", "narrow"), None),
            P(("wide", "narrow")),
            P(("wide", "narrow"), None),
            P(("wide", "narrow"), None),
            P(("wide", "narrow")),
            P(("wide", "narrow"), None),
            P(("wide", "narrow"), None),
            P(("wide", "narrow")),
            P(("wide", "narrow"), None),
            P(("wide", "narrow"), None, None),
            P(("wide", "narrow"), None, None),
        ),
        out_specs=(
            P(("wide", "narrow"), None),
            P(("wide", "narrow"), None),
            P("narrow"),
            P("narrow", None),
            P("narrow", None),
            P("narrow"),
            P("narrow", None),
            P("narrow", None, None),
            P("narrow", None, None),
        ),
        check_vma=False,
    )
```

```python
import jax
import jax.numpy as jnp
import numpy as np
from jax import lax
from jax.experimental import pallas as pl
from jax.experimental.pallas import tpu as pltpu
from jax.sharding import PartitionSpec as P

HEADS = 10
HEAD_DIM = 128
FF = 896
CAP = 72


epsilon = 1e-06


def shortened(x):
    return jax.tree.map(lambda a: a.astype(jnp.bfloat16) if a.dtype == jnp.float32 else a, x)


def rms_inverse(values):
    return lax.rsqrt(jnp.mean(values * values, axis=-1, keepdims=True) + epsilon)


def rotary(positions, head_size):
    half_dim = head_size // 2
    frequency = 10000.0 ** (-jnp.arange(half_dim, dtype=jnp.float32) / half_dim)
    angles = positions[:, None] * frequency[None, :]
    cosine = jnp.concatenate([jnp.cos(angles), jnp.cos(angles)], axis=1)[:, None, :]
    sine_table = jnp.concatenate([jnp.sin(angles), jnp.sin(angles)], axis=1)[:, None, :]
    return (cosine, sine_table)


def rotate(values, cosine, sine_table):
    half_dim = values.shape[-1] // 2
    turned = jnp.concatenate([-values[..., half_dim:], values[..., :half_dim]], axis=-1)
    return values * cosine + turned * sine_table


def rotate_back(grads, cosine, sine_table):
    half_dim = grads.shape[-1] // 2
    scaled = grads * sine_table
    turned = jnp.concatenate([scaled[..., half_dim:], -scaled[..., :half_dim]], axis=-1)
    return grads * cosine + turned


def expert_weight_terms(
    routed_in, routed_grad, shared_in, shared_grad, slot_grads, slot_acts, shared_grads, shared_acts
):
    up_routed = jnp.einsum(
        "ecd,ecf->def", routed_in, slot_grads, preferred_element_type=jnp.float32
    )
    up_shared = jnp.einsum("td,tf->df", shared_in, shared_grads, preferred_element_type=jnp.float32)
    down_routed = jnp.einsum(
        "ecd,ecf->def", routed_grad, slot_acts, preferred_element_type=jnp.float32
    )
    down_shared = jnp.einsum(
        "td,tf->df", shared_grad, shared_acts, preferred_element_type=jnp.float32
    )
    up_all = jnp.concatenate([up_shared[:, None], up_routed], axis=1)
    down_all = jnp.concatenate([down_shared[:, None], down_routed], axis=1)
    combined = jnp.concatenate([up_all, down_all], axis=2)
    return combined.reshape(combined.shape[0], -1)


def local(
    tokens, seq_ids, routes, cotangent, gain_attn, w_qkv, w_out, gain_ffn, w_router, w_up, w_down
):
    row_count = tokens.shape[0]
    model_width = tokens.shape[1]
    query_scale = HEAD_DIM ** (-0.5)
    hidden = FF
    capacity = CAP
    inputs = tokens.astype(jnp.float32)
    gain_one, qkv_weight, out_weight = (
        lax.all_gather(gain_attn, ("wide", "narrow"), axis=0, tiled=True),
        lax.all_gather(w_qkv, ("wide", "narrow"), axis=0, tiled=True),
        lax.all_gather(w_out, ("wide", "narrow"), axis=0, tiled=True),
    )
    inverse_one = rms_inverse(inputs)
    normed_one = inputs * inverse_one
    first_in = (normed_one * gain_one.astype(jnp.float32)).astype(jnp.bfloat16)
    projected = jnp.dot(first_in, qkv_weight, preferred_element_type=jnp.float32)
    offset = lax.axis_index("narrow") * row_count
    query_pos = offset + jnp.arange(row_count, dtype=jnp.int32)
    cosine, sine_table = rotary(query_pos.astype(jnp.float32), HEAD_DIM)
    query_rows = (
        rotate(projected[:, :model_width].reshape(row_count, HEADS, HEAD_DIM), cosine, sine_table)
        * query_scale
    ).astype(jnp.bfloat16)
    key_rows = (
        rotate(
            projected[:, model_width : 2 * model_width].reshape(row_count, HEADS, HEAD_DIM),
            cosine,
            sine_table,
        )
        .astype(jnp.bfloat16)
        .reshape(row_count, model_width)
    )
    value_rows = projected[:, 2 * model_width :].astype(jnp.bfloat16)
    all_keys, all_values, all_ids = (
        lax.all_gather(key_rows, "narrow", axis=0, tiled=True),
        lax.all_gather(value_rows, "narrow", axis=0, tiled=True),
        lax.all_gather(seq_ids.astype(jnp.bfloat16), "narrow", axis=0, tiled=True),
    )
    seqlen = all_keys.shape[0]
    block_len = min(512, seqlen)
    num_blocks = seqlen // block_len
    own_ids = seq_ids.astype(jnp.float32)

    def block_parts(block_index):
        first_row = block_index * block_len
        key_pos = first_row + jnp.arange(block_len, dtype=jnp.int32)
        key_ids = lax.dynamic_slice_in_dim(all_ids, first_row, block_len, 0).astype(jnp.float32)
        allowed = (key_pos[None, :] <= query_pos[:, None]) & (key_ids[None, :] == own_ids[:, None])
        key_block = lax.dynamic_slice_in_dim(all_keys, first_row, block_len, 0).reshape(
            block_len, HEADS, HEAD_DIM
        )
        value_block = lax.dynamic_slice_in_dim(all_values, first_row, block_len, 0).reshape(
            block_len, HEADS, HEAD_DIM
        )
        scores = jnp.einsum(
            "qhd,khd->hqk", query_rows, key_block, preferred_element_type=jnp.float32
        )
        return (allowed[None], key_block, value_block, scores)

    def max_step(state_pair, block_index):
        running_max, running_sum = state_pair
        allowed, key_block, value_block, scores = block_parts(block_index)
        masked = jnp.where(allowed, scores, -1e30)
        new_max = jnp.maximum(running_max, jnp.max(masked, axis=2))
        added = jnp.sum(jnp.where(allowed, jnp.exp(masked - new_max[..., None]), 0.0), axis=2)
        return ((new_max, running_sum * jnp.exp(running_max - new_max) + added), None)

    start_max = jnp.full((HEADS, row_count), -1e30, jnp.float32)
    start_sum = jnp.zeros((HEADS, row_count), jnp.float32)
    (top_score, exp_total), unused = lax.scan(
        max_step, (start_max, start_sum), jnp.arange(num_blocks)
    )
    log_total = top_score + jnp.log(exp_total)

    def out_step(accum, block_index):
        allowed, key_block, value_block, scores = block_parts(block_index)
        weights_low = jnp.where(allowed, jnp.exp(scores - log_total[..., None]), 0.0).astype(
            jnp.bfloat16
        )
        return (
            accum
            + jnp.einsum(
                "hqk,khd->hqd", weights_low, value_block, preferred_element_type=jnp.float32
            ),
            None,
        )

    accum_start = jnp.zeros((HEADS, row_count, HEAD_DIM), jnp.float32)
    mixed_heads, unused = lax.scan(out_step, accum_start, jnp.arange(num_blocks))
    mixed_exact = jnp.transpose(mixed_heads, (1, 0, 2))
    mixed = mixed_exact.reshape(row_count, model_width).astype(jnp.bfloat16)
    middle = inputs + jnp.dot(mixed, out_weight, preferred_element_type=jnp.float32)
    gain_two, router_weight, up_weight, down_weight = (
        lax.all_gather(gain_ffn, ("wide", "narrow"), axis=0, tiled=True),
        lax.all_gather(w_router, ("wide", "narrow"), axis=0, tiled=True),
        lax.all_gather(w_up, ("wide", "narrow"), axis=0, tiled=True),
        lax.all_gather(w_down, ("wide", "narrow"), axis=0, tiled=True),
    )
    inverse_two = rms_inverse(middle)
    normed_two = middle * inverse_two
    second_in = (normed_two * gain_two.astype(jnp.float32)).astype(jnp.bfloat16)
    logits = jnp.dot(second_in, router_weight, preferred_element_type=jnp.float32)
    router_probs = jax.nn.softmax(logits, axis=-1)
    experts = logits.shape[1]
    choose = routes[:, :, None] == jnp.arange(experts, dtype=jnp.int32)[None, None, :]
    member = jnp.sum(choose.astype(jnp.float32), axis=1)
    earlier = (jnp.arange(row_count)[:, None] > jnp.arange(row_count)[None, :]).astype(jnp.bfloat16)
    before = jnp.dot(earlier, member.astype(jnp.bfloat16), preferred_element_type=jnp.float32)
    slot_hit = (member.T[:, None, :] > 0.5) & (
        before.T[:, None, :] == jnp.arange(capacity, dtype=jnp.float32)[None, :, None]
    )
    dispatch = slot_hit.astype(jnp.bfloat16)
    gathered_in = jnp.einsum(
        "ect,td->ecd", dispatch, second_in, preferred_element_type=jnp.float32
    ).astype(jnp.bfloat16)
    gate_weights = router_probs * member
    gate_up = jnp.einsum(
        "ecd,def->ecf", gathered_in, up_weight[:, 1:], preferred_element_type=jnp.float32
    )
    gate_part = gate_up[..., :hidden]
    up_part = gate_up[..., hidden:]
    activated = (jax.nn.silu(gate_part) * up_part).astype(jnp.bfloat16)
    expert_rows = jnp.einsum(
        "ecf,def->ecd", activated, down_weight[:, 1:], preferred_element_type=jnp.float32
    ).astype(jnp.bfloat16)
    selected = jnp.einsum("ect,ecd->etd", dispatch, expert_rows, preferred_element_type=jnp.float32)
    routed = jnp.sum(gate_weights.T[:, :, None] * selected, axis=0)
    shared_up = jnp.dot(second_in, up_weight[:, 0], preferred_element_type=jnp.float32)
    shared_gate = shared_up[:, :hidden]
    shared_lin = shared_up[:, hidden:]
    shared_act = (jax.nn.silu(shared_gate) * shared_lin).astype(jnp.bfloat16)
    shared_out = jnp.einsum(
        "tf,df->td", shared_act, down_weight[:, 0], preferred_element_type=jnp.float32
    )
    output = (middle + shared_out + routed).astype(jnp.bfloat16)
    gain_two, router_weight, up_weight, down_weight = (
        lax.all_gather(gain_ffn, ("wide", "narrow"), axis=0, tiled=True),
        lax.all_gather(w_router, ("wide", "narrow"), axis=0, tiled=True),
        lax.all_gather(w_up, ("wide", "narrow"), axis=0, tiled=True),
        lax.all_gather(w_down, ("wide", "narrow"), axis=0, tiled=True),
    )
    grad_output = cotangent.astype(jnp.float32)
    slot_token = jnp.sum(
        jnp.where(slot_hit, jnp.arange(row_count, dtype=jnp.int32)[None, None, :], 0), axis=2
    )
    slot_gate = jnp.sum(jnp.where(slot_hit, gate_weights.T[:, None, :], 0.0), axis=2)
    grad_rows = (slot_gate[..., None] * grad_output[slot_token]).astype(jnp.bfloat16)
    grad_probs = jnp.sum(selected * grad_output[None], axis=2).T * member
    grad_logits = (
        router_probs * (grad_probs - jnp.sum(router_probs * grad_probs, axis=1, keepdims=True))
    ).astype(jnp.bfloat16)
    grad_act = jnp.einsum(
        "ecd,def->ecf", grad_rows, down_weight[:, 1:], preferred_element_type=jnp.float32
    )
    sigmoid_gate = jax.nn.sigmoid(gate_part)
    grad_gate_up = jnp.concatenate(
        [
            grad_act * up_part * sigmoid_gate * (1.0 + gate_part * (1.0 - sigmoid_gate)),
            grad_act * jax.nn.silu(gate_part),
        ],
        axis=-1,
    ).astype(jnp.bfloat16)
    grad_gathered = jnp.einsum(
        "ecf,def->ecd", grad_gate_up, up_weight[:, 1:], preferred_element_type=jnp.float32
    )
    slot_index = jnp.sum(jnp.where(choose, before[:, None, :], 0.0), axis=2).astype(jnp.int32)
    flat_index = routes * capacity + slot_index
    grad_second = jnp.sum(grad_gathered.reshape(-1, model_width)[flat_index], axis=1)
    grad_shared_act = jnp.einsum(
        "td,df->tf", cotangent, down_weight[:, 0], preferred_element_type=jnp.float32
    )
    sigmoid_shared = jax.nn.sigmoid(shared_gate)
    grad_shared_up = jnp.concatenate(
        [
            grad_shared_act
            * shared_lin
            * sigmoid_shared
            * (1.0 + shared_gate * (1.0 - sigmoid_shared)),
            grad_shared_act * jax.nn.silu(shared_gate),
        ],
        axis=-1,
    ).astype(jnp.bfloat16)
    grad_second = grad_second + jnp.einsum(
        "tf,df->td", grad_shared_up, up_weight[:, 0], preferred_element_type=jnp.float32
    )
    grad_second = grad_second + jnp.einsum(
        "te,de->td", grad_logits, router_weight, preferred_element_type=jnp.float32
    )
    grad_normed_two = grad_second * gain_two.astype(jnp.float32)
    grad_gain_two = jnp.sum(grad_second * normed_two, axis=0)
    grad_middle = grad_output + inverse_two * (
        grad_normed_two
        - normed_two * jnp.mean(grad_normed_two * normed_two, axis=-1, keepdims=True)
    )
    grad_router = jnp.einsum(
        "td,te->de", second_in, grad_logits, preferred_element_type=jnp.float32
    )
    narrow_rows = model_width // lax.axis_size("narrow")
    routed_cols, grad_cols, shared_cols, cotangent_cols = (
        lax.all_to_all(gathered_in, "narrow", split_axis=2, concat_axis=1, tiled=True),
        lax.all_to_all(grad_rows, "narrow", split_axis=2, concat_axis=1, tiled=True),
        lax.all_to_all(second_in[None], "narrow", split_axis=2, concat_axis=1, tiled=True),
        lax.all_to_all(cotangent[None], "narrow", split_axis=2, concat_axis=1, tiled=True),
    )
    slot_grads, slot_acts, shared_grads, shared_acts = (
        lax.all_gather(grad_gate_up, "narrow", axis=1, tiled=True),
        lax.all_gather(activated, "narrow", axis=1, tiled=True),
        lax.all_gather(grad_shared_up[None], "narrow", axis=1, tiled=True),
        lax.all_gather(shared_act[None], "narrow", axis=1, tiled=True),
    )
    expert_grads = expert_weight_terms(
        routed_cols,
        grad_cols,
        shared_cols[0],
        cotangent_cols[0],
        slot_grads,
        slot_acts,
        shared_grads[0],
        shared_acts[0],
    )
    gain_one, qkv_weight, out_weight = (
        lax.all_gather(gain_attn, ("wide", "narrow"), axis=0, tiled=True),
        lax.all_gather(w_qkv, ("wide", "narrow"), axis=0, tiled=True),
        lax.all_gather(w_out, ("wide", "narrow"), axis=0, tiled=True),
    )
    grad_attention = grad_middle.astype(jnp.bfloat16)
    grad_out_weight = jnp.einsum(
        "td,te->de", mixed, grad_attention, preferred_element_type=jnp.float32
    )
    grad_mixed = jnp.einsum(
        "te,de->td", grad_attention, out_weight, preferred_element_type=jnp.float32
    ).astype(jnp.bfloat16)
    grad_heads = grad_mixed.reshape(row_count, HEADS, HEAD_DIM)
    row_delta = jnp.sum(grad_heads.astype(jnp.float32) * mixed_exact, axis=2).T

    def back_step(grad_query, block_index):
        allowed, key_block, value_block, scores = block_parts(block_index)
        weights_exact = jnp.where(allowed, jnp.exp(scores - log_total[..., None]), 0.0)
        weights_low = weights_exact.astype(jnp.bfloat16)
        grad_value = jnp.einsum(
            "hqk,qhd->khd", weights_low, grad_heads, preferred_element_type=jnp.float32
        )
        grad_weights = jnp.einsum(
            "qhd,khd->hqk", grad_heads, value_block, preferred_element_type=jnp.float32
        )
        grad_scores = (weights_exact * (grad_weights - row_delta[..., None])).astype(jnp.bfloat16)
        grad_query = grad_query + jnp.einsum(
            "hqk,khd->qhd", grad_scores, key_block, preferred_element_type=jnp.float32
        )
        grad_key = jnp.einsum(
            "hqk,qhd->khd", grad_scores, query_rows, preferred_element_type=jnp.float32
        )
        return (
            grad_query,
            (grad_key.reshape(block_len, model_width), grad_value.reshape(block_len, model_width)),
        )

    query_start = jnp.zeros((row_count, HEADS, HEAD_DIM), jnp.float32)
    grad_query, (key_blocks, value_blocks) = lax.scan(
        back_step, query_start, jnp.arange(num_blocks)
    )
    key_partial = key_blocks.reshape(seqlen, model_width)
    value_partial = value_blocks.reshape(seqlen, model_width)
    grad_keys, grad_values = (
        lax.psum_scatter(
            key_partial.astype(jnp.bfloat16), "narrow", scatter_dimension=0, tiled=True
        ).astype(jnp.float32),
        lax.psum_scatter(
            value_partial.astype(jnp.bfloat16), "narrow", scatter_dimension=0, tiled=True
        ).astype(jnp.float32),
    )
    grad_query_raw = rotate_back(grad_query, cosine, sine_table) * query_scale
    grad_key_raw = rotate_back(grad_keys.reshape(row_count, HEADS, HEAD_DIM), cosine, sine_table)
    grad_projected = jnp.concatenate(
        [
            grad_query_raw.reshape(row_count, model_width),
            grad_key_raw.reshape(row_count, model_width),
            grad_values,
        ],
        axis=1,
    ).astype(jnp.bfloat16)
    grad_qkv_weight = jnp.einsum(
        "td,tf->df", first_in, grad_projected, preferred_element_type=jnp.float32
    )
    grad_first = jnp.einsum(
        "tf,df->td", grad_projected, qkv_weight, preferred_element_type=jnp.float32
    )
    grad_normed_one = grad_first * gain_one.astype(jnp.float32)
    grad_gain_one = jnp.sum(grad_first * normed_one, axis=0)
    grad_inputs = grad_middle + inverse_one * (
        grad_normed_one
        - normed_one * jnp.mean(grad_normed_one * normed_one, axis=-1, keepdims=True)
    )
    dense_parts = (
        lax.psum_scatter(
            grad_gain_one.astype(jnp.bfloat16), "narrow", scatter_dimension=0, tiled=True
        ).astype(jnp.float32),
        lax.psum_scatter(
            grad_qkv_weight.astype(jnp.bfloat16), "narrow", scatter_dimension=0, tiled=True
        ).astype(jnp.float32),
        lax.psum_scatter(
            grad_out_weight.astype(jnp.bfloat16), "narrow", scatter_dimension=0, tiled=True
        ).astype(jnp.float32),
        lax.psum_scatter(
            grad_gain_two.astype(jnp.bfloat16), "narrow", scatter_dimension=0, tiled=True
        ).astype(jnp.float32),
        lax.psum_scatter(
            grad_router.astype(jnp.bfloat16), "narrow", scatter_dimension=0, tiled=True
        ).astype(jnp.float32),
    )
    summed = jax.tree.map(
        lambda part: part.astype(jnp.float32),
        lax.psum(shortened((expert_grads,) + tuple(dense_parts)), "wide"),
    )
    expert_grads = summed[0]
    dense_parts = summed[1:]
    gain_one_sum, qkv_sum, out_sum, gain_two_sum, router_sum = dense_parts
    expert_table = expert_grads.reshape(narrow_rows, up_weight.shape[1], 3 * hidden)
    up_sum = expert_table[:, :, : 2 * hidden]
    down_sum = expert_table[:, :, 2 * hidden :]
    return (
        output,
        grad_inputs.astype(jnp.bfloat16),
        gain_one_sum,
        qkv_sum,
        out_sum,
        gain_two_sum,
        router_sum,
        up_sum,
        down_sum,
    )


PLANES = 4
WINDOW = 3
STARTS = (0, 3, 6, 7)
KEEP = ((0, 3), (0, 3), (0, 2), (1, 3))
MESH_IDS = pl.DeviceIdType.MESH
BF16 = jnp.bfloat16
F32 = jnp.float32


def place():
    w = lax.axis_index("wide")
    z = lax.axis_index("narrow")
    return w, z


def greet(w, z):
    barrier = pltpu.get_barrier_semaphore()
    peers = [(w, lax.rem(z + step, PLANES)) for step in (1, 2, 3)]
    peers += [(w ^ flip, z) for flip in (1, 2, 4, 6)]
    for peer in peers:
        pl.semaphore_signal(barrier, inc=1, device_id=peer, device_id_type=MESH_IDS)
    pl.semaphore_wait(barrier, len(peers))


def mul(a, b, over_a, over_b):
    return lax.dot_general(a, b, (((over_a,), (over_b,)), ((), ())), preferred_element_type=F32)


def at(start, size):
    return pl.ds(pl.multiple_of(start, 128), size)


def loop(first, last, body):
    def step(i, carry):
        body(i)
        return carry

    lax.fori_loop(first, last, step, 0)


class Links:
    def __init__(self, send_sems, recv_sems):
        self.w, self.z = place()
        self.send_sems, self.recv_sems = send_sems, recv_sems

    def copy(self, kind, step, src, dst, device):
        return pltpu.make_async_remote_copy(
            src_ref=src,
            dst_ref=dst,
            send_sem=self.send_sems.at[kind, step],
            recv_sem=self.recv_sems.at[kind, step],
            device_id=device,
            device_id_type=MESH_IDS,
        )

    def plane(self, step, sign):
        return lax.rem(self.z + PLANES + sign * step, PLANES)


def step_at(z, turn):
    step = 0
    for plane, steps in enumerate(((3, 2, 1, 0), (1, 3, 2, 0), (3, 1, 2, 0), (1, 2, 3, 0))):
        for number, value in enumerate(steps):
            step = jnp.where((z == plane) & (turn == number), value, step)
    return step


def direct_at(z, turn):
    even = lax.rem(z, 2) == 0
    first, second = jnp.where(even, 3, 1), jnp.where(even, 1, 3)
    return jnp.where(turn == 0, first, jnp.where(turn == 1, second, jnp.where(turn == 2, 2, 0)))


def send_next(z, send):
    @pl.when(z < PLANES - 1)
    def _():
        send(1)

    @pl.when(z > 0)
    def _():
        send(3)


def send_beyond(z, send):
    @pl.when(z == 0)
    def _():
        send(3)

    @pl.when(z == PLANES - 1)
    def _():
        send(1)

    send(2)


class Chain:
    def __init__(self, links, base, own, slot):
        self.links, self.base, self.own, self.slot = links, base, own, slot

    def goes(self, step, up):
        z = self.links.z
        if up:
            return (z >= step) & (z < PLANES - 1)
        return ((z < step) | (step == 0)) & (z > 0)

    def ring(self, step, up, own=False):
        links = self.links
        to = lax.rem(step + 1, 4) if up else lax.rem(step + 3, 4)
        ref = self.slot(links.plane(step, -1))
        return pltpu.make_async_remote_copy(
            src_ref=self.own if own else ref,
            dst_ref=ref,
            send_sem=links.send_sems.at[self.base if up else self.base + 1, step],
            recv_sem=links.recv_sems.at[self.base, to],
            device_id=(links.w, links.z + 1 if up else links.z - 1),
            device_id_type=MESH_IDS,
        )

    def hand_on(self, step, own=False):
        for up in (True, False):

            @pl.when(self.goes(step, up))
            def _():
                self.ring(step, up, own).start()

    def begin(self):
        self.hand_on(0, True)

    def arrive(self, turn):
        step = step_at(self.links.z, turn)
        ref = self.slot(self.links.plane(step, -1))
        self.links.copy(self.base, step, ref, ref, (self.links.w, self.links.z)).wait_recv()
        self.hand_on(step)

    def settle(self):
        def body(step):
            for up in (True, False):

                @pl.when(self.goes(step, up))
                def _():
                    self.ring(step, up).wait_send()

        loop(0, 4, body)


class Gather:
    def __init__(self, links, base, step, turn, slot, cores=True, half=0):
        self.links, self.base, self.step, self.slot, self.cores = links, base, step, slot, cores
        self.half = half
        self.first = 1 + lax.rem(turn, 2)
        self.second = 3 - self.first

    def copy(self, kind, owner, flip):
        ref = self.slot(owner)
        return self.links.copy(
            self.base + kind, self.step, ref, ref, (self.links.w ^ flip, self.links.z)
        )

    def begin(self):
        w = self.links.w
        self.copy(0, w, 2).start()
        self.copy(1, w, 4).start()
        if self.cores:
            self.copy(4, w, 1).start()

    def relay(self):
        w = self.links.w
        self.copy(0, w, 2).wait_recv()
        self.copy(1, w, 4).wait_recv()
        for copy in self.across():
            copy.start()
        if self.cores:
            self.copy(3, w ^ 2, 1).start()
            self.copy(5, w ^ 4, 1).start()

    def across(self):
        if not self.half:
            return [self.copy(2, self.links.w ^ (2 * self.first), 2 * self.second)]
        copies = []
        for kind, flip in ((2, 2), (7, 4)):
            ref = self.slot(self.links.w ^ flip).at[pl.ds((kind == 7) * self.half, self.half)]
            copies.append(
                self.links.copy(
                    self.base + kind, self.step, ref, ref, (self.links.w ^ (6 - flip), self.links.z)
                )
            )
        return copies

    def end(self):
        for copy in self.across():
            copy.wait_recv()
        if self.cores:
            self.copy(6, self.links.w ^ 6, 1).start()

    def settle(self):
        w = self.links.w
        self.copy(0, w, 2).wait_send()
        self.copy(1, w, 4).wait_send()
        for copy in self.across():
            copy.wait_send()
        if self.cores:
            for kind, owner in ((4, w), (3, w ^ 2), (5, w ^ 4), (6, w ^ 6)):
                copy = self.copy(kind, owner, 1)
                copy.wait_send()
                copy.wait_recv()


def softmax_rows(scores, mask):
    masked = scores + mask
    powers = jnp.exp(masked - jnp.max(masked, axis=1, keepdims=True))
    return powers * (1.0 / jnp.sum(powers, axis=1, keepdims=True))


def start_kernel(
    tok_in, wq_in, wo_in, seq_in, routes_in, router_in, gains_in, up_in, down_in, cot_in, cos_in, sin_in,
    we_o, cot_o, wq_out, wo_out, first_out, qkv_out, exact_out, mixed_out, mixed_rows_o, middle_o,
    second_o, hop,
    tok, ids, wq_blocks, wo_blocks, staged, mask, mixed_got, mixed_send, ids_in, we_in, cot_full,
    columns, misc_in, wq_o, wo_o, first_o, qkv_o, exact_o, mixed_o,
    load_sems, out_sems, send_sems, recv_sems,
):
    links = Links(send_sems, recv_sems)
    w, z = links.w, links.z
    chip = w // 2
    rows, width = tok_in.shape
    seqlen = PLANES * rows
    size = WINDOW * HEAD_DIM
    own = wo_in.shape[0]
    keeps = [
        pltpu.make_async_copy(src, dst, load_sems.at[i])
        for i, (src, dst) in enumerate(
            (
                (tok_in, tok.at[z]),
                (wo_in, wo_blocks.at[w, z]),
                (cot_full, cot_o.at[chip, z]),
            )
        )
    ]
    for keep in keeps[:2]:
        keep.start()
    window_starts = [jnp.int32(0)] * 4
    for plane, begin in enumerate(STARTS):
        for step in range(4):
            window_starts[step] = jnp.where(
                lax.rem(z + step, PLANES) == plane, begin, window_starts[step]
            )

    def window(step, kind):
        return wq_in.at[:, at(kind * width + window_starts[step] * HEAD_DIM, size)]

    def wq_own(kind):
        return pltpu.make_async_copy(
            window(0, kind),
            wq_blocks.at[w, z, :, pl.ds(kind * size, size)],
            load_sems.at[3 + kind],
        )

    for kind in range(3):
        wq_own(kind).start()
    routed = router_in.shape[0]
    columns[...] = jnp.zeros(columns.shape, F32)
    columns[1 : routed + 1, :own] = router_in[...].astype(F32)
    columns[routed + 1 : routed + 3, :own] = gains_in[...].astype(F32)
    misc_in[...] = jnp.transpose(columns[...])[:own, :].astype(BF16)
    wq_blocks[w, z, :, 3 * size :] = misc_in[...]
    row_ids = jnp.broadcast_to(seq_in[...].astype(F32), (rows, rows))
    ids_in[:rows, :] = row_ids.astype(BF16)
    ids_in[rows:, :] = jnp.transpose(row_ids).astype(BF16)
    ids[z] = ids_in[...]
    greet(w, z)

    tok_chain = Chain(links, 0, tok_in, lambda p: tok.at[p])
    ids_chain = Chain(links, 2, ids_in, lambda p: ids.at[p])
    wo_chain = Chain(links, 4, wo_in, lambda p: wo_blocks.at[w, p])
    cot_chain = Chain(links, 6, cot_full, lambda p: cot_o.at[chip, p])

    def wq_ring(step, kind):
        to = links.plane(step, 1)
        here = wq_blocks.at[w, z, :, pl.ds(kind * size, size if kind < 3 else 128)]
        src = window(step, kind) if kind < 3 else misc_in
        return links.copy(39 + kind if kind else 8, step, src, here, (w, to))

    def wq_gather(step):
        source = links.plane(step, -1)
        return Gather(links, 9, step, step, lambda i: wq_blocks.at[i, source])

    def wo_gather(turn):
        step = step_at(z, turn)
        source = links.plane(step, -1)
        return Gather(links, 16, step, turn, lambda i: wo_blocks.at[i, source])

    def cot_gather(turn):
        step = step_at(z, turn)
        source = links.plane(step, -1)
        return Gather(links, 23, step, turn, lambda i: cot_o.at[i // 2, source], False)

    def weights_ring(step, flip):
        to = links.plane(step, 1)
        return links.copy(
            26 + flip, step, we_in.at[to, chip ^ flip], hop.at[step - 1, chip ^ flip], (w, to)
        )

    def weights_step(turn):
        return 0 if turn == 3 else direct_at(z, turn)

    def weights_block(turn, flip):
        if turn == 3:
            return we_in.at[z, chip ^ flip]
        return hop.at[weights_step(turn) - 1, chip ^ flip]

    def weights_place(turn, owner):
        return we_o.at[owner, links.plane(weights_step(turn), -1)]

    def weights_plane(turn, flip):
        to = (w ^ (2 * flip), z)
        return links.copy(
            29 + flip, turn, weights_block(turn, flip), weights_place(turn, w), to
        )

    def weights_keep(turn):
        return pltpu.make_async_copy(
            weights_block(turn, 0), weights_place(turn, w), load_sems.at[6 + turn]
        )

    def weights_core(turn, flip):
        block = weights_place(turn, w ^ (2 * flip))
        return links.copy(
            34 + flip, turn, block if flip else weights_block(turn, 0), block, (w ^ 1, z)
        )

    def weights_send(step):
        for flip in (3, 1, 2, 0):
            weights_ring(step, flip).start()

    def weights_next(turn):
        for flip in (3, 1, 2):
            if turn < 3:
                weights_ring(weights_step(turn), flip).wait_recv()
            weights_plane(turn, flip).start()
        if turn < 3:
            weights_ring(weights_step(turn), 0).wait_recv()
        weights_core(turn, 0).start()
        weights_keep(turn).start()

    def weights_end(turn):
        for flip in (1, 2, 3):
            weights_plane(turn, flip).wait_recv()
            weights_core(turn, flip).start()

    def mixed_ring(step):
        to = links.plane(step, 1)
        return links.copy(38, step, mixed_send.at[to], mixed_got.at[z], (w, to))

    tok_chain.begin()
    ids_chain.begin()
    for step in (1, 2, 3):
        for kind in range(4):
            wq_ring(step, kind).start()
    for kind in range(3):
        wq_own(kind).wait()
    wq_gather(0).begin()
    for keep in keeps[:2]:
        keep.wait()

    expert = lax.broadcasted_iota(jnp.int32, (128, rows), 0)
    member = expert == 0
    for route in range(routes_in.shape[0]):
        member = member | (expert == routes_in[route : route + 1, :] + 1)
    cot_full[:, :width] = cot_in[...]
    cot_full[:, width:] = jnp.transpose(member.astype(F32)).astype(BF16)
    keeps[2].start()
    tok_chain.arrive(0)
    ids_chain.arrive(0)
    for step in (1, 2, 3):
        for kind in range(4):
            wq_ring(step, kind).wait_recv()
        wq_gather(step).begin()
    wo_chain.begin()
    tok_chain.arrive(1)
    ids_chain.arrive(1)
    cot_chain.begin()

    def experts_first(source, low):
        for i in range(0, source.shape[2], 128):
            part = jnp.swapaxes(source[:, :, i : i + 128].astype(F32), 0, 1).astype(BF16)
            for expert in range(source.shape[1]):
                we_in[expert % PLANES, expert // PLANES, :, low + i : low + i + 128] = part[expert]

    end_plane = (z == 0) | (z == PLANES - 1)

    @pl.when(jnp.logical_not(end_plane))
    def _():
        tok_chain.arrive(2)
        ids_chain.arrive(2)

    loop(0, 4, lambda step: wq_gather(step).relay())
    experts_first(up_in, 0)
    experts_first(down_in, up_in.shape[2])

    @pl.when(end_plane)
    def _():
        tok_chain.arrive(2)
        ids_chain.arrive(2)
        send_next(z, weights_send)

    wo_chain.arrive(0)
    wo_gather(0).begin()
    wo_gather(3).begin()
    keeps[2].wait()
    cot_gather(3).begin()
    weights_next(3)
    for i in range(PLANES):
        for j in range(PLANES):
            here = (slice(i * rows, (i + 1) * rows), slice(j * rows, (j + 1) * rows))
            if j > i:
                mask[here] = jnp.full((rows, rows), -1e30, F32)
            else:
                same = ids[i, rows:, :].astype(F32) == ids[j, :rows, :].astype(F32)
                if i == j:
                    same = same & (
                        lax.broadcasted_iota(jnp.int32, (rows, rows), 1)
                        <= lax.broadcasted_iota(jnp.int32, (rows, rows), 0)
                    )
                mask[here] = jnp.where(same, 0.0, -1e30)
    loop(0, 4, lambda step: wq_gather(step).end())
    loop(0, 4, lambda step: wq_gather(step).settle())

    def assemble(blocks, to):
        def body(i):
            for p in range(PLANES):
                staged[p * own : (p + 1) * own, :] = blocks[i, p].astype(F32)
            span = PLANES * own
            to[pl.ds(pl.multiple_of(i * span, 16), span), :] = staged[...].astype(BF16)

        loop(0, blocks.shape[0], body)

    cot_chain.arrive(0)
    cot_gather(0).begin()
    outputs = [
        pltpu.make_async_copy(src, dst, out_sems.at[i])
        for i, (src, dst) in enumerate(
            (
                (wq_o, wq_out),
                (first_o, first_out),
                (qkv_o, qkv_out),
                (exact_o, exact_out),
                (mixed_o, mixed_out),
                (wo_o, wo_out),
            )
        )
    ]
    assemble(wq_blocks, wq_o)
    outputs[0].start()
    gains = jnp.transpose(wq_o[:, size * 3 :].astype(F32))
    gain_one = gains[16:17, :]
    gain_two = gains[17:18, :]

    def normalise(p):
        block = tok[p].astype(F32)
        inverse = lax.rsqrt(jnp.mean(block * block, axis=1, keepdims=True) + epsilon)
        first_o[p] = (block * inverse * gain_one).astype(BF16)

    loop(0, PLANES, normalise)
    outputs[1].start()
    wo_chain.arrive(1)
    wo_gather(1).begin()
    cot_chain.arrive(1)
    cot_gather(1).begin()

    def project(p):
        span = pl.ds(pl.multiple_of(p * rows, 128), rows)
        cosine, sine = cos_in[span, :], sin_in[span, :]
        for kind in range(3):
            part = mul(first_o[p], wq_o[:, kind * size : (kind + 1) * size], 1, 0)
            for head in range(WINDOW):
                here = part[:, head * HEAD_DIM : (head + 1) * HEAD_DIM]
                if kind < 2:
                    here = here * cosine + pltpu.roll(here, HEAD_DIM // 2, 1) * sine
                if kind == 0:
                    here = here * (HEAD_DIM ** (-0.5))
                qkv_o[kind, head, span, :] = here.astype(BF16)

    loop(0, PLANES, project)
    outputs[2].start()
    wo_chain.arrive(2)
    wo_gather(2).begin()
    cot_chain.arrive(2)
    cot_gather(2).begin()

    @pl.when(jnp.logical_not(end_plane))
    def _():
        send_next(z, weights_send)

    def attend(head):
        exact = softmax_rows(mul(qkv_o[0, head], qkv_o[1, head], 1, 1), mask[...])
        exact_o[head] = exact
        mixed_o[head] = mul(exact.astype(BF16), qkv_o[2, head], 1, 0)

    loop(0, WINDOW, attend)
    outputs[3].start()
    outputs[4].start()
    for p in range(PLANES):
        for head in range(WINDOW):
            mixed_send[p, :, head * HEAD_DIM : (head + 1) * HEAD_DIM] = mixed_o[
                head, p * rows : (p + 1) * rows, :
            ].astype(BF16)
    for step in (1, 2, 3):
        mixed_ring(step).start()
    mixed_got[z] = mixed_send[z]
    send_beyond(z, weights_send)
    loop(0, 4, lambda turn: wo_gather(turn).relay())
    weights_next(0)
    loop(0, 4, lambda turn: wo_gather(turn).end())
    loop(0, 4, lambda turn: cot_gather(turn).relay())
    weights_end(3)
    weights_end(0)
    loop(0, 4, lambda turn: wo_gather(turn).settle())
    assemble(wo_blocks, wo_o)
    outputs[5].start()
    for step in (1, 2, 3):
        mixed_ring(step).wait_recv()
    column = 0
    for p, (a, b) in enumerate(KEEP):
        span = (b - a) * HEAD_DIM
        mixed_rows_o[:, column : column + span] = mixed_got[p, :, a * HEAD_DIM : b * HEAD_DIM]
        column += span

    def out_project(i):
        here = at(i * 256, 256)
        middle_o[:, here] = tok_in_f32(tok, z, here) + mul(mixed_rows_o[...], wo_o[:, here], 1, 0)

    loop(0, width // 256, out_project)
    middle = middle_o[...]
    inverse = lax.rsqrt(jnp.mean(middle * middle, axis=1, keepdims=True) + epsilon)
    second_o[...] = (middle * inverse * gain_two).astype(BF16)
    loop(0, 4, lambda turn: cot_gather(turn).end())
    weights_next(1)
    weights_next(2)
    weights_end(1)
    weights_end(2)
    loop(0, 4, lambda turn: cot_gather(turn).settle())
    for output in outputs:
        output.wait()
    for chain in (tok_chain, ids_chain, wo_chain, cot_chain):
        chain.settle()
    for step in (0, 1, 2, 3):
        weights_keep(step).wait()
        for flip in (0, 1, 2, 3):
            if step:
                weights_ring(step, flip).wait_send()
            if flip:
                weights_plane(step, flip).wait_send()
            weights_core(step, flip).wait_send()
            weights_core(step, flip).wait_recv()
        if step:
            for kind in range(4):
                wq_ring(step, kind).wait_send()
            mixed_ring(step).wait_send()


def tok_in_f32(tok, z, here):
    return tok[z, :, here].astype(F32)


def start(tok, wq, wo, seq, routes, router, gains, up, down, cot, tables, collective):
    rows, width = tok.shape
    own = wo.shape[0]
    experts = up.shape[1]
    hidden3 = up.shape[2] + down.shape[2]
    seqlen = PLANES * rows
    size = WINDOW * HEAD_DIM
    blocks = (8, PLANES, own, width)
    any_spec = pl.BlockSpec(memory_space=pl.ANY)
    vmem_spec = pl.BlockSpec(memory_space=pltpu.VMEM)
    kept = [
        ((width, width), BF16),
        ((width, width), BF16),
        ((PLANES, rows, width), BF16),
        ((3, WINDOW, seqlen, HEAD_DIM), BF16),
        ((WINDOW, seqlen, seqlen), F32),
        ((WINDOW, seqlen, HEAD_DIM), F32),
    ]
    shapes = [
        ((8, PLANES, own, hidden3), BF16),
        ((4, PLANES, rows, width + 128), BF16),
        *kept,
        ((rows, width), BF16),
        ((rows, width), F32),
        ((rows, width), BF16),
        ((3, 4, own, hidden3), BF16),
    ]
    return pl.pallas_call(
        start_kernel,
        out_shape=[jax.ShapeDtypeStruct(shape, kind) for shape, kind in shapes],
        in_specs=[any_spec] * 3 + [vmem_spec] * 9,
        out_specs=[any_spec] * 8 + [vmem_spec] * 3 + [any_spec],
        scratch_shapes=[
            pltpu.VMEM((PLANES, rows, width), BF16),
            pltpu.VMEM((PLANES, 2 * rows, rows), BF16),
            pltpu.VMEM(blocks, BF16),
            pltpu.VMEM(blocks, BF16),
            pltpu.VMEM((PLANES * own, width), F32),
            pltpu.VMEM((seqlen, seqlen), F32),
            pltpu.VMEM((PLANES, rows, size), BF16),
            pltpu.VMEM((PLANES, rows, size), BF16),
            pltpu.VMEM((2 * rows, rows), BF16),
            pltpu.VMEM((PLANES, experts // PLANES, own, hidden3), BF16),
            pltpu.VMEM((rows, width + 128), BF16),
            pltpu.VMEM((128, 128), F32),
            pltpu.VMEM((own, 128), BF16),
            *[pltpu.VMEM(shape, kind) for shape, kind in kept],
            pltpu.SemaphoreType.DMA((10,)),
            pltpu.SemaphoreType.DMA((6,)),
            pltpu.SemaphoreType.DMA((43, 4)),
            pltpu.SemaphoreType.DMA((43, 4)),
        ],
        compiler_params=pltpu.CompilerParams(
            collective_id=collective, has_side_effects=True, vmem_limit_bytes=60 * 2**20
        ),
        name="start",
    )(tok, wq, wo, seq, routes, router, gains, up, down, cot, *tables)[:-1]


def add_blocks(out, *terms):
    rows = out.shape[0]

    def body(i, carry):
        part = pl.ds(pl.multiple_of(i * 16, 16), 16)
        total = terms[0][part, :].astype(F32)
        for term in terms[1:]:
            total = total + term[part, :].astype(F32)
        out[part, :] = total.astype(out.dtype)
        return carry

    lax.fori_loop(0, rows // 16, body, 0)


def experts_kernel(
    x_in, cot_in, weights_in, misc_in, grads_o, outs_o, outs_one_o, sums_o,
    x, cot, weights, misc, act, scaled, slopes, gate, outs, parts, got_one, got_two, got_far, stage,
    load_sems, send_sems, recv_sems,
):
    w, z = place()
    chip = w // 2
    expert = chip * PLANES + z
    rows, width = x_in.shape
    hidden = weights.shape[1] // 3
    group_rows = 4 * rows

    def remote(kind, step, src, dst, device):
        return pltpu.make_async_remote_copy(
            src_ref=src,
            dst_ref=dst,
            send_sem=send_sems.at[kind, step],
            recv_sem=recv_sems.at[kind, step],
            device_id=device,
            device_id_type=MESH_IDS,
        )

    def plane_of(step, sign):
        return lax.rem(z + PLANES + sign * step, PLANES)

    def step_at(turn):
        step = 0
        for plane, steps in enumerate(((3, 2, 1, 0), (1, 3, 2, 0), (3, 1, 2, 0), (1, 2, 3, 0))):
            for number, value in enumerate(steps):
                step = jnp.where((z == plane) & (turn == number), value, step)
        return step

    def axes(turn):
        first = 1 + lax.rem(turn, 2)
        return first, 3 - first

    def ring(step, up):
        to = lax.rem(step + 1, 4) if up else lax.rem(step + 3, 4)
        return pltpu.make_async_remote_copy(
            src_ref=x.at[step, chip],
            dst_ref=x.at[to, chip],
            send_sem=send_sems.at[0 if up else 8, step],
            recv_sem=recv_sems.at[0, to],
            device_id=(w, z + 1 if up else z - 1),
            device_id_type=MESH_IDS,
        )

    def goes(step, up):
        if up:
            return (z >= step) & (z < PLANES - 1)
        return ((z < step) | (step == 0)) & (z > 0)

    def pass_on(step):
        for up in (True, False):

            @pl.when(goes(step, up))
            def _():
                ring(step, up).start()

    def arrive(step):
        pltpu.make_async_remote_copy(
            src_ref=x.at[step, chip],
            dst_ref=x.at[step, chip],
            send_sem=send_sems.at[0, step],
            recv_sem=recv_sems.at[0, step],
            device_id=(w, z),
            device_id_type=MESH_IDS,
        ).wait_recv()

    def direct(step, flip):
        block = x.at[step, chip]
        return remote(flip, step, block, block, (w ^ (2 * flip), z))

    def across(turn):
        first, second = axes(turn)
        step = step_at(turn)
        block = x.at[step, chip ^ first]
        return remote(3, step, block, block, (w ^ (2 * second), z))

    def near(turn, which):
        first, _ = axes(turn)
        step = step_at(turn)
        block = chip ^ 3 if which else chip ^ first
        return remote(
            4 + which, step, parts.at[step, block], got_one.at[step, which], (w ^ (2 * first), z)
        )

    def cross(turn):
        _, second = axes(turn)
        step = step_at(turn)
        return remote(
            6, step, parts.at[step, chip ^ second], got_two.at[step], (w ^ (2 * second), z)
        )

    def far(step):
        return remote(7, step, parts.at[step, chip], got_far.at[step - 1], (w, plane_of(step, -1)))

    def outs_near(step, which):
        first, _ = axes(step)
        block = chip ^ 3 if which else chip ^ first
        return remote(
            9 + which, step, outs_o.at[step, block], outs_one_o.at[step, which], (w ^ (2 * first), z)
        )

    def cot_load(step):
        return pltpu.make_async_copy(
            cot_in.at[:, plane_of(step, -1)], cot.at[step], load_sems.at[step]
        )

    def outs_out(turn):
        return pltpu.make_async_copy(
            outs.at[lax.rem(turn, 2)], outs_o.at[step_at(turn)], load_sems.at[9 + lax.rem(turn, 2)]
        )

    def grads_out(low, size, slot):
        return pltpu.make_async_copy(
            stage.at[slot, :, pl.ds(0, size)], grads_o.at[:, low], load_sems.at[4 + slot]
        )

    loads = [
        pltpu.make_async_copy(src, dst, load_sems.at[6 + i])
        for i, (src, dst) in enumerate(
            (
                (x_in, x.at[0, chip]),
                (misc_in.at[:, pl.ds(misc_in.shape[1] - 128, 128)], misc),
                (weights_in, weights),
            )
        )
    ]
    for load in loads:
        load.start()
    loop(0, 4, lambda step: cot_load(step).start())
    greet(w, z)
    loads[0].wait()
    pass_on(0)

    def begin(turn):
        step = step_at(turn)

        @pl.when(turn < 3)
        def _():
            arrive(step)
            pass_on(step)

        direct(step, 1).start()
        direct(step, 2).start()

    def relay(turn):
        step = step_at(turn)
        direct(step, 1).wait_recv()
        direct(step, 2).wait_recv()
        across(turn).start()

    begin(3)
    begin(0)
    begin(1)
    relay(0)
    begin(2)
    relay(1)
    loads[1].wait()
    loads[2].wait()

    def first_half(step):
        cot_load(step).wait()
        rows_in = x[step].reshape(group_rows, width)
        members = cot[step, :, :, width:].reshape(group_rows, 128).astype(F32)
        logits = mul(rows_in, misc[...], 1, 0)
        lane = lax.broadcasted_iota(jnp.int32, logits.shape, 1)
        routed = (lane > 0) & (lane < 16)
        top = jnp.max(jnp.where(routed, logits, -1e30), axis=1, keepdims=True)
        powers = jnp.where(routed, jnp.exp(logits - top), 0.0)
        probs = jnp.where(lane == 0, 1.0, powers / jnp.sum(powers, axis=1, keepdims=True))
        own = jnp.where(lane == expert, members, 0.0)
        gate[0] = jnp.broadcast_to(jnp.sum(probs * own, axis=1, keepdims=True), gate.shape[1:])
        gate[1] = own

        def hidden_chunk(low, size):
            here = x[step].reshape(group_rows, width)
            gate_part = mul(here, weights[:, at(low, size)], 1, 0)
            up_part = mul(here, weights[:, at(hidden + low, size)], 1, 0)
            grad_act = mul(
                cot[step, :, :, :width].reshape(group_rows, width),
                weights[:, at(2 * hidden + low, size)],
                1,
                0,
            )
            scale = gate[0][:, :1]
            grad_act = grad_act * scale
            sigmoid = 1.0 / (1.0 + jnp.exp(-gate_part))
            silu = gate_part * sigmoid
            activated = (silu * up_part).astype(BF16)
            act[:, at(low, size)] = activated
            scaled[step, :, at(low, size)] = (activated.astype(F32) * scale).astype(BF16)
            slopes[step, :, at(low, size)] = (
                grad_act * up_part * (sigmoid + silu * (1.0 - sigmoid))
            ).astype(BF16)
            slopes[step, :, at(hidden + low, size)] = (grad_act * silu).astype(BF16)

        loop(0, hidden // 256, lambda i: hidden_chunk(i * 256, 256))
        if hidden % 256:
            hidden_chunk(hidden // 256 * 256, hidden % 256)

    def second_half(turn, step):
        def width_body(i, total):
            low = i * 256
            expert_rows = mul(act[...], weights[at(low, 256), 2 * hidden :], 1, 1)
            expert_rows = expert_rows.astype(BF16).astype(F32)
            outs[lax.rem(turn, 2), :, :, at(low, 256)] = (
                (expert_rows * gate[0][:, :1]).astype(BF16).reshape(4, rows, 256)
            )
            product = expert_rows * cot[step, :, :, at(low, 256)].reshape(group_rows, 256).astype(F32)
            grad_in = mul(slopes[step], weights[at(low, 256), : 2 * hidden], 1, 1)
            parts[step, :, :, at(low, 256)] = grad_in.astype(BF16).reshape(4, rows, 256)
            return total + product[:, :128] + product[:, 128:]

        total = lax.fori_loop(0, width // 256, width_body, jnp.zeros((group_rows, 128), F32))
        prob = jnp.sum(total, axis=1, keepdims=True) * gate[1]
        high = prob.astype(BF16)
        low = (prob - high.astype(F32)).astype(BF16)
        low = pltpu.roll(low.astype(F32), 32, 1).astype(BF16)
        parts[step, :, :, width:] = (high + low).reshape(4, rows, 128)

    def send_cross(turn):
        _, second = axes(turn)
        step = step_at(turn)
        near(turn, 1).wait_recv()
        block = parts.at[step, chip ^ second]
        add_blocks(block, block, got_one.at[step, 1])
        cross(turn).start()

    def send_far(turn):
        step = step_at(turn)
        near(turn, 0).wait_recv()
        cross(turn).wait_recv()
        block = parts.at[step, chip]
        add_blocks(block, block, got_one.at[step, 0], got_two.at[step])
        far(step).start()

    def group(turn):
        step = step_at(turn)
        across(turn).wait_recv()
        first_half(step)

        @pl.when(turn < 2)
        def _():
            relay(turn + 2)

        @pl.when(turn > 1)
        def _():
            outs_out(turn - 2).wait()

        second_half(turn, step)
        outs_out(turn).start()

        near(turn, 1).start()

        @pl.when(turn > 0)
        def _():
            send_cross(turn - 1)

        near(turn, 0).start()

        @pl.when(turn > 1)
        def _():
            send_far(turn - 2)

    loop(0, 4, group)

    def weight_chunk(left, right, low, size, offset, i):
        slot = lax.rem(i, 2)

        @pl.when(i >= 2)
        def _():
            grads_out(pl.ds(0, 256), 256, slot).wait()

        total = None
        for step in range(4):
            term = mul(
                left[step, :, :, :width].reshape(group_rows, width), right[step, :, at(low, size)], 0, 0
            )
            total = term if total is None else total + term
        stage[slot, :, :size] = total.astype(BF16)
        grads_out(at(offset + low, size), size, slot).start()

    ups, downs = 2 * hidden // 256, hidden // 256

    def up_chunk(i):
        weight_chunk(x, slopes, i * 256, 256, 0, i)

    def down_chunk(i):
        weight_chunk(cot, scaled, (i - ups) * 256, 256, 2 * hidden, i)

    loop(0, 4, up_chunk)
    send_cross(3)
    outs_out(2).wait()
    outs_out(3).wait()
    loop(0, 4, lambda step: (outs_near(step, 1).start(), outs_near(step, 0).start()))
    loop(4, 6, up_chunk)
    send_far(2)
    loop(6, ups, up_chunk)
    loop(ups, ups + downs, down_chunk)
    last = ups + downs
    if hidden % 256:
        weight_chunk(cot, scaled, downs * 256, hidden % 256, 2 * hidden, jnp.int32(last))
        grads_out(pl.ds(0, 256), 256, (last - 1) % 2).wait()
        grads_out(pl.ds(0, hidden % 256), hidden % 256, last % 2).wait()
    else:
        grads_out(pl.ds(0, 256), 256, last % 2).wait()
        grads_out(pl.ds(0, 256), 256, (last - 1) % 2).wait()
    near(3, 0).wait_recv()
    cross(3).wait_recv()
    loop(1, 4, lambda step: far(step).wait_recv())
    add_blocks(
        sums_o,
        parts.at[0, chip],
        got_one.at[0, 0],
        got_two.at[0],
        got_far.at[0],
        got_far.at[1],
        got_far.at[2],
    )

    def settle(turn):
        step = step_at(turn)
        direct(step, 1).wait_send()
        direct(step, 2).wait_send()
        across(turn).wait_send()
        near(turn, 0).wait_send()
        near(turn, 1).wait_send()
        cross(turn).wait_send()
        for which in (0, 1):
            outs_near(turn, which).wait_send()
            outs_near(turn, which).wait_recv()

        @pl.when(turn < 3)
        def _():
            far(step).wait_send()

        for up in (True, False):

            @pl.when(goes(step, up))
            def _():
                ring(step, up).wait_send()

    loop(0, 4, settle)


def run_experts(second_in, cot_all, weights, misc, collective):
    rows, width = second_in.shape
    hidden = weights.shape[1] // 3
    sums_width = width + 128
    block = (rows, sums_width)
    return pl.pallas_call(
        experts_kernel,
        out_shape=[
            jax.ShapeDtypeStruct((width, 3 * hidden), BF16),
            jax.ShapeDtypeStruct((4, 4, rows, width), BF16),
            jax.ShapeDtypeStruct((4, 2, rows, width), BF16),
            jax.ShapeDtypeStruct((rows, sums_width), F32),
        ],
        in_specs=[pl.BlockSpec(memory_space=pl.ANY)] * 4,
        out_specs=[
            pl.BlockSpec(memory_space=pl.ANY),
            pl.BlockSpec(memory_space=pl.ANY),
            pl.BlockSpec(memory_space=pl.ANY),
            pl.BlockSpec(memory_space=pltpu.VMEM),
        ],
        scratch_shapes=[
            pltpu.VMEM((4, 4, rows, width), BF16),
            pltpu.VMEM((4, 4, rows, width + 128), BF16),
            pltpu.VMEM((width, 3 * hidden), BF16),
            pltpu.VMEM((width, 128), BF16),
            pltpu.VMEM((4 * rows, hidden), BF16),
            pltpu.VMEM((4, 4 * rows, hidden), BF16),
            pltpu.VMEM((4, 4 * rows, 2 * hidden), BF16),
            pltpu.VMEM((2, 4 * rows, 128), F32),
            pltpu.VMEM((2, 4, rows, width), BF16),
            pltpu.VMEM((4, 4) + block, BF16),
            pltpu.VMEM((4, 2) + block, BF16),
            pltpu.VMEM((4,) + block, BF16),
            pltpu.VMEM((3,) + block, BF16),
            pltpu.VMEM((2, width, 256), BF16),
            pltpu.SemaphoreType.DMA((11,)),
            pltpu.SemaphoreType.DMA((11, 4)),
            pltpu.SemaphoreType.DMA((11, 4)),
        ],
        compiler_params=pltpu.CompilerParams(
            collective_id=collective, has_side_effects=True, vmem_limit_bytes=62 * 2**20
        ),
        name="experts",
    )(second_in, cot_all, weights, misc)


def finish_kernel(
    outs_in, outs_one_in, grads_in, exact_in, mixed_in, qkv_in, first_in, wq_in, wo_in,
    cos_in, sin_in, rows_in, sums_in, second_in, middle_in, cot_in, tok_in,
    output_o, grad_o, table_o, q_o, o_o,
    outs, outs_one, outs_two, outs_far, grads_own, grads_got, heads, exact, mixed, qkv, first, wq,
    wo, heads_send, attn, grad_middle, first_got, projected, first_part, dense, dense_got, dense_one,
    dense_two, dense_far, dense_sum, load_sems, send_sems, recv_sems,
):
    links = Links(send_sems, recv_sems)
    w, z = links.w, links.z
    chip, core = w // 2, w % 2
    rows = outs.shape[2]
    width = outs.shape[3]
    size = WINDOW * HEAD_DIM
    steps = (1, 2, 3, 0)
    block_rows = o_o.shape[0] // 4
    half = o_o.shape[1] // 2
    plane_rows = o_o.shape[0]
    remote, plane_of = links.copy, links.plane

    def axes(step):
        one = 1 + lax.rem(step, 2)
        return one, 3 - one

    def heads_ring(step):
        to = plane_of(step, 1)
        return remote(37, step, heads_send.at[to], heads.at[z], (w, to))

    def grads_load(step):
        return pltpu.make_async_copy(
            grads_in.at[plane_of(step, 1), core], grads_own.at[step], load_sems.at[0, step]
        )

    def grads_swap(step):
        return remote(
            0, step, grads_in.at[plane_of(step, 1), 1 - core], grads_got.at[step], (w ^ 1, z)
        )

    def grads_ring(step):
        return remote(1, step, grads_own.at[step], table_o.at[chip, z, core], (w, plane_of(step, 1)))

    def grads_keep():
        return pltpu.make_async_copy(
            grads_own.at[0], table_o.at[chip, z, core], load_sems.at[1, 0]
        )

    def grads_gather(turn):
        step = direct_at(z, turn)
        source = plane_of(step, -1)
        half = grads_own.shape[1] // 2
        return Gather(
            links, 2, step, turn, lambda i: table_o.at[i // 2, source, i % 2], True, half
        )

    def outs_loads(step):
        _, two = axes(step)
        return [
            pltpu.make_async_copy(src, dst, load_sems.at[2 + 3 * (i > 0) + (i > 1), step])
            for i, (src, dst) in enumerate(
                (
                    (outs_in.at[step, chip], outs.at[step, 0]),
                    (outs_in.at[step, chip ^ two], outs.at[step, 1]),
                    (outs_one_in.at[step], outs_one.at[step]),
                )
            )
        ]

    def cross(step):
        _, two = axes(step)
        return remote(11, step, outs.at[step, 1], outs_two.at[step], (w ^ (2 * two), z))

    def far(step):
        return remote(12, step, outs.at[step, 0], outs_far.at[step - 1], (w, plane_of(step, -1)))

    def part(kind, step):
        return dense.at[0, kind, plane_of(step, 1)]

    def dense_swap(kind, step):
        to = plane_of(step, 1)
        return remote(
            13 + 4 * kind, step, dense.at[1, kind, to], dense_got.at[kind, step], (w ^ 1, z)
        )

    def rows_of(block):
        return pl.ds(pl.multiple_of(block * block_rows, 16), block_rows)

    def dense_axes(kind):
        return 1 + kind, 2 - kind

    def dense_near(kind, step, which):
        one, _ = dense_axes(kind)
        block = chip ^ 3 if which else chip ^ one
        return remote(
            14 + 4 * kind + which,
            step,
            part(kind, step).at[rows_of(block)],
            dense_one.at[kind, step, which],
            (w ^ (2 * one), z),
        )

    def dense_cross(kind, step):
        _, two = dense_axes(kind)
        return remote(
            16 + 4 * kind,
            step,
            part(kind, step).at[rows_of(chip ^ two)],
            dense_two.at[kind, step],
            (w ^ (2 * two), z),
        )

    def place_of(owner):
        return rows_of(owner // 2), at(lax.rem(owner, 2) * half, half)

    def dense_ring(kind, step):
        own = part(kind, step).at[rows_of(chip)]
        here, columns = place_of(w)
        to = q_o.at[z, here, columns] if kind == 0 else dense_far.at[step - 1]
        return remote(21 + kind, step, own, to, (w, plane_of(step, 1)))

    def dense_keep():
        here, columns = place_of(w)
        return pltpu.make_async_copy(
            part(0, 0).at[rows_of(chip)], q_o.at[z, here, columns], load_sems.at[1, 1]
        )

    def dense_last():
        here, columns = place_of(w)
        return pltpu.make_async_copy(dense_sum, o_o.at[here, columns], load_sems.at[1, 2])

    def q_slot(step):
        source = plane_of(step, -1)

        def slot(owner):
            here, columns = place_of(owner)
            return q_o.at[source, here, columns]

        return slot

    def o_slot(owner):
        here, columns = place_of(owner)
        return o_o.at[here, columns]

    def q_gather(step):
        return Gather(links, 23, step, step, q_slot(step))

    def o_gather():
        return Gather(links, 30, 0, 0, o_slot)

    def first_ring(step):
        to = plane_of(step, 1)
        return remote(38, step, first_part.at[to], first_got.at[step - 1], (w, to))

    loads = [
        pltpu.make_async_copy(src, dst, load_sems.at[3 + i // 4, i % 4])
        for i, (src, dst) in enumerate(
            (
                (wq_in, wq),
                (wo_in, wo),
                (exact_in, exact),
                (mixed_in, mixed),
                (qkv_in, qkv),
                (first_in, first),
            )
        )
    ]
    for step in range(4):
        for load in outs_loads(step):
            load.start()
    for load in loads[:2]:
        load.start()
    for step in steps:
        grads_load(step).start()
    for load in loads[2:]:
        load.start()
    greet(w, z)
    for step in steps:
        grads_swap(step).start()

    def grads_ready(step):
        grads_load(step).wait()
        grads_swap(step).wait_recv()
        add_blocks(grads_own.at[step], grads_own.at[step], grads_got.at[step])

    def outs_cross(step):
        for load in outs_loads(step):
            load.wait()
        add_blocks(outs.at[step, 1], outs.at[step, 1], outs_one.at[step, 1])
        cross(step).start()

    loop(0, 4, outs_cross)
    grads_ready(0)
    keep = grads_keep()
    keep.start()
    keep.wait()
    grads_gather(3).begin()
    for load in loads[:2]:
        load.wait()

    lane = lax.broadcasted_iota(jnp.int32, (rows, 128), 1)
    routed = (lane > 0) & (lane < 16)
    logits = jnp.where(routed, mul(second_in[...], wq[:, 3 * size :], 1, 0), -1e30)
    powers = jnp.where(routed, jnp.exp(logits - jnp.max(logits, axis=1, keepdims=True)), 0.0)
    probs = powers / jnp.sum(powers, axis=1, keepdims=True)
    high_low = sums_in[:, width:]
    grad_probs = jnp.where(routed, high_low + pltpu.roll(high_low, 96, 1), 0.0)
    grad_logits = probs * (grad_probs - jnp.sum(probs * grad_probs, axis=1, keepdims=True))
    grad_logits = grad_logits.astype(BF16)
    gains = jnp.transpose(wq[:, 3 * size :].astype(F32))
    gain_one, gain_two = gains[16:17, :], gains[17:18, :]
    grad_second = sums_in[:, :width] + mul(grad_logits, wq[:, 3 * size :], 1, 1)
    middle = middle_in[...]
    inverse = lax.rsqrt(jnp.mean(middle * middle, axis=1, keepdims=True) + epsilon)
    normed = middle * inverse
    grad_normed = grad_second * gain_two
    grad_here = cot_in[...].astype(F32) + inverse * (
        grad_normed - normed * jnp.mean(grad_normed * normed, axis=1, keepdims=True)
    )
    grad_middle[...] = grad_here
    attn[...] = grad_here.astype(BF16)
    gain_two_row = jnp.sum(grad_second * normed, axis=0, keepdims=True)
    router_part = mul(second_in[...], grad_logits, 0, 0)
    for plane, begin in enumerate(STARTS):
        grad_mixed = mul(
            attn[...], wo[begin * HEAD_DIM : begin * HEAD_DIM + size, :], 1, 1
        )
        heads_send[plane] = grad_mixed.astype(BF16)
    for step in (1, 2, 3):
        heads_ring(step).start()
    heads[z] = heads_send[z]
    loop(1, 4, grads_ready)
    for step in (1, 2, 3):
        heads_ring(step).wait_recv()
    send_next(z, lambda step: grads_ring(step).start())

    def out_weight(i):
        side = i // (half // 128)
        low = at((i - side * (half // 128)) * 128, 128)
        total = mul(rows_in[...], attn[:, at(i * 128, 128)], 0, 0).astype(BF16)
        dense[side ^ core, 1, :, :, low] = total.reshape(PLANES, plane_rows, 128)

    loop(0, width // 128, out_weight)
    for step in steps:
        dense_swap(1, step).start()
    for load in loads[2:]:
        load.wait()

    def head_back(head):
        keep_head = jnp.float32(0)
        for plane, (a, b) in enumerate(KEEP):
            keep_head = jnp.where((z == plane) & (head >= a) & (head < b), 1.0, keep_head)
        columns = at(head * HEAD_DIM, HEAD_DIM)
        grad_rows = heads[:, :, columns].reshape(PLANES * rows, HEAD_DIM).astype(F32) * keep_head
        delta = jnp.sum(grad_rows * mixed[head], axis=1, keepdims=True)
        grad_rows = grad_rows.astype(BF16)
        weights = exact[head]
        grad_value = mul(weights.astype(BF16), grad_rows, 0, 0)
        grad_scores = mul(grad_rows, qkv[2, head], 1, 1)
        grad_scores = (weights * (grad_scores - delta)).astype(BF16)
        grad_query = mul(grad_scores, qkv[1, head], 1, 0) * (HEAD_DIM ** (-0.5))
        grad_key = mul(grad_scores, qkv[0, head], 0, 0)

        def back(grads):
            return grads * cos_in[...] + pltpu.roll(grads * sin_in[...], HEAD_DIM // 2, 1)

        projected[:, columns] = back(grad_query).astype(BF16)
        projected[:, at(size + head * HEAD_DIM, HEAD_DIM)] = back(grad_key).astype(BF16)
        projected[:, at(2 * size + head * HEAD_DIM, HEAD_DIM)] = grad_value.astype(BF16)

    loop(0, WINDOW, head_back)

    def grads_next(turn):
        grads_ring(direct_at(z, turn)).wait_recv()
        grads_gather(turn).begin()

    grads_gather(3).relay()

    def qkv_weight(i):
        side = i // (half // 128)
        low = at((i - side * (half // 128)) * 128, 128)
        total = mul(first[...].reshape(PLANES * rows, width), projected[:, at(i * 128, 128)], 0, 0)
        dense[side ^ core, 0, :, :, low] = total.astype(BF16).reshape(PLANES, plane_rows, 128)

    loop(0, 3 * size // 128, qkv_weight)
    gain_parts = []
    for i in range(width // 256):
        here = slice(i * 256, (i + 1) * 256)
        total = mul(projected[...], wq[here, : 3 * size], 1, 1)
        first_part[:, :, here] = total.astype(BF16).reshape(PLANES, rows, 256)
        scaled = total * first[:, :, here].reshape(PLANES * rows, 256).astype(F32)
        gain_parts.append(jnp.sum(scaled, axis=0, keepdims=True))
    gain_one_row = jnp.concatenate(gain_parts, axis=1) / gain_one
    kind = lax.broadcasted_iota(jnp.int32, (128, width), 0)
    gain_rows = jnp.where(kind == 16, gain_one_row, jnp.where(kind == 17, gain_two_row, 0.0))
    misc = jnp.transpose(gain_rows) + router_part
    dense[1 ^ core, 0, :, :, half - 128 :] = misc.astype(BF16).reshape(PLANES, plane_rows, 128)
    for step in steps:
        dense_swap(0, step).start()

    loop(0, 1, grads_next)
    send_beyond(z, lambda step: grads_ring(step).start())

    def dense_ready(step):
        for kind in (0, 1):
            dense_swap(kind, step).wait_recv()
            block = part(kind, step)
            add_blocks(block, block, dense_got.at[kind, step])
            dense_near(kind, step, 1).start()
            dense_near(kind, step, 0).start()

    loop(0, 4, dense_ready)

    def outs_finish(step):
        cross(step).wait_recv()
        block = outs.at[step, 0]
        add_blocks(block, block, outs_one.at[step, 0], outs_two.at[step])

    loop(0, 4, outs_finish)
    grads_gather(0).relay()

    def dense_cross_start(step):
        for kind in (0, 1):
            _, two = dense_axes(kind)
            dense_near(kind, step, 1).wait_recv()
            block = part(kind, step).at[rows_of(chip ^ two)]
            add_blocks(block, block, dense_one.at[kind, step, 1])
            dense_cross(kind, step).start()

    loop(0, 4, dense_cross_start)
    loop(1, 3, grads_next)

    def dense_finish(step):
        for kind in (0, 1):
            dense_near(kind, step, 0).wait_recv()
            dense_cross(kind, step).wait_recv()
            block = part(kind, step).at[rows_of(chip)]
            add_blocks(block, block, dense_one.at[kind, step, 0], dense_two.at[kind, step])

        @pl.when(step > 0)
        def _():
            dense_ring(0, step).start()
            dense_ring(1, step).start()

    loop(0, 4, dense_finish)
    loop(1, 4, lambda step: far(step).start())
    loop(1, 4, lambda step: first_ring(step).start())
    keep = dense_keep()
    keep.start()
    grads_gather(3).end()
    grads_gather(0).end()
    grads_gather(1).relay()
    keep.wait()
    q_gather(0).begin()

    def q_next(step):
        dense_ring(0, step).wait_recv()
        q_gather(step).begin()
        dense_ring(1, step).wait_recv()

    loop(1, 4, q_next)
    add_blocks(
        dense_sum, part(1, 0).at[rows_of(chip)], dense_far.at[0], dense_far.at[1], dense_far.at[2]
    )
    keep = dense_last()
    keep.start()
    keep.wait()
    o_gather().begin()
    grads_gather(2).relay()
    grads_gather(1).end()
    loop(0, 4, lambda step: q_gather(step).relay())
    o_gather().relay()
    loop(1, 4, lambda step: far(step).wait_recv())

    def output_rows(i):
        here = pl.ds(pl.multiple_of(i * 16, 16), 16)
        total = middle_in[here, :] + outs[0, 0, here, :].astype(F32)
        for step in range(3):
            total = total + outs_far[step, here, :].astype(F32)
        output_o[here, :] = total.astype(BF16)

    loop(0, rows // 16, output_rows)
    for step in (1, 2, 3):
        first_ring(step).wait_recv()
    grad_first = first_part[z].astype(F32)
    for step in range(3):
        grad_first = grad_first + first_got[step].astype(F32)
    tokens = tok_in[...].astype(F32)
    inverse = lax.rsqrt(jnp.mean(tokens * tokens, axis=1, keepdims=True) + epsilon)
    normed = tokens * inverse
    grad_normed = grad_first * gain_one
    grad_o[...] = (
        grad_middle[...]
        + inverse
        * (grad_normed - normed * jnp.mean(grad_normed * normed, axis=1, keepdims=True))
    ).astype(BF16)
    loop(0, 4, lambda step: q_gather(step).end())
    o_gather().end()
    grads_gather(2).end()
    loop(0, 4, lambda turn: grads_gather(turn).settle())
    loop(0, 4, lambda step: q_gather(step).settle())
    o_gather().settle()

    def settle(step):
        grads_swap(step).wait_send()
        cross(step).wait_send()
        for kind in (0, 1):
            dense_swap(kind, step).wait_send()
            dense_near(kind, step, 0).wait_send()
            dense_near(kind, step, 1).wait_send()
            dense_cross(kind, step).wait_send()

    loop(0, 4, settle)

    def settle_rings(step):
        first_ring(step).wait_send()
        heads_ring(step).wait_send()
        grads_ring(step).wait_send()
        far(step).wait_send()
        dense_ring(0, step).wait_send()
        dense_ring(1, step).wait_send()

    loop(1, 4, settle_rings)


def finish(outs, outs_one, grads, saved, tables, at_rows, collective):
    exact, mixed, qkv, first, wq, wo = saved
    rows, width = first.shape[1:]
    seqlen = PLANES * rows
    size = WINDOW * HEAD_DIM
    plane_rows = width // PLANES
    block = (plane_rows // 4, width // 2)
    heads = (PLANES, rows, size)
    any_spec = pl.BlockSpec(memory_space=pl.ANY)
    vmem_spec = pl.BlockSpec(memory_space=pltpu.VMEM)
    return pl.pallas_call(
        finish_kernel,
        out_shape=[
            jax.ShapeDtypeStruct((rows, width), BF16),
            jax.ShapeDtypeStruct((rows, width), BF16),
            jax.ShapeDtypeStruct((4, PLANES) + grads.shape[1:], BF16),
            jax.ShapeDtypeStruct((PLANES, plane_rows, width), BF16),
            jax.ShapeDtypeStruct((plane_rows, width), BF16),
        ],
        in_specs=[any_spec] * 9 + [vmem_spec] * 8,
        out_specs=[vmem_spec] * 2 + [any_spec] * 3,
        scratch_shapes=[
            pltpu.VMEM((4, 2, rows, width), BF16),
            pltpu.VMEM((4, 2, rows, width), BF16),
            pltpu.VMEM((4, rows, width), BF16),
            pltpu.VMEM((3, rows, width), BF16),
            pltpu.VMEM((4,) + grads.shape[2:], BF16),
            pltpu.VMEM((4,) + grads.shape[2:], BF16),
            pltpu.VMEM(heads, BF16),
            pltpu.VMEM(exact.shape, F32),
            pltpu.VMEM(mixed.shape, F32),
            pltpu.VMEM(qkv.shape, BF16),
            pltpu.VMEM(first.shape, BF16),
            pltpu.VMEM(wq.shape, BF16),
            pltpu.VMEM(wo.shape, BF16),
            pltpu.VMEM(heads, BF16),
            pltpu.VMEM((rows, width), BF16),
            pltpu.VMEM((rows, width), F32),
            pltpu.VMEM((3, rows, width), BF16),
            pltpu.VMEM((seqlen, 3 * size), BF16),
            pltpu.VMEM(first.shape, BF16),
            pltpu.VMEM((2, 2, PLANES, plane_rows, width // 2), BF16),
            pltpu.VMEM((2, 4, plane_rows, width // 2), BF16),
            pltpu.VMEM((2, 4, 2) + block, BF16),
            pltpu.VMEM((2, 4) + block, BF16),
            pltpu.VMEM((3,) + block, BF16),
            pltpu.VMEM(block, BF16),
            pltpu.SemaphoreType.DMA((7, 4)),
            pltpu.SemaphoreType.DMA((39, 4)),
            pltpu.SemaphoreType.DMA((39, 4)),
        ],
        compiler_params=pltpu.CompilerParams(
            collective_id=collective, has_side_effects=True, vmem_limit_bytes=62 * 2**20
        ),
        name="finish",
    )(outs, outs_one, grads, *saved, *tables, *at_rows)


def widen_kernel(table, q, o, up_o, down_o, qkv_o, out_o, misc_o, router_o):
    columns = table.shape[2]
    split = up_o.shape[2]
    size = WINDOW * HEAD_DIM
    for low in range(0, columns, 128):
        part = jnp.swapaxes(table[:, :, low : low + 128].astype(F32), 0, 1)
        if low < split:
            up_o[:, :, low : low + 128] = part
        else:
            down_o[:, :, low - split : low - split + 128] = part
    out_o[...] = o[...].astype(F32)
    column = 0
    for kind in range(3):
        for plane, (a, b) in enumerate(KEEP):
            span = (b - a) * HEAD_DIM
            begin = kind * size + a * HEAD_DIM
            qkv_o[:, column : column + span] = q[plane, :, begin : begin + span].astype(F32)
            column += span
    total = q[0, :, 3 * size :].astype(F32)
    for plane in range(1, PLANES):
        total = total + q[plane, :, 3 * size :].astype(F32)
    misc_o[...] = total
    router_o[...] = total[:, 1 : 1 + router_o.shape[1]]


def widen(table, q, o):
    experts, rows, columns = table.shape
    width = o.shape[1]
    split = columns // 3 * 2
    step = rows // 4
    shapes = [
        (rows, experts, split),
        (rows, experts, columns - split),
        (rows, 3 * width),
        (rows, width),
        (rows, 128),
        (rows, experts - 1),
    ]
    return pl.pallas_call(
        widen_kernel,
        grid=(rows // step,),
        out_shape=[jax.ShapeDtypeStruct(shape, F32) for shape in shapes],
        in_specs=[
            pl.BlockSpec((experts, step, columns), lambda i: (0, i, 0)),
            pl.BlockSpec((PLANES, step, width), lambda i: (0, i, 0)),
            pl.BlockSpec((step, width), lambda i: (i, 0)),
        ],
        out_specs=[
            pl.BlockSpec((step,) + shape[1:], lambda i, n=len(shape): (i,) + (0,) * (n - 1))
            for shape in shapes
        ],
        compiler_params=pltpu.CompilerParams(vmem_limit_bytes=62 * 2**20),
        name="widen",
    )(table, q, o)


def windows(x):
    size = WINDOW * HEAD_DIM
    return jnp.stack([x[:, s * HEAD_DIM : s * HEAD_DIM + size] for s in STARTS])


def from_windows(x):
    return jnp.concatenate(
        [x[p, :, a * HEAD_DIM : b * HEAD_DIM] for p, (a, b) in enumerate(KEEP)], axis=1
    )


def dot(a, b, dims, out=F32):
    return lax.dot_general(a, b, ((dims[0], dims[1]), ((), ())), preferred_element_type=F32).astype(out)


def rotary_tables(seqlen):
    half_dim = HEAD_DIM // 2
    frequency = 10000.0 ** (-np.arange(half_dim, dtype=np.float32) / half_dim)
    angles = np.arange(seqlen, dtype=np.float32)[:, None] * frequency[None, :].astype(np.float32)
    cosine, sine = np.cos(angles), np.sin(angles)
    return (
        jnp.asarray(np.concatenate([cosine, cosine], axis=1), F32),
        jnp.asarray(np.concatenate([-sine, sine], axis=1), F32),
    )


def expert_local(
    tokens, seq_ids, routes, cotangent, gain_attn, w_qkv, w_out, gain_ffn, w_router, w_up, w_down
):
    rows, width = tokens.shape
    own = w_out.shape[0]
    experts = w_router.shape[1]
    seqlen = PLANES * rows
    size = WINDOW * HEAD_DIM

    tables = rotary_tables(seqlen)
    (
        we_all, cot_all, wq_all, out_weight, first_in, qkv, weights_exact, mixed_exact, mixed, middle,
        second_in,
    ) = start(
        tokens,
        w_qkv,
        w_out,
        seq_ids[None, :],
        routes.T,
        w_router.T,
        jnp.stack([gain_attn, gain_ffn]),
        w_up,
        w_down,
        cotangent,
        tables,
        1,
    )

    weights = we_all.reshape(width, 3 * FF)
    grads, outs, outs_one, sums = run_experts(second_in, cot_all, weights, wq_all, 3)

    output, grad_tokens, table, q_all, o_all = finish(
        outs,
        outs_one,
        grads.reshape(PLANES, 2, width // PLANES // 2, 3 * FF),
        (weights_exact, mixed_exact, qkv, first_in, wq_all, out_weight),
        tables,
        (mixed, sums, second_in, middle, cotangent, tokens),
        6,
    )
    up_sum, down_sum, qkv_sum, out_sum, misc_sum, router_sum = widen(
        table.reshape(experts + 1, width // PLANES, 3 * FF), q_all, o_all
    )
    return (
        output,
        grad_tokens,
        misc_sum[:, experts + 1],
        qkv_sum,
        out_sum,
        misc_sum[:, experts + 2],
        router_sum,
        up_sum,
        down_sum,
    )


def solution(mesh):
    fits = mesh.shape["wide"] == 8 and mesh.shape["narrow"] == PLANES
    return jax.shard_map(
        expert_local if fits else local,
        mesh=mesh,
        in_specs=(
            P(("wide", "narrow"), None),
            P(("wide", "narrow")),
            P(("wide", "narrow"), None),
            P(("wide", "narrow"), None),
            P(("wide", "narrow")),
            P(("wide", "narrow"), None),
            P(("wide", "narrow"), None),
            P(("wide", "narrow")),
            P(("wide", "narrow"), None),
            P(("wide", "narrow"), None, None),
            P(("wide", "narrow"), None, None),
        ),
        out_specs=(
            P(("wide", "narrow"), None),
            P(("wide", "narrow"), None),
            P("narrow"),
            P("narrow", None),
            P("narrow", None),
            P("narrow"),
            P("narrow", None),
            P("narrow", None, None),
            P("narrow", None, None),
        ),
        check_vma=False,
    )
```
